32 devices in a mesh: pair: 8 (over z, x), tp: 2 (over y), rep: 2 (over core).
Axes of the slice: x: 2, y: 2, z: 4, core: 2. Of those that a mesh axis runs over, the one named last changes fastest.
Arguments:
- normed: bfloat16 [2, 8, 8192], P(None, 'rep', 'pair'), parts along dimension 1, may hold values from -6 to 6
- w_query: bfloat16 [8192, 2048], P('pair', 'tp'), may hold values from -0.0625 to 0.0625
- b_query: float32 [2048], P('tp'), may hold values from -3 to 3
- w_key: bfloat16 [8192, 256], P('pair', 'tp'), may hold values from -0.25 to 0.25
- b_key: float32 [256], P('tp'), may hold values from -8 to 8
- w_value: bfloat16 [8192, 256], P('pair', 'tp'), may hold values from -0.0625 to 0.0625
- b_value: float32 [256], P('tp'), may hold values from -5 to 5
- w_out: bfloat16 [2048, 8192], P('tp', 'pair'), may hold values from -0.5 to 0.5
- pool: bfloat16 [16, 2, 512, 16, 256], P(('rep', 'pair'), 'tp'), parts along dimension 0, as said below
- page_table: int32 [16, 512], P(('rep', 'pair')), parts along dimension 0, may hold values from 0 to 511, as said below
- lengths: int32 [8], P('rep'), parts along dimension 0, may hold values from 8192 to 12286, as said below
- plan: int32 [8, 2], P('rep'), parts along dimension 0, may hold values from 0 to 64, as said below
Outputs:
- attended: float32 [2, 8, 8192], P(None, 'rep', 'pair'), parts along dimension 1
- new_pool: bfloat16 [16, 2, 512, 16, 256], P(('rep', 'pair'), 'tp'), parts along dimension 0
The draws below stay inside these ranges and needn't reach their ends.
There are 2 independent parts, one for each index of `rep`. The reference program is written for one: setup_inputs(seed, part) draws one part's arguments, and reference() takes and returns one part's arrays. A program takes and returns all parts, laid end to end along the dimension named above; an argument that names none is the same for every part. Nothing has to cross between parts.
Inputs may be any that keep to these rules, and one draw needn't show every extreme that they name: `pool`: cached keys (first 128 entries of a slot row, already rotated) and values. `page_table`: each row is an order of the 512 slots of one pool. `lengths`: some request reaches the most. `plan`: some entry reaches the most.
All inputs are finite; a program needn't handle non-finite values.
Results may differ from the reference program's by a relative error of at most 0.011.
The reference program's roundings to bfloat16 on the way count: a program that leaves them out, or rounds other values in their place, can miss the bound.
Values may be sent and summed in bfloat16 or wider, within the bound.
No kernel may reach another device: no remote copies, remote signals or barrier semaphores. Data moves between devices by JAX's collectives and lax.ppermute only.
A program may use at most 64 MiB of HBM per device.

```python
import math
import jax
import jax.numpy as jnp
from jax import lax

D = 8192
HD = 128
GROUP = 8
PAGE = 16
PAGES_HALF = 384
STEPS = 2
KV_HEADS = 2
Q_HEADS = 16
SECTION = 64
POOL_PAGES = 512
HALF = 6144
REQS = 4
N_PAIR = 8


def draw_pool(key, part):
    key = jax.random.fold_in(key, 11)
    key_part, value_part = jax.random.split(key, 2)
    half_shape = (N_PAIR, KV_HEADS, POOL_PAGES, PAGE, HD)
    key_rows = 1.5 * jax.random.normal(key_part, half_shape, jnp.float32)
    value_rows = jax.random.normal(value_part, half_shape, jnp.float32)
    return jnp.concatenate([key_rows, value_rows], -1).astype(jnp.bfloat16)


def draw_page_table(key, part):
    key = jax.random.fold_in(key, 12)
    row_keys = jax.random.split(key, N_PAIR)
    orders = jax.vmap(lambda row_key: jax.random.permutation(row_key, POOL_PAGES))(row_keys)
    return orders.astype(jnp.int32)


def draw_lengths(key, part):
    key = jax.random.fold_in(key, 13)
    spread_part, pick_part = jax.random.split(key, 2)
    lowest = HALF + PAGE * STEPS * SECTION
    span = HALF - PAGE * STEPS * SECTION - STEPS
    drawn = lowest + jax.random.randint(spread_part, (REQS,), 0, span + 1)
    chosen = jax.random.randint(pick_part, (), 0, REQS)
    return jnp.where(jnp.arange(REQS) == chosen, lowest + span, drawn).astype(jnp.int32)


def draw_plan(key, part):
    key = jax.random.fold_in(key, 14)
    count_part, pick_part = jax.random.split(key, 2)
    drawn = jax.random.randint(count_part, (REQS * STEPS,), 0, SECTION + 1)
    chosen = jax.random.randint(pick_part, (), 0, REQS * STEPS)
    filled = jnp.where(jnp.arange(REQS * STEPS) == chosen, SECTION, drawn)
    return filled.reshape(REQS, STEPS).astype(jnp.int32)


def block_scale(key, shape, cuts, low, largest):
    loudness, own = 1.0, jax.random.fold_in(key, 6)
    for axis_at, blocks in cuts:
        steps = jnp.exp(jax.random.uniform(jax.random.fold_in(own, axis_at), (blocks,), jnp.float32, low / len(cuts), largest / len(cuts)))
        loudness = loudness * jnp.repeat(steps, shape[axis_at] // blocks).reshape([-1 if axis == axis_at else 1 for axis in range(len(shape))])
    return loudness


def normal_values(stream_key, dims, spread, most, cuts=(), kind=jnp.bfloat16):
    gain = block_scale(stream_key, dims, cuts, -0.22, 0.18) if cuts else 1.0
    array = jax.random.normal(stream_key, dims, jnp.float32) * spread * gain
    return jnp.minimum(jnp.maximum(array, -most), most).astype(kind)


def setup_inputs(seed: int = 0, part: int = 0) -> dict:
    arg_keys = jax.random.split(jax.random.key(seed), 13)
    part_keys = jax.random.split(jax.random.fold_in(arg_keys[12], part), 13)
    normed = normal_values(part_keys[0], (STEPS, REQS, D), 1.0, 6.0, ((2, 8),))
    w_query = normal_values(arg_keys[1], (D, Q_HEADS * HD), D ** -0.5, 0.0625, ((0, 8), (1, 2)))
    b_query = normal_values(arg_keys[2], (Q_HEADS * HD,), 0.5, 3.0, ((0, 2),), jnp.float32)
    w_key = normal_values(arg_keys[3], (D, KV_HEADS * HD), (D // 16) ** -0.5, 0.25, ((0, 8), (1, 2)))
    b_key = normal_values(arg_keys[4], (KV_HEADS * HD,), 2.0, 8.0, ((0, 2),), jnp.float32)
    w_value = normal_values(arg_keys[5], (D, KV_HEADS * HD), D ** -0.5, 0.0625, ((0, 8), (1, 2)))
    b_value = normal_values(arg_keys[6], (KV_HEADS * HD,), 1.0, 5.0, ((0, 2),), jnp.float32)
    w_out = normal_values(arg_keys[7], (Q_HEADS * HD, D), HD ** -0.5, 0.5, ((0, 2), (1, 8)))
    pool = draw_pool(jax.random.fold_in(jax.random.fold_in(arg_keys[12], part), 71), part)
    page_table = draw_page_table(jax.random.fold_in(jax.random.fold_in(arg_keys[12], part), 71), part)
    lengths = draw_lengths(jax.random.fold_in(jax.random.fold_in(arg_keys[12], part), 71), part)
    plan = draw_plan(jax.random.fold_in(jax.random.fold_in(arg_keys[12], part), 71), part)
    return dict(normed=normed, w_query=w_query, b_query=b_query, w_key=w_key, b_key=b_key, w_value=w_value, b_value=b_value, w_out=w_out, pool=pool, page_table=page_table, lengths=lengths, plan=plan)


rope_base = 1000000.0

def rotate(vectors, position):
    half_size = vectors.shape[-1] // 2
    frequency = rope_base ** (-(jnp.arange(half_size, dtype=jnp.float32) * 2.0 / vectors.shape[-1]))
    angles = position * frequency
    cosine = jnp.cos(angles)
    sine_val = jnp.sin(angles)
    first_half = vectors[..., :half_size]
    second_half = vectors[..., half_size:]
    return jnp.concatenate([first_half * cosine - second_half * sine_val, second_half * cosine + first_half * sine_val], -1)

def reference(normed, w_query, b_query, w_key, b_key, w_value, b_value, w_out, pool, page_table, lengths, plan):
    score_scale = 1.0 / math.sqrt(HD)
    target_pools = [pool[request] for request in range(REQS)]
    source_pools = [pool[REQS + request] for request in range(REQS)]
    section_ids = jnp.arange(SECTION, dtype=jnp.int32)
    anchor = jnp.int32(0)
    results = []
    for step_index in range(STEPS):
        hidden = normed[step_index]
        query = jnp.dot(hidden, w_query, preferred_element_type=jnp.float32) + b_query
        key_new = jnp.dot(hidden, w_key, preferred_element_type=jnp.float32) + b_key
        value_new = jnp.dot(hidden, w_value, preferred_element_type=jnp.float32) + b_value
        position = (lengths + step_index).astype(jnp.float32)[:, None, None]
        query_rot = rotate(query.reshape(REQS, Q_HEADS, HD), position).astype(jnp.bfloat16)
        key_rot = rotate(key_new.reshape(REQS, KV_HEADS, HD), position).astype(jnp.bfloat16)
        value_rot = value_new.reshape(REQS, KV_HEADS, HD).astype(jnp.bfloat16)
        head_list = []
        for request in range(REQS):
            offset = (lengths[request] - HALF + step_index).astype(jnp.int32)
            write_slot = page_table[REQS + request, offset // PAGE].astype(jnp.int32)
            new_entry = jnp.concatenate([key_rot[request], value_rot[request]], -1)[:, None, None, :]
            source_pools[request] = lax.dynamic_update_slice(source_pools[request], new_entry, (anchor, write_slot, (offset % PAGE).astype(jnp.int32), anchor))
            before = jnp.sum(plan[request, :step_index]).astype(jnp.int32)
            page_picks = before + section_ids
            from_slots = page_table[REQS + request][page_picks]
            to_slots = page_table[request][PAGES_HALF + page_picks]
            keep_mask = section_ids < plan[request, step_index]
            moved = jnp.where(keep_mask[None, :, None, None], source_pools[request][:, from_slots], target_pools[request][:, to_slots])
            target_pools[request] = target_pools[request].at[:, to_slots].set(moved)
            own_pages = target_pools[request][:, page_table[request, :PAGES_HALF]]
            far_pages = source_pools[request][:, page_table[REQS + request, :PAGES_HALF]]
            context = jnp.concatenate([own_pages, far_pages], 1).reshape(KV_HEADS, 2 * HALF, 2 * HD)
            token_ids = jnp.arange(2 * HALF, dtype=jnp.int32)
            visible = token_ids <= lengths[request] + step_index
            key_rows = context[:, :, :HD].astype(jnp.float32)
            value_rows = context[:, :, HD:].astype(jnp.float32)
            head_query = query_rot[request].reshape(KV_HEADS, GROUP, HD).astype(jnp.float32)
            scores = jnp.einsum('hgd,htd->hgt', head_query, key_rows) * score_scale
            scores = jnp.where(visible[None, None, :], scores, -1e+30)
            row_max = lax.optimization_barrier(jnp.max(scores, -1, keepdims=True))
            weights = jnp.where(visible[None, None, :], jnp.exp(scores - row_max), 0.0)
            row_sum = lax.optimization_barrier(jnp.sum(weights, -1, keepdims=True))
            rounded = weights.astype(jnp.bfloat16).astype(jnp.float32)
            head_out = jnp.einsum('hgt,htd->hgd', rounded, value_rows) / row_sum
            head_list.append(head_out.reshape(Q_HEADS * HD))
        attended_rows = jnp.stack(head_list).astype(jnp.bfloat16)
        results.append(jnp.dot(attended_rows, w_out, preferred_element_type=jnp.float32))
    new_pool = jnp.stack(target_pools + source_pools)
    return (jnp.stack(results), new_pool)
```

```python
import functools
import math

import jax
import jax.numpy as jnp
from jax import lax
from jax.experimental import pallas as pl
from jax.experimental.pallas import tpu as pltpu
from jax.sharding import PartitionSpec as P

PAGES_HALF = 384
STEPS = 2
SECTION = 64
MOVED_MAX = STEPS * SECTION
CHUNKS = 8
NEG = -1e30

rope_base = 1000000.0


def gather_kernel(table, meta, pool, out, sem):
    @pl.when(meta[2] == 1)
    def _():
        def start(j, carry):
            pltpu.make_async_copy(pool.at[table[j]], out.at[j], sem).start()
            return carry

        lax.fori_loop(0, MOVED_MAX, start, 0, unroll=8)
        pltpu.make_async_copy(pool.at[pl.ds(0, MOVED_MAX)], out, sem).wait()


def gather_pages(table, meta, pool):
    return pl.pallas_call(
        gather_kernel,
        out_shape=jax.ShapeDtypeStruct((MOVED_MAX,) + pool.shape[1:], pool.dtype),
        grid_spec=pltpu.PrefetchScalarGridSpec(
            num_scalar_prefetch=2,
            in_specs=[pl.BlockSpec(memory_space=pl.ANY)],
            out_specs=pl.BlockSpec(memory_space=pl.ANY),
            scratch_shapes=[pltpu.SemaphoreType.DMA],
        ),
        name="gather_pages",
    )(table, meta, pool)


def scatter_kernel(table, meta, pages, base, out, sem):
    del base
    count = jnp.where(meta[2] == 1, 0, meta[3])

    def start(j, carry):
        pltpu.make_async_copy(pages.at[j], out.at[table[PAGES_HALF + j]], sem).start()
        return carry

    def wait(j, carry):
        pltpu.make_async_copy(pages.at[0], out.at[0], sem).wait()
        return carry

    lax.fori_loop(0, count, start, 0)
    lax.fori_loop(0, count, wait, 0)


def scatter_pages(table, meta, pages, base):
    return pl.pallas_call(
        scatter_kernel,
        out_shape=jax.ShapeDtypeStruct(base.shape, base.dtype),
        grid_spec=pltpu.PrefetchScalarGridSpec(
            num_scalar_prefetch=2,
            in_specs=[pl.BlockSpec(memory_space=pl.ANY), pl.BlockSpec(memory_space=pl.ANY)],
            out_specs=pl.BlockSpec(memory_space=pl.ANY),
            scratch_shapes=[pltpu.SemaphoreType.DMA],
        ),
        input_output_aliases={3: 0},
        name="scatter_pages",
    )(table, meta, pages, base)


def attention_kernel(
    table, meta, sums, bias, cosine, sine, tokens, pool, new_pool, packed, buf, score, in_sems, out_sems, page_sems
):
    slots, page_len, _ = buf.shape
    per = slots // CHUNKS
    width = per * page_len
    head = cosine.shape[1]
    group = sums.shape[2] // head - 2
    rows = STEPS * group

    def fetch(c):
        return pltpu.make_async_copy(
            pool.at[pl.ds(c * per, per)], buf.at[pl.ds(c * per, per)], in_sems.at[c]
        )

    def store(c):
        return pltpu.make_async_copy(
            buf.at[pl.ds(c * per, per)], new_pool.at[pl.ds(c * per, per)], out_sems.at[c]
        )

    for c in range(CHUNKS):
        fetch(c).start()

    total = sums[0]
    for p in range(1, sums.shape[0]):
        total = total + sums[p]
    total = total + bias[...]
    pieces = []
    for s in range(STEPS):
        for h in range(group):
            pieces.append(total[s : s + 1, h * head : (h + 1) * head])
    query = jnp.concatenate(pieces, 0)
    row = lax.broadcasted_iota(jnp.int32, (rows, head), 0)
    cos_rows = jnp.where(row < group, cosine[0:1], cosine[1:2])
    sin_rows = jnp.where(row < group, sine[0:1], sine[1:2])
    query = (query * cos_rows + pltpu.roll(query, head // 2, 1) * sin_rows).astype(jnp.bfloat16)
    key_new = total[:, group * head : (group + 1) * head]
    key_new = jnp.concatenate([key_new, jnp.zeros((8 - STEPS, head), jnp.float32)], 0)
    cos_new = jnp.concatenate([cosine[...], jnp.zeros((8 - STEPS, head), jnp.float32)], 0)
    sin_new = jnp.concatenate([sine[...], jnp.zeros((8 - STEPS, head), jnp.float32)], 0)
    key_new = (key_new * cos_new + pltpu.roll(key_new, head // 2, 1) * sin_new).astype(jnp.bfloat16)
    value_new = total[:, (group + 1) * head :].astype(jnp.bfloat16)
    scale = 1.0 / math.sqrt(head)
    limit = meta[0]
    is_source = meta[2] == 1

    column = lax.broadcasted_iota(jnp.int32, (rows, 1), 0)
    query_wide = query.astype(jnp.float32)
    fresh = []
    for s in range(STEPS):
        dots = jnp.sum(query_wide * key_new[s : s + 1].astype(jnp.float32), 1, keepdims=True) * scale
        seen = jnp.logical_and(is_source, column >= s * group)
        fresh.append((jnp.where(seen, dots, NEG), seen))
    row_max = jnp.maximum(fresh[0][0], fresh[1][0])
    for c in range(CHUNKS):
        fetch(c).wait()
        store(c).start()
        keys = buf[c * per : (c + 1) * per, :, :head].reshape(width, head)
        part = lax.dot_general(query, keys, (((1,), (1,)), ((), ())), preferred_element_type=jnp.float32)
        visible = tokens[:, c * width : (c + 1) * width] < limit
        part = jnp.where(visible, part * scale, NEG)
        score[:, c * width : (c + 1) * width] = part
        row_max = jnp.maximum(row_max, jnp.max(part, 1, keepdims=True))
    row_sum = jnp.zeros((rows, 1), jnp.float32)
    out = jnp.zeros((rows, head), jnp.float32)
    for s in range(STEPS):
        weight = jnp.where(fresh[s][1], jnp.exp(fresh[s][0] - row_max), 0.0)
        row_sum = row_sum + weight
        out = out + weight.astype(jnp.bfloat16).astype(jnp.float32) * value_new[s : s + 1].astype(jnp.float32)
    for c in range(CHUNKS):
        visible = tokens[:, c * width : (c + 1) * width] < limit
        weight = jnp.where(visible, jnp.exp(score[:, c * width : (c + 1) * width] - row_max), 0.0)
        row_sum = row_sum + jnp.sum(weight, 1, keepdims=True)
        values = buf[c * per : (c + 1) * per, :, head:].reshape(width, head)
        out = out + jnp.dot(weight.astype(jnp.bfloat16), values, preferred_element_type=jnp.float32)

    lane = lax.broadcasted_iota(jnp.int32, (rows, head), 1)
    diagonal = lane == row
    packed[0:rows] = out
    packed[rows : rows + 1] = jnp.sum(jnp.where(diagonal, row_max, 0.0), 0, keepdims=True)
    packed[rows + 1 : rows + 2] = jnp.sum(jnp.where(diagonal, row_sum, 0.0), 0, keepdims=True)
    packed[rows + 2 :] = jnp.zeros((packed.shape[0] - rows - 2, head), jnp.float32)

    for c in range(CHUNKS):
        store(c).wait()

    @pl.when(is_source)
    def _():
        page_row = lax.broadcasted_iota(jnp.int32, (page_len, 2 * head), 0)
        for s in range(STEPS):
            offset = meta[1] + s
            slot = table[offset // page_len]
            entry = jnp.concatenate([key_new[s : s + 1], value_new[s : s + 1]], 1)
            fixed = jnp.where(
                page_row == offset % page_len, entry.astype(jnp.float32), buf[slot].astype(jnp.float32)
            )
            buf[slot] = fixed.astype(jnp.bfloat16)
            copy = pltpu.make_async_copy(buf.at[slot], new_pool.at[slot], page_sems.at[s])
            copy.start()
            copy.wait()


def attend(table, meta, sums, bias, cosine, sine, tokens, pool):
    head = cosine.shape[1]
    rows = STEPS * (sums.shape[2] // head - 2)
    packed_rows = rows + 8
    vmem = pl.BlockSpec(memory_space=pltpu.VMEM)
    return pl.pallas_call(
        attention_kernel,
        out_shape=(
            jax.ShapeDtypeStruct(pool.shape, pool.dtype),
            jax.ShapeDtypeStruct((packed_rows, head), jnp.float32),
        ),
        grid_spec=pltpu.PrefetchScalarGridSpec(
            num_scalar_prefetch=2,
            in_specs=[vmem] * 5 + [pl.BlockSpec(memory_space=pl.ANY)],
            out_specs=(pl.BlockSpec(memory_space=pl.ANY), vmem),
            scratch_shapes=[
                pltpu.VMEM(pool.shape, pool.dtype),
                pltpu.VMEM((rows, pool.shape[0] * pool.shape[1]), jnp.float32),
                pltpu.SemaphoreType.DMA((CHUNKS,)),
                pltpu.SemaphoreType.DMA((CHUNKS,)),
                pltpu.SemaphoreType.DMA((STEPS,)),
            ],
        ),
        compiler_params=pltpu.CompilerParams(vmem_limit_bytes=24 * 1024 * 1024),
        name="attend",
    )(table, meta, sums, bias, cosine, sine, tokens, pool)


def project_kernel(parts, w_out, out):
    pairs, packed_rows, head = parts.shape
    rows = packed_rows - 8
    group = rows // STEPS
    requests = pairs // 2
    lane = lax.broadcasted_iota(jnp.int32, (rows, head), 1)
    diagonal = lane == lax.broadcasted_iota(jnp.int32, (rows, head), 0)

    def as_column(line):
        return jnp.sum(jnp.where(diagonal, line, 0.0), 1, keepdims=True)

    merged = []
    for r in range(requests):
        first_max, first_sum = (as_column(parts[r, rows + i : rows + i + 1]) for i in range(2))
        second_max, second_sum = (as_column(parts[r + requests, rows + i : rows + i + 1]) for i in range(2))
        top = jnp.maximum(first_max, second_max)
        first_weight = jnp.exp(first_max - top)
        second_weight = jnp.exp(second_max - top)
        joined = first_weight * parts[r, :rows] + second_weight * parts[r + requests, :rows]
        merged.append(joined / (first_weight * first_sum + second_weight * second_sum))
    lines = []
    for s in range(STEPS):
        for r in range(requests):
            lines.append(
                jnp.concatenate(
                    [merged[r][s * group + h : s * group + h + 1] for h in range(group)], 1
                )
            )
    attended = jnp.concatenate(lines, 0).astype(jnp.bfloat16)
    out[...] = jnp.dot(attended, w_out[...], preferred_element_type=jnp.float32)


def project(parts, w_out):
    vmem = pl.BlockSpec(memory_space=pltpu.VMEM)
    return pl.pallas_call(
        project_kernel,
        out_shape=jax.ShapeDtypeStruct((STEPS * parts.shape[0] // 2, w_out.shape[1]), jnp.float32),
        in_specs=[vmem, vmem],
        out_specs=vmem,
        compiler_params=pltpu.CompilerParams(vmem_limit_bytes=24 * 1024 * 1024),
        name="project",
    )(parts, w_out)


def local(
    normed, w_query, b_query, w_key, b_key, w_value, b_value, w_out, pool, page_table, lengths, plan
):
    pair_count = lax.axis_size("pair")
    tp_count = lax.axis_size("tp")
    requests = pair_count // 2
    pair_index = lax.axis_index("pair")
    request_index = pair_index % requests
    source = pair_index >= requests
    head = w_key.shape[1]
    kv_store = pool[0, 0]
    table = page_table[0]
    slot_count, page_len, _ = kv_store.shape
    half_tokens = PAGES_HALF * page_len
    picker = jnp.arange(requests, dtype=jnp.int32) == request_index
    length = jnp.sum(jnp.where(picker, lengths, 0))
    moved = jnp.sum(jnp.where(picker[:, None], plan, 0))
    offset = length - half_tokens
    limit = jnp.where(source, offset, half_tokens)
    meta = jnp.stack([limit, offset, source.astype(jnp.int32), moved]).astype(jnp.int32)

    outgoing = gather_pages(table, meta, kv_store)
    route = [(i + requests, i) for i in range(requests)]
    incoming = lax.ppermute(outgoing, "pair", route)

    slot_ids = jnp.arange(slot_count, dtype=jnp.int32)
    inverse = jnp.sum(jnp.where(table[:, None] == slot_ids[None, :], slot_ids[:, None], 0), 0)
    tokens = (inverse[:, None] * page_len + jnp.arange(page_len, dtype=jnp.int32)[None, :]).reshape(1, -1)

    hidden = normed.reshape(STEPS * requests, normed.shape[2])
    partial = jnp.concatenate(
        [jnp.dot(hidden, w, preferred_element_type=jnp.float32) for w in (w_query, w_key, w_value)], 1
    )
    by_request = partial.reshape(STEPS, requests, partial.shape[1]).transpose(1, 0, 2)
    sums = lax.all_to_all(
        jnp.concatenate([by_request, by_request], 0), "pair", split_axis=0, concat_axis=0, tiled=True
    )
    bias = jnp.concatenate([b_query, b_key, b_value])[None, :]
    frequency = rope_base ** (-(jnp.arange(head // 2, dtype=jnp.float32) * 2.0 / head))
    position = (length + jnp.arange(STEPS, dtype=jnp.int32)).astype(jnp.float32)[:, None]
    angles = position * frequency[None, :]
    cosine = jnp.cos(angles)
    sine = jnp.sin(angles)
    cosine = jnp.concatenate([cosine, cosine], 1)
    sine = jnp.concatenate([-sine, sine], 1)

    new_pool, packed = attend(table, meta, sums, bias, cosine, sine, tokens, kv_store)
    spread = jnp.broadcast_to(packed[None], (pair_count,) + packed.shape)
    parts = lax.all_to_all(spread, "pair", split_axis=0, concat_axis=0, tiled=True)
    projected = project(parts, w_out)
    if tp_count == 2:
        projected = projected + lax.ppermute(projected, "tp", [(0, 1), (1, 0)])
    else:
        projected = lax.psum(projected, "tp")
    attended = projected.reshape(STEPS, requests, w_out.shape[1])
    new_pool = scatter_pages(table, meta, incoming, new_pool)
    return attended, new_pool[None, None]


def solution(mesh):
    return jax.shard_map(
        local,
        mesh=mesh,
        in_specs=(
            P(None, "rep", "pair"),
            P("pair", "tp"),
            P("tp"),
            P("pair", "tp"),
            P("tp"),
            P("pair", "tp"),
            P("tp"),
            P("tp", "pair"),
            P(("rep", "pair"), "tp", None, None, None),
            P(("rep", "pair"), None),
            P("rep"),
            P("rep", None),
        ),
        out_specs=(P(None, "rep", "pair"), P(("rep", "pair"), "tp", None, None, None)),
        check_vma=False,
    )
```

```python
import math

import jax
import jax.numpy as jnp
from jax import lax
from jax.experimental import pallas as pl
from jax.experimental.pallas import tpu as pltpu
from jax.sharding import PartitionSpec as P

PAGES_HALF = 384
STEPS = 2
SECTION = 64
MOVED_MAX = STEPS * SECTION
CHUNKS = 8
NEG = -1e30

rope_base = 1000000.0

VMEM = pl.BlockSpec(memory_space=pltpu.VMEM)
SMEM = pl.BlockSpec(memory_space=pltpu.SMEM)
HBM = pl.BlockSpec(memory_space=pltpu.HBM)


def params(mib):
    return pltpu.CompilerParams(vmem_limit_bytes=mib * 1024 * 1024)


def prepare_kernel(table, normed, w_query, w_key, w_value, pool, partial, held, first, rest, sems):
    slots = held.shape[0]
    per = slots // CHUNKS
    pairs = partial.shape[0]
    requests = pairs // 2
    wide = w_query.shape[1]
    head = w_key.shape[1]

    def fetch(c):
        part = pl.ds(c * per, per)
        return pltpu.make_async_copy(pool.at[part], held.at[part], sems.at[c])

    for c in range(CHUNKS):
        fetch(c).start()
    hidden = jnp.concatenate([normed[s].astype(jnp.float32) for s in range(STEPS)], 0).astype(jnp.bfloat16)
    start = 0
    for weight, width in ((w_query, wide), (w_key, head), (w_value, head)):
        result = jnp.dot(hidden, weight[...], preferred_element_type=jnp.float32)
        for p in range(pairs):
            for s in range(STEPS):
                row = s * requests + p % requests
                partial[p, s : s + 1, start : start + width] = result[row : row + 1]
        start += width
    for c in range(CHUNKS):
        fetch(c).wait()

    def sort_first(j, carry):
        first[j] = held[table[0, j]]
        return carry

    def sort_rest(j, carry):
        rest[j] = held[table[0, MOVED_MAX + j]]
        return carry

    lax.fori_loop(0, first.shape[0], sort_first, 0, unroll=8)
    lax.fori_loop(0, rest.shape[0], sort_rest, 0, unroll=8)


def prepare(table, normed, w_query, w_key, w_value, pool, pairs):
    page = pool.shape[1:]
    wide = w_query.shape[1] + 2 * w_key.shape[1]
    return pl.pallas_call(
        prepare_kernel,
        out_shape=(
            jax.ShapeDtypeStruct((pairs, STEPS, wide), jnp.float32),
            jax.ShapeDtypeStruct(pool.shape, pool.dtype),
            jax.ShapeDtypeStruct((MOVED_MAX,) + page, pool.dtype),
            jax.ShapeDtypeStruct((PAGES_HALF - MOVED_MAX,) + page, pool.dtype),
        ),
        in_specs=[SMEM, VMEM, VMEM, VMEM, VMEM, HBM],
        out_specs=(VMEM, VMEM, VMEM, VMEM),
        scratch_shapes=[pltpu.SemaphoreType.DMA((CHUNKS,))],
        compiler_params=params(32),
        name="prepare",
    )(table, normed, w_query, w_key, w_value, pool)


def attention_kernel(lengths, sums, b_query, b_key, b_value, cosine, sine, first, rest, packed, entries, score):
    requests = sums.shape[0] // 2
    page_len = first.shape[1]
    group, head = b_query.shape
    rows = STEPS * group
    pair_index = lax.axis_index("pair")
    is_source = pair_index >= requests
    request = jnp.where(is_source, pair_index - requests, pair_index)
    half_tokens = PAGES_HALF * page_len
    limit = jnp.where(is_source, lengths[request] - half_tokens, half_tokens)

    total = sums[0]
    for p in range(1, sums.shape[0]):
        total = total + sums[p]
    query = jnp.concatenate(
        [total[s : s + 1, h * head : (h + 1) * head] for s in range(STEPS) for h in range(group)], 0
    )
    query = query + jnp.concatenate([b_query[...]] * STEPS, 0)
    cos_new = cosine[request]
    sin_new = sine[request]
    row = lax.broadcasted_iota(jnp.int32, (rows, head), 0)
    cos_rows = jnp.where(row < group, cos_new[0:1], cos_new[1:2])
    sin_rows = jnp.where(row < group, sin_new[0:1], sin_new[1:2])
    query = (query * cos_rows + pltpu.roll(query, head // 2, 1) * sin_rows).astype(jnp.bfloat16)
    key_new = total[:, group * head : (group + 1) * head] + b_key[...]
    key_new = jnp.concatenate([key_new, jnp.zeros((8 - STEPS, head), jnp.float32)], 0)
    key_new = key_new * cos_new + pltpu.roll(key_new, head // 2, 1) * sin_new
    key_new = key_new.astype(jnp.bfloat16).astype(jnp.float32)
    value_new = total[:, (group + 1) * head :] + b_value[...]
    value_new = value_new.astype(jnp.bfloat16).astype(jnp.float32)
    entries[:, :head] = key_new
    entries[0:STEPS, head:] = value_new
    entries[STEPS:, head:] = jnp.zeros((8 - STEPS, head), jnp.float32)
    scale = 1.0 / math.sqrt(head)

    column = lax.broadcasted_iota(jnp.int32, (rows, 1), 0)
    query_wide = query.astype(jnp.float32)
    fresh = []
    for s in range(STEPS):
        dots = jnp.sum(query_wide * key_new[s : s + 1], 1, keepdims=True) * scale
        seen = jnp.logical_and(is_source, column >= s * group)
        fresh.append((jnp.where(seen, dots, NEG), seen))
    row_max = jnp.maximum(fresh[0][0], fresh[1][0])

    per = 64
    width = per * page_len
    blocks = [(ref, i, i + per) for ref in (first, rest) for i in range(0, ref.shape[0], per)]
    lane = lax.broadcasted_iota(jnp.int32, (rows, width), 1)
    for c, (ref, low, high) in enumerate(blocks):
        keys = ref[low:high, :, :head].reshape(width, head)
        part = lax.dot_general(query, keys, (((1,), (1,)), ((), ())), preferred_element_type=jnp.float32)
        part = jnp.where(lane < limit - c * width, part * scale, NEG)
        score[:, c * width : (c + 1) * width] = part
        row_max = jnp.maximum(row_max, jnp.max(part, 1, keepdims=True))
    row_sum = jnp.zeros((rows, 1), jnp.float32)
    out = jnp.zeros((rows, head), jnp.float32)
    for s in range(STEPS):
        weight = jnp.where(fresh[s][1], jnp.exp(fresh[s][0] - row_max), 0.0)
        row_sum = row_sum + weight
        out = out + weight.astype(jnp.bfloat16).astype(jnp.float32) * value_new[s : s + 1]
    for c, (ref, low, high) in enumerate(blocks):
        weight = jnp.exp(score[:, c * width : (c + 1) * width] - row_max)
        weight = jnp.where(lane < limit - c * width, weight, 0.0)
        row_sum = row_sum + jnp.sum(weight, 1, keepdims=True)
        values = ref[low:high, :, head:].reshape(width, head)
        out = out + jnp.dot(weight.astype(jnp.bfloat16), values, preferred_element_type=jnp.float32)

    diagonal = lax.broadcasted_iota(jnp.int32, (rows, head), 1) == row
    packed[0:rows] = out
    packed[rows : rows + 1] = jnp.sum(jnp.where(diagonal, row_max, 0.0), 0, keepdims=True)
    packed[rows + 1 : rows + 2] = jnp.sum(jnp.where(diagonal, row_sum, 0.0), 0, keepdims=True)
    packed[rows + 2 :] = jnp.zeros((packed.shape[0] - rows - 2, head), jnp.float32)


def attend(lengths, sums, b_query, b_key, b_value, cosine, sine, first, rest):
    group, head = b_query.shape
    rows = STEPS * group
    tokens = PAGES_HALF * first.shape[1]
    return pl.pallas_call(
        attention_kernel,
        out_shape=(
            jax.ShapeDtypeStruct((rows + 8, head), jnp.float32),
            jax.ShapeDtypeStruct((8, 2 * head), jnp.float32),
        ),
        in_specs=[SMEM] + [VMEM] * 8,
        out_specs=(VMEM, VMEM),
        scratch_shapes=[pltpu.VMEM((rows, tokens), jnp.float32)],
        compiler_params=params(24),
        name="attend",
    )(lengths, sums, b_query, b_key, b_value, cosine, sine, first, rest)


def project_kernel(parts, w_out, out):
    pairs, packed_rows, head = parts.shape
    rows = packed_rows - 8
    group = rows // STEPS
    requests = pairs // 2
    lane = lax.broadcasted_iota(jnp.int32, (rows, head), 1)
    diagonal = lane == lax.broadcasted_iota(jnp.int32, (rows, head), 0)

    def as_column(line):
        return jnp.sum(jnp.where(diagonal, line, 0.0), 1, keepdims=True)

    merged = []
    for r in range(requests):
        first_max, first_sum = (as_column(parts[r, rows + i : rows + i + 1]) for i in range(2))
        second_max, second_sum = (as_column(parts[r + requests, rows + i : rows + i + 1]) for i in range(2))
        top = jnp.maximum(first_max, second_max)
        first_weight = jnp.exp(first_max - top)
        second_weight = jnp.exp(second_max - top)
        joined = first_weight * parts[r, :rows] + second_weight * parts[r + requests, :rows]
        merged.append(joined / (first_weight * first_sum + second_weight * second_sum))
    lines = []
    for s in range(STEPS):
        for r in range(requests):
            lines.append(
                jnp.concatenate(
                    [merged[r][s * group + h : s * group + h + 1] for h in range(group)], 1
                )
            )
    attended = jnp.concatenate(lines, 0).astype(jnp.bfloat16)
    out[...] = jnp.dot(attended, w_out[...], preferred_element_type=jnp.float32)


def project(parts, w_out):
    return pl.pallas_call(
        project_kernel,
        out_shape=jax.ShapeDtypeStruct((STEPS * parts.shape[0] // 2, w_out.shape[1]), jnp.float32),
        in_specs=[VMEM, VMEM],
        out_specs=VMEM,
        compiler_params=params(16),
        name="project",
    )(parts, w_out)


def finish_kernel(table, lengths, plan, entries, pages, held_in, held, new_pool, sems):
    del held_in
    slots, page_len, width = held.shape
    requests = lengths.shape[0]
    pair_index = lax.axis_index("pair")
    is_source = pair_index >= requests

    @pl.when(is_source)
    def _():
        page_row = lax.broadcasted_iota(jnp.int32, (page_len, width), 0)
        first_new = lengths[pair_index - requests] - PAGES_HALF * page_len
        for s in range(STEPS):
            offset = first_new + s
            slot = table[0, offset // page_len]
            old = held[slot].astype(jnp.float32)
            held[slot] = jnp.where(page_row == offset % page_len, entries[s : s + 1], old).astype(held.dtype)

    @pl.when(jnp.logical_not(is_source))
    def _():
        def place(j, carry):
            held[table[0, PAGES_HALF + j]] = pages[j]
            return carry

        count = plan[pair_index, 0]
        for s in range(1, STEPS):
            count = count + plan[pair_index, s]
        lax.fori_loop(0, count, place, 0)

    per = slots // CHUNKS

    def store(c):
        part = pl.ds(c * per, per)
        return pltpu.make_async_copy(held.at[part], new_pool.at[part], sems.at[c])

    for c in range(CHUNKS):
        store(c).start()
    for c in range(CHUNKS):
        store(c).wait()


def finish(table, lengths, plan, entries, pages, held):
    return pl.pallas_call(
        finish_kernel,
        out_shape=(
            jax.ShapeDtypeStruct(held.shape, held.dtype),
            jax.ShapeDtypeStruct(held.shape, held.dtype),
        ),
        in_specs=[SMEM, SMEM, SMEM, VMEM, VMEM, VMEM],
        out_specs=(VMEM, HBM),
        scratch_shapes=[pltpu.SemaphoreType.DMA((CHUNKS,))],
        input_output_aliases={5: 0},
        compiler_params=params(24),
        name="finish",
    )(table, lengths, plan, entries, pages, held)[1]


def local(
    normed, w_query, b_query, w_key, b_key, w_value, b_value, w_out, pool, page_table, lengths, plan
):
    pair_count = lax.axis_size("pair")
    tp_count = lax.axis_size("tp")
    requests = pair_count // 2
    head = w_key.shape[1]

    partial, held, first, rest = prepare(
        page_table, normed, w_query, w_key, w_value, pool[0, 0], pair_count
    )
    route = [(i + requests, i) for i in range(requests)]
    incoming = lax.ppermute(first, "pair", route)
    sums = lax.all_to_all(partial, "pair", split_axis=0, concat_axis=0, tiled=True)

    frequency = rope_base ** (-(jnp.arange(head // 2, dtype=jnp.float32) * 2.0 / head))
    steps = jnp.minimum(jnp.arange(8, dtype=jnp.int32), STEPS - 1)
    position = (lengths[:, None] + steps[None, :]).astype(jnp.float32)[..., None]
    angles = position * frequency
    cosine = jnp.cos(angles)
    sine = jnp.sin(angles)
    cosine = jnp.concatenate([cosine, cosine], -1)
    sine = jnp.concatenate([-sine, sine], -1)

    packed, entries = attend(
        lengths,
        sums,
        b_query.reshape(-1, head),
        b_key[None, :],
        b_value[None, :],
        cosine,
        sine,
        first,
        rest,
    )
    spread = jnp.broadcast_to(packed[None], (pair_count,) + packed.shape)
    parts = lax.all_to_all(spread, "pair", split_axis=0, concat_axis=0, tiled=True)
    projected = project(parts, w_out)
    if tp_count == 2:
        projected = projected + lax.ppermute(projected, "tp", [(0, 1), (1, 0)])
    else:
        projected = lax.psum(projected, "tp")
    attended = projected.reshape(STEPS, requests, w_out.shape[1])
    new_pool = finish(page_table, lengths, plan, entries, incoming, held)
    return attended, new_pool[None, None]


def solution(mesh):
    return jax.shard_map(
        local,
        mesh=mesh,
        in_specs=(
            P(None, "rep", "pair"),
            P("pair", "tp"),
            P("tp"),
            P("pair", "tp"),
            P("tp"),
            P("pair", "tp"),
            P("tp"),
            P("tp", "pair"),
            P(("rep", "pair"), "tp", None, None, None),
            P(("rep", "pair"), None),
            P("rep"),
            P("rep", None),
        ),
        out_specs=(P(None, "rep", "pair"), P(("rep", "pair"), "tp", None, None, None)),
        check_vma=False,
    )
```

```python
import math

import jax
import jax.numpy as jnp
from jax import lax
from jax.experimental import pallas as pl
from jax.experimental.pallas import tpu as pltpu
from jax.sharding import PartitionSpec as P

PAGES_HALF = 384
STEPS = 2
SECTION = 64
MOVED_MAX = STEPS * SECTION
PIECES = (16, 16, 96, 128, 128)
MOVED_PIECES = 3
CHUNKS = 8
NEG = -1e30

rope_base = 1000000.0

VMEM = pl.BlockSpec(memory_space=pltpu.VMEM)
SMEM = pl.BlockSpec(memory_space=pltpu.SMEM)
HBM = pl.BlockSpec(memory_space=pltpu.HBM)


def in_hbm(*arrays):
    return tuple(pltpu.with_memory_space_constraint(a, pltpu.HBM) for a in arrays)


def params(mib):
    return pltpu.CompilerParams(vmem_limit_bytes=mib * 1024 * 1024)


def prepare_kernel(
    table, normed, w_query, w_key, w_value, pool, partial, *refs
):
    pieces, (held, order, w_all, sems, out_sems, w_sems) = refs[: len(refs) - 6], refs[len(refs) - 6 :]
    slots = held.shape[0]
    per = slots // CHUNKS
    pairs = partial.shape[0]
    requests = pairs // 2
    head = w_key.shape[1]

    weights = []
    start = 0
    for i, weight in enumerate((w_query, w_key, w_value)):
        part = w_all.at[:, start : start + weight.shape[1]]
        weights.append(pltpu.make_async_copy(weight, part, w_sems.at[i]))
        start += weight.shape[1]

    def fetch(c):
        part = pl.ds(c * per, per)
        return pltpu.make_async_copy(pool.at[part], held.at[part], sems.at[c])

    for copy in weights:
        copy.start()
    for c in range(CHUNKS):
        fetch(c).start()
    hidden = jnp.concatenate([normed[s].astype(jnp.float32) for s in range(STEPS)], 0).astype(jnp.bfloat16)
    for copy in weights:
        copy.wait()
    result = jnp.dot(hidden, w_all[...], preferred_element_type=jnp.float32)
    for p in range(pairs):
        for s in range(STEPS):
            row = s * requests + p % requests
            partial[p, s : s + 1] = result[row : row + 1]
    for c in range(CHUNKS):
        fetch(c).wait()

    def sort(j, carry):
        order[j] = held[table[0, j]]
        return carry

    copies = []
    low = 0
    for i, piece in enumerate(pieces):
        high = low + piece.shape[0]
        lax.fori_loop(low, high, sort, 0, unroll=8)
        copies.append(pltpu.make_async_copy(order.at[pl.ds(low, piece.shape[0])], piece, out_sems.at[i]))
        copies[-1].start()
        low = high
    for copy in copies:
        copy.wait()


def prepare(table, normed, w_query, w_key, w_value, pool, pairs):
    page = pool.shape[1:]
    wide = w_query.shape[1] + 2 * w_key.shape[1]
    return pl.pallas_call(
        prepare_kernel,
        out_shape=(jax.ShapeDtypeStruct((pairs, STEPS, wide), jnp.float32),)
        + tuple(pltpu.HBM((n,) + page, pool.dtype) for n in PIECES),
        in_specs=[SMEM, VMEM, HBM, HBM, HBM, HBM],
        out_specs=(VMEM,) + (HBM,) * len(PIECES),
        scratch_shapes=[
            pltpu.VMEM(pool.shape, pool.dtype),
            pltpu.VMEM((PAGES_HALF,) + page, pool.dtype),
            pltpu.VMEM((w_query.shape[0], wide), w_query.dtype),
            pltpu.SemaphoreType.DMA((CHUNKS,)),
            pltpu.SemaphoreType.DMA((len(PIECES),)),
            pltpu.SemaphoreType.DMA((3,)),
        ],
        compiler_params=params(24),
        name="prepare",
    )(table, normed, *in_hbm(w_query, w_key, w_value, pool))


def attention_kernel(lengths, sums, b_query, b_key, b_value, cosine, sine, *refs):
    pieces, (packed, entries, held, score, sems) = refs[: len(PIECES)], refs[len(PIECES) :]
    copies = []
    low = 0
    for i, piece in enumerate(pieces):
        size = piece.shape[0]
        copies.append((low, pltpu.make_async_copy(piece, held.at[pl.ds(low, size)], sems.at[i])))
        copies[-1][1].start()
        low += size
    requests = sums.shape[0] // 2
    page_len = held.shape[1]
    group, head = b_query.shape
    rows = STEPS * group
    pair_index = lax.axis_index("pair")
    is_source = pair_index >= requests
    request = jnp.where(is_source, pair_index - requests, pair_index)
    half_tokens = PAGES_HALF * page_len
    limit = jnp.where(is_source, lengths[request] - half_tokens, half_tokens)

    total = sums[0]
    for p in range(1, sums.shape[0]):
        total = total + sums[p]
    query = jnp.concatenate(
        [total[s : s + 1, h * head : (h + 1) * head] for s in range(STEPS) for h in range(group)], 0
    )
    query = query + jnp.concatenate([b_query[...]] * STEPS, 0)
    cos_new = cosine[request]
    sin_new = sine[request]
    row = lax.broadcasted_iota(jnp.int32, (rows, head), 0)
    cos_rows = jnp.where(row < group, cos_new[0:1], cos_new[1:2])
    sin_rows = jnp.where(row < group, sin_new[0:1], sin_new[1:2])
    query = (query * cos_rows + pltpu.roll(query, head // 2, 1) * sin_rows).astype(jnp.bfloat16)
    key_new = total[:, group * head : (group + 1) * head] + b_key[...]
    key_new = jnp.concatenate([key_new, jnp.zeros((8 - STEPS, head), jnp.float32)], 0)
    key_new = key_new * cos_new + pltpu.roll(key_new, head // 2, 1) * sin_new
    key_new = key_new.astype(jnp.bfloat16).astype(jnp.float32)
    value_new = total[:, (group + 1) * head :] + b_value[...]
    value_new = value_new.astype(jnp.bfloat16).astype(jnp.float32)
    entries[:, :head] = key_new
    entries[0:STEPS, head:] = value_new
    entries[STEPS:, head:] = jnp.zeros((8 - STEPS, head), jnp.float32)
    scale = 1.0 / math.sqrt(head)

    column = lax.broadcasted_iota(jnp.int32, (rows, 1), 0)
    query_wide = query.astype(jnp.float32)
    fresh = []
    for s in range(STEPS):
        dots = jnp.sum(query_wide * key_new[s : s + 1], 1, keepdims=True) * scale
        seen = jnp.logical_and(is_source, column >= s * group)
        fresh.append((jnp.where(seen, dots, NEG), seen))
    row_max = jnp.maximum(fresh[0][0], fresh[1][0])

    per = 64
    width = per * page_len
    blocks = PAGES_HALF // per
    lane = lax.broadcasted_iota(jnp.int32, (rows, width), 1)
    for c in range(blocks):
        low, high = c * per, (c + 1) * per
        while copies and copies[0][0] < high:
            copies.pop(0)[1].wait()
        keys = held[low:high, :, :head].reshape(width, head)
        part = lax.dot_general(query, keys, (((1,), (1,)), ((), ())), preferred_element_type=jnp.float32)
        part = jnp.where(lane < limit - c * width, part * scale, NEG)
        score[:, c * width : (c + 1) * width] = part
        row_max = jnp.maximum(row_max, jnp.max(part, 1, keepdims=True))
    row_sum = jnp.zeros((rows, 1), jnp.float32)
    out = jnp.zeros((rows, head), jnp.float32)
    for s in range(STEPS):
        weight = jnp.where(fresh[s][1], jnp.exp(fresh[s][0] - row_max), 0.0)
        row_sum = row_sum + weight
        out = out + weight.astype(jnp.bfloat16).astype(jnp.float32) * value_new[s : s + 1]
    for c in range(blocks):
        low, high = c * per, (c + 1) * per
        weight = jnp.exp(score[:, c * width : (c + 1) * width] - row_max)
        weight = jnp.where(lane < limit - c * width, weight, 0.0)
        row_sum = row_sum + jnp.sum(weight, 1, keepdims=True)
        values = held[low:high, :, head:].reshape(width, head)
        out = out + jnp.dot(weight.astype(jnp.bfloat16), values, preferred_element_type=jnp.float32)

    diagonal = lax.broadcasted_iota(jnp.int32, (rows, head), 1) == row
    packed[0:rows] = out
    packed[rows : rows + 1] = jnp.sum(jnp.where(diagonal, row_max, 0.0), 0, keepdims=True)
    packed[rows + 1 : rows + 2] = jnp.sum(jnp.where(diagonal, row_sum, 0.0), 0, keepdims=True)
    packed[rows + 2 :] = jnp.zeros((packed.shape[0] - rows - 2, head), jnp.float32)


def attend(lengths, sums, b_query, b_key, b_value, cosine, sine, pieces):
    group, head = b_query.shape
    rows = STEPS * group
    page = pieces[0].shape[1:]
    return pl.pallas_call(
        attention_kernel,
        out_shape=(
            jax.ShapeDtypeStruct((rows + 8, head), jnp.float32),
            jax.ShapeDtypeStruct((8, 2 * head), jnp.float32),
        ),
        in_specs=[SMEM] + [VMEM] * 6 + [HBM] * len(pieces),
        out_specs=(VMEM, VMEM),
        scratch_shapes=[
            pltpu.VMEM((PAGES_HALF,) + page, pieces[0].dtype),
            pltpu.VMEM((rows, PAGES_HALF * page[0]), jnp.float32),
            pltpu.SemaphoreType.DMA((len(pieces),)),
        ],
        compiler_params=params(24),
        name="attend",
    )(lengths, sums, b_query, b_key, b_value, cosine, sine, *in_hbm(*pieces))


def project_kernel(parts, w_out, out):
    pairs, packed_rows, head = parts.shape
    rows = packed_rows - 8
    group = rows // STEPS
    requests = pairs // 2
    lane = lax.broadcasted_iota(jnp.int32, (rows, head), 1)
    diagonal = lane == lax.broadcasted_iota(jnp.int32, (rows, head), 0)

    def as_column(line):
        return jnp.sum(jnp.where(diagonal, line, 0.0), 1, keepdims=True)

    merged = []
    for r in range(requests):
        first_max, first_sum = (as_column(parts[r, rows + i : rows + i + 1]) for i in range(2))
        second_max, second_sum = (as_column(parts[r + requests, rows + i : rows + i + 1]) for i in range(2))
        top = jnp.maximum(first_max, second_max)
        first_weight = jnp.exp(first_max - top)
        second_weight = jnp.exp(second_max - top)
        joined = first_weight * parts[r, :rows] + second_weight * parts[r + requests, :rows]
        merged.append(joined / (first_weight * first_sum + second_weight * second_sum))
    lines = []
    for s in range(STEPS):
        for r in range(requests):
            lines.append(
                jnp.concatenate(
                    [merged[r][s * group + h : s * group + h + 1] for h in range(group)], 1
                )
            )
    attended = jnp.concatenate(lines, 0).astype(jnp.bfloat16)
    result = jnp.dot(attended, w_out[...], preferred_element_type=jnp.float32)
    for s in range(STEPS):
        out[s] = result[s * requests : (s + 1) * requests]


def project(parts, w_out):
    return pl.pallas_call(
        project_kernel,
        out_shape=jax.ShapeDtypeStruct((STEPS, parts.shape[0] // 2, w_out.shape[1]), jnp.float32),
        in_specs=[VMEM, VMEM],
        out_specs=VMEM,
        compiler_params=params(16),
        name="project",
    )(parts, w_out)


def moved_pages(plan, request):
    count = plan[request, 0]
    for s in range(1, STEPS):
        count = count + plan[request, s]
    return count


def copy_kernel(table, lengths, plan, entries, pool, *refs):
    early, (new_pool, held, pages, sems, out_sems, page_sems) = refs[:-6], refs[-6:]
    slots, page_len, width = held.shape
    per = slots // CHUNKS
    requests = lengths.shape[0]
    pair_index = lax.axis_index("pair")
    is_source = pair_index >= requests

    def fetch(c):
        part = pl.ds(c * per, per)
        return pltpu.make_async_copy(pool.at[part], held.at[part], sems.at[c])

    def store(c):
        part = pl.ds(c * per, per)
        return pltpu.make_async_copy(held.at[part], new_pool.at[part], out_sems.at[c])

    for c in range(CHUNKS):
        fetch(c).start()
    copies = []
    low = 0
    for i, piece in enumerate(early):
        size = piece.shape[0]
        copies.append(pltpu.make_async_copy(piece, pages.at[pl.ds(low, size)], page_sems.at[i]))
        copies[-1].start()
        low += size
    for copy in copies:
        copy.wait()
    for c in range(CHUNKS):
        fetch(c).wait()

    @pl.when(is_source)
    def _():
        page_row = lax.broadcasted_iota(jnp.int32, (page_len, width), 0)
        first_new = lengths[pair_index - requests] - PAGES_HALF * page_len
        for s in range(STEPS):
            offset = first_new + s
            slot = table[0, offset // page_len]
            old = held[slot].astype(jnp.float32)
            held[slot] = jnp.where(page_row == offset % page_len, entries[s : s + 1], old).astype(held.dtype)

    @pl.when(jnp.logical_not(is_source))
    def _():
        def place(j, carry):
            held[table[0, PAGES_HALF + j]] = pages[j]
            return carry

        lax.fori_loop(0, jnp.minimum(moved_pages(plan, pair_index), pages.shape[0]), place, 0)

    for c in range(CHUNKS):
        store(c).start()
    for c in range(CHUNKS):
        store(c).wait()


def copy_pool(table, lengths, plan, entries, pool, early):
    return pl.pallas_call(
        copy_kernel,
        out_shape=jax.ShapeDtypeStruct(pool.shape, pool.dtype),
        in_specs=[SMEM, SMEM, SMEM, VMEM, HBM] + [HBM] * len(early),
        out_specs=HBM,
        scratch_shapes=[
            pltpu.VMEM(pool.shape, pool.dtype),
            pltpu.VMEM((sum(PIECES[: MOVED_PIECES - 1]),) + pool.shape[1:], pool.dtype),
            pltpu.SemaphoreType.DMA((CHUNKS,)),
            pltpu.SemaphoreType.DMA((CHUNKS,)),
            pltpu.SemaphoreType.DMA((len(early),)),
        ],
        compiler_params=params(24),
        name="copy_pool",
    )(table, lengths, plan, entries, *in_hbm(pool, *early))


def finish_kernel(table, plan, pages, base, new_pool, sem):
    del base
    requests = plan.shape[0]
    pair_index = lax.axis_index("pair")
    done = MOVED_MAX - pages.shape[0]
    request = jnp.where(pair_index >= requests, 0, pair_index)
    count = jnp.where(pair_index >= requests, 0, moved_pages(plan, request) - done)

    def start(j, carry):
        slot = table[0, PAGES_HALF + done + j]
        pltpu.make_async_copy(pages.at[j], new_pool.at[slot], sem).start()
        return carry

    def wait(j, carry):
        pltpu.make_async_copy(pages.at[0], new_pool.at[0], sem).wait()
        return carry

    lax.fori_loop(0, count, start, 0)
    lax.fori_loop(0, count, wait, 0)


def finish(table, plan, pages, base):
    return pl.pallas_call(
        finish_kernel,
        out_shape=jax.ShapeDtypeStruct(base.shape, base.dtype),
        in_specs=[SMEM, SMEM, VMEM, HBM],
        out_specs=HBM,
        scratch_shapes=[pltpu.SemaphoreType.DMA],
        input_output_aliases={3: 0},
        compiler_params=params(16),
        name="finish",
    )(table, plan, pages, base)


def local(
    normed, w_query, b_query, w_key, b_key, w_value, b_value, w_out, pool, page_table, lengths, plan
):
    pair_count = lax.axis_size("pair")
    tp_count = lax.axis_size("tp")
    requests = pair_count // 2
    head = w_key.shape[1]

    partial, *pieces = prepare(page_table, normed, w_query, w_key, w_value, pool[0, 0], pair_count)
    route = [(i + requests, i) for i in range(requests)]

    def migrate(pages, after):
        return lax.ppermute(lax.optimization_barrier((pages, after))[0], "pair", route)

    incoming = [lax.ppermute(pieces[0], "pair", route)]
    sums = lax.all_to_all(partial, "pair", split_axis=0, concat_axis=0, tiled=True)
    sums, incoming[0] = lax.optimization_barrier((sums, incoming[0]))
    incoming.append(migrate(pieces[1], sums))

    frequency = rope_base ** (-(jnp.arange(head // 2, dtype=jnp.float32) * 2.0 / head))
    steps = jnp.minimum(jnp.arange(8, dtype=jnp.int32), STEPS - 1)
    position = (lengths[:, None] + steps[None, :]).astype(jnp.float32)[..., None]
    angles = position * frequency
    cosine = jnp.cos(angles)
    sine = jnp.sin(angles)
    cosine = jnp.concatenate([cosine, cosine], -1)
    sine = jnp.concatenate([-sine, sine], -1)

    packed, entries = attend(
        lengths,
        sums,
        b_query.reshape(-1, head),
        b_key[None, :],
        b_value[None, :],
        cosine,
        sine,
        pieces,
    )
    spread = jnp.broadcast_to(packed[None], (pair_count,) + packed.shape)
    parts = lax.all_to_all(spread, "pair", split_axis=0, concat_axis=0, tiled=True)
    parts, incoming[1] = lax.optimization_barrier((parts, incoming[1]))
    incoming.append(migrate(pieces[2], parts))
    new_pool = copy_pool(page_table, lengths, plan, entries, pool[0, 0], incoming[:-1])
    projected = project(parts, w_out)
    if tp_count == 2:
        projected = projected + lax.ppermute(projected, "tp", [(0, 1), (1, 0)])
    else:
        projected = lax.psum(projected, "tp")
    new_pool = finish(page_table, plan, incoming[-1], new_pool)
    return projected, new_pool[None, None]


def solution(mesh):
    return jax.shard_map(
        local,
        mesh=mesh,
        in_specs=(
            P(None, "rep", "pair"),
            P("pair", "tp"),
            P("tp"),
            P("pair", "tp"),
            P("tp"),
            P("pair", "tp"),
            P("tp"),
            P("tp", "pair"),
            P(("rep", "pair"), "tp", None, None, None),
            P(("rep", "pair"), None),
            P("rep"),
            P("rep", None),
        ),
        out_specs=(P(None, "rep", "pair"), P(("rep", "pair"), "tp", None, None, None)),
        check_vma=False,
    )
```

```python
import math

import jax
import jax.numpy as jnp
from jax import lax
from jax.experimental import pallas as pl
from jax.experimental.pallas import tpu as pltpu
from jax.sharding import PartitionSpec as P

PAGES_HALF = 384
STEPS = 2
SECTION = 64
MOVED_MAX = STEPS * SECTION
PIECES = (16, 16, 96)
CHUNKS = 8
NEG = -1e30

rope_base = 1000000.0

VMEM = pl.BlockSpec(memory_space=pltpu.VMEM)
SMEM = pl.BlockSpec(memory_space=pltpu.SMEM)
HBM = pl.BlockSpec(memory_space=pltpu.HBM)


def in_hbm(*arrays):
    return tuple(pltpu.with_memory_space_constraint(a, pltpu.HBM) for a in arrays)


def params(mib):
    return pltpu.CompilerParams(vmem_limit_bytes=mib * 1024 * 1024)


def prepare_kernel(table_in, normed_in, w_query, w_key, w_value, pool, partial, *refs):
    pieces, (table, normed, weights, table_sem, sems, page_sems) = refs[:-6], refs[-6:]
    pairs = partial.shape[0]
    requests = pairs // 2
    table_copy = pltpu.make_async_copy(table_in, table, table_sem)
    table_copy.start()
    loads = [pltpu.make_async_copy(normed_in, normed, sems.at[3])]
    low = 0
    for i, weight in enumerate((w_query, w_key, w_value)):
        part = weights.at[:, low : low + weight.shape[1]]
        loads.append(pltpu.make_async_copy(weight, part, sems.at[i]))
        low += weight.shape[1]
    for copy in loads:
        copy.start()
    table_copy.wait()

    @pl.when(lax.axis_index("pair") >= requests)
    def _():
        low = 0
        for i, piece in enumerate(pieces):

            def start(j, carry):
                pltpu.make_async_copy(pool.at[table[0, low + j]], piece.at[j], page_sems.at[i]).start()
                return carry

            lax.fori_loop(0, piece.shape[0], start, 0, unroll=8)
            low += piece.shape[0]

    for copy in loads:
        copy.wait()
    hidden = jnp.concatenate([normed[s].astype(jnp.float32) for s in range(STEPS)], 0).astype(jnp.bfloat16)
    result = jnp.dot(hidden, weights[...], preferred_element_type=jnp.float32)
    for p in range(pairs):
        for s in range(STEPS):
            row = s * requests + p % requests
            partial[p, s : s + 1] = result[row : row + 1]

    @pl.when(lax.axis_index("pair") >= requests)
    def _():
        for i, piece in enumerate(pieces):
            pltpu.make_async_copy(pool.at[pl.ds(0, piece.shape[0])], piece, page_sems.at[i]).wait()


def prepare(table, normed, w_query, w_key, w_value, pool, pairs):
    page = pool.shape[1:]
    wide = w_query.shape[1] + 2 * w_key.shape[1]
    return pl.pallas_call(
        prepare_kernel,
        out_shape=(jax.ShapeDtypeStruct((pairs, STEPS, wide), jnp.float32),)
        + tuple(pltpu.VMEM((n,) + page, pool.dtype) for n in PIECES),
        in_specs=[HBM] * 6,
        out_specs=(VMEM,) + (VMEM,) * len(PIECES),
        scratch_shapes=[
            pltpu.SMEM(table.shape, table.dtype),
            pltpu.VMEM(normed.shape, normed.dtype),
            pltpu.VMEM((w_query.shape[0], wide), w_query.dtype),
            pltpu.SemaphoreType.DMA,
            pltpu.SemaphoreType.DMA((4,)),
            pltpu.SemaphoreType.DMA((len(PIECES),)),
        ],
        compiler_params=params(16),
        name="prepare",
    )(*in_hbm(table, normed, w_query, w_key, w_value, pool))


def page_order(table, slots):
    slot = lax.broadcasted_iota(jnp.int32, (slots, slots), 0)
    holds = jnp.where(slot == table, 1.0, 0.0).astype(jnp.bfloat16)
    index = lax.broadcasted_iota(jnp.int32, (8, slots), 1)
    digit = lax.broadcasted_iota(jnp.int32, (8, slots), 0)
    digits = jnp.where(digit == 0, index // 16, jnp.where(digit == 1, index % 16, 0))
    digits = digits.astype(jnp.float32).astype(jnp.bfloat16)
    return lax.dot_general(digits, holds, (((1,), (1,)), ((), ())), preferred_element_type=jnp.float32)


def attention_kernel(
    lengths, table, sums, b_query, b_key, b_value, cosine, sine, pool, packed, entries, held, score, sems
):
    slots, page_len, _ = held.shape
    per = slots // CHUNKS
    copies = []
    for c in range(CHUNKS):
        part = pl.ds(c * per, per)
        copies.append(pltpu.make_async_copy(pool.at[part], held.at[part], sems.at[c]))
        copies[-1].start()
    requests = sums.shape[0] // 2
    group, head = b_query.shape
    rows = STEPS * group
    pair_index = lax.axis_index("pair")
    is_source = pair_index >= requests
    request = jnp.where(is_source, pair_index - requests, pair_index)
    half_tokens = PAGES_HALF * page_len
    limit = jnp.where(is_source, lengths[request] - half_tokens, half_tokens)

    blocks = CHUNKS // 2
    block = slots // blocks
    width = block * page_len
    digits = page_order(table[...], slots)
    digits = jnp.concatenate(
        [digits[d : d + 1, c * block : (c + 1) * block] for d in range(2) for c in range(blocks)], 0
    ).astype(jnp.bfloat16)
    spread = lax.broadcasted_iota(jnp.int32, (block, width), 1) // page_len
    spread = jnp.where(spread == lax.broadcasted_iota(jnp.int32, (block, width), 0), 1.0, 0.0)
    digits = jnp.dot(digits, spread.astype(jnp.bfloat16), preferred_element_type=jnp.float32)
    tokens = (digits[:blocks] * 16.0 + digits[blocks:]).astype(jnp.int32) * page_len
    tokens = tokens + lax.broadcasted_iota(jnp.int32, (blocks, width), 1) % page_len

    total = sums[0]
    for p in range(1, sums.shape[0]):
        total = total + sums[p]
    query = jnp.concatenate(
        [total[s : s + 1, h * head : (h + 1) * head] for s in range(STEPS) for h in range(group)], 0
    )
    query = query + jnp.concatenate([b_query[...]] * STEPS, 0)
    cos_new = cosine[request]
    sin_new = sine[request]
    row = lax.broadcasted_iota(jnp.int32, (rows, head), 0)
    cos_rows = jnp.where(row < group, cos_new[0:1], cos_new[1:2])
    sin_rows = jnp.where(row < group, sin_new[0:1], sin_new[1:2])
    query = (query * cos_rows + pltpu.roll(query, head // 2, 1) * sin_rows).astype(jnp.bfloat16)
    key_new = total[:, group * head : (group + 1) * head] + b_key[...]
    key_new = jnp.concatenate([key_new, jnp.zeros((8 - STEPS, head), jnp.float32)], 0)
    key_new = key_new * cos_new + pltpu.roll(key_new, head // 2, 1) * sin_new
    key_new = key_new.astype(jnp.bfloat16).astype(jnp.float32)
    value_new = total[:, (group + 1) * head :] + b_value[...]
    value_new = value_new.astype(jnp.bfloat16).astype(jnp.float32)
    entries[:, :head] = key_new
    entries[0:STEPS, head:] = value_new
    entries[STEPS:, head:] = jnp.zeros((8 - STEPS, head), jnp.float32)
    scale = 1.0 / math.sqrt(head)

    column = lax.broadcasted_iota(jnp.int32, (rows, 1), 0)
    query_wide = query.astype(jnp.float32)
    fresh = []
    for s in range(STEPS):
        dots = jnp.sum(query_wide * key_new[s : s + 1], 1, keepdims=True) * scale
        seen = jnp.logical_and(is_source, column >= s * group)
        fresh.append((jnp.where(seen, dots, NEG), seen))
    row_max = jnp.maximum(fresh[0][0], fresh[1][0])

    for c in range(blocks):
        copies[2 * c].wait()
        copies[2 * c + 1].wait()
        keys = held[c * block : (c + 1) * block, :, :head].reshape(width, head)
        part = lax.dot_general(query, keys, (((1,), (1,)), ((), ())), preferred_element_type=jnp.float32)
        part = jnp.where(tokens[c : c + 1] < limit, part * scale, NEG)
        score[:, c * width : (c + 1) * width] = part
        row_max = jnp.maximum(row_max, jnp.max(part, 1, keepdims=True))
    row_sum = jnp.zeros((rows, 1), jnp.float32)
    out = jnp.zeros((rows, head), jnp.float32)
    for s in range(STEPS):
        weight = jnp.where(fresh[s][1], jnp.exp(fresh[s][0] - row_max), 0.0)
        row_sum = row_sum + weight
        out = out + weight.astype(jnp.bfloat16).astype(jnp.float32) * value_new[s : s + 1]
    for c in range(blocks):
        weight = jnp.exp(score[:, c * width : (c + 1) * width] - row_max)
        weight = jnp.where(tokens[c : c + 1] < limit, weight, 0.0)
        row_sum = row_sum + jnp.sum(weight, 1, keepdims=True)
        values = held[c * block : (c + 1) * block, :, head:].reshape(width, head)
        out = out + jnp.dot(weight.astype(jnp.bfloat16), values, preferred_element_type=jnp.float32)

    diagonal = lax.broadcasted_iota(jnp.int32, (rows, head), 1) == row
    for p in range(packed.shape[0]):
        packed[p, 0:rows] = out
        packed[p, rows : rows + 1] = jnp.sum(jnp.where(diagonal, row_max, 0.0), 0, keepdims=True)
        packed[p, rows + 1 : rows + 2] = jnp.sum(jnp.where(diagonal, row_sum, 0.0), 0, keepdims=True)
        packed[p, rows + 2 :] = jnp.zeros((packed.shape[1] - rows - 2, head), jnp.float32)


def attend(lengths, table, sums, b_query, b_key, b_value, cosine, sine, pool):
    group, head = b_query.shape
    rows = STEPS * group
    return pl.pallas_call(
        attention_kernel,
        out_shape=(
            jax.ShapeDtypeStruct((sums.shape[0], rows + 8, head), jnp.float32),
            jax.ShapeDtypeStruct((8, 2 * head), jnp.float32),
        ),
        in_specs=[SMEM] + [VMEM] * 7 + [HBM],
        out_specs=(VMEM, VMEM),
        scratch_shapes=[
            pltpu.VMEM(pool.shape, pool.dtype),
            pltpu.VMEM((rows, pool.shape[0] * pool.shape[1]), jnp.float32),
            pltpu.SemaphoreType.DMA((CHUNKS,)),
        ],
        compiler_params=params(24),
        name="attend",
    )(lengths, table, sums, b_query, b_key, b_value, cosine, sine, *in_hbm(pool))


def project_kernel(parts, w_out, out):
    pairs, packed_rows, head = parts.shape
    rows = packed_rows - 8
    group = rows // STEPS
    requests = pairs // 2
    lane = lax.broadcasted_iota(jnp.int32, (rows, head), 1)
    diagonal = lane == lax.broadcasted_iota(jnp.int32, (rows, head), 0)

    def as_column(line):
        return jnp.sum(jnp.where(diagonal, line, 0.0), 1, keepdims=True)

    merged = []
    for r in range(requests):
        first_max, first_sum = (as_column(parts[r, rows + i : rows + i + 1]) for i in range(2))
        second_max, second_sum = (as_column(parts[r + requests, rows + i : rows + i + 1]) for i in range(2))
        top = jnp.maximum(first_max, second_max)
        first_weight = jnp.exp(first_max - top)
        second_weight = jnp.exp(second_max - top)
        joined = first_weight * parts[r, :rows] + second_weight * parts[r + requests, :rows]
        merged.append(joined / (first_weight * first_sum + second_weight * second_sum))
    lines = []
    for s in range(STEPS):
        for r in range(requests):
            lines.append(
                jnp.concatenate(
                    [merged[r][s * group + h : s * group + h + 1] for h in range(group)], 1
                )
            )
    attended = jnp.concatenate(lines, 0).astype(jnp.bfloat16)
    result = jnp.dot(attended, w_out[...], preferred_element_type=jnp.float32)
    for s in range(STEPS):
        out[s] = result[s * requests : (s + 1) * requests]


def project(parts, w_out):
    return pl.pallas_call(
        project_kernel,
        out_shape=jax.ShapeDtypeStruct((STEPS, parts.shape[0] // 2, w_out.shape[1]), jnp.float32),
        in_specs=[VMEM, VMEM],
        out_specs=VMEM,
        compiler_params=params(16),
        name="project",
    )(parts, w_out)


def moved_pages(plan, request):
    count = plan[request, 0]
    for s in range(1, STEPS):
        count = count + plan[request, s]
    return count


def copy_kernel(table, lengths, plan, entries, pool, *refs):
    early, (new_pool, held, sems, out_sems) = refs[:-4], refs[-4:]
    slots, page_len, width = held.shape
    per = slots // CHUNKS
    requests = lengths.shape[0]
    pair_index = lax.axis_index("pair")
    is_source = pair_index >= requests

    def fetch(c):
        part = pl.ds(c * per, per)
        return pltpu.make_async_copy(pool.at[part], held.at[part], sems.at[c])

    def store(c):
        part = pl.ds(c * per, per)
        return pltpu.make_async_copy(held.at[part], new_pool.at[part], out_sems.at[c])

    for c in range(CHUNKS):
        fetch(c).start()
    for c in range(CHUNKS):
        fetch(c).wait()

    @pl.when(is_source)
    def _():
        page_row = lax.broadcasted_iota(jnp.int32, (page_len, width), 0)
        first_new = lengths[pair_index - requests] - PAGES_HALF * page_len
        for s in range(STEPS):
            offset = first_new + s
            slot = table[0, offset // page_len]
            old = held[slot].astype(jnp.float32)
            held[slot] = jnp.where(page_row == offset % page_len, entries[s : s + 1], old).astype(held.dtype)

    @pl.when(jnp.logical_not(is_source))
    def _():
        count = moved_pages(plan, pair_index)
        low = 0
        for pages in early:

            def place(j, carry):
                held[table[0, PAGES_HALF + low + j]] = pages[j]
                return carry

            lax.fori_loop(0, jnp.clip(count - low, 0, pages.shape[0]), place, 0)
            low += pages.shape[0]

    for c in range(CHUNKS):
        store(c).start()
    for c in range(CHUNKS):
        store(c).wait()


def copy_pool(table, lengths, plan, entries, pool, early):
    return pl.pallas_call(
        copy_kernel,
        out_shape=jax.ShapeDtypeStruct(pool.shape, pool.dtype),
        in_specs=[SMEM, SMEM, SMEM, VMEM, HBM] + [VMEM] * len(early),
        out_specs=HBM,
        scratch_shapes=[
            pltpu.VMEM(pool.shape, pool.dtype),
            pltpu.SemaphoreType.DMA((CHUNKS,)),
            pltpu.SemaphoreType.DMA((CHUNKS,)),
        ],
        compiler_params=params(24),
        name="copy_pool",
    )(table, lengths, plan, entries, *in_hbm(pool), *early)


def finish_kernel(table, plan, pages, base, new_pool, sem):
    del base
    requests = plan.shape[0]
    pair_index = lax.axis_index("pair")
    done = MOVED_MAX - pages.shape[0]
    request = jnp.where(pair_index >= requests, 0, pair_index)
    count = jnp.where(pair_index >= requests, 0, moved_pages(plan, request) - done)

    def start(j, carry):
        slot = table[0, PAGES_HALF + done + j]
        pltpu.make_async_copy(pages.at[j], new_pool.at[slot], sem).start()
        return carry

    def wait(j, carry):
        pltpu.make_async_copy(pages.at[0], new_pool.at[0], sem).wait()
        return carry

    lax.fori_loop(0, count, start, 0)
    lax.fori_loop(0, count, wait, 0)


def finish(table, plan, pages, base):
    return pl.pallas_call(
        finish_kernel,
        out_shape=jax.ShapeDtypeStruct(base.shape, base.dtype),
        in_specs=[SMEM, SMEM, VMEM, HBM],
        out_specs=HBM,
        scratch_shapes=[pltpu.SemaphoreType.DMA],
        input_output_aliases={3: 0},
        compiler_params=params(16),
        name="finish",
    )(table, plan, pages, base)


def local(
    normed, w_query, b_query, w_key, b_key, w_value, b_value, w_out, pool, page_table, lengths, plan
):
    pair_count = lax.axis_size("pair")
    tp_count = lax.axis_size("tp")
    requests = pair_count // 2
    head = w_key.shape[1]

    partial, *pieces = prepare(page_table, normed, w_query, w_key, w_value, pool[0, 0], pair_count)
    route = [(i + requests, i) for i in range(requests)]

    def migrate(pages, after):
        return lax.ppermute(lax.optimization_barrier((pages, after))[0], "pair", route)

    incoming = [lax.ppermute(pieces[0], "pair", route)]
    sums = lax.all_to_all(partial, "pair", split_axis=0, concat_axis=0, tiled=True)
    incoming.append(migrate(pieces[1], sums))

    frequency = rope_base ** (-(jnp.arange(head // 2, dtype=jnp.float32) * 2.0 / head))
    steps = jnp.minimum(jnp.arange(8, dtype=jnp.int32), STEPS - 1)
    position = (lengths[:, None] + steps[None, :]).astype(jnp.float32)[..., None]
    angles = position * frequency
    cosine = jnp.cos(angles)
    sine = jnp.sin(angles)
    cosine = jnp.concatenate([cosine, cosine], -1)
    sine = jnp.concatenate([-sine, sine], -1)

    packed, entries = attend(
        lengths,
        page_table,
        sums,
        b_query.reshape(-1, head),
        b_key[None, :],
        b_value[None, :],
        cosine,
        sine,
        pool[0, 0],
    )
    parts = lax.all_to_all(packed, "pair", split_axis=0, concat_axis=0, tiled=True)
    incoming.append(migrate(pieces[2], parts))
    new_pool = copy_pool(page_table, lengths, plan, entries, pool[0, 0], incoming[:-1])
    projected = project(parts, w_out)
    if tp_count == 2:
        projected = projected + lax.ppermute(projected, "tp", [(0, 1), (1, 0)])
    else:
        projected = lax.psum(projected, "tp")
    new_pool = finish(page_table, plan, incoming[-1], new_pool)
    return projected, new_pool[None, None]


def solution(mesh):
    return jax.shard_map(
        local,
        mesh=mesh,
        in_specs=(
            P(None, "rep", "pair"),
            P("pair", "tp"),
            P("tp"),
            P("pair", "tp"),
            P("tp"),
            P("pair", "tp"),
            P("tp"),
            P("tp", "pair"),
            P(("rep", "pair"), "tp", None, None, None),
            P(("rep", "pair"), None),
            P("rep"),
            P("rep", None),
        ),
        out_specs=(P(None, "rep", "pair"), P(("rep", "pair"), "tp", None, None, None)),
        check_vma=False,
    )
```

```python
import functools
import math

import jax
import jax.numpy as jnp
from jax import lax
from jax.experimental import pallas as pl
from jax.experimental.pallas import tpu as pltpu
from jax.sharding import PartitionSpec as P

PAGES_HALF = 384
STEPS = 2
SECTION = 64
MOVED_MAX = STEPS * SECTION
EARLY = (16, 32)
LATE = (16,) * 5
PIECES = EARLY + LATE
CHUNKS = 8
NEG = -1e30

rope_base = 1000000.0

VMEM = pl.BlockSpec(memory_space=pltpu.VMEM)
SMEM = pl.BlockSpec(memory_space=pltpu.SMEM)
HBM = pl.BlockSpec(memory_space=pltpu.HBM)


def in_hbm(*arrays):
    return tuple(pltpu.with_memory_space_constraint(a, pltpu.HBM) for a in arrays)


def params(mib):
    return pltpu.CompilerParams(vmem_limit_bytes=mib * 1024 * 1024)


def prepare_kernel(table_in, normed_in, w_query, w_key, w_value, pool, partial, *refs):
    pieces, (table, normed, weights, table_sem, sems, page_sems) = refs[:-6], refs[-6:]
    pairs = partial.shape[0]
    requests = pairs // 2
    table_copy = pltpu.make_async_copy(table_in, table, table_sem)
    table_copy.start()
    loads = [pltpu.make_async_copy(normed_in, normed, sems.at[3])]
    low = 0
    for i, weight in enumerate((w_query, w_key, w_value)):
        part = weights.at[:, low : low + weight.shape[1]]
        loads.append(pltpu.make_async_copy(weight, part, sems.at[i]))
        low += weight.shape[1]
    for copy in loads:
        copy.start()
    table_copy.wait()

    @pl.when(lax.axis_index("pair") >= requests)
    def _():
        low = 0
        for i, piece in enumerate(pieces):

            def start(j, carry):
                pltpu.make_async_copy(pool.at[table[0, low + j]], piece.at[j], page_sems.at[i]).start()
                return carry

            lax.fori_loop(0, piece.shape[0], start, 0, unroll=8)
            low += piece.shape[0]

    for copy in loads:
        copy.wait()
    hidden = jnp.concatenate([normed[s].astype(jnp.float32) for s in range(STEPS)], 0).astype(jnp.bfloat16)
    result = jnp.dot(hidden, weights[...], preferred_element_type=jnp.float32)
    for p in range(pairs):
        for s in range(STEPS):
            row = s * requests + p % requests
            partial[p, s : s + 1] = result[row : row + 1]

    @pl.when(lax.axis_index("pair") >= requests)
    def _():
        for i, piece in enumerate(pieces):
            pltpu.make_async_copy(pool.at[pl.ds(0, piece.shape[0])], piece, page_sems.at[i]).wait()


def prepare(table, normed, w_query, w_key, w_value, pool, pairs):
    page = pool.shape[1:]
    wide = w_query.shape[1] + 2 * w_key.shape[1]
    return pl.pallas_call(
        prepare_kernel,
        out_shape=(jax.ShapeDtypeStruct((pairs, STEPS, wide), jnp.float32),)
        + tuple(pltpu.VMEM((n,) + page, pool.dtype) for n in PIECES),
        in_specs=[HBM] * 6,
        out_specs=(VMEM,) + (VMEM,) * len(PIECES),
        scratch_shapes=[
            pltpu.SMEM(table.shape, table.dtype),
            pltpu.VMEM(normed.shape, normed.dtype),
            pltpu.VMEM((w_query.shape[0], wide), w_query.dtype),
            pltpu.SemaphoreType.DMA,
            pltpu.SemaphoreType.DMA((4,)),
            pltpu.SemaphoreType.DMA((len(PIECES),)),
        ],
        compiler_params=params(16),
        name="prepare",
    )(*in_hbm(table, normed, w_query, w_key, w_value, pool))


def page_order(table, slots):
    slot = lax.broadcasted_iota(jnp.int32, (slots, slots), 0)
    holds = jnp.where(slot == table, 1.0, 0.0).astype(jnp.bfloat16)
    index = lax.broadcasted_iota(jnp.int32, (8, slots), 1)
    digit = lax.broadcasted_iota(jnp.int32, (8, slots), 0)
    digits = jnp.where(digit == 0, index // 16, jnp.where(digit == 1, index % 16, 0))
    digits = digits.astype(jnp.float32).astype(jnp.bfloat16)
    return lax.dot_general(digits, holds, (((1,), (1,)), ((), ())), preferred_element_type=jnp.float32)


def attention_kernel(
    lengths, table, sums, b_query, b_key, b_value, cosine, sine, pool, packed, entries, held, score, sems
):
    slots, page_len, _ = held.shape
    per = slots // CHUNKS
    copies = []
    for c in range(CHUNKS):
        part = pl.ds(c * per, per)
        copies.append(pltpu.make_async_copy(pool.at[part], held.at[part], sems.at[c]))
        copies[-1].start()
    requests = sums.shape[0] // 2
    group, head = b_query.shape
    rows = STEPS * group
    pair_index = lax.axis_index("pair")
    is_source = pair_index >= requests
    request = jnp.where(is_source, pair_index - requests, pair_index)
    half_tokens = PAGES_HALF * page_len
    limit = jnp.where(is_source, lengths[request] - half_tokens, half_tokens)

    blocks = CHUNKS // 2
    block = slots // blocks
    width = block * page_len
    digits = page_order(table[...], slots)
    digits = jnp.concatenate(
        [digits[d : d + 1, c * block : (c + 1) * block] for d in range(2) for c in range(blocks)], 0
    ).astype(jnp.bfloat16)
    spread = lax.broadcasted_iota(jnp.int32, (block, width), 1) // page_len
    spread = jnp.where(spread == lax.broadcasted_iota(jnp.int32, (block, width), 0), 1.0, 0.0)
    digits = jnp.dot(digits, spread.astype(jnp.bfloat16), preferred_element_type=jnp.float32)
    tokens = (digits[:blocks] * 16.0 + digits[blocks:]).astype(jnp.int32) * page_len
    tokens = tokens + lax.broadcasted_iota(jnp.int32, (blocks, width), 1) % page_len

    total = sums[0]
    for p in range(1, sums.shape[0]):
        total = total + sums[p]
    query = jnp.concatenate(
        [total[s : s + 1, h * head : (h + 1) * head] for s in range(STEPS) for h in range(group)], 0
    )
    query = query + jnp.concatenate([b_query[...]] * STEPS, 0)
    cos_new = cosine[request]
    sin_new = sine[request]
    row = lax.broadcasted_iota(jnp.int32, (rows, head), 0)
    cos_rows = jnp.where(row < group, cos_new[0:1], cos_new[1:2])
    sin_rows = jnp.where(row < group, sin_new[0:1], sin_new[1:2])
    query = (query * cos_rows + pltpu.roll(query, head // 2, 1) * sin_rows).astype(jnp.bfloat16)
    key_new = total[:, group * head : (group + 1) * head] + b_key[...]
    key_new = jnp.concatenate([key_new, jnp.zeros((8 - STEPS, head), jnp.float32)], 0)
    key_new = key_new * cos_new + pltpu.roll(key_new, head // 2, 1) * sin_new
    key_new = key_new.astype(jnp.bfloat16).astype(jnp.float32)
    value_new = total[:, (group + 1) * head :] + b_value[...]
    value_new = value_new.astype(jnp.bfloat16).astype(jnp.float32)
    entries[:, :head] = key_new
    entries[0:STEPS, head:] = value_new
    entries[STEPS:, head:] = jnp.zeros((8 - STEPS, head), jnp.float32)
    scale = 1.0 / math.sqrt(head)

    column = lax.broadcasted_iota(jnp.int32, (rows, 1), 0)
    query_wide = query.astype(jnp.float32)
    fresh = []
    for s in range(STEPS):
        dots = jnp.sum(query_wide * key_new[s : s + 1], 1, keepdims=True) * scale
        seen = jnp.logical_and(is_source, column >= s * group)
        fresh.append((jnp.where(seen, dots, NEG), seen))
    row_max = jnp.maximum(fresh[0][0], fresh[1][0])

    for c in range(blocks):
        copies[2 * c].wait()
        copies[2 * c + 1].wait()
        keys = held[c * block : (c + 1) * block, :, :head].reshape(width, head)
        part = lax.dot_general(query, keys, (((1,), (1,)), ((), ())), preferred_element_type=jnp.float32)
        part = jnp.where(tokens[c : c + 1] < limit, part * scale, NEG)
        score[:, c * width : (c + 1) * width] = part
        row_max = jnp.maximum(row_max, jnp.max(part, 1, keepdims=True))
    row_sum = jnp.zeros((rows, 1), jnp.float32)
    out = jnp.zeros((rows, head), jnp.float32)
    for s in range(STEPS):
        weight = jnp.where(fresh[s][1], jnp.exp(fresh[s][0] - row_max), 0.0)
        row_sum = row_sum + weight
        out = out + weight.astype(jnp.bfloat16).astype(jnp.float32) * value_new[s : s + 1]
    for c in range(blocks):
        weight = jnp.exp(score[:, c * width : (c + 1) * width] - row_max)
        weight = jnp.where(tokens[c : c + 1] < limit, weight, 0.0)
        row_sum = row_sum + jnp.sum(weight, 1, keepdims=True)
        values = held[c * block : (c + 1) * block, :, head:].reshape(width, head)
        out = out + jnp.dot(weight.astype(jnp.bfloat16), values, preferred_element_type=jnp.float32)

    diagonal = lax.broadcasted_iota(jnp.int32, (rows, head), 1) == row
    for p in range(packed.shape[0]):
        packed[p, 0:rows] = out
        packed[p, rows : rows + 1] = jnp.sum(jnp.where(diagonal, row_max, 0.0), 0, keepdims=True)
        packed[p, rows + 1 : rows + 2] = jnp.sum(jnp.where(diagonal, row_sum, 0.0), 0, keepdims=True)
        packed[p, rows + 2 :] = jnp.zeros((packed.shape[1] - rows - 2, head), jnp.float32)


def attend(lengths, table, sums, b_query, b_key, b_value, cosine, sine, pool):
    group, head = b_query.shape
    rows = STEPS * group
    return pl.pallas_call(
        attention_kernel,
        out_shape=(
            jax.ShapeDtypeStruct((sums.shape[0], rows + 8, head), jnp.float32),
            jax.ShapeDtypeStruct((8, 2 * head), jnp.float32),
        ),
        in_specs=[SMEM] + [VMEM] * 7 + [HBM],
        out_specs=(VMEM, VMEM),
        scratch_shapes=[
            pltpu.VMEM(pool.shape, pool.dtype),
            pltpu.VMEM((rows, pool.shape[0] * pool.shape[1]), jnp.float32),
            pltpu.SemaphoreType.DMA((CHUNKS,)),
        ],
        compiler_params=params(24),
        name="attend",
    )(lengths, table, sums, b_query, b_key, b_value, cosine, sine, *in_hbm(pool))


def project_kernel(parts, w_out, out):
    pairs, packed_rows, head = parts.shape
    rows = packed_rows - 8
    group = rows // STEPS
    requests = pairs // 2
    lane = lax.broadcasted_iota(jnp.int32, (rows, head), 1)
    diagonal = lane == lax.broadcasted_iota(jnp.int32, (rows, head), 0)

    def as_column(line):
        return jnp.sum(jnp.where(diagonal, line, 0.0), 1, keepdims=True)

    merged = []
    for r in range(requests):
        first_max, first_sum = (as_column(parts[r, rows + i : rows + i + 1]) for i in range(2))
        second_max, second_sum = (as_column(parts[r + requests, rows + i : rows + i + 1]) for i in range(2))
        top = jnp.maximum(first_max, second_max)
        first_weight = jnp.exp(first_max - top)
        second_weight = jnp.exp(second_max - top)
        joined = first_weight * parts[r, :rows] + second_weight * parts[r + requests, :rows]
        merged.append(joined / (first_weight * first_sum + second_weight * second_sum))
    lines = []
    for s in range(STEPS):
        for r in range(requests):
            lines.append(
                jnp.concatenate(
                    [merged[r][s * group + h : s * group + h + 1] for h in range(group)], 1
                )
            )
    attended = jnp.concatenate(lines, 0).astype(jnp.bfloat16)
    result = jnp.dot(attended, w_out[...], preferred_element_type=jnp.float32)
    for s in range(STEPS):
        out[s] = result[s * requests : (s + 1) * requests]


def project(parts, w_out):
    return pl.pallas_call(
        project_kernel,
        out_shape=jax.ShapeDtypeStruct((STEPS, parts.shape[0] // 2, w_out.shape[1]), jnp.float32),
        in_specs=[VMEM, VMEM],
        out_specs=VMEM,
        compiler_params=params(16),
        name="project",
    )(parts, w_out)


def moved_pages(plan, request):
    count = plan[request, 0]
    for s in range(1, STEPS):
        count = count + plan[request, s]
    return count


def copy_kernel(table, lengths, plan, entries, pool, *refs):
    early, (new_pool, held, sems, out_sems) = refs[:-4], refs[-4:]
    slots, page_len, width = held.shape
    per = slots // CHUNKS
    requests = lengths.shape[0]
    pair_index = lax.axis_index("pair")
    is_source = pair_index >= requests

    def fetch(c):
        part = pl.ds(c * per, per)
        return pltpu.make_async_copy(pool.at[part], held.at[part], sems.at[c])

    def store(c):
        part = pl.ds(c * per, per)
        return pltpu.make_async_copy(held.at[part], new_pool.at[part], out_sems.at[c])

    for c in range(CHUNKS):
        fetch(c).start()
    for c in range(CHUNKS):
        fetch(c).wait()

    @pl.when(is_source)
    def _():
        page_row = lax.broadcasted_iota(jnp.int32, (page_len, width), 0)
        first_new = lengths[pair_index - requests] - PAGES_HALF * page_len
        for s in range(STEPS):
            offset = first_new + s
            slot = table[0, offset // page_len]
            old = held[slot].astype(jnp.float32)
            held[slot] = jnp.where(page_row == offset % page_len, entries[s : s + 1], old).astype(held.dtype)

    @pl.when(jnp.logical_not(is_source))
    def _():
        count = moved_pages(plan, pair_index)
        low = 0
        for pages in early:

            def place(j, carry):
                held[table[0, PAGES_HALF + low + j]] = pages[j]
                return carry

            lax.fori_loop(0, jnp.clip(count - low, 0, pages.shape[0]), place, 0)
            low += pages.shape[0]

    for c in range(CHUNKS):
        store(c).start()
    for c in range(CHUNKS):
        store(c).wait()


def copy_pool(table, lengths, plan, entries, pool, early):
    return pl.pallas_call(
        copy_kernel,
        out_shape=jax.ShapeDtypeStruct(pool.shape, pool.dtype),
        in_specs=[SMEM, SMEM, SMEM, VMEM, HBM] + [VMEM] * len(early),
        out_specs=HBM,
        scratch_shapes=[
            pltpu.VMEM(pool.shape, pool.dtype),
            pltpu.SemaphoreType.DMA((CHUNKS,)),
            pltpu.SemaphoreType.DMA((CHUNKS,)),
        ],
        compiler_params=params(24),
        name="copy_pool",
    )(table, lengths, plan, entries, *in_hbm(pool), *early)


def place_kernel(table, plan, *refs, done, only):
    pages, (base, new_pool, sem) = refs[:-3], refs[-3:]
    del base
    requests = plan.shape[0]
    pair_index = lax.axis_index("pair")
    targets = pair_index < requests if only is None else pair_index == only

    @pl.when(targets)
    def _():
        count = moved_pages(plan, pair_index)
        low = done
        for part in pages:
            here = jnp.clip(count - low, 0, part.shape[0])

            def start(j, carry):
                slot = table[0, PAGES_HALF + low + j]
                pltpu.make_async_copy(part.at[j], new_pool.at[slot], sem).start()
                return carry

            lax.fori_loop(0, here, start, 0)
            low += part.shape[0]

        def wait(j, carry):
            pltpu.make_async_copy(pages[0].at[0], new_pool.at[0], sem).wait()
            return carry

        lax.fori_loop(0, jnp.clip(count - done, 0, low - done), wait, 0)


def place(table, plan, pages, base, done, only=None):
    return pl.pallas_call(
        functools.partial(place_kernel, done=done, only=only),
        out_shape=pltpu.HBM(base.shape, base.dtype),
        in_specs=[SMEM, SMEM] + [VMEM] * len(pages) + [HBM],
        out_specs=HBM,
        scratch_shapes=[pltpu.SemaphoreType.DMA],
        input_output_aliases={2 + len(pages): 0},
        compiler_params=params(16),
        name="place",
    )(table, plan, *pages, *in_hbm(base))


def local(
    normed, w_query, b_query, w_key, b_key, w_value, b_value, w_out, pool, page_table, lengths, plan
):
    pair_count = lax.axis_size("pair")
    tp_count = lax.axis_size("tp")
    requests = pair_count // 2
    head = w_key.shape[1]

    partial, *pieces = prepare(page_table, normed, w_query, w_key, w_value, pool[0, 0], pair_count)
    route = [(i + requests, i) for i in range(requests)]

    def migrate(pages, after):
        return lax.ppermute(lax.optimization_barrier((pages, after))[0], "pair", route)

    incoming = [lax.ppermute(pieces[0], "pair", route)]
    sums = lax.all_to_all(partial, "pair", split_axis=0, concat_axis=0, tiled=True)

    frequency = rope_base ** (-(jnp.arange(head // 2, dtype=jnp.float32) * 2.0 / head))
    steps = jnp.minimum(jnp.arange(8, dtype=jnp.int32), STEPS - 1)
    position = (lengths[:, None] + steps[None, :]).astype(jnp.float32)[..., None]
    angles = position * frequency
    cosine = jnp.cos(angles)
    sine = jnp.sin(angles)
    cosine = jnp.concatenate([cosine, cosine], -1)
    sine = jnp.concatenate([-sine, sine], -1)

    packed, entries = attend(
        lengths,
        page_table,
        sums,
        b_query.reshape(-1, head),
        b_key[None, :],
        b_value[None, :],
        cosine,
        sine,
        pool[0, 0],
    )
    packed, early = lax.optimization_barrier((packed, incoming[0]))
    parts = lax.all_to_all(packed, "pair", split_axis=0, concat_axis=0, tiled=True)
    more = migrate(pieces[1], parts)
    new_pool = copy_pool(page_table, lengths, plan, entries, pool[0, 0], [early])
    projected = project(parts, w_out)
    if tp_count == 2:
        projected = projected + lax.ppermute(projected, "tp", [(0, 1), (1, 0)])
    else:
        projected = lax.psum(projected, "tp")
    new_pool = place(page_table, plan, [more], new_pool, EARLY[0])
    static = sum(EARLY)
    levels = jnp.clip((jnp.sum(plan, 1) - static + LATE[0] - 1) // LATE[0], 0, len(LATE))
    new_pool, projected = lax.optimization_barrier((new_pool, projected))
    late = pieces[len(EARLY) :]

    def send(level, request, base, *chunks):
        if level == 0:
            return base
        pair_route = [(request + requests, request)]
        arrived = [lax.ppermute(chunk, "pair", pair_route) for chunk in chunks[:level]]
        return place(page_table, plan, arrived, base, static, request)

    for request in range(requests):
        branches = [functools.partial(send, level, request) for level in range(len(LATE) + 1)]
        new_pool = lax.switch(levels[request], branches, new_pool, *late)
    return projected, new_pool[None, None]


def solution(mesh):
    return jax.shard_map(
        local,
        mesh=mesh,
        in_specs=(
            P(None, "rep", "pair"),
            P("pair", "tp"),
            P("tp"),
            P("pair", "tp"),
            P("tp"),
            P("pair", "tp"),
            P("tp"),
            P("tp", "pair"),
            P(("rep", "pair"), "tp", None, None, None),
            P(("rep", "pair"), None),
            P("rep"),
            P("rep", None),
        ),
        out_specs=(P(None, "rep", "pair"), P(("rep", "pair"), "tp", None, None, None)),
        check_vma=False,
    )
```

```python
import functools
import math

import jax
import jax.numpy as jnp
from jax import lax
from jax.experimental import pallas as pl
from jax.experimental.pallas import tpu as pltpu
from jax.sharding import PartitionSpec as P

PAGES_HALF = 384
STEPS = 2
SECTION = 64
MOVED_MAX = STEPS * SECTION
EARLY = (32, 12, 28)
LATE = (28, 28)
JOINT = 4
PIECES = EARLY + LATE
CHUNKS = 8
NEG = -1e30

rope_base = 1000000.0

VMEM = pl.BlockSpec(memory_space=pltpu.VMEM)
SMEM = pl.BlockSpec(memory_space=pltpu.SMEM)
HBM = pl.BlockSpec(memory_space=pltpu.HBM)


def in_hbm(*arrays):
    return tuple(pltpu.with_memory_space_constraint(a, pltpu.HBM) for a in arrays)


def params(mib):
    return pltpu.CompilerParams(vmem_limit_bytes=mib * 1024 * 1024)


def prepare_kernel(table_in, normed_in, w_query, w_key, w_value, pool, partial, held, *refs):
    pieces, (table, normed, weights, table_sem, sems, pool_sems) = refs[:-6], refs[-6:]
    pairs = partial.shape[0]
    requests = pairs // 2
    per = held.shape[0] // CHUNKS
    table_copy = pltpu.make_async_copy(table_in, table, table_sem)
    table_copy.start()
    loads = [pltpu.make_async_copy(normed_in, normed, sems.at[3])]
    low = 0
    for i, weight in enumerate((w_query, w_key, w_value)):
        part = weights.at[:, low : low + weight.shape[1]]
        loads.append(pltpu.make_async_copy(weight, part, sems.at[i]))
        low += weight.shape[1]
    for c in range(CHUNKS):
        part = pl.ds(c * per, per)
        loads.append(pltpu.make_async_copy(pool.at[part], held.at[part], pool_sems.at[c]))
    for copy in loads:
        copy.start()
    for copy in loads[:4]:
        copy.wait()
    hidden = jnp.concatenate([normed[s].astype(jnp.float32) for s in range(STEPS)], 0).astype(jnp.bfloat16)
    result = jnp.dot(hidden, weights[...], preferred_element_type=jnp.float32)
    for p in range(pairs):
        for s in range(STEPS):
            row = s * requests + p % requests
            partial[p, s : s + 1] = result[row : row + 1]
    table_copy.wait()
    for copy in loads[4:]:
        copy.wait()

    @pl.when(lax.axis_index("pair") >= requests)
    def _():
        low = 0
        for piece in pieces:

            def take(j, carry):
                piece[j] = held[table[0, low + j]]
                return carry

            lax.fori_loop(0, piece.shape[0], take, 0, unroll=4)
            low += piece.shape[0]


def prepare(table, normed, w_query, w_key, w_value, pool, pairs):
    page = pool.shape[1:]
    wide = w_query.shape[1] + 2 * w_key.shape[1]
    return pl.pallas_call(
        prepare_kernel,
        out_shape=(jax.ShapeDtypeStruct((pairs, STEPS, wide), jnp.float32), pltpu.VMEM(pool.shape, pool.dtype))
        + tuple(pltpu.VMEM((n,) + page, pool.dtype) for n in PIECES),
        in_specs=[HBM] * 6,
        out_specs=(VMEM,) * (2 + len(PIECES)),
        scratch_shapes=[
            pltpu.SMEM(table.shape, table.dtype),
            pltpu.VMEM(normed.shape, normed.dtype),
            pltpu.VMEM((w_query.shape[0], wide), w_query.dtype),
            pltpu.SemaphoreType.DMA,
            pltpu.SemaphoreType.DMA((4,)),
            pltpu.SemaphoreType.DMA((CHUNKS,)),
        ],
        compiler_params=params(16),
        name="prepare",
    )(*in_hbm(table, normed, w_query, w_key, w_value, pool))


def page_order(table, slots):
    slot = lax.broadcasted_iota(jnp.int32, (slots, slots), 0)
    holds = jnp.where(slot == table, 1.0, 0.0).astype(jnp.bfloat16)
    index = lax.broadcasted_iota(jnp.int32, (8, slots), 1)
    digit = lax.broadcasted_iota(jnp.int32, (8, slots), 0)
    digits = jnp.where(digit == 0, index // 16, jnp.where(digit == 1, index % 16, 0))
    digits = digits.astype(jnp.float32).astype(jnp.bfloat16)
    return lax.dot_general(digits, holds, (((1,), (1,)), ((), ())), preferred_element_type=jnp.float32)


def attention_kernel(
    lengths, table, sums, b_query, b_key, b_value, cosine, sine, held, packed, entries, score
):
    slots, page_len, _ = held.shape
    requests = sums.shape[0] // 2
    group, head = b_query.shape
    rows = STEPS * group
    pair_index = lax.axis_index("pair")
    is_source = pair_index >= requests
    request = jnp.where(is_source, pair_index - requests, pair_index)
    half_tokens = PAGES_HALF * page_len
    limit = jnp.where(is_source, lengths[request] - half_tokens, half_tokens)

    blocks = 4
    block = slots // blocks
    width = block * page_len
    digits = page_order(table[...], slots)
    digits = jnp.concatenate(
        [digits[d : d + 1, c * block : (c + 1) * block] for d in range(2) for c in range(blocks)], 0
    ).astype(jnp.bfloat16)
    spread = lax.broadcasted_iota(jnp.int32, (block, width), 1) // page_len
    spread = jnp.where(spread == lax.broadcasted_iota(jnp.int32, (block, width), 0), 1.0, 0.0)
    digits = jnp.dot(digits, spread.astype(jnp.bfloat16), preferred_element_type=jnp.float32)
    tokens = (digits[:blocks] * 16.0 + digits[blocks:]).astype(jnp.int32) * page_len
    tokens = tokens + lax.broadcasted_iota(jnp.int32, (blocks, width), 1) % page_len

    total = sums[0]
    for p in range(1, sums.shape[0]):
        total = total + sums[p]
    query = jnp.concatenate(
        [total[s : s + 1, h * head : (h + 1) * head] for s in range(STEPS) for h in range(group)], 0
    )
    query = query + jnp.concatenate([b_query[...]] * STEPS, 0)
    cos_new = cosine[request]
    sin_new = sine[request]
    row = lax.broadcasted_iota(jnp.int32, (rows, head), 0)
    cos_rows = jnp.where(row < group, cos_new[0:1], cos_new[1:2])
    sin_rows = jnp.where(row < group, sin_new[0:1], sin_new[1:2])
    query = (query * cos_rows + pltpu.roll(query, head // 2, 1) * sin_rows).astype(jnp.bfloat16)
    key_new = total[:, group * head : (group + 1) * head] + b_key[...]
    key_new = jnp.concatenate([key_new, jnp.zeros((8 - STEPS, head), jnp.float32)], 0)
    key_new = key_new * cos_new + pltpu.roll(key_new, head // 2, 1) * sin_new
    key_new = key_new.astype(jnp.bfloat16).astype(jnp.float32)
    value_new = total[:, (group + 1) * head :] + b_value[...]
    value_new = value_new.astype(jnp.bfloat16).astype(jnp.float32)
    entries[:, :head] = key_new
    entries[0:STEPS, head:] = value_new
    entries[STEPS:, head:] = jnp.zeros((8 - STEPS, head), jnp.float32)
    scale = 1.0 / math.sqrt(head)

    column = lax.broadcasted_iota(jnp.int32, (rows, 1), 0)
    query_wide = query.astype(jnp.float32)
    fresh = []
    for s in range(STEPS):
        dots = jnp.sum(query_wide * key_new[s : s + 1], 1, keepdims=True) * scale
        seen = jnp.logical_and(is_source, column >= s * group)
        fresh.append((jnp.where(seen, dots, NEG), seen))
    row_max = jnp.maximum(fresh[0][0], fresh[1][0])

    for c in range(blocks):
        keys = held[c * block : (c + 1) * block, :, :head].reshape(width, head)
        part = lax.dot_general(query, keys, (((1,), (1,)), ((), ())), preferred_element_type=jnp.float32)
        part = jnp.where(tokens[c : c + 1] < limit, part * scale, NEG)
        score[:, c * width : (c + 1) * width] = part
        row_max = jnp.maximum(row_max, jnp.max(part, 1, keepdims=True))
    row_sum = jnp.zeros((rows, 1), jnp.float32)
    out = jnp.zeros((rows, head), jnp.float32)
    for s in range(STEPS):
        weight = jnp.where(fresh[s][1], jnp.exp(fresh[s][0] - row_max), 0.0)
        row_sum = row_sum + weight
        out = out + weight.astype(jnp.bfloat16).astype(jnp.float32) * value_new[s : s + 1]
    for c in range(blocks):
        weight = jnp.exp(score[:, c * width : (c + 1) * width] - row_max)
        weight = jnp.where(tokens[c : c + 1] < limit, weight, 0.0)
        row_sum = row_sum + jnp.sum(weight, 1, keepdims=True)
        values = held[c * block : (c + 1) * block, :, head:].reshape(width, head)
        out = out + jnp.dot(weight.astype(jnp.bfloat16), values, preferred_element_type=jnp.float32)

    diagonal = lax.broadcasted_iota(jnp.int32, (rows, head), 1) == row
    for p in range(packed.shape[0]):
        packed[p, 0:rows] = out
        packed[p, rows : rows + 1] = jnp.sum(jnp.where(diagonal, row_max, 0.0), 0, keepdims=True)
        packed[p, rows + 1 : rows + 2] = jnp.sum(jnp.where(diagonal, row_sum, 0.0), 0, keepdims=True)
        packed[p, rows + 2 :] = jnp.zeros((packed.shape[1] - rows - 2, head), jnp.float32)


def attend(lengths, table, sums, b_query, b_key, b_value, cosine, sine, held):
    group, head = b_query.shape
    rows = STEPS * group
    return pl.pallas_call(
        attention_kernel,
        out_shape=(
            jax.ShapeDtypeStruct((sums.shape[0], rows + 8, head), jnp.float32),
            jax.ShapeDtypeStruct((8, 2 * head), jnp.float32),
        ),
        in_specs=[SMEM] + [VMEM] * 8,
        out_specs=(VMEM, VMEM),
        scratch_shapes=[pltpu.VMEM((rows, held.shape[0] * held.shape[1]), jnp.float32)],
        compiler_params=params(16),
        name="attend",
    )(lengths, table, sums, b_query, b_key, b_value, cosine, sine, held)


def project_kernel(parts, w_out, out):
    pairs, packed_rows, head = parts.shape
    rows = packed_rows - 8
    group = rows // STEPS
    requests = pairs // 2
    lane = lax.broadcasted_iota(jnp.int32, (rows, head), 1)
    diagonal = lane == lax.broadcasted_iota(jnp.int32, (rows, head), 0)

    def as_column(line):
        return jnp.sum(jnp.where(diagonal, line, 0.0), 1, keepdims=True)

    merged = []
    for r in range(requests):
        first_max, first_sum = (as_column(parts[r, rows + i : rows + i + 1]) for i in range(2))
        second_max, second_sum = (as_column(parts[r + requests, rows + i : rows + i + 1]) for i in range(2))
        top = jnp.maximum(first_max, second_max)
        first_weight = jnp.exp(first_max - top)
        second_weight = jnp.exp(second_max - top)
        joined = first_weight * parts[r, :rows] + second_weight * parts[r + requests, :rows]
        merged.append(joined / (first_weight * first_sum + second_weight * second_sum))
    lines = []
    for s in range(STEPS):
        for r in range(requests):
            lines.append(
                jnp.concatenate(
                    [merged[r][s * group + h : s * group + h + 1] for h in range(group)], 1
                )
            )
    attended = jnp.concatenate(lines, 0).astype(jnp.bfloat16)
    result = jnp.dot(attended, w_out[...], preferred_element_type=jnp.float32)
    for s in range(STEPS):
        out[s] = result[s * requests : (s + 1) * requests]


def project(parts, w_out):
    return pl.pallas_call(
        project_kernel,
        out_shape=jax.ShapeDtypeStruct((STEPS, parts.shape[0] // 2, w_out.shape[1]), jnp.float32),
        in_specs=[VMEM, VMEM],
        out_specs=VMEM,
        compiler_params=params(16),
        name="project",
    )(parts, w_out)


def moved_pages(plan, request):
    count = plan[request, 0]
    for s in range(1, STEPS):
        count = count + plan[request, s]
    return count


def copy_kernel(table, lengths, plan, entries, held_in, *refs):
    early, (new_pool, held, out_sems) = refs[:-3], refs[-3:]
    del held_in
    slots, page_len, width = held.shape
    per = slots // CHUNKS
    requests = lengths.shape[0]
    pair_index = lax.axis_index("pair")
    is_source = pair_index >= requests

    @pl.when(is_source)
    def _():
        page_row = lax.broadcasted_iota(jnp.int32, (page_len, width), 0)
        first_new = lengths[pair_index - requests] - PAGES_HALF * page_len
        for s in range(STEPS):
            offset = first_new + s
            slot = table[0, offset // page_len]
            old = held[slot].astype(jnp.float32)
            held[slot] = jnp.where(page_row == offset % page_len, entries[s : s + 1], old).astype(held.dtype)

    @pl.when(jnp.logical_not(is_source))
    def _():
        count = moved_pages(plan, pair_index)
        low = 0
        for pages in early:

            def place(j, carry):
                held[table[0, PAGES_HALF + low + j]] = pages[j]
                return carry

            lax.fori_loop(0, jnp.clip(count - low, 0, pages.shape[0]), place, 0)
            low += pages.shape[0]

    copies = []
    for c in range(CHUNKS):
        part = pl.ds(c * per, per)
        copies.append(pltpu.make_async_copy(held.at[part], new_pool.at[part], out_sems.at[c]))
        copies[-1].start()
    for copy in copies:
        copy.wait()


def copy_pool(table, lengths, plan, entries, held, early):
    return pl.pallas_call(
        copy_kernel,
        out_shape=(pltpu.HBM(held.shape, held.dtype), pltpu.VMEM(held.shape, held.dtype)),
        in_specs=[SMEM, SMEM, SMEM, VMEM, VMEM] + [VMEM] * len(early),
        out_specs=(HBM, VMEM),
        scratch_shapes=[pltpu.SemaphoreType.DMA((CHUNKS,))],
        input_output_aliases={4: 1},
        compiler_params=params(16),
        name="copy_pool",
    )(table, lengths, plan, entries, held, *early)[0]


def place_kernel(table, plan, *refs, done, only):
    pages, (base, new_pool, sem) = refs[:-3], refs[-3:]
    del base
    pair_index = lax.axis_index("pair")
    targets = jnp.logical_and(pair_index >= only[0], pair_index < only[1])

    @pl.when(targets)
    def _():
        count = moved_pages(plan, pair_index)
        low = done
        for part in pages:
            here = jnp.clip(count - low, 0, part.shape[0])

            def start(j, carry):
                slot = table[0, PAGES_HALF + low + j]
                pltpu.make_async_copy(part.at[j], new_pool.at[slot], sem).start()
                return carry

            lax.fori_loop(0, here, start, 0)
            low += part.shape[0]

        def wait(j, carry):
            pltpu.make_async_copy(pages[0].at[0], new_pool.at[0], sem).wait()
            return carry

        lax.fori_loop(0, jnp.clip(count - done, 0, low - done), wait, 0)


def place(table, plan, pages, base, done, only):
    return pl.pallas_call(
        functools.partial(place_kernel, done=done, only=only),
        out_shape=pltpu.HBM(base.shape, base.dtype),
        in_specs=[SMEM, SMEM] + [VMEM] * len(pages) + [HBM],
        out_specs=HBM,
        scratch_shapes=[pltpu.SemaphoreType.DMA],
        input_output_aliases={2 + len(pages): 0},
        compiler_params=params(16),
        name="place",
    )(table, plan, *pages, *in_hbm(base))


def local(
    normed, w_query, b_query, w_key, b_key, w_value, b_value, w_out, pool, page_table, lengths, plan
):
    pair_count = lax.axis_size("pair")
    tp_count = lax.axis_size("tp")
    requests = pair_count // 2
    head = w_key.shape[1]

    partial, held, *pieces = prepare(page_table, normed, w_query, w_key, w_value, pool[0, 0], pair_count)

    def migrate(pages, after, members):
        pages = lax.optimization_barrier((pages, after))[0]
        return lax.ppermute(pages, "pair", [(r + requests, r) for r in members])

    everyone = range(requests)
    first = lax.ppermute(pieces[0], "pair", [(r + requests, r) for r in everyone])
    sums = lax.all_to_all(partial, "pair", split_axis=0, concat_axis=0, tiled=True)

    frequency = rope_base ** (-(jnp.arange(head // 2, dtype=jnp.float32) * 2.0 / head))
    steps = jnp.minimum(jnp.arange(8, dtype=jnp.int32), STEPS - 1)
    position = (lengths[:, None] + steps[None, :]).astype(jnp.float32)[..., None]
    angles = position * frequency
    cosine = jnp.cos(angles)
    sine = jnp.sin(angles)
    cosine = jnp.concatenate([cosine, cosine], -1)
    sine = jnp.concatenate([-sine, sine], -1)

    packed, entries = attend(
        lengths,
        page_table,
        sums,
        b_query.reshape(-1, head),
        b_key[None, :],
        b_value[None, :],
        cosine,
        sine,
        held,
    )
    second = migrate(pieces[1], packed, everyone)
    packed, first = lax.optimization_barrier((packed, first))
    parts = lax.all_to_all(packed, "pair", split_axis=0, concat_axis=0, tiled=True)
    third = migrate(pieces[2], parts, everyone)
    parts, second = lax.optimization_barrier((parts, second))
    projected = project(parts, w_out)
    new_pool = copy_pool(page_table, lengths, plan, entries, held, [first, second])
    if tp_count == 2:
        projected = projected + lax.ppermute(projected, "tp", [(0, 1), (1, 0)])
    else:
        projected = lax.psum(projected, "tp")

    static = sum(EARLY)
    late = pieces[len(EARLY) :]
    bounds = [static + sum(LATE[:i]) for i in range(len(LATE))]
    choices = len(LATE) + 1
    new_pool, third, projected = lax.optimization_barrier((new_pool, third, projected))

    def send(levels, low, base, third, *chunks):
        arrived = []
        for i, chunk in enumerate(chunks):
            members = [low + r for r, level in enumerate(levels) if level > i]
            if members:
                arrived.append(lax.ppermute(chunk, "pair", [(r + requests, r) for r in members]))
        return place(page_table, plan, [third] + arrived, base, static - EARLY[-1], (low, low + len(levels)))

    for low in range(0, requests, JOINT):
        size = min(JOINT, requests - low)
        counts = jnp.sum(plan[low : low + size], 1)
        levels = sum((counts > bound).astype(jnp.int32) for bound in bounds)
        index = jnp.sum(levels * jnp.array([choices**r for r in range(size)], jnp.int32))
        branches = [
            functools.partial(send, [code // choices**r % choices for r in range(size)], low)
            for code in range(choices**size)
        ]
        new_pool = lax.switch(index, branches, new_pool, third, *late)
    return projected, new_pool[None, None]


def solution(mesh):
    return jax.shard_map(
        local,
        mesh=mesh,
        in_specs=(
            P(None, "rep", "pair"),
            P("pair", "tp"),
            P("tp"),
            P("pair", "tp"),
            P("tp"),
            P("pair", "tp"),
            P("tp"),
            P("tp", "pair"),
            P(("rep", "pair"), "tp", None, None, None),
            P(("rep", "pair"), None),
            P("rep"),
            P("rep", None),
        ),
        out_specs=(P(None, "rep", "pair"), P(("rep", "pair"), "tp", None, None, None)),
        check_vma=False,
    )
```

```python
import functools
import math

import jax
import jax.numpy as jnp
from jax import lax
from jax.experimental import pallas as pl
from jax.experimental.pallas import tpu as pltpu
from jax.sharding import PartitionSpec as P

PAGES_HALF = 384
STEPS = 2
SECTION = 64
MOVED_MAX = STEPS * SECTION
EARLY = (40, 14, 32)
LATE = (21, 42)
PIECES = EARLY + LATE
CHUNKS = 8
NEG = -1e30

rope_base = 1000000.0

VMEM = pl.BlockSpec(memory_space=pltpu.VMEM)
SMEM = pl.BlockSpec(memory_space=pltpu.SMEM)
HBM = pl.BlockSpec(memory_space=pltpu.HBM)


def in_hbm(*arrays):
    return tuple(pltpu.with_memory_space_constraint(a, pltpu.HBM) for a in arrays)


def params(mib):
    return pltpu.CompilerParams(vmem_limit_bytes=mib * 1024 * 1024)


def prepare_kernel(table_in, normed_in, w_query, w_key, w_value, pool, partial, *refs):
    pieces, (table, normed, weights, table_sem, sems, page_sems) = refs[:-6], refs[-6:]
    pairs = partial.shape[0]
    requests = pairs // 2
    table_copy = pltpu.make_async_copy(table_in, table, table_sem)
    table_copy.start()
    loads = [pltpu.make_async_copy(normed_in, normed, sems.at[3])]
    low = 0
    for i, weight in enumerate((w_query, w_key, w_value)):
        part = weights.at[:, low : low + weight.shape[1]]
        loads.append(pltpu.make_async_copy(weight, part, sems.at[i]))
        low += weight.shape[1]
    for copy in loads:
        copy.start()
    table_copy.wait()

    @pl.when(lax.axis_index("pair") >= requests)
    def _():
        low = 0
        for i, piece in enumerate(pieces):

            def start(j, carry):
                pltpu.make_async_copy(pool.at[table[0, low + j]], piece.at[j], page_sems.at[i]).start()
                return carry

            lax.fori_loop(0, piece.shape[0], start, 0, unroll=7 if i >= len(EARLY) else 8)
            if i < len(EARLY):
                low += piece.shape[0]

    for copy in loads:
        copy.wait()
    hidden = jnp.concatenate([normed[s].astype(jnp.float32) for s in range(STEPS)], 0).astype(jnp.bfloat16)
    result = jnp.dot(hidden, weights[...], preferred_element_type=jnp.float32)
    for p in range(pairs):
        for s in range(STEPS):
            row = s * requests + p % requests
            partial[p, s : s + 1] = result[row : row + 1]

    @pl.when(lax.axis_index("pair") >= requests)
    def _():
        for i, piece in enumerate(pieces):
            pltpu.make_async_copy(pool.at[pl.ds(0, piece.shape[0])], piece, page_sems.at[i]).wait()


def prepare(table, normed, w_query, w_key, w_value, pool, pairs):
    page = pool.shape[1:]
    wide = w_query.shape[1] + 2 * w_key.shape[1]
    return pl.pallas_call(
        prepare_kernel,
        out_shape=(jax.ShapeDtypeStruct((pairs, STEPS, wide), jnp.float32),)
        + tuple(pltpu.VMEM((n,) + page, pool.dtype) for n in PIECES),
        in_specs=[HBM] * 6,
        out_specs=(VMEM,) + (VMEM,) * len(PIECES),
        scratch_shapes=[
            pltpu.SMEM(table.shape, table.dtype),
            pltpu.VMEM(normed.shape, normed.dtype),
            pltpu.VMEM((w_query.shape[0], wide), w_query.dtype),
            pltpu.SemaphoreType.DMA,
            pltpu.SemaphoreType.DMA((4,)),
            pltpu.SemaphoreType.DMA((len(PIECES),)),
        ],
        compiler_params=params(16),
        name="prepare",
    )(*in_hbm(table, normed, w_query, w_key, w_value, pool))


def page_order(table, slots):
    slot = lax.broadcasted_iota(jnp.int32, (slots, slots), 0)
    holds = jnp.where(slot == table, 1.0, 0.0).astype(jnp.bfloat16)
    index = lax.broadcasted_iota(jnp.int32, (8, slots), 1)
    digit = lax.broadcasted_iota(jnp.int32, (8, slots), 0)
    digits = jnp.where(digit == 0, index // 16, jnp.where(digit == 1, index % 16, 0))
    digits = digits.astype(jnp.float32).astype(jnp.bfloat16)
    return lax.dot_general(digits, holds, (((1,), (1,)), ((), ())), preferred_element_type=jnp.float32)


def attention_kernel(
    lengths, table, sums, b_query, b_key, b_value, cosine, sine, pool, packed, entries, held, score, sems
):
    slots, page_len, _ = held.shape
    per = slots // CHUNKS
    copies = []
    for c in range(CHUNKS):
        part = pl.ds(c * per, per)
        copies.append(pltpu.make_async_copy(pool.at[part], held.at[part], sems.at[c]))
        copies[-1].start()
    requests = sums.shape[0] // 2
    group, head = b_query.shape
    rows = STEPS * group
    pair_index = lax.axis_index("pair")
    is_source = pair_index >= requests
    request = jnp.where(is_source, pair_index - requests, pair_index)
    half_tokens = PAGES_HALF * page_len
    limit = jnp.where(is_source, lengths[request] - half_tokens, half_tokens)

    blocks = CHUNKS // 2
    block = slots // blocks
    width = block * page_len
    digits = page_order(table[...], slots)
    digits = jnp.concatenate(
        [digits[d : d + 1, c * block : (c + 1) * block] for d in range(2) for c in range(blocks)], 0
    ).astype(jnp.bfloat16)
    spread = lax.broadcasted_iota(jnp.int32, (block, width), 1) // page_len
    spread = jnp.where(spread == lax.broadcasted_iota(jnp.int32, (block, width), 0), 1.0, 0.0)
    digits = jnp.dot(digits, spread.astype(jnp.bfloat16), preferred_element_type=jnp.float32)
    tokens = (digits[:blocks] * 16.0 + digits[blocks:]).astype(jnp.int32) * page_len
    tokens = tokens + lax.broadcasted_iota(jnp.int32, (blocks, width), 1) % page_len

    total = sums[0]
    for p in range(1, sums.shape[0]):
        total = total + sums[p]
    query = jnp.concatenate(
        [total[s : s + 1, h * head : (h + 1) * head] for s in range(STEPS) for h in range(group)], 0
    )
    query = query + jnp.concatenate([b_query[...]] * STEPS, 0)
    cos_new = cosine[request]
    sin_new = sine[request]
    row = lax.broadcasted_iota(jnp.int32, (rows, head), 0)
    cos_rows = jnp.where(row < group, cos_new[0:1], cos_new[1:2])
    sin_rows = jnp.where(row < group, sin_new[0:1], sin_new[1:2])
    query = (query * cos_rows + pltpu.roll(query, head // 2, 1) * sin_rows).astype(jnp.bfloat16)
    key_new = total[:, group * head : (group + 1) * head] + b_key[...]
    key_new = jnp.concatenate([key_new, jnp.zeros((8 - STEPS, head), jnp.float32)], 0)
    key_new = key_new * cos_new + pltpu.roll(key_new, head // 2, 1) * sin_new
    key_new = key_new.astype(jnp.bfloat16).astype(jnp.float32)
    value_new = total[:, (group + 1) * head :] + b_value[...]
    value_new = value_new.astype(jnp.bfloat16).astype(jnp.float32)
    entries[:, :head] = key_new
    entries[0:STEPS, head:] = value_new
    entries[STEPS:, head:] = jnp.zeros((8 - STEPS, head), jnp.float32)
    scale = 1.0 / math.sqrt(head)

    column = lax.broadcasted_iota(jnp.int32, (rows, 1), 0)
    query_wide = query.astype(jnp.float32)
    fresh = []
    for s in range(STEPS):
        dots = jnp.sum(query_wide * key_new[s : s + 1], 1, keepdims=True) * scale
        seen = jnp.logical_and(is_source, column >= s * group)
        fresh.append((jnp.where(seen, dots, NEG), seen))
    row_max = jnp.maximum(fresh[0][0], fresh[1][0])

    for c in range(blocks):
        copies[2 * c].wait()
        copies[2 * c + 1].wait()
        keys = held[c * block : (c + 1) * block, :, :head].reshape(width, head)
        part = lax.dot_general(query, keys, (((1,), (1,)), ((), ())), preferred_element_type=jnp.float32)
        part = jnp.where(tokens[c : c + 1] < limit, part * scale, NEG)
        score[:, c * width : (c + 1) * width] = part
        row_max = jnp.maximum(row_max, jnp.max(part, 1, keepdims=True))
    row_sum = jnp.zeros((rows, 1), jnp.float32)
    out = jnp.zeros((rows, head), jnp.float32)
    for s in range(STEPS):
        weight = jnp.where(fresh[s][1], jnp.exp(fresh[s][0] - row_max), 0.0)
        row_sum = row_sum + weight
        out = out + weight.astype(jnp.bfloat16).astype(jnp.float32) * value_new[s : s + 1]
    for c in range(blocks):
        weight = jnp.exp(score[:, c * width : (c + 1) * width] - row_max)
        weight = jnp.where(tokens[c : c + 1] < limit, weight, 0.0)
        row_sum = row_sum + jnp.sum(weight, 1, keepdims=True)
        values = held[c * block : (c + 1) * block, :, head:].reshape(width, head)
        out = out + jnp.dot(weight.astype(jnp.bfloat16), values, preferred_element_type=jnp.float32)

    diagonal = lax.broadcasted_iota(jnp.int32, (rows, head), 1) == row
    for p in range(packed.shape[0]):
        packed[p, 0:rows] = out
        packed[p, rows : rows + 1] = jnp.sum(jnp.where(diagonal, row_max, 0.0), 0, keepdims=True)
        packed[p, rows + 1 : rows + 2] = jnp.sum(jnp.where(diagonal, row_sum, 0.0), 0, keepdims=True)
        packed[p, rows + 2 :] = jnp.zeros((packed.shape[1] - rows - 2, head), jnp.float32)


def attend(lengths, table, sums, b_query, b_key, b_value, cosine, sine, pool):
    group, head = b_query.shape
    rows = STEPS * group
    return pl.pallas_call(
        attention_kernel,
        out_shape=(
            jax.ShapeDtypeStruct((sums.shape[0], rows + 8, head), jnp.float32),
            jax.ShapeDtypeStruct((8, 2 * head), jnp.float32),
        ),
        in_specs=[SMEM] + [VMEM] * 7 + [HBM],
        out_specs=(VMEM, VMEM),
        scratch_shapes=[
            pltpu.VMEM(pool.shape, pool.dtype),
            pltpu.VMEM((rows, pool.shape[0] * pool.shape[1]), jnp.float32),
            pltpu.SemaphoreType.DMA((CHUNKS,)),
        ],
        compiler_params=params(24),
        name="attend",
    )(lengths, table, sums, b_query, b_key, b_value, cosine, sine, *in_hbm(pool))


def project_kernel(parts, w_out, out):
    pairs, packed_rows, head = parts.shape
    rows = packed_rows - 8
    group = rows // STEPS
    requests = pairs // 2
    lane = lax.broadcasted_iota(jnp.int32, (rows, head), 1)
    diagonal = lane == lax.broadcasted_iota(jnp.int32, (rows, head), 0)

    def as_column(line):
        return jnp.sum(jnp.where(diagonal, line, 0.0), 1, keepdims=True)

    merged = []
    for r in range(requests):
        first_max, first_sum = (as_column(parts[r, rows + i : rows + i + 1]) for i in range(2))
        second_max, second_sum = (as_column(parts[r + requests, rows + i : rows + i + 1]) for i in range(2))
        top = jnp.maximum(first_max, second_max)
        first_weight = jnp.exp(first_max - top)
        second_weight = jnp.exp(second_max - top)
        joined = first_weight * parts[r, :rows] + second_weight * parts[r + requests, :rows]
        merged.append(joined / (first_weight * first_sum + second_weight * second_sum))
    lines = []
    for s in range(STEPS):
        for r in range(requests):
            lines.append(
                jnp.concatenate(
                    [merged[r][s * group + h : s * group + h + 1] for h in range(group)], 1
                )
            )
    attended = jnp.concatenate(lines, 0).astype(jnp.bfloat16)
    result = jnp.dot(attended, w_out[...], preferred_element_type=jnp.float32)
    for s in range(STEPS):
        out[s] = result[s * requests : (s + 1) * requests]


def project(parts, w_out):
    return pl.pallas_call(
        project_kernel,
        out_shape=jax.ShapeDtypeStruct((STEPS, parts.shape[0] // 2, w_out.shape[1]), jnp.float32),
        in_specs=[VMEM, VMEM],
        out_specs=VMEM,
        compiler_params=params(16),
        name="project",
    )(parts, w_out)


def moved_pages(plan, request):
    count = plan[request, 0]
    for s in range(1, STEPS):
        count = count + plan[request, s]
    return count


def copy_kernel(table, lengths, plan, entries, pool, *refs):
    early, (new_pool, held, sems, out_sems) = refs[:-4], refs[-4:]
    slots, page_len, width = held.shape
    per = slots // CHUNKS
    requests = lengths.shape[0]
    pair_index = lax.axis_index("pair")
    is_source = pair_index >= requests

    def fetch(c):
        part = pl.ds(c * per, per)
        return pltpu.make_async_copy(pool.at[part], held.at[part], sems.at[c])

    def store(c):
        part = pl.ds(c * per, per)
        return pltpu.make_async_copy(held.at[part], new_pool.at[part], out_sems.at[c])

    for c in range(CHUNKS):
        fetch(c).start()
    for c in range(CHUNKS):
        fetch(c).wait()

    @pl.when(is_source)
    def _():
        page_row = lax.broadcasted_iota(jnp.int32, (page_len, width), 0)
        first_new = lengths[pair_index - requests] - PAGES_HALF * page_len
        for s in range(STEPS):
            offset = first_new + s
            slot = table[0, offset // page_len]
            old = held[slot].astype(jnp.float32)
            held[slot] = jnp.where(page_row == offset % page_len, entries[s : s + 1], old).astype(held.dtype)

    @pl.when(jnp.logical_not(is_source))
    def _():
        count = moved_pages(plan, pair_index)
        low = 0
        for pages in early:

            def place(j, carry):
                held[table[0, PAGES_HALF + low + j]] = pages[j]
                return carry

            lax.fori_loop(0, jnp.clip(count - low, 0, pages.shape[0]), place, 0)
            low += pages.shape[0]

    for c in range(CHUNKS):
        store(c).start()
    for c in range(CHUNKS):
        store(c).wait()


def copy_pool(table, lengths, plan, entries, pool, early):
    return pl.pallas_call(
        copy_kernel,
        out_shape=jax.ShapeDtypeStruct(pool.shape, pool.dtype),
        in_specs=[SMEM, SMEM, SMEM, VMEM, HBM] + [VMEM] * len(early),
        out_specs=HBM,
        scratch_shapes=[
            pltpu.VMEM(pool.shape, pool.dtype),
            pltpu.SemaphoreType.DMA((CHUNKS,)),
            pltpu.SemaphoreType.DMA((CHUNKS,)),
        ],
        compiler_params=params(24),
        name="copy_pool",
    )(table, lengths, plan, entries, *in_hbm(pool), *early)


def place_kernel(table_in, plan_in, pages, base, new_pool, table, plan, sems, sem, *, done, only):
    del base
    pair_index = lax.axis_index("pair")

    @pl.when(jnp.logical_and(pair_index >= only[0], pair_index < only[1]))
    def _():
        table_copy = pltpu.make_async_copy(table_in, table, sems.at[0])
        plan_copy = pltpu.make_async_copy(plan_in, plan, sems.at[1])
        table_copy.start()
        plan_copy.start()
        table_copy.wait()
        plan_copy.wait()
        count = jnp.clip(moved_pages(plan, pair_index) - done, 0, pages.shape[0])

        def start(j, carry):
            slot = table[0, PAGES_HALF + done + j]
            pltpu.make_async_copy(pages.at[j], new_pool.at[slot], sem).start()
            return carry

        def wait(j, carry):
            pltpu.make_async_copy(pages.at[0], new_pool.at[0], sem).wait()
            return carry

        lax.fori_loop(0, count, start, 0)
        lax.fori_loop(0, count, wait, 0)


def place(table, plan, pages, base, done, only):
    return pl.pallas_call(
        functools.partial(place_kernel, done=done, only=only),
        out_shape=pltpu.HBM(base.shape, base.dtype),
        in_specs=[HBM, HBM, VMEM, HBM],
        out_specs=HBM,
        scratch_shapes=[
            pltpu.SMEM(table.shape, table.dtype),
            pltpu.SMEM(plan.shape, plan.dtype),
            pltpu.SemaphoreType.DMA((2,)),
            pltpu.SemaphoreType.DMA,
        ],
        input_output_aliases={3: 0},
        compiler_params=params(16),
        name="place",
    )(*in_hbm(table, plan), pages, *in_hbm(base))


def local(
    normed, w_query, b_query, w_key, b_key, w_value, b_value, w_out, pool, page_table, lengths, plan
):
    pair_count = lax.axis_size("pair")
    tp_count = lax.axis_size("tp")
    requests = pair_count // 2
    head = w_key.shape[1]

    partial, *pieces = prepare(page_table, normed, w_query, w_key, w_value, pool[0, 0], pair_count)
    route = [(i + requests, i) for i in range(requests)]

    def migrate(pages):
        return lax.ppermute(pages, "pair", route)

    def tie(*values):
        return lax.optimization_barrier(values)

    first = migrate(pieces[0])
    sums = lax.all_to_all(partial, "pair", split_axis=0, concat_axis=0, tiled=True)
    sums, first = tie(sums, first)
    second = migrate(pieces[1])

    frequency = rope_base ** (-(jnp.arange(head // 2, dtype=jnp.float32) * 2.0 / head))
    steps = jnp.minimum(jnp.arange(8, dtype=jnp.int32), STEPS - 1)
    position = (lengths[:, None] + steps[None, :]).astype(jnp.float32)[..., None]
    angles = position * frequency
    cosine = jnp.cos(angles)
    sine = jnp.sin(angles)
    cosine = jnp.concatenate([cosine, cosine], -1)
    sine = jnp.concatenate([-sine, sine], -1)

    packed, entries = attend(
        lengths,
        page_table,
        sums,
        b_query.reshape(-1, head),
        b_key[None, :],
        b_value[None, :],
        cosine,
        sine,
        pool[0, 0],
    )
    packed, second = tie(packed, second)
    parts = lax.all_to_all(packed, "pair", split_axis=0, concat_axis=0, tiled=True)
    third = migrate(tie(pieces[2], parts)[0])
    new_pool = copy_pool(page_table, lengths, plan, entries, pool[0, 0], [first, second])
    projected = project(parts, w_out)
    if tp_count == 2:
        projected = projected + lax.ppermute(projected, "tp", [(0, 1), (1, 0)])
    else:
        projected = lax.psum(projected, "tp")
    new_pool = place(page_table, plan, third, new_pool, EARLY[0] + EARLY[1], (0, requests))

    static = sum(EARLY)
    counts = jnp.sum(plan, 1)
    levels = (counts > static).astype(jnp.int32) + (counts > static + LATE[0]).astype(jnp.int32)
    new_pool, projected = tie(new_pool, projected)
    late = pieces[len(EARLY) :]

    def send(level, request, base, *chunks):
        if level == 0:
            return base
        arrived = lax.ppermute(chunks[level - 1], "pair", [(request + requests, request)])
        return place(page_table, plan, arrived, base, static, (request, request + 1))

    for request in range(requests):
        branches = [functools.partial(send, level, request) for level in range(len(LATE) + 1)]
        new_pool = lax.switch(levels[request], branches, new_pool, *late)
    return projected, new_pool[None, None]


def solution(mesh):
    return jax.shard_map(
        local,
        mesh=mesh,
        in_specs=(
            P(None, "rep", "pair"),
            P("pair", "tp"),
            P("tp"),
            P("pair", "tp"),
            P("tp"),
            P("pair", "tp"),
            P("tp"),
            P("tp", "pair"),
            P(("rep", "pair"), "tp", None, None, None),
            P(("rep", "pair"), None),
            P("rep"),
            P("rep", None),
        ),
        out_specs=(P(None, "rep", "pair"), P(("rep", "pair"), "tp", None, None, None)),
        check_vma=False,
    )
```

```python
import functools
import math

import jax
import jax.numpy as jnp
from jax import lax
from jax.experimental import pallas as pl
from jax.experimental.pallas import tpu as pltpu
from jax.sharding import PartitionSpec as P

PAGES_HALF = 384
STEPS = 2
SECTION = 64
MOVED_MAX = STEPS * SECTION
EARLY = (40, 28, 32)
LATE = 28
PIECES = EARLY + (LATE,)
CHUNKS = 8
NEG = -1e30

rope_base = 1000000.0

VMEM = pl.BlockSpec(memory_space=pltpu.VMEM)
SMEM = pl.BlockSpec(memory_space=pltpu.SMEM)
HBM = pl.BlockSpec(memory_space=pltpu.HBM)


def in_hbm(*arrays):
    return tuple(pltpu.with_memory_space_constraint(a, pltpu.HBM) for a in arrays)


SMALL = pl.CostEstimate(flops=0, bytes_accessed=0, transcendentals=0)


def params(mib):
    return pltpu.CompilerParams(vmem_limit_bytes=mib * 1024 * 1024)


def prepare_kernel(table_in, normed_in, w_query, w_key, w_value, pool, partial, *refs):
    pieces, (table, normed, weights, table_sem, sems, page_sems) = refs[:-6], refs[-6:]
    pairs = partial.shape[0]
    requests = pairs // 2
    table_copy = pltpu.make_async_copy(table_in, table, table_sem)
    table_copy.start()
    loads = [pltpu.make_async_copy(normed_in, normed, sems.at[3])]
    low = 0
    for i, weight in enumerate((w_query, w_key, w_value)):
        part = weights.at[:, low : low + weight.shape[1]]
        loads.append(pltpu.make_async_copy(weight, part, sems.at[i]))
        low += weight.shape[1]
    for copy in loads:
        copy.start()
    table_copy.wait()

    @pl.when(lax.axis_index("pair") >= requests)
    def _():
        low = 0
        for i, piece in enumerate(pieces):

            def start(j, carry):
                pltpu.make_async_copy(pool.at[table[0, low + j]], piece.at[j], page_sems.at[i]).start()
                return carry

            lax.fori_loop(0, piece.shape[0], start, 0, unroll=4)
            low += piece.shape[0]

    for copy in loads:
        copy.wait()
    hidden = jnp.concatenate([normed[s].astype(jnp.float32) for s in range(STEPS)], 0).astype(jnp.bfloat16)
    result = jnp.dot(hidden, weights[...], preferred_element_type=jnp.float32)
    for p in range(pairs):
        for s in range(STEPS):
            row = s * requests + p % requests
            partial[p, s : s + 1] = result[row : row + 1]

    @pl.when(lax.axis_index("pair") >= requests)
    def _():
        for i, piece in enumerate(pieces):
            pltpu.make_async_copy(pool.at[pl.ds(0, piece.shape[0])], piece, page_sems.at[i]).wait()


def prepare(table, normed, w_query, w_key, w_value, pool, pairs):
    page = pool.shape[1:]
    wide = w_query.shape[1] + 2 * w_key.shape[1]
    return pl.pallas_call(
        prepare_kernel,
        out_shape=(jax.ShapeDtypeStruct((pairs, STEPS, wide), jnp.float32),)
        + tuple(pltpu.VMEM((n,) + page, pool.dtype) for n in PIECES),
        in_specs=[HBM] * 6,
        out_specs=(VMEM,) + (VMEM,) * len(PIECES),
        scratch_shapes=[
            pltpu.SMEM(table.shape, table.dtype),
            pltpu.VMEM(normed.shape, normed.dtype),
            pltpu.VMEM((w_query.shape[0], wide), w_query.dtype),
            pltpu.SemaphoreType.DMA,
            pltpu.SemaphoreType.DMA((4,)),
            pltpu.SemaphoreType.DMA((len(PIECES),)),
        ],
        compiler_params=params(16),
        cost_estimate=SMALL,
        name="prepare",
    )(*in_hbm(table, normed, w_query, w_key, w_value, pool))


def page_order(table, slots):
    slot = lax.broadcasted_iota(jnp.int32, (slots, slots), 0)
    holds = jnp.where(slot == table, 1.0, 0.0).astype(jnp.bfloat16)
    index = lax.broadcasted_iota(jnp.int32, (8, slots), 1)
    digit = lax.broadcasted_iota(jnp.int32, (8, slots), 0)
    digits = jnp.where(digit == 0, index // 16, jnp.where(digit == 1, index % 16, 0))
    digits = digits.astype(jnp.float32).astype(jnp.bfloat16)
    return lax.dot_general(digits, holds, (((1,), (1,)), ((), ())), preferred_element_type=jnp.float32)


def attention_kernel(
    lengths, table, sums, b_query, b_key, b_value, cosine, sine, pool, packed, entries, held, score, sems
):
    slots, page_len, _ = held.shape
    per = slots // CHUNKS
    copies = []
    for c in range(CHUNKS):
        part = pl.ds(c * per, per)
        copies.append(pltpu.make_async_copy(pool.at[part], held.at[part], sems.at[c]))
        copies[-1].start()
    requests = sums.shape[0] // 2
    group, head = b_query.shape
    rows = STEPS * group
    pair_index = lax.axis_index("pair")
    is_source = pair_index >= requests
    request = jnp.where(is_source, pair_index - requests, pair_index)
    half_tokens = PAGES_HALF * page_len
    limit = jnp.where(is_source, lengths[request] - half_tokens, half_tokens)

    blocks = CHUNKS // 2
    block = slots // blocks
    width = block * page_len
    digits = page_order(table[...], slots)
    digits = jnp.concatenate(
        [digits[d : d + 1, c * block : (c + 1) * block] for d in range(2) for c in range(blocks)], 0
    ).astype(jnp.bfloat16)
    spread = lax.broadcasted_iota(jnp.int32, (block, width), 1) // page_len
    spread = jnp.where(spread == lax.broadcasted_iota(jnp.int32, (block, width), 0), 1.0, 0.0)
    digits = jnp.dot(digits, spread.astype(jnp.bfloat16), preferred_element_type=jnp.float32)
    tokens = (digits[:blocks] * 16.0 + digits[blocks:]).astype(jnp.int32) * page_len
    tokens = tokens + lax.broadcasted_iota(jnp.int32, (blocks, width), 1) % page_len

    total = sums[0]
    for p in range(1, sums.shape[0]):
        total = total + sums[p]
    query = jnp.concatenate(
        [total[s : s + 1, h * head : (h + 1) * head] for s in range(STEPS) for h in range(group)], 0
    )
    query = query + jnp.concatenate([b_query[...]] * STEPS, 0)
    cos_new = cosine[request]
    sin_new = sine[request]
    row = lax.broadcasted_iota(jnp.int32, (rows, head), 0)
    cos_rows = jnp.where(row < group, cos_new[0:1], cos_new[1:2])
    sin_rows = jnp.where(row < group, sin_new[0:1], sin_new[1:2])
    query = (query * cos_rows + pltpu.roll(query, head // 2, 1) * sin_rows).astype(jnp.bfloat16)
    key_new = total[:, group * head : (group + 1) * head] + b_key[...]
    key_new = jnp.concatenate([key_new, jnp.zeros((8 - STEPS, head), jnp.float32)], 0)
    key_new = key_new * cos_new + pltpu.roll(key_new, head // 2, 1) * sin_new
    key_new = key_new.astype(jnp.bfloat16).astype(jnp.float32)
    value_new = total[:, (group + 1) * head :] + b_value[...]
    value_new = value_new.astype(jnp.bfloat16).astype(jnp.float32)
    entries[:, :head] = key_new
    entries[0:STEPS, head:] = value_new
    entries[STEPS:, head:] = jnp.zeros((8 - STEPS, head), jnp.float32)
    scale = 1.0 / math.sqrt(head)

    column = lax.broadcasted_iota(jnp.int32, (rows, 1), 0)
    query_wide = query.astype(jnp.float32)
    fresh = []
    for s in range(STEPS):
        dots = jnp.sum(query_wide * key_new[s : s + 1], 1, keepdims=True) * scale
        seen = jnp.logical_and(is_source, column >= s * group)
        fresh.append((jnp.where(seen, dots, NEG), seen))
    row_max = jnp.maximum(fresh[0][0], fresh[1][0])

    for c in range(blocks):
        copies[2 * c].wait()
        copies[2 * c + 1].wait()
        keys = held[c * block : (c + 1) * block, :, :head].reshape(width, head)
        part = lax.dot_general(query, keys, (((1,), (1,)), ((), ())), preferred_element_type=jnp.float32)
        part = jnp.where(tokens[c : c + 1] < limit, part * scale, NEG)
        score[:, c * width : (c + 1) * width] = part
        row_max = jnp.maximum(row_max, jnp.max(part, 1, keepdims=True))
    row_sum = jnp.zeros((rows, 1), jnp.float32)
    out = jnp.zeros((rows, head), jnp.float32)
    for s in range(STEPS):
        weight = jnp.where(fresh[s][1], jnp.exp(fresh[s][0] - row_max), 0.0)
        row_sum = row_sum + weight
        out = out + weight.astype(jnp.bfloat16).astype(jnp.float32) * value_new[s : s + 1]
    for c in range(blocks):
        weight = jnp.exp(score[:, c * width : (c + 1) * width] - row_max)
        weight = jnp.where(tokens[c : c + 1] < limit, weight, 0.0)
        row_sum = row_sum + jnp.sum(weight, 1, keepdims=True)
        values = held[c * block : (c + 1) * block, :, head:].reshape(width, head)
        out = out + jnp.dot(weight.astype(jnp.bfloat16), values, preferred_element_type=jnp.float32)

    diagonal = lax.broadcasted_iota(jnp.int32, (rows, head), 1) == row
    for p in range(packed.shape[0]):
        packed[p, 0:rows] = out
        packed[p, rows : rows + 1] = jnp.sum(jnp.where(diagonal, row_max, 0.0), 0, keepdims=True)
        packed[p, rows + 1 : rows + 2] = jnp.sum(jnp.where(diagonal, row_sum, 0.0), 0, keepdims=True)
        packed[p, rows + 2 :] = jnp.zeros((packed.shape[1] - rows - 2, head), jnp.float32)


def attend(lengths, table, sums, b_query, b_key, b_value, cosine, sine, pool):
    group, head = b_query.shape
    rows = STEPS * group
    return pl.pallas_call(
        attention_kernel,
        out_shape=(
            jax.ShapeDtypeStruct((sums.shape[0], rows + 8, head), jnp.float32),
            jax.ShapeDtypeStruct((8, 2 * head), jnp.float32),
        ),
        in_specs=[SMEM] + [VMEM] * 7 + [HBM],
        out_specs=(VMEM, VMEM),
        scratch_shapes=[
            pltpu.VMEM(pool.shape, pool.dtype),
            pltpu.VMEM((rows, pool.shape[0] * pool.shape[1]), jnp.float32),
            pltpu.SemaphoreType.DMA((CHUNKS,)),
        ],
        compiler_params=params(24),
        cost_estimate=SMALL,
        name="attend",
    )(lengths, table, sums, b_query, b_key, b_value, cosine, sine, *in_hbm(pool))


def project_kernel(parts, w_out, out):
    pairs, packed_rows, head = parts.shape
    rows = packed_rows - 8
    group = rows // STEPS
    requests = pairs // 2
    lane = lax.broadcasted_iota(jnp.int32, (rows, head), 1)
    diagonal = lane == lax.broadcasted_iota(jnp.int32, (rows, head), 0)

    def as_column(line):
        return jnp.sum(jnp.where(diagonal, line, 0.0), 1, keepdims=True)

    merged = []
    for r in range(requests):
        first_max, first_sum = (as_column(parts[r, rows + i : rows + i + 1]) for i in range(2))
        second_max, second_sum = (as_column(parts[r + requests, rows + i : rows + i + 1]) for i in range(2))
        top = jnp.maximum(first_max, second_max)
        first_weight = jnp.exp(first_max - top)
        second_weight = jnp.exp(second_max - top)
        joined = first_weight * parts[r, :rows] + second_weight * parts[r + requests, :rows]
        merged.append(joined / (first_weight * first_sum + second_weight * second_sum))
    lines = []
    for s in range(STEPS):
        for r in range(requests):
            lines.append(
                jnp.concatenate(
                    [merged[r][s * group + h : s * group + h + 1] for h in range(group)], 1
                )
            )
    attended = jnp.concatenate(lines, 0).astype(jnp.bfloat16)
    result = jnp.dot(attended, w_out[...], preferred_element_type=jnp.float32)
    for s in range(STEPS):
        out[s] = result[s * requests : (s + 1) * requests]


def project(parts, w_out):
    return pl.pallas_call(
        project_kernel,
        out_shape=jax.ShapeDtypeStruct((STEPS, parts.shape[0] // 2, w_out.shape[1]), jnp.float32),
        in_specs=[VMEM, VMEM],
        out_specs=VMEM,
        compiler_params=params(16),
        cost_estimate=SMALL,
        name="project",
    )(parts, w_out)


def moved_pages(plan, request):
    count = plan[0, request]
    for s in range(1, STEPS):
        count = count + plan[s, request]
    return count


def copy_kernel(table, lengths, plan, entries, pool, *refs):
    early, (new_pool, held, sems, out_sems) = refs[:-4], refs[-4:]
    slots, page_len, width = held.shape
    per = slots // CHUNKS
    requests = lengths.shape[0]
    pair_index = lax.axis_index("pair")
    is_source = pair_index >= requests

    def fetch(c):
        part = pl.ds(c * per, per)
        return pltpu.make_async_copy(pool.at[part], held.at[part], sems.at[c])

    def store(c):
        part = pl.ds(c * per, per)
        return pltpu.make_async_copy(held.at[part], new_pool.at[part], out_sems.at[c])

    for c in range(CHUNKS):
        fetch(c).start()
    for c in range(CHUNKS):
        fetch(c).wait()

    @pl.when(is_source)
    def _():
        page_row = lax.broadcasted_iota(jnp.int32, (page_len, width), 0)
        first_new = lengths[pair_index - requests] - PAGES_HALF * page_len
        for s in range(STEPS):
            offset = first_new + s
            slot = table[0, offset // page_len]
            old = held[slot].astype(jnp.float32)
            held[slot] = jnp.where(page_row == offset % page_len, entries[s : s + 1], old).astype(held.dtype)

    @pl.when(jnp.logical_not(is_source))
    def _():
        count = moved_pages(plan, pair_index)
        low = 0
        for pages in early:

            def place(j, carry):
                held[table[0, PAGES_HALF + low + j]] = pages[j]
                return carry

            lax.fori_loop(0, jnp.clip(count - low, 0, pages.shape[0]), place, 0)
            low += pages.shape[0]

    for c in range(CHUNKS):
        store(c).start()
    for c in range(CHUNKS):
        store(c).wait()


def copy_pool(table, lengths, plan, entries, pool, early):
    return pl.pallas_call(
        copy_kernel,
        out_shape=jax.ShapeDtypeStruct(pool.shape, pool.dtype),
        in_specs=[SMEM, SMEM, SMEM, VMEM, HBM] + [VMEM] * len(early),
        out_specs=HBM,
        scratch_shapes=[
            pltpu.VMEM(pool.shape, pool.dtype),
            pltpu.SemaphoreType.DMA((CHUNKS,)),
            pltpu.SemaphoreType.DMA((CHUNKS,)),
        ],
        compiler_params=params(24),
        cost_estimate=SMALL,
        name="copy_pool",
    )(table, lengths, plan, entries, *in_hbm(pool), *early)


def place_kernel(table_in, plan_in, pages, base, new_pool, table, plan, sems, sem, *, done, only):
    del base
    pair_index = lax.axis_index("pair")

    @pl.when(jnp.logical_and(pair_index >= only[0], pair_index < only[1]))
    def _():
        table_copy = pltpu.make_async_copy(table_in, table, sems.at[0])
        plan_copy = pltpu.make_async_copy(plan_in, plan, sems.at[1])
        table_copy.start()
        plan_copy.start()
        table_copy.wait()
        plan_copy.wait()
        count = jnp.clip(moved_pages(plan, pair_index) - done, 0, pages.shape[0])

        def start(j, carry):
            slot = table[0, PAGES_HALF + done + j]
            pltpu.make_async_copy(pages.at[j], new_pool.at[slot], sem).start()
            return carry

        def wait(j, carry):
            pltpu.make_async_copy(pages.at[0], new_pool.at[0], sem).wait()
            return carry

        lax.fori_loop(0, count, start, 0)
        lax.fori_loop(0, count, wait, 0)


def place(table, plan, pages, base, done, only):
    return pl.pallas_call(
        functools.partial(place_kernel, done=done, only=only),
        out_shape=pltpu.HBM(base.shape, base.dtype),
        in_specs=[HBM, HBM, VMEM, HBM],
        out_specs=HBM,
        scratch_shapes=[
            pltpu.SMEM(table.shape, table.dtype),
            pltpu.SMEM(plan.shape, plan.dtype),
            pltpu.SemaphoreType.DMA((2,)),
            pltpu.SemaphoreType.DMA,
        ],
        input_output_aliases={3: 0},
        compiler_params=params(16),
        cost_estimate=SMALL,
        name="place",
    )(*in_hbm(table, plan), pages, *in_hbm(base))


def local(
    normed, w_query, b_query, w_key, b_key, w_value, b_value, w_out, pool, page_table, lengths, plan
):
    pair_count = lax.axis_size("pair")
    tp_count = lax.axis_size("tp")
    requests = pair_count // 2
    head = w_key.shape[1]

    partial, *pieces = prepare(page_table, normed, w_query, w_key, w_value, pool[0, 0], pair_count)
    route = [(i + requests, i) for i in range(requests)]

    def migrate(pages):
        return lax.ppermute(pages, "pair", route)

    def tie(*values):
        return lax.optimization_barrier(values)

    first = migrate(pieces[0])
    planned = plan.T
    sums = lax.all_to_all(partial, "pair", split_axis=0, concat_axis=0, tiled=True)
    second = migrate(tie(pieces[1], sums)[0])

    frequency = rope_base ** (-(jnp.arange(head // 2, dtype=jnp.float32) * 2.0 / head))
    steps = jnp.minimum(jnp.arange(8, dtype=jnp.int32), STEPS - 1)
    position = (lengths[:, None] + steps[None, :]).astype(jnp.float32)[..., None]
    angles = position * frequency
    cosine = jnp.cos(angles)
    sine = jnp.sin(angles)
    cosine = jnp.concatenate([cosine, cosine], -1)
    sine = jnp.concatenate([-sine, sine], -1)

    packed, entries = attend(
        lengths,
        page_table,
        sums,
        b_query.reshape(-1, head),
        b_key[None, :],
        b_value[None, :],
        cosine,
        sine,
        pool[0, 0],
    )
    parts = lax.all_to_all(packed, "pair", split_axis=0, concat_axis=0, tiled=True)
    third = migrate(tie(pieces[2], parts)[0])
    new_pool = copy_pool(page_table, lengths, planned, entries, pool[0, 0], [first, second])
    projected = project(parts, w_out)
    if tp_count == 2:
        projected = projected + lax.ppermute(projected, "tp", [(0, 1), (1, 0)])
    else:
        projected = lax.psum(projected, "tp")
    new_pool = place(page_table, planned, third, new_pool, EARLY[0] + EARLY[1], (0, requests))
    new_pool, projected = tie(new_pool, projected)
    rest = jnp.sum(plan, 1) > sum(EARLY)

    def send(request, base, pages):
        arrived = lax.ppermute(pages, "pair", [(request + requests, request)])
        return place(page_table, planned, arrived, base, sum(EARLY), (request, request + 1))

    for request in range(requests):
        new_pool = lax.cond(
            rest[request], functools.partial(send, request), lambda base, pages: base, new_pool, pieces[-1]
        )
    return projected, new_pool[None, None]


def solution(mesh):
    return jax.shard_map(
        local,
        mesh=mesh,
        in_specs=(
            P(None, "rep", "pair"),
            P("pair", "tp"),
            P("tp"),
            P("pair", "tp"),
            P("tp"),
            P("pair", "tp"),
            P("tp"),
            P("tp", "pair"),
            P(("rep", "pair"), "tp", None, None, None),
            P(("rep", "pair"), None),
            P("rep"),
            P("rep", None),
        ),
        out_specs=(P(None, "rep", "pair"), P(("rep", "pair"), "tp", None, None, None)),
        check_vma=False,
    )
```

```python
import functools
import math

import jax
import jax.numpy as jnp
from jax import lax
from jax.experimental import pallas as pl
from jax.experimental.pallas import tpu as pltpu
from jax.sharding import PartitionSpec as P

PAGES_HALF = 384
STEPS = 2
SECTION = 64
MOVED_MAX = STEPS * SECTION
EARLY = (24, 24, 32)
LATE = (24, 24)
PIECES = EARLY + LATE
CHUNKS = 8
NEG = -1e30

rope_base = 1000000.0

VMEM = pl.BlockSpec(memory_space=pltpu.VMEM)
SMEM = pl.BlockSpec(memory_space=pltpu.SMEM)
HBM = pl.BlockSpec(memory_space=pltpu.HBM)


def in_hbm(*arrays):
    return tuple(pltpu.with_memory_space_constraint(a, pltpu.HBM) for a in arrays)


def params(mib):
    return pltpu.CompilerParams(vmem_limit_bytes=mib * 1024 * 1024)


def prepare_kernel(table_in, normed_in, w_query, w_key, w_value, pool, partial, *refs):
    pieces, (table, normed, weights, table_sem, sems, page_sems) = refs[:-6], refs[-6:]
    pairs = partial.shape[0]
    requests = pairs // 2
    table_copy = pltpu.make_async_copy(table_in, table, table_sem)
    table_copy.start()
    loads = [pltpu.make_async_copy(normed_in, normed, sems.at[3])]
    low = 0
    for i, weight in enumerate((w_query, w_key, w_value)):
        part = weights.at[:, low : low + weight.shape[1]]
        loads.append(pltpu.make_async_copy(weight, part, sems.at[i]))
        low += weight.shape[1]
    for copy in loads:
        copy.start()
    table_copy.wait()

    @pl.when(lax.axis_index("pair") >= requests)
    def _():
        low = 0
        for i, piece in enumerate(pieces):

            def start(j, carry):
                pltpu.make_async_copy(pool.at[table[0, low + j]], piece.at[j], page_sems.at[i]).start()
                return carry

            lax.fori_loop(0, piece.shape[0], start, 0, unroll=4)
            low += piece.shape[0]

    for copy in loads:
        copy.wait()
    hidden = jnp.concatenate([normed[s].astype(jnp.float32) for s in range(STEPS)], 0).astype(jnp.bfloat16)
    result = jnp.dot(hidden, weights[...], preferred_element_type=jnp.float32)
    for p in range(pairs):
        for s in range(STEPS):
            row = s * requests + p % requests
            partial[p, s : s + 1] = result[row : row + 1]

    @pl.when(lax.axis_index("pair") >= requests)
    def _():
        for i, piece in enumerate(pieces):
            pltpu.make_async_copy(pool.at[pl.ds(0, piece.shape[0])], piece, page_sems.at[i]).wait()


def prepare(table, normed, w_query, w_key, w_value, pool, pairs):
    page = pool.shape[1:]
    wide = w_query.shape[1] + 2 * w_key.shape[1]
    return pl.pallas_call(
        prepare_kernel,
        out_shape=(jax.ShapeDtypeStruct((pairs, STEPS, wide), jnp.float32),)
        + tuple(pltpu.VMEM((n,) + page, pool.dtype) for n in PIECES),
        in_specs=[HBM] * 6,
        out_specs=(VMEM,) + (VMEM,) * len(PIECES),
        scratch_shapes=[
            pltpu.SMEM(table.shape, table.dtype),
            pltpu.VMEM(normed.shape, normed.dtype),
            pltpu.VMEM((w_query.shape[0], wide), w_query.dtype),
            pltpu.SemaphoreType.DMA,
            pltpu.SemaphoreType.DMA((4,)),
            pltpu.SemaphoreType.DMA((len(PIECES),)),
        ],
        compiler_params=params(16),
        name="prepare",
    )(*in_hbm(table, normed, w_query, w_key, w_value, pool))


def page_order(table, slots):
    slot = lax.broadcasted_iota(jnp.int32, (slots, slots), 0)
    holds = jnp.where(slot == table, 1.0, 0.0).astype(jnp.bfloat16)
    index = lax.broadcasted_iota(jnp.int32, (8, slots), 1)
    digit = lax.broadcasted_iota(jnp.int32, (8, slots), 0)
    digits = jnp.where(digit == 0, index // 16, jnp.where(digit == 1, index % 16, 0))
    digits = digits.astype(jnp.float32).astype(jnp.bfloat16)
    return lax.dot_general(digits, holds, (((1,), (1,)), ((), ())), preferred_element_type=jnp.float32)


def attention_kernel(
    lengths, table_in, sums, b_query, b_key, b_value, cosine, sine, pool, packed, entries, held, score, table, sems
):
    slots, page_len, _ = held.shape
    per = slots // CHUNKS
    table_copy = pltpu.make_async_copy(table_in, table, sems.at[CHUNKS])
    table_copy.start()
    copies = []
    for c in range(CHUNKS):
        part = pl.ds(c * per, per)
        copies.append(pltpu.make_async_copy(pool.at[part], held.at[part], sems.at[c]))
        copies[-1].start()
    requests = sums.shape[0] // 2
    group, head = b_query.shape
    rows = STEPS * group
    pair_index = lax.axis_index("pair")
    is_source = pair_index >= requests
    request = jnp.where(is_source, pair_index - requests, pair_index)
    half_tokens = PAGES_HALF * page_len
    limit = jnp.where(is_source, lengths[request] - half_tokens, half_tokens)

    blocks = CHUNKS // 2
    block = slots // blocks
    width = block * page_len
    table_copy.wait()
    digits = page_order(table[...], slots)
    digits = jnp.concatenate(
        [digits[d : d + 1, c * block : (c + 1) * block] for d in range(2) for c in range(blocks)], 0
    ).astype(jnp.bfloat16)
    spread = lax.broadcasted_iota(jnp.int32, (block, width), 1) // page_len
    spread = jnp.where(spread == lax.broadcasted_iota(jnp.int32, (block, width), 0), 1.0, 0.0)
    digits = jnp.dot(digits, spread.astype(jnp.bfloat16), preferred_element_type=jnp.float32)
    tokens = (digits[:blocks] * 16.0 + digits[blocks:]).astype(jnp.int32) * page_len
    tokens = tokens + lax.broadcasted_iota(jnp.int32, (blocks, width), 1) % page_len

    total = sums[0]
    for p in range(1, sums.shape[0]):
        total = total + sums[p]
    query = jnp.concatenate(
        [total[s : s + 1, h * head : (h + 1) * head] for s in range(STEPS) for h in range(group)], 0
    )
    query = query + jnp.concatenate([b_query[...]] * STEPS, 0)
    cos_new = cosine[request]
    sin_new = sine[request]
    row = lax.broadcasted_iota(jnp.int32, (rows, head), 0)
    cos_rows = jnp.where(row < group, cos_new[0:1], cos_new[1:2])
    sin_rows = jnp.where(row < group, sin_new[0:1], sin_new[1:2])
    query = (query * cos_rows + pltpu.roll(query, head // 2, 1) * sin_rows).astype(jnp.bfloat16)
    key_new = total[:, group * head : (group + 1) * head] + b_key[...]
    key_new = jnp.concatenate([key_new, jnp.zeros((8 - STEPS, head), jnp.float32)], 0)
    key_new = key_new * cos_new + pltpu.roll(key_new, head // 2, 1) * sin_new
    key_new = key_new.astype(jnp.bfloat16).astype(jnp.float32)
    value_new = total[:, (group + 1) * head :] + b_value[...]
    value_new = value_new.astype(jnp.bfloat16).astype(jnp.float32)
    entries[:, :head] = key_new
    entries[0:STEPS, head:] = value_new
    entries[STEPS:, head:] = jnp.zeros((8 - STEPS, head), jnp.float32)
    scale = 1.0 / math.sqrt(head)

    column = lax.broadcasted_iota(jnp.int32, (rows, 1), 0)
    query_wide = query.astype(jnp.float32)
    fresh = []
    for s in range(STEPS):
        dots = jnp.sum(query_wide * key_new[s : s + 1], 1, keepdims=True) * scale
        seen = jnp.logical_and(is_source, column >= s * group)
        fresh.append((jnp.where(seen, dots, NEG), seen))
    row_max = jnp.maximum(fresh[0][0], fresh[1][0])

    for c in range(blocks):
        copies[2 * c].wait()
        copies[2 * c + 1].wait()
        keys = held[c * block : (c + 1) * block, :, :head].reshape(width, head)
        part = lax.dot_general(query, keys, (((1,), (1,)), ((), ())), preferred_element_type=jnp.float32)
        part = jnp.where(tokens[c : c + 1] < limit, part * scale, NEG)
        score[:, c * width : (c + 1) * width] = part
        row_max = jnp.maximum(row_max, jnp.max(part, 1, keepdims=True))
    row_sum = jnp.zeros((rows, 1), jnp.float32)
    out = jnp.zeros((rows, head), jnp.float32)
    for s in range(STEPS):
        weight = jnp.where(fresh[s][1], jnp.exp(fresh[s][0] - row_max), 0.0)
        row_sum = row_sum + weight
        out = out + weight.astype(jnp.bfloat16).astype(jnp.float32) * value_new[s : s + 1]
    for c in range(blocks):
        weight = jnp.exp(score[:, c * width : (c + 1) * width] - row_max)
        weight = jnp.where(tokens[c : c + 1] < limit, weight, 0.0)
        row_sum = row_sum + jnp.sum(weight, 1, keepdims=True)
        values = held[c * block : (c + 1) * block, :, head:].reshape(width, head)
        out = out + jnp.dot(weight.astype(jnp.bfloat16), values, preferred_element_type=jnp.float32)

    diagonal = lax.broadcasted_iota(jnp.int32, (rows, head), 1) == row
    for p in range(packed.shape[0]):
        packed[p, 0:rows] = out
        packed[p, rows : rows + 1] = jnp.sum(jnp.where(diagonal, row_max, 0.0), 0, keepdims=True)
        packed[p, rows + 1 : rows + 2] = jnp.sum(jnp.where(diagonal, row_sum, 0.0), 0, keepdims=True)
        packed[p, rows + 2 :] = jnp.zeros((packed.shape[1] - rows - 2, head), jnp.float32)


def attend(lengths, table, sums, b_query, b_key, b_value, cosine, sine, pool):
    group, head = b_query.shape
    rows = STEPS * group
    return pl.pallas_call(
        attention_kernel,
        out_shape=(
            jax.ShapeDtypeStruct((sums.shape[0], rows + 8, head), jnp.float32),
            jax.ShapeDtypeStruct((8, 2 * head), jnp.float32),
        ),
        in_specs=[SMEM, HBM] + [VMEM] * 6 + [HBM],
        out_specs=(VMEM, VMEM),
        scratch_shapes=[
            pltpu.VMEM(pool.shape, pool.dtype),
            pltpu.VMEM((rows, pool.shape[0] * pool.shape[1]), jnp.float32),
            pltpu.VMEM(table.shape, table.dtype),
            pltpu.SemaphoreType.DMA((CHUNKS + 1,)),
        ],
        compiler_params=params(24),
        name="attend",
    )(lengths, *in_hbm(table), sums, b_query, b_key, b_value, cosine, sine, *in_hbm(pool))


def project_kernel(parts, w_out, out):
    pairs, packed_rows, head = parts.shape
    rows = packed_rows - 8
    group = rows // STEPS
    requests = pairs // 2
    lane = lax.broadcasted_iota(jnp.int32, (rows, head), 1)
    diagonal = lane == lax.broadcasted_iota(jnp.int32, (rows, head), 0)

    def as_column(line):
        return jnp.sum(jnp.where(diagonal, line, 0.0), 1, keepdims=True)

    merged = []
    for r in range(requests):
        first_max, first_sum = (as_column(parts[r, rows + i : rows + i + 1]) for i in range(2))
        second_max, second_sum = (as_column(parts[r + requests, rows + i : rows + i + 1]) for i in range(2))
        top = jnp.maximum(first_max, second_max)
        first_weight = jnp.exp(first_max - top)
        second_weight = jnp.exp(second_max - top)
        joined = first_weight * parts[r, :rows] + second_weight * parts[r + requests, :rows]
        merged.append(joined / (first_weight * first_sum + second_weight * second_sum))
    lines = []
    for s in range(STEPS):
        for r in range(requests):
            lines.append(
                jnp.concatenate(
                    [merged[r][s * group + h : s * group + h + 1] for h in range(group)], 1
                )
            )
    attended = jnp.concatenate(lines, 0).astype(jnp.bfloat16)
    result = jnp.dot(attended, w_out[...], preferred_element_type=jnp.float32)
    for s in range(STEPS):
        out[s] = result[s * requests : (s + 1) * requests]


def project(parts, w_out):
    return pl.pallas_call(
        project_kernel,
        out_shape=jax.ShapeDtypeStruct((STEPS, parts.shape[0] // 2, w_out.shape[1]), jnp.float32),
        in_specs=[VMEM, VMEM],
        out_specs=VMEM,
        compiler_params=params(16),
        name="project",
    )(parts, w_out)


def moved_pages(plan, request):
    count = plan[0, request]
    for s in range(1, STEPS):
        count = count + plan[s, request]
    return count


def copy_kernel(table, lengths, plan, entries, pool, *refs):
    early, (new_pool, held, sems, out_sems) = refs[:-4], refs[-4:]
    slots, page_len, width = held.shape
    per = slots // CHUNKS
    requests = lengths.shape[0]
    pair_index = lax.axis_index("pair")
    is_source = pair_index >= requests

    def fetch(c):
        part = pl.ds(c * per, per)
        return pltpu.make_async_copy(pool.at[part], held.at[part], sems.at[c])

    def store(c):
        part = pl.ds(c * per, per)
        return pltpu.make_async_copy(held.at[part], new_pool.at[part], out_sems.at[c])

    for c in range(CHUNKS):
        fetch(c).start()
    for c in range(CHUNKS):
        fetch(c).wait()

    @pl.when(is_source)
    def _():
        page_row = lax.broadcasted_iota(jnp.int32, (page_len, width), 0)
        first_new = lengths[pair_index - requests] - PAGES_HALF * page_len
        for s in range(STEPS):
            offset = first_new + s
            slot = table[0, offset // page_len]
            old = held[slot].astype(jnp.float32)
            held[slot] = jnp.where(page_row == offset % page_len, entries[s : s + 1], old).astype(held.dtype)

    @pl.when(jnp.logical_not(is_source))
    def _():
        count = moved_pages(plan, pair_index)
        low = 0
        for pages in early:

            def place(j, carry):
                held[table[0, PAGES_HALF + low + j]] = pages[j]
                return carry

            lax.fori_loop(0, jnp.clip(count - low, 0, pages.shape[0]), place, 0)
            low += pages.shape[0]

    for c in range(CHUNKS):
        store(c).start()
    for c in range(CHUNKS):
        store(c).wait()


def copy_pool(table, lengths, plan, entries, pool, early):
    return pl.pallas_call(
        copy_kernel,
        out_shape=jax.ShapeDtypeStruct(pool.shape, pool.dtype),
        in_specs=[SMEM, SMEM, SMEM, VMEM, HBM] + [VMEM] * len(early),
        out_specs=HBM,
        scratch_shapes=[
            pltpu.VMEM(pool.shape, pool.dtype),
            pltpu.SemaphoreType.DMA((CHUNKS,)),
            pltpu.SemaphoreType.DMA((CHUNKS,)),
        ],
        compiler_params=params(24),
        name="copy_pool",
    )(table, lengths, plan, entries, *in_hbm(pool), *early)


def place_kernel(table_in, plan_in, *refs, done, only):
    parts, (base, new_pool, table, plan, sems, sem) = refs[:-6], refs[-6:]
    del base
    pair_index = lax.axis_index("pair")

    @pl.when(jnp.logical_and(pair_index >= only[0], pair_index < only[1]))
    def _():
        table_copy = pltpu.make_async_copy(table_in, table, sems.at[0])
        plan_copy = pltpu.make_async_copy(plan_in, plan, sems.at[1])
        table_copy.start()
        plan_copy.start()
        table_copy.wait()
        plan_copy.wait()
        count = moved_pages(plan, pair_index) - done
        low = 0
        for pages in parts:

            def start(j, carry):
                slot = table[0, PAGES_HALF + done + low + j]
                pltpu.make_async_copy(pages.at[j], new_pool.at[slot], sem).start()
                return carry

            lax.fori_loop(0, jnp.clip(count - low, 0, pages.shape[0]), start, 0)
            low += pages.shape[0]

        def wait(j, carry):
            pltpu.make_async_copy(parts[0].at[0], new_pool.at[0], sem).wait()
            return carry

        lax.fori_loop(0, jnp.clip(count, 0, low), wait, 0)


def place(table, plan, parts, base, done, only):
    return pl.pallas_call(
        functools.partial(place_kernel, done=done, only=only),
        out_shape=pltpu.HBM(base.shape, base.dtype),
        in_specs=[HBM, HBM] + [VMEM] * len(parts) + [HBM],
        out_specs=HBM,
        scratch_shapes=[
            pltpu.SMEM(table.shape, table.dtype),
            pltpu.SMEM(plan.shape, plan.dtype),
            pltpu.SemaphoreType.DMA((2,)),
            pltpu.SemaphoreType.DMA,
        ],
        input_output_aliases={2 + len(parts): 0},
        compiler_params=params(16),
        name="place",
    )(*in_hbm(table, plan), *parts, *in_hbm(base))


def local(
    normed, w_query, b_query, w_key, b_key, w_value, b_value, w_out, pool, page_table, lengths, plan
):
    pair_count = lax.axis_size("pair")
    tp_count = lax.axis_size("tp")
    requests = pair_count // 2
    head = w_key.shape[1]

    partial, *pieces = prepare(page_table, normed, w_query, w_key, w_value, pool[0, 0], pair_count)
    route = [(i + requests, i) for i in range(requests)]

    def migrate(pages):
        return lax.ppermute(pages, "pair", route)

    def tie(*values):
        return lax.optimization_barrier(values)

    planned = plan.T
    counts = jnp.sum(plan, 1)
    more = jnp.max(counts) > sum(EARLY)

    def exchange(values):
        def send(values):
            return lax.all_to_all(values, "pair", split_axis=0, concat_axis=0, tiled=True)

        return lax.cond(more, send, send, values)

    first = migrate(pieces[0])
    sums, first = tie(exchange(partial), first)
    second = migrate(tie(pieces[1], sums)[0])

    frequency = rope_base ** (-(jnp.arange(head // 2, dtype=jnp.float32) * 2.0 / head))
    steps = jnp.minimum(jnp.arange(8, dtype=jnp.int32), STEPS - 1)
    position = (lengths[:, None] + steps[None, :]).astype(jnp.float32)[..., None]
    angles = position * frequency
    cosine = jnp.cos(angles)
    sine = jnp.sin(angles)
    cosine = jnp.concatenate([cosine, cosine], -1)
    sine = jnp.concatenate([-sine, sine], -1)

    packed, entries = attend(
        lengths,
        page_table,
        sums,
        b_query.reshape(-1, head),
        b_key[None, :],
        b_value[None, :],
        cosine,
        sine,
        pool[0, 0],
    )
    parts, second = tie(exchange(packed), second)
    third = migrate(tie(pieces[2], parts)[0])
    new_pool = copy_pool(page_table, lengths, planned, entries, pool[0, 0], [first, second])
    projected = project(parts, w_out)
    if tp_count == 2:
        projected = projected + lax.ppermute(projected, "tp", [(0, 1), (1, 0)])
    else:
        projected = lax.psum(projected, "tp")
    new_pool = place(page_table, planned, [third], new_pool, EARLY[0] + EARLY[1], (0, requests))
    new_pool, projected = tie(new_pool, projected)
    static = sum(EARLY)
    levels = (counts > static).astype(jnp.int32) + (counts > static + LATE[0]).astype(jnp.int32)

    def send(level, request, base, *chunks):
        if level == 0:
            return base
        arrived = [lax.ppermute(chunk, "pair", [(request + requests, request)]) for chunk in chunks[:level]]
        return place(page_table, planned, arrived, base, static, (request, request + 1))

    for request in range(requests):
        branches = [functools.partial(send, level, request) for level in range(len(LATE) + 1)]
        new_pool = lax.switch(levels[request], branches, new_pool, *pieces[len(EARLY) :])
    return projected, new_pool[None, None]


def solution(mesh):
    return jax.shard_map(
        local,
        mesh=mesh,
        in_specs=(
            P(None, "rep", "pair"),
            P("pair", "tp"),
            P("tp"),
            P("pair", "tp"),
            P("tp"),
            P("pair", "tp"),
            P("tp"),
            P("tp", "pair"),
            P(("rep", "pair"), "tp", None, None, None),
            P(("rep", "pair"), None),
            P("rep"),
            P("rep", None),
        ),
        out_specs=(P(None, "rep", "pair"), P(("rep", "pair"), "tp", None, None, None)),
        check_vma=False,
    )
```

```python
import functools
import math

import jax
import jax.numpy as jnp
from jax import lax
from jax.experimental import pallas as pl
from jax.experimental.pallas import tpu as pltpu
from jax.sharding import PartitionSpec as P

PAGES_HALF = 384
STEPS = 2
SECTION = 64
MOVED_MAX = STEPS * SECTION
EARLY = (18, 32, 24)
LATE = (18, 18, 18)
PIECES = EARLY + LATE
CHUNKS = 8
NEG = -1e30

rope_base = 1000000.0

VMEM = pl.BlockSpec(memory_space=pltpu.VMEM)
SMEM = pl.BlockSpec(memory_space=pltpu.SMEM)
HBM = pl.BlockSpec(memory_space=pltpu.HBM)


def in_hbm(*arrays):
    return tuple(pltpu.with_memory_space_constraint(a, pltpu.HBM) for a in arrays)


def params(mib):
    return pltpu.CompilerParams(vmem_limit_bytes=mib * 1024 * 1024)


def prepare_kernel(table_in, normed_in, w_query, w_key, w_value, pool, partial, *refs):
    pieces, (table, normed, weights, table_sem, sems, page_sems) = refs[:-6], refs[-6:]
    pairs = partial.shape[0]
    requests = pairs // 2
    table_copy = pltpu.make_async_copy(table_in, table, table_sem)
    table_copy.start()
    loads = [pltpu.make_async_copy(normed_in, normed, sems.at[3])]
    low = 0
    for i, weight in enumerate((w_query, w_key, w_value)):
        part = weights.at[:, low : low + weight.shape[1]]
        loads.append(pltpu.make_async_copy(weight, part, sems.at[i]))
        low += weight.shape[1]
    for copy in loads:
        copy.start()
    table_copy.wait()

    @pl.when(lax.axis_index("pair") >= requests)
    def _():
        low = 0
        for i, piece in enumerate(pieces):

            def start(j, carry):
                pltpu.make_async_copy(pool.at[table[0, low + j]], piece.at[j], page_sems.at[i]).start()
                return carry

            lax.fori_loop(0, piece.shape[0], start, 0, unroll=2)
            low += piece.shape[0]

    for copy in loads:
        copy.wait()
    hidden = jnp.concatenate([normed[s].astype(jnp.float32) for s in range(STEPS)], 0).astype(jnp.bfloat16)
    result = jnp.dot(hidden, weights[...], preferred_element_type=jnp.float32)
    for p in range(pairs):
        for s in range(STEPS):
            row = s * requests + p % requests
            partial[p, s : s + 1] = result[row : row + 1]

    @pl.when(lax.axis_index("pair") >= requests)
    def _():
        for i, piece in enumerate(pieces):
            pltpu.make_async_copy(pool.at[pl.ds(0, piece.shape[0])], piece, page_sems.at[i]).wait()


def prepare(table, normed, w_query, w_key, w_value, pool, pairs):
    page = pool.shape[1:]
    wide = w_query.shape[1] + 2 * w_key.shape[1]
    return pl.pallas_call(
        prepare_kernel,
        out_shape=(jax.ShapeDtypeStruct((pairs, STEPS, wide), jnp.float32),)
        + tuple(pltpu.VMEM((n,) + page, pool.dtype) for n in PIECES),
        in_specs=[HBM] * 6,
        out_specs=(VMEM,) + (VMEM,) * len(PIECES),
        scratch_shapes=[
            pltpu.SMEM(table.shape, table.dtype),
            pltpu.VMEM(normed.shape, normed.dtype),
            pltpu.VMEM((w_query.shape[0], wide), w_query.dtype),
            pltpu.SemaphoreType.DMA,
            pltpu.SemaphoreType.DMA((4,)),
            pltpu.SemaphoreType.DMA((len(PIECES),)),
        ],
        compiler_params=params(16),
        name="prepare",
    )(*in_hbm(table, normed, w_query, w_key, w_value, pool))


def page_order(table, slots):
    slot = lax.broadcasted_iota(jnp.int32, (slots, slots), 0)
    holds = jnp.where(slot == table, 1.0, 0.0).astype(jnp.bfloat16)
    index = lax.broadcasted_iota(jnp.int32, (8, slots), 1)
    digit = lax.broadcasted_iota(jnp.int32, (8, slots), 0)
    digits = jnp.where(digit == 0, index // 16, jnp.where(digit == 1, index % 16, 0))
    digits = digits.astype(jnp.float32).astype(jnp.bfloat16)
    return lax.dot_general(digits, holds, (((1,), (1,)), ((), ())), preferred_element_type=jnp.float32)


def attention_kernel(
    lengths, table_in, sums, b_query, b_key, b_value, cosine, sine, pool, packed, entries, held, score, table, sems
):
    slots, page_len, _ = held.shape
    per = slots // CHUNKS
    table_copy = pltpu.make_async_copy(table_in, table, sems.at[CHUNKS])
    table_copy.start()
    copies = []
    for c in range(CHUNKS):
        part = pl.ds(c * per, per)
        copies.append(pltpu.make_async_copy(pool.at[part], held.at[part], sems.at[c]))
        copies[-1].start()
    requests = sums.shape[0] // 2
    group, head = b_query.shape
    rows = STEPS * group
    pair_index = lax.axis_index("pair")
    is_source = pair_index >= requests
    request = jnp.where(is_source, pair_index - requests, pair_index)
    half_tokens = PAGES_HALF * page_len
    limit = jnp.where(is_source, lengths[request] - half_tokens, half_tokens)

    blocks = CHUNKS // 2
    block = slots // blocks
    width = block * page_len
    table_copy.wait()
    digits = page_order(table[...], slots)
    digits = jnp.concatenate(
        [digits[d : d + 1, c * block : (c + 1) * block] for d in range(2) for c in range(blocks)], 0
    ).astype(jnp.bfloat16)
    spread = lax.broadcasted_iota(jnp.int32, (block, width), 1) // page_len
    spread = jnp.where(spread == lax.broadcasted_iota(jnp.int32, (block, width), 0), 1.0, 0.0)
    digits = jnp.dot(digits, spread.astype(jnp.bfloat16), preferred_element_type=jnp.float32)
    tokens = (digits[:blocks] * 16.0 + digits[blocks:]).astype(jnp.int32) * page_len
    tokens = tokens + lax.broadcasted_iota(jnp.int32, (blocks, width), 1) % page_len

    total = sums[0]
    for p in range(1, sums.shape[0]):
        total = total + sums[p]
    query = jnp.concatenate(
        [total[s : s + 1, h * head : (h + 1) * head] for s in range(STEPS) for h in range(group)], 0
    )
    query = query + jnp.concatenate([b_query[...]] * STEPS, 0)
    cos_new = cosine[request]
    sin_new = sine[request]
    row = lax.broadcasted_iota(jnp.int32, (rows, head), 0)
    cos_rows = jnp.where(row < group, cos_new[0:1], cos_new[1:2])
    sin_rows = jnp.where(row < group, sin_new[0:1], sin_new[1:2])
    query = (query * cos_rows + pltpu.roll(query, head // 2, 1) * sin_rows).astype(jnp.bfloat16)
    key_new = total[:, group * head : (group + 1) * head] + b_key[...]
    key_new = jnp.concatenate([key_new, jnp.zeros((8 - STEPS, head), jnp.float32)], 0)
    key_new = key_new * cos_new + pltpu.roll(key_new, head // 2, 1) * sin_new
    key_new = key_new.astype(jnp.bfloat16).astype(jnp.float32)
    value_new = total[:, (group + 1) * head :] + b_value[...]
    value_new = value_new.astype(jnp.bfloat16).astype(jnp.float32)
    entries[:, :head] = key_new
    entries[0:STEPS, head:] = value_new
    entries[STEPS:, head:] = jnp.zeros((8 - STEPS, head), jnp.float32)
    scale = 1.0 / math.sqrt(head)

    column = lax.broadcasted_iota(jnp.int32, (rows, 1), 0)
    query_wide = query.astype(jnp.float32)
    fresh = []
    for s in range(STEPS):
        dots = jnp.sum(query_wide * key_new[s : s + 1], 1, keepdims=True) * scale
        seen = jnp.logical_and(is_source, column >= s * group)
        fresh.append((jnp.where(seen, dots, NEG), seen))
    row_max = jnp.maximum(fresh[0][0], fresh[1][0])

    for c in range(blocks):
        copies[2 * c].wait()
        copies[2 * c + 1].wait()
        keys = held[c * block : (c + 1) * block, :, :head].reshape(width, head)
        part = lax.dot_general(query, keys, (((1,), (1,)), ((), ())), preferred_element_type=jnp.float32)
        part = jnp.where(tokens[c : c + 1] < limit, part * scale, NEG)
        score[:, c * width : (c + 1) * width] = part
        row_max = jnp.maximum(row_max, jnp.max(part, 1, keepdims=True))
    row_sum = jnp.zeros((rows, 1), jnp.float32)
    out = jnp.zeros((rows, head), jnp.float32)
    for s in range(STEPS):
        weight = jnp.where(fresh[s][1], jnp.exp(fresh[s][0] - row_max), 0.0)
        row_sum = row_sum + weight
        out = out + weight.astype(jnp.bfloat16).astype(jnp.float32) * value_new[s : s + 1]
    for c in range(blocks):
        weight = jnp.exp(score[:, c * width : (c + 1) * width] - row_max)
        weight = jnp.where(tokens[c : c + 1] < limit, weight, 0.0)
        row_sum = row_sum + jnp.sum(weight, 1, keepdims=True)
        values = held[c * block : (c + 1) * block, :, head:].reshape(width, head)
        out = out + jnp.dot(weight.astype(jnp.bfloat16), values, preferred_element_type=jnp.float32)

    diagonal = lax.broadcasted_iota(jnp.int32, (rows, head), 1) == row
    for p in range(packed.shape[0]):
        packed[p, 0:rows] = out
        packed[p, rows : rows + 1] = jnp.sum(jnp.where(diagonal, row_max, 0.0), 0, keepdims=True)
        packed[p, rows + 1 : rows + 2] = jnp.sum(jnp.where(diagonal, row_sum, 0.0), 0, keepdims=True)
        packed[p, rows + 2 :] = jnp.zeros((packed.shape[1] - rows - 2, head), jnp.float32)


def attend(lengths, table, sums, b_query, b_key, b_value, cosine, sine, pool):
    group, head = b_query.shape
    rows = STEPS * group
    return pl.pallas_call(
        attention_kernel,
        out_shape=(
            jax.ShapeDtypeStruct((sums.shape[0], rows + 8, head), jnp.float32),
            jax.ShapeDtypeStruct((8, 2 * head), jnp.float32),
        ),
        in_specs=[SMEM, HBM] + [VMEM] * 6 + [HBM],
        out_specs=(VMEM, VMEM),
        scratch_shapes=[
            pltpu.VMEM(pool.shape, pool.dtype),
            pltpu.VMEM((rows, pool.shape[0] * pool.shape[1]), jnp.float32),
            pltpu.VMEM(table.shape, table.dtype),
            pltpu.SemaphoreType.DMA((CHUNKS + 1,)),
        ],
        compiler_params=params(24),
        name="attend",
    )(lengths, *in_hbm(table), sums, b_query, b_key, b_value, cosine, sine, *in_hbm(pool))


def project_kernel(parts, w_out, out):
    pairs, packed_rows, head = parts.shape
    rows = packed_rows - 8
    group = rows // STEPS
    requests = pairs // 2
    lane = lax.broadcasted_iota(jnp.int32, (rows, head), 1)
    diagonal = lane == lax.broadcasted_iota(jnp.int32, (rows, head), 0)

    def as_column(line):
        return jnp.sum(jnp.where(diagonal, line, 0.0), 1, keepdims=True)

    merged = []
    for r in range(requests):
        first_max, first_sum = (as_column(parts[r, rows + i : rows + i + 1]) for i in range(2))
        second_max, second_sum = (as_column(parts[r + requests, rows + i : rows + i + 1]) for i in range(2))
        top = jnp.maximum(first_max, second_max)
        first_weight = jnp.exp(first_max - top)
        second_weight = jnp.exp(second_max - top)
        joined = first_weight * parts[r, :rows] + second_weight * parts[r + requests, :rows]
        merged.append(joined / (first_weight * first_sum + second_weight * second_sum))
    lines = []
    for s in range(STEPS):
        for r in range(requests):
            lines.append(
                jnp.concatenate(
                    [merged[r][s * group + h : s * group + h + 1] for h in range(group)], 1
                )
            )
    attended = jnp.concatenate(lines, 0).astype(jnp.bfloat16)
    result = jnp.dot(attended, w_out[...], preferred_element_type=jnp.float32)
    for s in range(STEPS):
        out[s] = result[s * requests : (s + 1) * requests]


def project(parts, w_out):
    return pl.pallas_call(
        project_kernel,
        out_shape=jax.ShapeDtypeStruct((STEPS, parts.shape[0] // 2, w_out.shape[1]), jnp.float32),
        in_specs=[VMEM, VMEM],
        out_specs=VMEM,
        compiler_params=params(16),
        name="project",
    )(parts, w_out)


def moved_pages(plan, request):
    count = plan[0, request]
    for s in range(1, STEPS):
        count = count + plan[s, request]
    return count


def copy_kernel(table, lengths, plan, entries, pool, *refs):
    early, (new_pool, *levels) = refs[: len(EARLY) - 1], refs[len(EARLY) - 1 : -5]
    held, fixed, sems, out_sems, sem = refs[-5:]
    slots, page_len, width = held.shape
    per = slots // CHUNKS
    requests = lengths.shape[0]
    pair_index = lax.axis_index("pair")
    is_source = pair_index >= requests
    fetches, stores = [], []
    for c in range(CHUNKS):
        part = pl.ds(c * per, per)
        fetches.append(pltpu.make_async_copy(pool.at[part], held.at[part], sems.at[c]))
        stores.append(pltpu.make_async_copy(held.at[part], new_pool.at[part], out_sems.at[c]))
        fetches[c].start()
    for r in range(requests):
        level = jnp.int32(0)
        for i in range(len(LATE)):
            bound = sum(EARLY) + sum(LATE[:i])
            level = level + jnp.where(moved_pages(plan, r) > bound, 1, 0)
        levels[r][0] = level
    for c in range(CHUNKS):
        fetches[c].wait()
        stores[c].start()
    first_new = lengths[jnp.where(is_source, pair_index - requests, 0)] - PAGES_HALF * page_len
    page_row = lax.broadcasted_iota(jnp.int32, (page_len, width), 0)
    first_slot = table[0, first_new // page_len]
    last_slot = table[0, (first_new + STEPS - 1) // page_len]
    for i, slot in enumerate((first_slot, last_slot)):
        page = held[slot].astype(jnp.float32)
        for s in range(STEPS):
            offset = first_new + s
            here = jnp.logical_and(table[0, offset // page_len] == slot, page_row == offset % page_len)
            page = jnp.where(here, entries[s : s + 1], page)
        fixed[i] = page.astype(held.dtype)
    for c in range(CHUNKS):
        stores[c].wait()

    @pl.when(is_source)
    def _():
        for i, slot in enumerate((first_slot, last_slot)):
            copy = pltpu.make_async_copy(fixed.at[i], new_pool.at[slot], sem)
            copy.start()
            copy.wait()

    @pl.when(jnp.logical_not(is_source))
    def _():
        count = moved_pages(plan, pair_index)
        low = 0
        for pages in early:

            def start(j, carry):
                slot = table[0, PAGES_HALF + low + j]
                pltpu.make_async_copy(pages.at[j], new_pool.at[slot], sem).start()
                return carry

            lax.fori_loop(0, jnp.clip(count - low, 0, pages.shape[0]), start, 0)
            low += pages.shape[0]

        def wait(j, carry):
            pltpu.make_async_copy(early[0].at[0], new_pool.at[0], sem).wait()
            return carry

        lax.fori_loop(0, jnp.minimum(count, low), wait, 0)


def copy_pool(table, lengths, plan, entries, pool, early):
    requests = lengths.shape[0]
    result = pl.pallas_call(
        copy_kernel,
        out_shape=(pltpu.HBM(pool.shape, pool.dtype),)
        + (jax.ShapeDtypeStruct((1,), jnp.int32),) * requests,
        in_specs=[SMEM, SMEM, SMEM, VMEM, HBM] + [VMEM] * len(early),
        out_specs=(HBM,) + (SMEM,) * requests,
        scratch_shapes=[
            pltpu.VMEM(pool.shape, pool.dtype),
            pltpu.VMEM((2,) + pool.shape[1:], pool.dtype),
            pltpu.SemaphoreType.DMA((CHUNKS,)),
            pltpu.SemaphoreType.DMA((CHUNKS,)),
            pltpu.SemaphoreType.DMA,
        ],
        compiler_params=params(16),
        name="copy_pool",
    )(table, lengths, plan, entries, *in_hbm(pool), *early)
    return result[0], [level.reshape(()) for level in result[1:]]


def place_kernel(table_in, plan_in, *refs, done, only):
    parts, (base, new_pool, table, plan, sems, sem) = refs[:-6], refs[-6:]
    del base
    pair_index = lax.axis_index("pair")

    @pl.when(jnp.logical_and(pair_index >= only[0], pair_index < only[1]))
    def _():
        table_copy = pltpu.make_async_copy(table_in, table, sems.at[0])
        plan_copy = pltpu.make_async_copy(plan_in, plan, sems.at[1])
        table_copy.start()
        plan_copy.start()
        table_copy.wait()
        plan_copy.wait()
        count = moved_pages(plan, pair_index) - done
        low = 0
        for pages in parts:

            def start(j, carry):
                slot = table[0, PAGES_HALF + done + low + j]
                pltpu.make_async_copy(pages.at[j], new_pool.at[slot], sem).start()
                return carry

            lax.fori_loop(0, jnp.clip(count - low, 0, pages.shape[0]), start, 0)
            low += pages.shape[0]

        def wait(j, carry):
            pltpu.make_async_copy(parts[0].at[0], new_pool.at[0], sem).wait()
            return carry

        lax.fori_loop(0, jnp.clip(count, 0, low), wait, 0)


def place(table, plan, parts, base, done, only):
    return pl.pallas_call(
        functools.partial(place_kernel, done=done, only=only),
        out_shape=pltpu.HBM(base.shape, base.dtype),
        in_specs=[HBM, HBM] + [VMEM] * len(parts) + [HBM],
        out_specs=HBM,
        scratch_shapes=[
            pltpu.SMEM(table.shape, table.dtype),
            pltpu.SMEM(plan.shape, plan.dtype),
            pltpu.SemaphoreType.DMA((2,)),
            pltpu.SemaphoreType.DMA,
        ],
        input_output_aliases={2 + len(parts): 0},
        compiler_params=params(16),
        name="place",
    )(*in_hbm(table, plan), *parts, *in_hbm(base))


def local(
    normed, w_query, b_query, w_key, b_key, w_value, b_value, w_out, pool, page_table, lengths, plan
):
    pair_count = lax.axis_size("pair")
    tp_count = lax.axis_size("tp")
    requests = pair_count // 2
    head = w_key.shape[1]

    partial, *pieces = prepare(page_table, normed, w_query, w_key, w_value, pool[0, 0], pair_count)
    route = [(i + requests, i) for i in range(requests)]

    def migrate(pages):
        return lax.ppermute(pages, "pair", route)

    def tie(*values):
        return lax.optimization_barrier(values)

    planned = plan.T
    either = lax.axis_index("rep") == 0

    def exchange(values):
        def send(values):
            return lax.all_to_all(values, "pair", split_axis=0, concat_axis=0, tiled=True)

        return lax.cond(either, send, send, values)

    first = migrate(pieces[0])
    sums, first = tie(exchange(partial), first)
    second = migrate(tie(pieces[1], sums)[0])

    frequency = rope_base ** (-(jnp.arange(head // 2, dtype=jnp.float32) * 2.0 / head))
    steps = jnp.minimum(jnp.arange(8, dtype=jnp.int32), STEPS - 1)
    position = (lengths[:, None] + steps[None, :]).astype(jnp.float32)[..., None]
    angles = position * frequency
    cosine = jnp.cos(angles)
    sine = jnp.sin(angles)
    cosine = jnp.concatenate([cosine, cosine], -1)
    sine = jnp.concatenate([-sine, sine], -1)

    packed, entries = attend(
        lengths,
        page_table,
        sums,
        b_query.reshape(-1, head),
        b_key[None, :],
        b_value[None, :],
        cosine,
        sine,
        pool[0, 0],
    )
    parts, second = tie(exchange(packed), second)
    third = migrate(tie(pieces[2], parts)[0])
    new_pool, levels = copy_pool(page_table, lengths, planned, entries, pool[0, 0], [first, second])
    projected = project(parts, w_out)
    if tp_count == 2:
        projected = projected + lax.ppermute(projected, "tp", [(0, 1), (1, 0)])
    else:
        projected = lax.psum(projected, "tp")
    new_pool, projected = tie(new_pool, projected)
    static = sum(EARLY)

    def send(level, request, base, *chunks):
        if level == 0:
            return base
        arrived = [lax.ppermute(chunk, "pair", [(request + requests, request)]) for chunk in chunks[:level]]
        return place(page_table, planned, arrived, base, static, (request, request + 1))

    for request in range(requests):
        branches = [functools.partial(send, level, request) for level in range(len(LATE) + 1)]
        new_pool = lax.switch(levels[request], branches, new_pool, *pieces[len(EARLY) :])
    new_pool = place(page_table, planned, [third], new_pool, EARLY[0] + EARLY[1], (0, requests))
    return projected, new_pool[None, None]


def solution(mesh):
    return jax.shard_map(
        local,
        mesh=mesh,
        in_specs=(
            P(None, "rep", "pair"),
            P("pair", "tp"),
            P("tp"),
            P("pair", "tp"),
            P("tp"),
            P("pair", "tp"),
            P("tp"),
            P("tp", "pair"),
            P(("rep", "pair"), "tp", None, None, None),
            P(("rep", "pair"), None),
            P("rep"),
            P("rep", None),
        ),
        out_specs=(P(None, "rep", "pair"), P(("rep", "pair"), "tp", None, None, None)),
        check_vma=False,
    )
```

```python
import functools
import math

import jax
import jax.numpy as jnp
from jax import lax
from jax.experimental import pallas as pl
from jax.experimental.pallas import tpu as pltpu
from jax.sharding import PartitionSpec as P

PAGES_HALF = 384
STEPS = 2
SECTION = 64
MOVED_MAX = STEPS * SECTION
EARLY = (18, 32, 21)
LATE = (19, 19, 19)
PIECES = EARLY[:2]
LATER = EARLY[2:] + LATE
CHUNKS = 8
NEG = -1e30

rope_base = 1000000.0

VMEM = pl.BlockSpec(memory_space=pltpu.VMEM)
SMEM = pl.BlockSpec(memory_space=pltpu.SMEM)
HBM = pl.BlockSpec(memory_space=pltpu.HBM)


def in_hbm(*arrays):
    return tuple(pltpu.with_memory_space_constraint(a, pltpu.HBM) for a in arrays)


def params(mib):
    return pltpu.CompilerParams(vmem_limit_bytes=mib * 1024 * 1024)


def prepare_kernel(table_in, normed_in, w_query, w_key, w_value, pool, partial, *refs):
    pieces, (table, normed, weights, table_sem, sems, page_sems) = refs[:-6], refs[-6:]
    pairs = partial.shape[0]
    requests = pairs // 2
    table_copy = pltpu.make_async_copy(table_in, table, table_sem)
    table_copy.start()
    loads = [pltpu.make_async_copy(normed_in, normed, sems.at[3])]
    low = 0
    for i, weight in enumerate((w_query, w_key, w_value)):
        part = weights.at[:, low : low + weight.shape[1]]
        loads.append(pltpu.make_async_copy(weight, part, sems.at[i]))
        low += weight.shape[1]
    for copy in loads:
        copy.start()
    table_copy.wait()

    @pl.when(lax.axis_index("pair") >= requests)
    def _():
        low = 0
        for i, piece in enumerate(pieces):

            def start(j, carry):
                pltpu.make_async_copy(pool.at[table[0, low + j]], piece.at[j], page_sems.at[i]).start()
                return carry

            lax.fori_loop(0, piece.shape[0], start, 0, unroll=2)
            low += piece.shape[0]

    for copy in loads:
        copy.wait()
    hidden = jnp.concatenate([normed[s].astype(jnp.float32) for s in range(STEPS)], 0).astype(jnp.bfloat16)
    result = jnp.dot(hidden, weights[...], preferred_element_type=jnp.float32)
    for p in range(pairs):
        for s in range(STEPS):
            row = s * requests + p % requests
            partial[p, s : s + 1] = result[row : row + 1]

    @pl.when(lax.axis_index("pair") >= requests)
    def _():
        for i, piece in enumerate(pieces):
            pltpu.make_async_copy(pool.at[pl.ds(0, piece.shape[0])], piece, page_sems.at[i]).wait()


def prepare(table, normed, w_query, w_key, w_value, pool, pairs):
    page = pool.shape[1:]
    wide = w_query.shape[1] + 2 * w_key.shape[1]
    return pl.pallas_call(
        prepare_kernel,
        out_shape=(jax.ShapeDtypeStruct((pairs, STEPS, wide), jnp.float32),)
        + tuple(pltpu.VMEM((n,) + page, pool.dtype) for n in PIECES),
        in_specs=[HBM] * 6,
        out_specs=(VMEM,) + (VMEM,) * len(PIECES),
        scratch_shapes=[
            pltpu.SMEM(table.shape, table.dtype),
            pltpu.VMEM(normed.shape, normed.dtype),
            pltpu.VMEM((w_query.shape[0], wide), w_query.dtype),
            pltpu.SemaphoreType.DMA,
            pltpu.SemaphoreType.DMA((4,)),
            pltpu.SemaphoreType.DMA((len(PIECES),)),
        ],
        compiler_params=params(16),
        name="prepare",
    )(*in_hbm(table, normed, w_query, w_key, w_value, pool))


def page_order(table, slots):
    slot = lax.broadcasted_iota(jnp.int32, (slots, slots), 0)
    holds = jnp.where(slot == table, 1.0, 0.0).astype(jnp.bfloat16)
    index = lax.broadcasted_iota(jnp.int32, (8, slots), 1)
    digit = lax.broadcasted_iota(jnp.int32, (8, slots), 0)
    digits = jnp.where(digit == 0, index // 16, jnp.where(digit == 1, index % 16, 0))
    digits = digits.astype(jnp.float32).astype(jnp.bfloat16)
    return lax.dot_general(digits, holds, (((1,), (1,)), ((), ())), preferred_element_type=jnp.float32)


def attention_kernel(lengths, table_in, sums, b_query, b_key, b_value, cosine, sine, pool, packed, new_pool, fixed, *refs):
    pieces, (held, score, table, slots_of, sems, out_sems) = refs[: len(LATER)], refs[len(LATER) :]
    slots, page_len, _ = held.shape
    per = slots // CHUNKS
    table_copy = pltpu.make_async_copy(table_in, table, sems.at[CHUNKS])
    table_copy.start()
    slots_copy = pltpu.make_async_copy(table_in, slots_of, sems.at[CHUNKS + 1])
    slots_copy.start()
    copies = []
    for c in range(CHUNKS):
        part = pl.ds(c * per, per)
        copies.append(pltpu.make_async_copy(pool.at[part], held.at[part], sems.at[c]))
        copies[-1].start()
    requests = sums.shape[0] // 2
    group, head = b_query.shape
    rows = STEPS * group
    pair_index = lax.axis_index("pair")
    is_source = pair_index >= requests
    request = jnp.where(is_source, pair_index - requests, pair_index)
    half_tokens = PAGES_HALF * page_len
    limit = jnp.where(is_source, lengths[request] - half_tokens, half_tokens)

    blocks = CHUNKS // 2
    block = slots // blocks
    width = block * page_len
    table_copy.wait()
    digits = page_order(table[...], slots)
    digits = jnp.concatenate(
        [digits[d : d + 1, c * block : (c + 1) * block] for d in range(2) for c in range(blocks)], 0
    ).astype(jnp.bfloat16)
    spread = lax.broadcasted_iota(jnp.int32, (block, width), 1) // page_len
    spread = jnp.where(spread == lax.broadcasted_iota(jnp.int32, (block, width), 0), 1.0, 0.0)
    digits = jnp.dot(digits, spread.astype(jnp.bfloat16), preferred_element_type=jnp.float32)
    tokens = (digits[:blocks] * 16.0 + digits[blocks:]).astype(jnp.int32) * page_len
    tokens = tokens + lax.broadcasted_iota(jnp.int32, (blocks, width), 1) % page_len

    total = sums[0]
    for p in range(1, sums.shape[0]):
        total = total + sums[p]
    query = jnp.concatenate(
        [total[s : s + 1, h * head : (h + 1) * head] for s in range(STEPS) for h in range(group)], 0
    )
    query = query + jnp.concatenate([b_query[...]] * STEPS, 0)
    cos_new = cosine[request]
    sin_new = sine[request]
    row = lax.broadcasted_iota(jnp.int32, (rows, head), 0)
    cos_rows = jnp.where(row < group, cos_new[0:1], cos_new[1:2])
    sin_rows = jnp.where(row < group, sin_new[0:1], sin_new[1:2])
    query = (query * cos_rows + pltpu.roll(query, head // 2, 1) * sin_rows).astype(jnp.bfloat16)
    key_new = total[:, group * head : (group + 1) * head] + b_key[...]
    key_new = jnp.concatenate([key_new, jnp.zeros((8 - STEPS, head), jnp.float32)], 0)
    key_new = key_new * cos_new + pltpu.roll(key_new, head // 2, 1) * sin_new
    key_new = key_new.astype(jnp.bfloat16).astype(jnp.float32)
    value_new = total[:, (group + 1) * head :] + b_value[...]
    value_new = value_new.astype(jnp.bfloat16).astype(jnp.float32)
    scale = 1.0 / math.sqrt(head)

    column = lax.broadcasted_iota(jnp.int32, (rows, 1), 0)
    query_wide = query.astype(jnp.float32)
    fresh = []
    for s in range(STEPS):
        dots = jnp.sum(query_wide * key_new[s : s + 1], 1, keepdims=True) * scale
        seen = jnp.logical_and(is_source, column >= s * group)
        fresh.append((jnp.where(seen, dots, NEG), seen))
    row_max = jnp.maximum(fresh[0][0], fresh[1][0])

    stores = []
    for c in range(blocks):
        for i in range(c * CHUNKS // blocks, (c + 1) * CHUNKS // blocks):
            copies[i].wait()
            part = pl.ds(i * per, per)
            stores.append(pltpu.make_async_copy(held.at[part], new_pool.at[part], out_sems.at[i]))
            stores[-1].start()
        keys = held[c * block : (c + 1) * block, :, :head].reshape(width, head)
        part = lax.dot_general(query, keys, (((1,), (1,)), ((), ())), preferred_element_type=jnp.float32)
        part = jnp.where(tokens[c : c + 1] < limit, part * scale, NEG)
        score[:, c * width : (c + 1) * width] = part
        row_max = jnp.maximum(row_max, jnp.max(part, 1, keepdims=True))
    row_sum = jnp.zeros((rows, 1), jnp.float32)
    out = jnp.zeros((rows, head), jnp.float32)
    for s in range(STEPS):
        weight = jnp.where(fresh[s][1], jnp.exp(fresh[s][0] - row_max), 0.0)
        row_sum = row_sum + weight
        out = out + weight.astype(jnp.bfloat16).astype(jnp.float32) * value_new[s : s + 1]
    for c in range(blocks):
        weight = jnp.exp(score[:, c * width : (c + 1) * width] - row_max)
        weight = jnp.where(tokens[c : c + 1] < limit, weight, 0.0)
        row_sum = row_sum + jnp.sum(weight, 1, keepdims=True)
        values = held[c * block : (c + 1) * block, :, head:].reshape(width, head)
        out = out + jnp.dot(weight.astype(jnp.bfloat16), values, preferred_element_type=jnp.float32)

    diagonal = lax.broadcasted_iota(jnp.int32, (rows, head), 1) == row
    for p in range(packed.shape[0]):
        packed[p, 0:rows] = out
        packed[p, rows : rows + 1] = jnp.sum(jnp.where(diagonal, row_max, 0.0), 0, keepdims=True)
        packed[p, rows + 1 : rows + 2] = jnp.sum(jnp.where(diagonal, row_sum, 0.0), 0, keepdims=True)
        packed[p, rows + 2 :] = jnp.zeros((packed.shape[1] - rows - 2, head), jnp.float32)

    slots_copy.wait()

    @pl.when(is_source)
    def _():
        low = sum(PIECES)
        for piece in pieces:

            def take(j, carry):
                piece[j] = held[slots_of[0, low + j]]
                return carry

            lax.fori_loop(0, piece.shape[0], take, 0)
            low += piece.shape[0]
        page_row = lax.broadcasted_iota(jnp.int32, (page_len, 2 * head), 0)
        entries = jnp.concatenate([key_new[:STEPS], value_new], 1)
        offsets = [limit + s for s in range(STEPS)]
        homes = [slots_of[0, offset // page_len] for offset in offsets]
        for i, slot in enumerate((homes[0], homes[-1])):
            page = held[slot].astype(jnp.float32)
            for s, offset in enumerate(offsets):
                here = jnp.logical_and(homes[s] == slot, page_row == offset % page_len)
                page = jnp.where(here, entries[s : s + 1], page)
            fixed[i] = page.astype(held.dtype)

    for store in stores:
        store.wait()


def attend(lengths, table, sums, b_query, b_key, b_value, cosine, sine, pool):
    group, head = b_query.shape
    rows = STEPS * group
    page = pool.shape[1:]
    return pl.pallas_call(
        attention_kernel,
        out_shape=(
            jax.ShapeDtypeStruct((sums.shape[0], rows + 8, head), jnp.float32),
            pltpu.HBM(pool.shape, pool.dtype),
            jax.ShapeDtypeStruct((2,) + page, pool.dtype),
        )
        + tuple(pltpu.VMEM((n,) + page, pool.dtype) for n in LATER),
        in_specs=[SMEM, HBM] + [VMEM] * 6 + [HBM],
        out_specs=(VMEM, HBM, VMEM) + (VMEM,) * len(LATER),
        scratch_shapes=[
            pltpu.VMEM(pool.shape, pool.dtype),
            pltpu.VMEM((rows, pool.shape[0] * pool.shape[1]), jnp.float32),
            pltpu.VMEM(table.shape, table.dtype),
            pltpu.SMEM(table.shape, table.dtype),
            pltpu.SemaphoreType.DMA((CHUNKS + 2,)),
            pltpu.SemaphoreType.DMA((CHUNKS,)),
        ],
        compiler_params=params(24),
        name="attend",
    )(lengths, *in_hbm(table), sums, b_query, b_key, b_value, cosine, sine, *in_hbm(pool))


def moved_pages(plan, request):
    count = plan[0, request]
    for s in range(1, STEPS):
        count = count + plan[s, request]
    return count


def project_kernel(plan, parts, w_out, out, *levels):
    for r, level in enumerate(levels):
        bounds = [sum(EARLY) + sum(LATE[:i]) for i in range(len(LATE))]
        level[0] = sum(jnp.where(moved_pages(plan, r) > bound, 1, 0) for bound in bounds)
    pairs, packed_rows, head = parts.shape
    rows = packed_rows - 8
    group = rows // STEPS
    requests = pairs // 2
    lane = lax.broadcasted_iota(jnp.int32, (rows, head), 1)
    diagonal = lane == lax.broadcasted_iota(jnp.int32, (rows, head), 0)

    def as_column(line):
        return jnp.sum(jnp.where(diagonal, line, 0.0), 1, keepdims=True)

    merged = []
    for r in range(requests):
        first_max, first_sum = (as_column(parts[r, rows + i : rows + i + 1]) for i in range(2))
        second_max, second_sum = (as_column(parts[r + requests, rows + i : rows + i + 1]) for i in range(2))
        top = jnp.maximum(first_max, second_max)
        first_weight = jnp.exp(first_max - top)
        second_weight = jnp.exp(second_max - top)
        joined = first_weight * parts[r, :rows] + second_weight * parts[r + requests, :rows]
        merged.append(joined / (first_weight * first_sum + second_weight * second_sum))
    lines = []
    for s in range(STEPS):
        for r in range(requests):
            lines.append(
                jnp.concatenate(
                    [merged[r][s * group + h : s * group + h + 1] for h in range(group)], 1
                )
            )
    attended = jnp.concatenate(lines, 0).astype(jnp.bfloat16)
    result = jnp.dot(attended, w_out[...], preferred_element_type=jnp.float32)
    for s in range(STEPS):
        out[s] = result[s * requests : (s + 1) * requests]


def project(plan, parts, w_out):
    requests = parts.shape[0] // 2
    out, *levels = pl.pallas_call(
        project_kernel,
        out_shape=(jax.ShapeDtypeStruct((STEPS, requests, w_out.shape[1]), jnp.float32),)
        + (jax.ShapeDtypeStruct((1,), jnp.int32),) * requests,
        in_specs=[SMEM, VMEM, VMEM],
        out_specs=(VMEM,) + (SMEM,) * requests,
        compiler_params=params(16),
        name="project",
    )(plan, parts, w_out)
    return out, [level.reshape(()) for level in levels]


def place_kernel(table_in, plan_in, lengths, *refs, done, only, patch):
    parts, (base, new_pool, table, plan, sems, sem) = refs[:-6], refs[-6:]
    del base
    pair_index = lax.axis_index("pair")
    requests = lengths.shape[0]
    is_target = jnp.logical_and(pair_index >= only[0], pair_index < only[1])
    table_copy = pltpu.make_async_copy(table_in, table, sems.at[0])
    plan_copy = pltpu.make_async_copy(plan_in, plan, sems.at[1])

    @pl.when(is_target)
    def _():
        table_copy.start()
        plan_copy.start()
        table_copy.wait()
        plan_copy.wait()
        count = moved_pages(plan, pair_index) - done
        low = 0
        for pages in parts[1:] if patch else parts:

            def start(j, carry):
                slot = table[0, PAGES_HALF + done + low + j]
                pltpu.make_async_copy(pages.at[j], new_pool.at[slot], sem).start()
                return carry

            lax.fori_loop(0, jnp.clip(count - low, 0, pages.shape[0]), start, 0)
            low += pages.shape[0]

        def wait(j, carry):
            pltpu.make_async_copy(parts[-1].at[0], new_pool.at[0], sem).wait()
            return carry

        lax.fori_loop(0, jnp.clip(count, 0, low), wait, 0)

    if patch:

        @pl.when(pair_index >= requests)
        def _():
            table_copy.start()
            table_copy.wait()
            page_len = new_pool.shape[1]
            first = lengths[pair_index - requests] - PAGES_HALF * page_len
            for i, offset in enumerate((first, first + STEPS - 1)):
                slot = table[0, offset // page_len]
                copy = pltpu.make_async_copy(parts[0].at[i], new_pool.at[slot], sem)
                copy.start()
                copy.wait()


def place(table, plan, lengths, parts, base, done, only, patch=False):
    return pl.pallas_call(
        functools.partial(place_kernel, done=done, only=only, patch=patch),
        out_shape=pltpu.HBM(base.shape, base.dtype),
        in_specs=[HBM, HBM, SMEM] + [VMEM] * len(parts) + [HBM],
        out_specs=HBM,
        scratch_shapes=[
            pltpu.SMEM(table.shape, table.dtype),
            pltpu.SMEM(plan.shape, plan.dtype),
            pltpu.SemaphoreType.DMA((2,)),
            pltpu.SemaphoreType.DMA,
        ],
        input_output_aliases={3 + len(parts): 0},
        compiler_params=params(16),
        name="place",
    )(*in_hbm(table, plan), lengths, *parts, *in_hbm(base))


def local(
    normed, w_query, b_query, w_key, b_key, w_value, b_value, w_out, pool, page_table, lengths, plan
):
    pair_count = lax.axis_size("pair")
    tp_count = lax.axis_size("tp")
    requests = pair_count // 2
    head = w_key.shape[1]

    partial, *pieces = prepare(page_table, normed, w_query, w_key, w_value, pool[0, 0], pair_count)
    route = [(i + requests, i) for i in range(requests)]

    def migrate(pages):
        return lax.ppermute(pages, "pair", route)

    def tie(*values):
        return lax.optimization_barrier(values)

    planned = plan.T
    either = lax.axis_index("rep") == 0

    def exchange(values):
        def send(values):
            return lax.all_to_all(values, "pair", split_axis=0, concat_axis=0, tiled=True)

        return lax.cond(either, send, send, values)

    first = migrate(pieces[0])
    sums, first = tie(exchange(partial), first)
    second = migrate(tie(pieces[1], sums)[0])

    frequency = rope_base ** (-(jnp.arange(head // 2, dtype=jnp.float32) * 2.0 / head))
    steps = jnp.minimum(jnp.arange(8, dtype=jnp.int32), STEPS - 1)
    position = (lengths[:, None] + steps[None, :]).astype(jnp.float32)[..., None]
    angles = position * frequency
    cosine = jnp.cos(angles)
    sine = jnp.sin(angles)
    cosine = jnp.concatenate([cosine, cosine], -1)
    sine = jnp.concatenate([-sine, sine], -1)

    packed, new_pool, fixed, *later = attend(
        lengths,
        page_table,
        sums,
        b_query.reshape(-1, head),
        b_key[None, :],
        b_value[None, :],
        cosine,
        sine,
        pool[0, 0],
    )
    parts, second = tie(exchange(packed), second)
    third = migrate(tie(later[0], parts)[0])
    projected, levels = project(planned, parts, w_out)
    new_pool = place(page_table, planned, lengths, [fixed, first, second], new_pool, 0, (0, requests), True)
    if tp_count == 2:
        projected = projected + lax.ppermute(projected, "tp", [(0, 1), (1, 0)])
    else:
        projected = lax.psum(projected, "tp")

    new_pool, projected = tie(new_pool, projected)
    static = sum(EARLY)

    def send(level, request, base, *chunks):
        if level == 0:
            return base
        arrived = [lax.ppermute(chunk, "pair", [(request + requests, request)]) for chunk in chunks[:level]]
        return place(page_table, planned, lengths, arrived, base, static, (request, request + 1))

    for request in range(requests):
        branches = [functools.partial(send, level, request) for level in range(len(LATE) + 1)]
        new_pool = lax.switch(levels[request], branches, new_pool, *later[1:])
    new_pool = place(page_table, planned, lengths, [third], new_pool, EARLY[0] + EARLY[1], (0, requests))
    return projected, new_pool[None, None]


def solution(mesh):
    return jax.shard_map(
        local,
        mesh=mesh,
        in_specs=(
            P(None, "rep", "pair"),
            P("pair", "tp"),
            P("tp"),
            P("pair", "tp"),
            P("tp"),
            P("pair", "tp"),
            P("tp"),
            P("tp", "pair"),
            P(("rep", "pair"), "tp", None, None, None),
            P(("rep", "pair"), None),
            P("rep"),
            P("rep", None),
        ),
        out_specs=(P(None, "rep", "pair"), P(("rep", "pair"), "tp", None, None, None)),
        check_vma=False,
    )
```

```python
import functools
import math

import jax
import jax.numpy as jnp
from jax import lax
from jax.experimental import pallas as pl
from jax.experimental.pallas import tpu as pltpu
from jax.sharding import PartitionSpec as P

PAGES_HALF = 384
STEPS = 2
SECTION = 64
MOVED_MAX = STEPS * SECTION
EARLY = (18, 10, 32, 12, 22)
LATE = MOVED_MAX - sum(EARLY)
PIECES = EARLY[:3]
LATER = EARLY[3:] + (LATE,)
JOINT = 4
CHUNKS = 8
NEG = -1e30

rope_base = 1000000.0

VMEM = pl.BlockSpec(memory_space=pltpu.VMEM)
SMEM = pl.BlockSpec(memory_space=pltpu.SMEM)
HBM = pl.BlockSpec(memory_space=pltpu.HBM)


def in_hbm(*arrays):
    return tuple(pltpu.with_memory_space_constraint(a, pltpu.HBM) for a in arrays)


def params(mib):
    return pltpu.CompilerParams(vmem_limit_bytes=mib * 1024 * 1024)


def prepare_kernel(table_in, normed_in, w_query, w_key, w_value, pool, partial, *refs):
    pieces, (table, normed, weights, table_sem, sems, page_sems) = refs[:-6], refs[-6:]
    pairs = partial.shape[0]
    requests = pairs // 2
    table_copy = pltpu.make_async_copy(table_in, table, table_sem)
    table_copy.start()
    loads = [pltpu.make_async_copy(normed_in, normed, sems.at[3])]
    low = 0
    for i, weight in enumerate((w_query, w_key, w_value)):
        part = weights.at[:, low : low + weight.shape[1]]
        loads.append(pltpu.make_async_copy(weight, part, sems.at[i]))
        low += weight.shape[1]
    for copy in loads:
        copy.start()
    table_copy.wait()

    @pl.when(lax.axis_index("pair") >= requests)
    def _():
        low = 0
        for i, piece in enumerate(pieces):

            def start(j, carry):
                pltpu.make_async_copy(pool.at[table[0, low + j]], piece.at[j], page_sems.at[i]).start()
                return carry

            lax.fori_loop(0, piece.shape[0], start, 0, unroll=2)
            low += piece.shape[0]

    for copy in loads:
        copy.wait()
    hidden = jnp.concatenate([normed[s].astype(jnp.float32) for s in range(STEPS)], 0).astype(jnp.bfloat16)
    result = jnp.dot(hidden, weights[...], preferred_element_type=jnp.float32)
    for p in range(pairs):
        for s in range(STEPS):
            row = s * requests + p % requests
            partial[p, s : s + 1] = result[row : row + 1]

    @pl.when(lax.axis_index("pair") >= requests)
    def _():
        for i, piece in enumerate(pieces):
            pltpu.make_async_copy(pool.at[pl.ds(0, piece.shape[0])], piece, page_sems.at[i]).wait()


def prepare(table, normed, w_query, w_key, w_value, pool, pairs):
    page = pool.shape[1:]
    wide = w_query.shape[1] + 2 * w_key.shape[1]
    return pl.pallas_call(
        prepare_kernel,
        out_shape=(jax.ShapeDtypeStruct((pairs, STEPS, wide), jnp.float32),)
        + tuple(pltpu.VMEM((n,) + page, pool.dtype) for n in PIECES),
        in_specs=[HBM] * 6,
        out_specs=(VMEM,) + (VMEM,) * len(PIECES),
        scratch_shapes=[
            pltpu.SMEM(table.shape, table.dtype),
            pltpu.VMEM(normed.shape, normed.dtype),
            pltpu.VMEM((w_query.shape[0], wide), w_query.dtype),
            pltpu.SemaphoreType.DMA,
            pltpu.SemaphoreType.DMA((4,)),
            pltpu.SemaphoreType.DMA((len(PIECES),)),
        ],
        compiler_params=params(16),
        name="prepare",
    )(*in_hbm(table, normed, w_query, w_key, w_value, pool))


def page_order(table, slots):
    slot = lax.broadcasted_iota(jnp.int32, (slots, slots), 0)
    holds = jnp.where(slot == table, 1.0, 0.0).astype(jnp.bfloat16)
    index = lax.broadcasted_iota(jnp.int32, (8, slots), 1)
    digit = lax.broadcasted_iota(jnp.int32, (8, slots), 0)
    digits = jnp.where(digit == 0, index // 16, jnp.where(digit == 1, index % 16, 0))
    digits = digits.astype(jnp.float32).astype(jnp.bfloat16)
    return lax.dot_general(digits, holds, (((1,), (1,)), ((), ())), preferred_element_type=jnp.float32)


def attention_kernel(lengths, table_in, sums, b_query, b_key, b_value, cosine, sine, pool, packed, new_pool, fixed, *refs):
    pieces, (held, score, table, slots_of, sems, out_sems) = refs[: len(LATER)], refs[len(LATER) :]
    slots, page_len, _ = held.shape
    per = slots // CHUNKS
    table_copy = pltpu.make_async_copy(table_in, table, sems.at[CHUNKS])
    table_copy.start()
    slots_copy = pltpu.make_async_copy(table_in, slots_of, sems.at[CHUNKS + 1])
    slots_copy.start()
    copies = []
    for c in range(CHUNKS):
        part = pl.ds(c * per, per)
        copies.append(pltpu.make_async_copy(pool.at[part], held.at[part], sems.at[c]))
        copies[-1].start()
    requests = sums.shape[0] // 2
    group, head = b_query.shape
    rows = STEPS * group
    pair_index = lax.axis_index("pair")
    is_source = pair_index >= requests
    request = jnp.where(is_source, pair_index - requests, pair_index)
    half_tokens = PAGES_HALF * page_len
    limit = jnp.where(is_source, lengths[request] - half_tokens, half_tokens)

    blocks = CHUNKS // 2
    block = slots // blocks
    width = block * page_len
    table_copy.wait()
    digits = page_order(table[...], slots)
    digits = jnp.concatenate(
        [digits[d : d + 1, c * block : (c + 1) * block] for d in range(2) for c in range(blocks)], 0
    ).astype(jnp.bfloat16)
    spread = lax.broadcasted_iota(jnp.int32, (block, width), 1) // page_len
    spread = jnp.where(spread == lax.broadcasted_iota(jnp.int32, (block, width), 0), 1.0, 0.0)
    digits = jnp.dot(digits, spread.astype(jnp.bfloat16), preferred_element_type=jnp.float32)
    tokens = (digits[:blocks] * 16.0 + digits[blocks:]).astype(jnp.int32) * page_len
    tokens = tokens + lax.broadcasted_iota(jnp.int32, (blocks, width), 1) % page_len

    total = sums[0]
    for p in range(1, sums.shape[0]):
        total = total + sums[p]
    query = jnp.concatenate(
        [total[s : s + 1, h * head : (h + 1) * head] for s in range(STEPS) for h in range(group)], 0
    )
    query = query + jnp.concatenate([b_query[...]] * STEPS, 0)
    cos_new = cosine[request]
    sin_new = sine[request]
    row = lax.broadcasted_iota(jnp.int32, (rows, head), 0)
    cos_rows = jnp.where(row < group, cos_new[0:1], cos_new[1:2])
    sin_rows = jnp.where(row < group, sin_new[0:1], sin_new[1:2])
    query = (query * cos_rows + pltpu.roll(query, head // 2, 1) * sin_rows).astype(jnp.bfloat16)
    key_new = total[:, group * head : (group + 1) * head] + b_key[...]
    key_new = jnp.concatenate([key_new, jnp.zeros((8 - STEPS, head), jnp.float32)], 0)
    key_new = key_new * cos_new + pltpu.roll(key_new, head // 2, 1) * sin_new
    key_new = key_new.astype(jnp.bfloat16).astype(jnp.float32)
    value_new = total[:, (group + 1) * head :] + b_value[...]
    value_new = value_new.astype(jnp.bfloat16).astype(jnp.float32)
    scale = 1.0 / math.sqrt(head)

    column = lax.broadcasted_iota(jnp.int32, (rows, 1), 0)
    query_wide = query.astype(jnp.float32)
    fresh = []
    for s in range(STEPS):
        dots = jnp.sum(query_wide * key_new[s : s + 1], 1, keepdims=True) * scale
        seen = jnp.logical_and(is_source, column >= s * group)
        fresh.append((jnp.where(seen, dots, NEG), seen))
    row_max = jnp.maximum(fresh[0][0], fresh[1][0])

    stores = []
    for c in range(blocks):
        for i in range(c * CHUNKS // blocks, (c + 1) * CHUNKS // blocks):
            copies[i].wait()
            part = pl.ds(i * per, per)
            stores.append(pltpu.make_async_copy(held.at[part], new_pool.at[part], out_sems.at[i]))
            stores[-1].start()
        keys = held[c * block : (c + 1) * block, :, :head].reshape(width, head)
        part = lax.dot_general(query, keys, (((1,), (1,)), ((), ())), preferred_element_type=jnp.float32)
        part = jnp.where(tokens[c : c + 1] < limit, part * scale, NEG)
        score[:, c * width : (c + 1) * width] = part
        row_max = jnp.maximum(row_max, jnp.max(part, 1, keepdims=True))
    row_sum = jnp.zeros((rows, 1), jnp.float32)
    out = jnp.zeros((rows, head), jnp.float32)
    for s in range(STEPS):
        weight = jnp.where(fresh[s][1], jnp.exp(fresh[s][0] - row_max), 0.0)
        row_sum = row_sum + weight
        out = out + weight.astype(jnp.bfloat16).astype(jnp.float32) * value_new[s : s + 1]
    for c in range(blocks):
        weight = jnp.exp(score[:, c * width : (c + 1) * width] - row_max)
        weight = jnp.where(tokens[c : c + 1] < limit, weight, 0.0)
        row_sum = row_sum + jnp.sum(weight, 1, keepdims=True)
        values = held[c * block : (c + 1) * block, :, head:].reshape(width, head)
        out = out + jnp.dot(weight.astype(jnp.bfloat16), values, preferred_element_type=jnp.float32)

    diagonal = lax.broadcasted_iota(jnp.int32, (rows, head), 1) == row
    for p in range(packed.shape[0]):
        packed[p, 0:rows] = out
        packed[p, rows : rows + 1] = jnp.sum(jnp.where(diagonal, row_max, 0.0), 0, keepdims=True)
        packed[p, rows + 1 : rows + 2] = jnp.sum(jnp.where(diagonal, row_sum, 0.0), 0, keepdims=True)
        packed[p, rows + 2 :] = jnp.zeros((packed.shape[1] - rows - 2, head), jnp.float32)

    slots_copy.wait()

    @pl.when(is_source)
    def _():
        low = sum(PIECES)
        for piece in pieces:

            def take(j, carry):
                piece[j] = held[slots_of[0, low + j]]
                return carry

            lax.fori_loop(0, piece.shape[0], take, 0)
            low += piece.shape[0]
        page_row = lax.broadcasted_iota(jnp.int32, (page_len, 2 * head), 0)
        entries = jnp.concatenate([key_new[:STEPS], value_new], 1)
        offsets = [limit + s for s in range(STEPS)]
        homes = [slots_of[0, offset // page_len] for offset in offsets]
        for i, slot in enumerate((homes[0], homes[-1])):
            page = held[slot].astype(jnp.float32)
            for s, offset in enumerate(offsets):
                here = jnp.logical_and(homes[s] == slot, page_row == offset % page_len)
                page = jnp.where(here, entries[s : s + 1], page)
            fixed[i] = page.astype(held.dtype)

    for store in stores:
        store.wait()


def attend(lengths, table, sums, b_query, b_key, b_value, cosine, sine, pool):
    group, head = b_query.shape
    rows = STEPS * group
    page = pool.shape[1:]
    return pl.pallas_call(
        attention_kernel,
        out_shape=(
            jax.ShapeDtypeStruct((sums.shape[0], rows + 8, head), jnp.float32),
            pltpu.HBM(pool.shape, pool.dtype),
            jax.ShapeDtypeStruct((2,) + page, pool.dtype),
        )
        + tuple(pltpu.VMEM((n,) + page, pool.dtype) for n in LATER),
        in_specs=[SMEM, HBM] + [VMEM] * 6 + [HBM],
        out_specs=(VMEM, HBM, VMEM) + (VMEM,) * len(LATER),
        scratch_shapes=[
            pltpu.VMEM(pool.shape, pool.dtype),
            pltpu.VMEM((rows, pool.shape[0] * pool.shape[1]), jnp.float32),
            pltpu.VMEM(table.shape, table.dtype),
            pltpu.SMEM(table.shape, table.dtype),
            pltpu.SemaphoreType.DMA((CHUNKS + 2,)),
            pltpu.SemaphoreType.DMA((CHUNKS,)),
        ],
        compiler_params=params(24),
        name="attend",
    )(lengths, *in_hbm(table), sums, b_query, b_key, b_value, cosine, sine, *in_hbm(pool))


def moved_pages(plan, request):
    count = plan[0, request]
    for s in range(1, STEPS):
        count = count + plan[s, request]
    return count


def project_kernel(plan, parts, w_out, out, *members):
    for g, member in enumerate(members):
        code = jnp.int32(0)
        for r in range(g * JOINT, min((g + 1) * JOINT, plan.shape[1])):
            code = code + jnp.where(moved_pages(plan, r) > sum(EARLY), 1 << (r - g * JOINT), 0)
        member[0] = code
    pairs, packed_rows, head = parts.shape
    rows = packed_rows - 8
    group = rows // STEPS
    requests = pairs // 2
    lane = lax.broadcasted_iota(jnp.int32, (rows, head), 1)
    diagonal = lane == lax.broadcasted_iota(jnp.int32, (rows, head), 0)

    def as_column(line):
        return jnp.sum(jnp.where(diagonal, line, 0.0), 1, keepdims=True)

    merged = []
    for r in range(requests):
        first_max, first_sum = (as_column(parts[r, rows + i : rows + i + 1]) for i in range(2))
        second_max, second_sum = (as_column(parts[r + requests, rows + i : rows + i + 1]) for i in range(2))
        top = jnp.maximum(first_max, second_max)
        first_weight = jnp.exp(first_max - top)
        second_weight = jnp.exp(second_max - top)
        joined = first_weight * parts[r, :rows] + second_weight * parts[r + requests, :rows]
        merged.append(joined / (first_weight * first_sum + second_weight * second_sum))
    lines = []
    for s in range(STEPS):
        for r in range(requests):
            lines.append(
                jnp.concatenate(
                    [merged[r][s * group + h : s * group + h + 1] for h in range(group)], 1
                )
            )
    attended = jnp.concatenate(lines, 0).astype(jnp.bfloat16)
    result = jnp.dot(attended, w_out[...], preferred_element_type=jnp.float32)
    for s in range(STEPS):
        out[s] = result[s * requests : (s + 1) * requests]


def project(plan, parts, w_out):
    requests = parts.shape[0] // 2
    groups = pl.cdiv(requests, JOINT)
    out, *members = pl.pallas_call(
        project_kernel,
        out_shape=(jax.ShapeDtypeStruct((STEPS, requests, w_out.shape[1]), jnp.float32),)
        + (jax.ShapeDtypeStruct((1,), jnp.int32),) * groups,
        in_specs=[SMEM, VMEM, VMEM],
        out_specs=(VMEM,) + (SMEM,) * groups,
        compiler_params=params(16),
        name="project",
    )(plan, parts, w_out)
    return out, [member.reshape(()) for member in members]


def place_kernel(table_in, plan_in, lengths, *refs, done, only, patch):
    parts, (base, new_pool, table, plan, sems, sem) = refs[:-6], refs[-6:]
    del base
    pair_index = lax.axis_index("pair")
    requests = lengths.shape[0]
    is_target = jnp.logical_and(pair_index >= only[0], pair_index < only[1])
    table_copy = pltpu.make_async_copy(table_in, table, sems.at[0])
    plan_copy = pltpu.make_async_copy(plan_in, plan, sems.at[1])

    @pl.when(is_target)
    def _():
        table_copy.start()
        plan_copy.start()
        table_copy.wait()
        plan_copy.wait()
        count = moved_pages(plan, pair_index) - done
        low = 0
        for pages in parts[1:] if patch else parts:

            def start(j, carry):
                slot = table[0, PAGES_HALF + done + low + j]
                pltpu.make_async_copy(pages.at[j], new_pool.at[slot], sem).start()
                return carry

            lax.fori_loop(0, jnp.clip(count - low, 0, pages.shape[0]), start, 0)
            low += pages.shape[0]

        def wait(j, carry):
            pltpu.make_async_copy(parts[-1].at[0], new_pool.at[0], sem).wait()
            return carry

        lax.fori_loop(0, jnp.clip(count, 0, low), wait, 0)

    if patch:

        @pl.when(pair_index >= requests)
        def _():
            table_copy.start()
            table_copy.wait()
            page_len = new_pool.shape[1]
            first = lengths[pair_index - requests] - PAGES_HALF * page_len
            for i, offset in enumerate((first, first + STEPS - 1)):
                slot = table[0, offset // page_len]
                copy = pltpu.make_async_copy(parts[0].at[i], new_pool.at[slot], sem)
                copy.start()
                copy.wait()


def place(table, plan, lengths, parts, base, done, only, patch=False):
    return pl.pallas_call(
        functools.partial(place_kernel, done=done, only=only, patch=patch),
        out_shape=pltpu.HBM(base.shape, base.dtype),
        in_specs=[HBM, HBM, SMEM] + [VMEM] * len(parts) + [HBM],
        out_specs=HBM,
        scratch_shapes=[
            pltpu.SMEM(table.shape, table.dtype),
            pltpu.SMEM(plan.shape, plan.dtype),
            pltpu.SemaphoreType.DMA((2,)),
            pltpu.SemaphoreType.DMA,
        ],
        input_output_aliases={3 + len(parts): 0},
        compiler_params=params(16),
        name="place",
    )(*in_hbm(table, plan), lengths, *parts, *in_hbm(base))


def local(
    normed, w_query, b_query, w_key, b_key, w_value, b_value, w_out, pool, page_table, lengths, plan
):
    pair_count = lax.axis_size("pair")
    tp_count = lax.axis_size("tp")
    requests = pair_count // 2
    head = w_key.shape[1]

    partial, *pieces = prepare(page_table, normed, w_query, w_key, w_value, pool[0, 0], pair_count)
    route = [(i + requests, i) for i in range(requests)]

    def migrate(pages):
        return lax.ppermute(pages, "pair", route)

    def tie(*values):
        return lax.optimization_barrier(values)

    planned = plan.T
    either = lax.axis_index("rep") == 0

    def exchange(values, pages):
        def send(values, pages):
            gathered = lax.all_to_all(values, "pair", split_axis=0, concat_axis=0, tiled=True)
            return gathered, migrate(pages)

        return lax.cond(either, send, send, values, pages)

    arrived = [migrate(pieces[0])]
    sums, pages = exchange(partial, pieces[1])
    sums, arrived[0] = tie(sums, arrived[0])
    arrived.append(pages)
    arrived.append(migrate(tie(pieces[2], sums)[0]))

    frequency = rope_base ** (-(jnp.arange(head // 2, dtype=jnp.float32) * 2.0 / head))
    steps = jnp.minimum(jnp.arange(8, dtype=jnp.int32), STEPS - 1)
    position = (lengths[:, None] + steps[None, :]).astype(jnp.float32)[..., None]
    angles = position * frequency
    cosine = jnp.cos(angles)
    sine = jnp.sin(angles)
    cosine = jnp.concatenate([cosine, cosine], -1)
    sine = jnp.concatenate([-sine, sine], -1)

    packed, new_pool, fixed, *later = attend(
        lengths,
        page_table,
        sums,
        b_query.reshape(-1, head),
        b_key[None, :],
        b_value[None, :],
        cosine,
        sine,
        pool[0, 0],
    )
    parts, pages = exchange(packed, later[0])
    parts, arrived[2] = tie(parts, arrived[2])
    arrived.append(pages)
    last = migrate(tie(later[1], parts)[0])
    projected, members = project(planned, parts, w_out)
    new_pool = place(page_table, planned, lengths, [fixed] + arrived, new_pool, 0, (0, requests), True)
    if tp_count == 2:
        projected = projected + lax.ppermute(projected, "tp", [(0, 1), (1, 0)])
    else:
        projected = lax.psum(projected, "tp")
    new_pool, projected = tie(new_pool, projected)

    def late(code, low, base, pages):
        if code == 0:
            return base
        chosen = [low + r for r in range(JOINT) if code >> r & 1]
        pages = lax.ppermute(pages, "pair", [(r + requests, r) for r in chosen])
        return place(page_table, planned, lengths, [pages], base, sum(EARLY), (low, low + JOINT))

    for g, member in enumerate(members):
        low = g * JOINT
        branches = [functools.partial(late, code, low) for code in range(1 << min(JOINT, requests - low))]
        new_pool = lax.switch(member, branches, new_pool, later[2])
    new_pool = place(page_table, planned, lengths, [last], new_pool, sum(EARLY[:-1]), (0, requests))
    return projected, new_pool[None, None]


def solution(mesh):
    return jax.shard_map(
        local,
        mesh=mesh,
        in_specs=(
            P(None, "rep", "pair"),
            P("pair", "tp"),
            P("tp"),
            P("pair", "tp"),
            P("tp"),
            P("pair", "tp"),
            P("tp"),
            P("tp", "pair"),
            P(("rep", "pair"), "tp", None, None, None),
            P(("rep", "pair"), None),
            P("rep"),
            P("rep", None),
        ),
        out_specs=(P(None, "rep", "pair"), P(("rep", "pair"), "tp", None, None, None)),
        check_vma=False,
    )
```

```python
import functools
import math

import jax
import jax.numpy as jnp
from jax import lax
from jax.experimental import pallas as pl
from jax.experimental.pallas import tpu as pltpu
from jax.sharding import PartitionSpec as P

PAGES_HALF = 384
STEPS = 2
SECTION = 64
MOVED_MAX = STEPS * SECTION
FIRST, SECOND, THIRD = 18, 32, 22
NEAR, FAR = 24, 32
NEAR_AT = FIRST + SECOND + THIRD
FAR_AT = NEAR_AT + NEAR
PIECES = ((0, FIRST), (FIRST, SECOND), (FAR_AT, FAR))
LATER = ((FIRST + SECOND, THIRD), (NEAR_AT, NEAR))
JOINT = 4
CHUNKS = 8
NEG = -1e30

rope_base = 1000000.0

VMEM = pl.BlockSpec(memory_space=pltpu.VMEM)
SMEM = pl.BlockSpec(memory_space=pltpu.SMEM)
HBM = pl.BlockSpec(memory_space=pltpu.HBM)


def in_hbm(*arrays):
    return tuple(pltpu.with_memory_space_constraint(a, pltpu.HBM) for a in arrays)


def params(mib):
    return pltpu.CompilerParams(vmem_limit_bytes=mib * 1024 * 1024)


def moved_pages(plan, request):
    count = plan[0, request]
    for s in range(1, STEPS):
        count = count + plan[s, request]
    return count


def prepare_kernel(table_in, plan_in, normed_in, w_query, w_key, w_value, pool, partial, near, far, *refs):
    pieces, (table, plan, normed, weights, index_sems, sems, page_sems) = refs[:-7], refs[-7:]
    pairs = partial.shape[0]
    requests = pairs // 2
    table_copy = pltpu.make_async_copy(table_in, table, index_sems.at[0])
    plan_copy = pltpu.make_async_copy(plan_in, plan, index_sems.at[1])
    table_copy.start()
    plan_copy.start()
    loads = [pltpu.make_async_copy(normed_in, normed, sems.at[3])]
    low = 0
    for i, weight in enumerate((w_query, w_key, w_value)):
        part = weights.at[:, low : low + weight.shape[1]]
        loads.append(pltpu.make_async_copy(weight, part, sems.at[i]))
        low += weight.shape[1]
    for copy in loads:
        copy.start()
    table_copy.wait()

    @pl.when(lax.axis_index("pair") >= requests)
    def _():
        for i, (low, size) in enumerate(PIECES):

            def start(j, carry):
                pltpu.make_async_copy(pool.at[table[0, low + j]], pieces[i].at[j], page_sems.at[i]).start()
                return carry

            lax.fori_loop(0, size, start, 0, unroll=2)

    plan_copy.wait()
    bits = min(JOINT, requests)
    for code, bound in ((near, NEAR_AT), (far, FAR_AT)):
        total = jnp.int32(0)
        for bit in range(bits):
            most = moved_pages(plan, bit)
            for r in range(bit + bits, requests, bits):
                most = jnp.maximum(most, moved_pages(plan, r))
            total = total + jnp.where(most > bound, 1 << bit, 0)
        code[0] = total
    for copy in loads:
        copy.wait()
    hidden = jnp.concatenate([normed[s].astype(jnp.float32) for s in range(STEPS)], 0).astype(jnp.bfloat16)
    result = jnp.dot(hidden, weights[...], preferred_element_type=jnp.float32)
    for p in range(pairs):
        for s in range(STEPS):
            row = s * requests + p % requests
            partial[p, s : s + 1] = result[row : row + 1]

    @pl.when(lax.axis_index("pair") >= requests)
    def _():
        for i, (_, size) in enumerate(PIECES):
            pltpu.make_async_copy(pool.at[pl.ds(0, size)], pieces[i], page_sems.at[i]).wait()


def prepare(table, plan, normed, w_query, w_key, w_value, pool, pairs):
    page = pool.shape[1:]
    wide = w_query.shape[1] + 2 * w_key.shape[1]
    partial, near, far, *pieces = pl.pallas_call(
        prepare_kernel,
        out_shape=(pltpu.VMEM((pairs, STEPS, wide), jnp.float32),)
        + (jax.ShapeDtypeStruct((1,), jnp.int32),) * 2
        + tuple(pltpu.VMEM((size,) + page, pool.dtype) for _, size in PIECES),
        in_specs=[HBM] * 7,
        out_specs=(VMEM, SMEM, SMEM) + (VMEM,) * len(PIECES),
        scratch_shapes=[
            pltpu.SMEM(table.shape, table.dtype),
            pltpu.SMEM(plan.shape, plan.dtype),
            pltpu.VMEM(normed.shape, normed.dtype),
            pltpu.VMEM((w_query.shape[0], wide), w_query.dtype),
            pltpu.SemaphoreType.DMA((2,)),
            pltpu.SemaphoreType.DMA((4,)),
            pltpu.SemaphoreType.DMA((len(PIECES),)),
        ],
        compiler_params=params(16),
        name="prepare",
    )(*in_hbm(table, plan, normed, w_query, w_key, w_value, pool))
    return partial, near.reshape(()), far.reshape(()), pieces


def page_order(table, slots):
    slot = lax.broadcasted_iota(jnp.int32, (slots, slots), 0)
    holds = jnp.where(slot == table, 1.0, 0.0).astype(jnp.bfloat16)
    index = lax.broadcasted_iota(jnp.int32, (8, slots), 1)
    digit = lax.broadcasted_iota(jnp.int32, (8, slots), 0)
    digits = jnp.where(digit == 0, index // 16, jnp.where(digit == 1, index % 16, 0))
    digits = digits.astype(jnp.float32).astype(jnp.bfloat16)
    return lax.dot_general(digits, holds, (((1,), (1,)), ((), ())), preferred_element_type=jnp.float32)


def attention_kernel(lengths, table_in, sums, b_query, b_key, b_value, cosine, sine, pool, packed, new_pool, fixed, *refs):
    pieces, (held, score, table, slots_of, sems, out_sems) = refs[: len(LATER)], refs[len(LATER) :]
    slots, page_len, _ = held.shape
    per = slots // CHUNKS
    table_copy = pltpu.make_async_copy(table_in, table, sems.at[CHUNKS])
    table_copy.start()
    slots_copy = pltpu.make_async_copy(table_in, slots_of, sems.at[CHUNKS + 1])
    slots_copy.start()
    copies = []
    for c in range(CHUNKS):
        part = pl.ds(c * per, per)
        copies.append(pltpu.make_async_copy(pool.at[part], held.at[part], sems.at[c]))
        copies[-1].start()
    requests = sums.shape[0] // 2
    group, head = b_query.shape
    rows = STEPS * group
    pair_index = lax.axis_index("pair")
    is_source = pair_index >= requests
    request = jnp.where(is_source, pair_index - requests, pair_index)
    half_tokens = PAGES_HALF * page_len
    limit = jnp.where(is_source, lengths[request] - half_tokens, half_tokens)

    blocks = CHUNKS // 2
    block = slots // blocks
    width = block * page_len
    table_copy.wait()
    digits = page_order(table[...], slots)
    digits = jnp.concatenate(
        [digits[d : d + 1, c * block : (c + 1) * block] for d in range(2) for c in range(blocks)], 0
    ).astype(jnp.bfloat16)
    spread = lax.broadcasted_iota(jnp.int32, (block, width), 1) // page_len
    spread = jnp.where(spread == lax.broadcasted_iota(jnp.int32, (block, width), 0), 1.0, 0.0)
    digits = jnp.dot(digits, spread.astype(jnp.bfloat16), preferred_element_type=jnp.float32)
    tokens = (digits[:blocks] * 16.0 + digits[blocks:]).astype(jnp.int32) * page_len
    tokens = tokens + lax.broadcasted_iota(jnp.int32, (blocks, width), 1) % page_len

    total = sums[0]
    for p in range(1, sums.shape[0]):
        total = total + sums[p]
    query = jnp.concatenate(
        [total[s : s + 1, h * head : (h + 1) * head] for s in range(STEPS) for h in range(group)], 0
    )
    query = query + jnp.concatenate([b_query[...]] * STEPS, 0)
    cos_new = cosine[request]
    sin_new = sine[request]
    row = lax.broadcasted_iota(jnp.int32, (rows, head), 0)
    cos_rows = jnp.where(row < group, cos_new[0:1], cos_new[1:2])
    sin_rows = jnp.where(row < group, sin_new[0:1], sin_new[1:2])
    query = (query * cos_rows + pltpu.roll(query, head // 2, 1) * sin_rows).astype(jnp.bfloat16)
    key_new = total[:, group * head : (group + 1) * head] + b_key[...]
    key_new = jnp.concatenate([key_new, jnp.zeros((8 - STEPS, head), jnp.float32)], 0)
    key_new = key_new * cos_new + pltpu.roll(key_new, head // 2, 1) * sin_new
    key_new = key_new.astype(jnp.bfloat16).astype(jnp.float32)
    value_new = total[:, (group + 1) * head :] + b_value[...]
    value_new = value_new.astype(jnp.bfloat16).astype(jnp.float32)
    scale = 1.0 / math.sqrt(head)

    column = lax.broadcasted_iota(jnp.int32, (rows, 1), 0)
    query_wide = query.astype(jnp.float32)
    fresh = []
    for s in range(STEPS):
        dots = jnp.sum(query_wide * key_new[s : s + 1], 1, keepdims=True) * scale
        seen = jnp.logical_and(is_source, column >= s * group)
        fresh.append((jnp.where(seen, dots, NEG), seen))
    row_max = jnp.maximum(fresh[0][0], fresh[1][0])

    stores = []
    for c in range(blocks):
        for i in range(c * CHUNKS // blocks, (c + 1) * CHUNKS // blocks):
            copies[i].wait()
            part = pl.ds(i * per, per)
            stores.append(pltpu.make_async_copy(held.at[part], new_pool.at[part], out_sems.at[i]))
            stores[-1].start()
        keys = held[c * block : (c + 1) * block, :, :head].reshape(width, head)
        part = lax.dot_general(query, keys, (((1,), (1,)), ((), ())), preferred_element_type=jnp.float32)
        part = jnp.where(tokens[c : c + 1] < limit, part * scale, NEG)
        score[:, c * width : (c + 1) * width] = part
        row_max = jnp.maximum(row_max, jnp.max(part, 1, keepdims=True))
    row_sum = jnp.zeros((rows, 1), jnp.float32)
    out = jnp.zeros((rows, head), jnp.float32)
    for s in range(STEPS):
        weight = jnp.where(fresh[s][1], jnp.exp(fresh[s][0] - row_max), 0.0)
        row_sum = row_sum + weight
        out = out + weight.astype(jnp.bfloat16).astype(jnp.float32) * value_new[s : s + 1]
    for c in range(blocks):
        weight = jnp.exp(score[:, c * width : (c + 1) * width] - row_max)
        weight = jnp.where(tokens[c : c + 1] < limit, weight, 0.0)
        row_sum = row_sum + jnp.sum(weight, 1, keepdims=True)
        values = held[c * block : (c + 1) * block, :, head:].reshape(width, head)
        out = out + jnp.dot(weight.astype(jnp.bfloat16), values, preferred_element_type=jnp.float32)

    diagonal = lax.broadcasted_iota(jnp.int32, (rows, head), 1) == row
    for p in range(packed.shape[0]):
        packed[p, 0:rows] = out
        packed[p, rows : rows + 1] = jnp.sum(jnp.where(diagonal, row_max, 0.0), 0, keepdims=True)
        packed[p, rows + 1 : rows + 2] = jnp.sum(jnp.where(diagonal, row_sum, 0.0), 0, keepdims=True)
        packed[p, rows + 2 :] = jnp.zeros((packed.shape[1] - rows - 2, head), jnp.float32)

    slots_copy.wait()

    @pl.when(is_source)
    def _():
        for piece, (low, size) in zip(pieces, LATER):

            def take(j, carry):
                piece[j] = held[slots_of[0, low + j]]
                return carry

            lax.fori_loop(0, size, take, 0)
        page_row = lax.broadcasted_iota(jnp.int32, (page_len, 2 * head), 0)
        entries = jnp.concatenate([key_new[:STEPS], value_new], 1)
        offsets = [limit + s for s in range(STEPS)]
        homes = [slots_of[0, offset // page_len] for offset in offsets]
        for i, slot in enumerate((homes[0], homes[-1])):
            page = held[slot].astype(jnp.float32)
            for s, offset in enumerate(offsets):
                here = jnp.logical_and(homes[s] == slot, page_row == offset % page_len)
                page = jnp.where(here, entries[s : s + 1], page)
            fixed[i] = page.astype(held.dtype)

    for store in stores:
        store.wait()


def attend(lengths, table, sums, b_query, b_key, b_value, cosine, sine, pool):
    group, head = b_query.shape
    rows = STEPS * group
    page = pool.shape[1:]
    return pl.pallas_call(
        attention_kernel,
        out_shape=(
            pltpu.VMEM((sums.shape[0], rows + 8, head), jnp.float32),
            pltpu.HBM(pool.shape, pool.dtype),
            jax.ShapeDtypeStruct((2,) + page, pool.dtype),
        )
        + tuple(pltpu.VMEM((size,) + page, pool.dtype) for _, size in LATER),
        in_specs=[SMEM, HBM] + [VMEM] * 6 + [HBM],
        out_specs=(VMEM, HBM, VMEM) + (VMEM,) * len(LATER),
        scratch_shapes=[
            pltpu.VMEM(pool.shape, pool.dtype),
            pltpu.VMEM((rows, pool.shape[0] * pool.shape[1]), jnp.float32),
            pltpu.VMEM(table.shape, table.dtype),
            pltpu.SMEM(table.shape, table.dtype),
            pltpu.SemaphoreType.DMA((CHUNKS + 2,)),
            pltpu.SemaphoreType.DMA((CHUNKS,)),
        ],
        compiler_params=params(24),
        name="attend",
    )(lengths, *in_hbm(table), sums, b_query, b_key, b_value, cosine, sine, *in_hbm(pool))


def project_kernel(parts, w_out, out):
    pairs, packed_rows, head = parts.shape
    rows = packed_rows - 8
    group = rows // STEPS
    requests = pairs // 2
    lane = lax.broadcasted_iota(jnp.int32, (rows, head), 1)
    diagonal = lane == lax.broadcasted_iota(jnp.int32, (rows, head), 0)

    def as_column(line):
        return jnp.sum(jnp.where(diagonal, line, 0.0), 1, keepdims=True)

    merged = []
    for r in range(requests):
        first_max, first_sum = (as_column(parts[r, rows + i : rows + i + 1]) for i in range(2))
        second_max, second_sum = (as_column(parts[r + requests, rows + i : rows + i + 1]) for i in range(2))
        top = jnp.maximum(first_max, second_max)
        first_weight = jnp.exp(first_max - top)
        second_weight = jnp.exp(second_max - top)
        joined = first_weight * parts[r, :rows] + second_weight * parts[r + requests, :rows]
        merged.append(joined / (first_weight * first_sum + second_weight * second_sum))
    lines = []
    for s in range(STEPS):
        for r in range(requests):
            lines.append(
                jnp.concatenate(
                    [merged[r][s * group + h : s * group + h + 1] for h in range(group)], 1
                )
            )
    attended = jnp.concatenate(lines, 0).astype(jnp.bfloat16)
    result = jnp.dot(attended, w_out[...], preferred_element_type=jnp.float32)
    for s in range(STEPS):
        out[s] = result[s * requests : (s + 1) * requests]


def project(parts, w_out):
    return pl.pallas_call(
        project_kernel,
        out_shape=jax.ShapeDtypeStruct((STEPS, parts.shape[0] // 2, w_out.shape[1]), jnp.float32),
        in_specs=[VMEM, VMEM],
        out_specs=VMEM,
        compiler_params=params(16),
        name="project",
    )(parts, w_out)


def place_kernel(table_in, plan_in, lengths, *refs, starts, patch):
    parts, (base, new_pool, table, plan, sems, sem) = refs[:-6], refs[-6:]
    del base
    pair_index = lax.axis_index("pair")
    requests = lengths.shape[0]
    table_copy = pltpu.make_async_copy(table_in, table, sems.at[0])
    plan_copy = pltpu.make_async_copy(plan_in, plan, sems.at[1])

    @pl.when(pair_index < requests)
    def _():
        table_copy.start()
        plan_copy.start()
        table_copy.wait()
        plan_copy.wait()
        count = moved_pages(plan, pair_index)
        placed = jnp.int32(0)
        for low, pages in zip(starts, parts):
            here = jnp.clip(count - low, 0, pages.shape[0])

            def start(j, carry):
                slot = table[0, PAGES_HALF + low + j]
                pltpu.make_async_copy(pages.at[j], new_pool.at[slot], sem).start()
                return carry

            lax.fori_loop(0, here, start, 0)
            placed = placed + here

        def wait(j, carry):
            pltpu.make_async_copy(parts[0].at[0], new_pool.at[0], sem).wait()
            return carry

        lax.fori_loop(0, placed, wait, 0)

    if patch:

        @pl.when(pair_index >= requests)
        def _():
            table_copy.start()
            table_copy.wait()
            page_len = new_pool.shape[1]
            first = lengths[pair_index - requests] - PAGES_HALF * page_len
            for i, offset in enumerate((first, first + STEPS - 1)):
                slot = table[0, offset // page_len]
                copy = pltpu.make_async_copy(parts[-1].at[i], new_pool.at[slot], sem)
                copy.start()
                copy.wait()


def place(table, plan, lengths, parts, starts, base, fixed=None):
    patch = fixed is not None
    parts = list(parts) + [fixed] * patch
    return pl.pallas_call(
        functools.partial(place_kernel, starts=starts, patch=patch),
        out_shape=pltpu.HBM(base.shape, base.dtype),
        in_specs=[HBM, HBM, SMEM] + [VMEM] * len(parts) + [HBM],
        out_specs=HBM,
        scratch_shapes=[
            pltpu.SMEM(table.shape, table.dtype),
            pltpu.SMEM(plan.shape, plan.dtype),
            pltpu.SemaphoreType.DMA((2,)),
            pltpu.SemaphoreType.DMA,
        ],
        input_output_aliases={3 + len(parts): 0},
        compiler_params=params(16),
        name="place",
    )(*in_hbm(table, plan), lengths, *parts, *in_hbm(base))


def local(
    normed, w_query, b_query, w_key, b_key, w_value, b_value, w_out, pool, page_table, lengths, plan
):
    pair_count = lax.axis_size("pair")
    tp_count = lax.axis_size("tp")
    requests = pair_count // 2
    head = w_key.shape[1]

    planned = plan.T
    partial, near, far, pieces = prepare(
        page_table, planned, normed, w_query, w_key, w_value, pool[0, 0], pair_count
    )
    bits = min(JOINT, requests)

    def tie(*values):
        return lax.optimization_barrier(values)

    def migrate(pages, members=range(requests)):
        return lax.ppermute(pages, "pair", [(r + requests, r) for r in members])

    def exchange(code, values, pages):
        def send(members, values, pages):
            gathered = lax.all_to_all(values, "pair", split_axis=0, concat_axis=0, tiled=True)
            return gathered, migrate(pages, members) if members else pages

        members = [[r for r in range(requests) if code >> r % bits & 1] for code in range(1 << bits)]
        return lax.switch(code, [functools.partial(send, chosen) for chosen in members], values, pages)

    first = migrate(pieces[0])
    sums, far_pages = exchange(far, partial, pieces[2])
    sums, first = tie(sums, first)
    second = migrate(tie(pieces[1], sums)[0])

    frequency = rope_base ** (-(jnp.arange(head // 2, dtype=jnp.float32) * 2.0 / head))
    steps = jnp.minimum(jnp.arange(8, dtype=jnp.int32), STEPS - 1)
    position = (lengths[:, None] + steps[None, :]).astype(jnp.float32)[..., None]
    angles = position * frequency
    cosine = jnp.cos(angles)
    sine = jnp.sin(angles)
    cosine = jnp.concatenate([cosine, cosine], -1)
    sine = jnp.concatenate([-sine, sine], -1)

    packed, new_pool, fixed, *later = attend(
        lengths,
        page_table,
        sums,
        b_query.reshape(-1, head),
        b_key[None, :],
        b_value[None, :],
        cosine,
        sine,
        pool[0, 0],
    )
    parts, near_pages = exchange(near, packed, later[1])
    parts, second = tie(parts, second)
    third = migrate(tie(later[0], parts)[0])
    projected = project(parts, w_out)
    here = [first, second, near_pages, far_pages]
    starts = [0, FIRST, NEAR_AT, FAR_AT]
    new_pool = place(page_table, planned, lengths, here, starts, new_pool, fixed)
    if tp_count == 2:
        projected = projected + lax.ppermute(projected, "tp", [(0, 1), (1, 0)])
    else:
        projected = lax.psum(projected, "tp")
    new_pool = place(page_table, planned, lengths, [third], [FIRST + SECOND], new_pool)
    return projected, new_pool[None, None]


def solution(mesh):
    return jax.shard_map(
        local,
        mesh=mesh,
        in_specs=(
            P(None, "rep", "pair"),
            P("pair", "tp"),
            P("tp"),
            P("pair", "tp"),
            P("tp"),
            P("pair", "tp"),
            P("tp"),
            P("tp", "pair"),
            P(("rep", "pair"), "tp", None, None, None),
            P(("rep", "pair"), None),
            P("rep"),
            P("rep", None),
        ),
        out_specs=(P(None, "rep", "pair"), P(("rep", "pair"), "tp", None, None, None)),
        check_vma=False,
    )
```

```python
import functools
import math

import jax
import jax.numpy as jnp
from jax import lax
from jax.experimental import pallas as pl
from jax.experimental.pallas import tpu as pltpu
from jax.sharding import PartitionSpec as P

PAGES_HALF = 384
STEPS = 2
SECTION = 64
MOVED_MAX = STEPS * SECTION
FIRST, SECOND, THIRD = 18, 32, 22
NEAR, FAR = 24, 32
NEAR_AT = FIRST + SECOND + THIRD
FAR_AT = NEAR_AT + NEAR
PIECES = ((0, FIRST), (FIRST, SECOND), (FAR_AT, FAR))
LATER = ((FIRST + SECOND, THIRD), (NEAR_AT, NEAR))
JOINT = 4
CHUNKS = 8
NEG = -1e30

rope_base = 1000000.0

VMEM = pl.BlockSpec(memory_space=pltpu.VMEM)
SMEM = pl.BlockSpec(memory_space=pltpu.SMEM)
HBM = pl.BlockSpec(memory_space=pltpu.HBM)


def in_hbm(*arrays):
    return tuple(pltpu.with_memory_space_constraint(a, pltpu.HBM) for a in arrays)


def params(mib):
    return pltpu.CompilerParams(vmem_limit_bytes=mib * 1024 * 1024)


def moved_pages(plan, request):
    count = plan[0, request]
    for s in range(1, STEPS):
        count = count + plan[s, request]
    return count


def prepare_kernel(table_in, plan_in, normed_in, w_query, w_key, w_value, pool, partial, near, far, *refs):
    pieces, (table, plan, normed, weights, index_sems, sems, page_sems) = refs[:-7], refs[-7:]
    pairs = partial.shape[0]
    requests = pairs // 2
    table_copy = pltpu.make_async_copy(table_in, table, index_sems.at[0])
    plan_copy = pltpu.make_async_copy(plan_in, plan, index_sems.at[1])
    table_copy.start()
    plan_copy.start()
    loads = [pltpu.make_async_copy(normed_in, normed, sems.at[3])]
    low = 0
    for i, weight in enumerate((w_query, w_key, w_value)):
        part = weights.at[:, low : low + weight.shape[1]]
        loads.append(pltpu.make_async_copy(weight, part, sems.at[i]))
        low += weight.shape[1]
    for copy in loads:
        copy.start()
    table_copy.wait()

    @pl.when(lax.axis_index("pair") >= requests)
    def _():
        for i, (low, size) in enumerate(PIECES):

            def start(j, carry):
                pltpu.make_async_copy(pool.at[table[0, low + j]], pieces[i].at[j], page_sems.at[i]).start()
                return carry

            lax.fori_loop(0, size, start, 0, unroll=2)

    plan_copy.wait()
    bits = min(JOINT, requests)
    for code, bound in ((near, NEAR_AT), (far, FAR_AT)):
        total = jnp.int32(0)
        for bit in range(bits):
            most = moved_pages(plan, bit)
            for r in range(bit + bits, requests, bits):
                most = jnp.maximum(most, moved_pages(plan, r))
            total = total + jnp.where(most > bound, 1 << bit, 0)
        code[0] = total
    for copy in loads:
        copy.wait()
    hidden = jnp.concatenate([normed[s].astype(jnp.float32) for s in range(STEPS)], 0).astype(jnp.bfloat16)
    result = jnp.dot(hidden, weights[...], preferred_element_type=jnp.float32)
    for p in range(pairs):
        for s in range(STEPS):
            row = s * requests + p % requests
            partial[p, s : s + 1] = result[row : row + 1]

    @pl.when(lax.axis_index("pair") >= requests)
    def _():
        for i, (_, size) in enumerate(PIECES):
            pltpu.make_async_copy(pool.at[pl.ds(0, size)], pieces[i], page_sems.at[i]).wait()


def prepare(table, plan, normed, w_query, w_key, w_value, pool, pairs):
    page = pool.shape[1:]
    wide = w_query.shape[1] + 2 * w_key.shape[1]
    partial, near, far, *pieces = pl.pallas_call(
        prepare_kernel,
        out_shape=(pltpu.VMEM((pairs, STEPS, wide), jnp.float32),)
        + (jax.ShapeDtypeStruct((1,), jnp.int32),) * 2
        + tuple(pltpu.VMEM((size,) + page, pool.dtype) for _, size in PIECES),
        in_specs=[HBM] * 7,
        out_specs=(VMEM, SMEM, SMEM) + (VMEM,) * len(PIECES),
        scratch_shapes=[
            pltpu.SMEM(table.shape, table.dtype),
            pltpu.SMEM(plan.shape, plan.dtype),
            pltpu.VMEM(normed.shape, normed.dtype),
            pltpu.VMEM((w_query.shape[0], wide), w_query.dtype),
            pltpu.SemaphoreType.DMA((2,)),
            pltpu.SemaphoreType.DMA((4,)),
            pltpu.SemaphoreType.DMA((len(PIECES),)),
        ],
        compiler_params=params(16),
        name="prepare",
    )(*in_hbm(table, plan, normed, w_query, w_key, w_value, pool))
    return partial, near.reshape(()), far.reshape(()), pieces


def page_order(table, slots):
    slot = lax.broadcasted_iota(jnp.int32, (slots, slots), 0)
    holds = jnp.where(slot == table, 1.0, 0.0).astype(jnp.bfloat16)
    index = lax.broadcasted_iota(jnp.int32, (8, slots), 1)
    digit = lax.broadcasted_iota(jnp.int32, (8, slots), 0)
    digits = jnp.where(digit == 0, index // 16, jnp.where(digit == 1, index % 16, 0))
    digits = digits.astype(jnp.float32).astype(jnp.bfloat16)
    return lax.dot_general(digits, holds, (((1,), (1,)), ((), ())), preferred_element_type=jnp.float32)


def attention_kernel(lengths, table_in, sums, b_query, b_key, b_value, cosine, sine, pool, packed, new_pool, fixed, *refs):
    pieces, (held, score, table, slots_of, sems, out_sems) = refs[: len(LATER)], refs[len(LATER) :]
    slots, page_len, _ = held.shape
    per = slots // CHUNKS
    table_copy = pltpu.make_async_copy(table_in, table, sems.at[CHUNKS])
    table_copy.start()
    slots_copy = pltpu.make_async_copy(table_in, slots_of, sems.at[CHUNKS + 1])
    slots_copy.start()
    copies = []
    for c in range(CHUNKS):
        part = pl.ds(c * per, per)
        copies.append(pltpu.make_async_copy(pool.at[part], held.at[part], sems.at[c]))
        copies[-1].start()
    requests = sums.shape[0] // 2
    group, head = b_query.shape
    rows = STEPS * group
    pair_index = lax.axis_index("pair")
    is_source = pair_index >= requests
    request = jnp.where(is_source, pair_index - requests, pair_index)
    half_tokens = PAGES_HALF * page_len
    limit = jnp.where(is_source, lengths[request] - half_tokens, half_tokens)

    blocks = CHUNKS // 2
    block = slots // blocks
    width = block * page_len
    table_copy.wait()
    digits = page_order(table[...], slots)
    digits = jnp.concatenate(
        [digits[d : d + 1, c * block : (c + 1) * block] for d in range(2) for c in range(blocks)], 0
    ).astype(jnp.bfloat16)
    spread = lax.broadcasted_iota(jnp.int32, (block, width), 1) // page_len
    spread = jnp.where(spread == lax.broadcasted_iota(jnp.int32, (block, width), 0), 1.0, 0.0)
    digits = jnp.dot(digits, spread.astype(jnp.bfloat16), preferred_element_type=jnp.float32)
    tokens = (digits[:blocks] * 16.0 + digits[blocks:]).astype(jnp.int32) * page_len
    tokens = tokens + lax.broadcasted_iota(jnp.int32, (blocks, width), 1) % page_len

    total = sums[0]
    for p in range(1, sums.shape[0]):
        total = total + sums[p]
    query = jnp.concatenate(
        [total[s : s + 1, h * head : (h + 1) * head] for s in range(STEPS) for h in range(group)], 0
    )
    query = query + jnp.concatenate([b_query[...]] * STEPS, 0)
    cos_new = cosine[request]
    sin_new = sine[request]
    row = lax.broadcasted_iota(jnp.int32, (rows, head), 0)
    cos_rows = jnp.where(row < group, cos_new[0:1], cos_new[1:2])
    sin_rows = jnp.where(row < group, sin_new[0:1], sin_new[1:2])
    query = (query * cos_rows + pltpu.roll(query, head // 2, 1) * sin_rows).astype(jnp.bfloat16)
    key_new = total[:, group * head : (group + 1) * head] + b_key[...]
    key_new = jnp.concatenate([key_new, jnp.zeros((8 - STEPS, head), jnp.float32)], 0)
    key_new = key_new * cos_new + pltpu.roll(key_new, head // 2, 1) * sin_new
    key_new = key_new.astype(jnp.bfloat16).astype(jnp.float32)
    value_new = total[:, (group + 1) * head :] + b_value[...]
    value_new = value_new.astype(jnp.bfloat16).astype(jnp.float32)
    scale = 1.0 / math.sqrt(head)

    column = lax.broadcasted_iota(jnp.int32, (rows, 1), 0)
    query_wide = query.astype(jnp.float32)
    fresh = []
    for s in range(STEPS):
        dots = jnp.sum(query_wide * key_new[s : s + 1], 1, keepdims=True) * scale
        seen = jnp.logical_and(is_source, column >= s * group)
        fresh.append((jnp.where(seen, dots, NEG), seen))
    row_max = jnp.maximum(fresh[0][0], fresh[1][0])

    stores = []
    for c in range(blocks):
        for i in range(c * CHUNKS // blocks, (c + 1) * CHUNKS // blocks):
            copies[i].wait()
            part = pl.ds(i * per, per)
            stores.append(pltpu.make_async_copy(held.at[part], new_pool.at[part], out_sems.at[i]))
            stores[-1].start()
        keys = held[c * block : (c + 1) * block, :, :head].reshape(width, head)
        part = lax.dot_general(query, keys, (((1,), (1,)), ((), ())), preferred_element_type=jnp.float32)
        part = jnp.where(tokens[c : c + 1] < limit, part * scale, NEG)
        score[:, c * width : (c + 1) * width] = part
        row_max = jnp.maximum(row_max, jnp.max(part, 1, keepdims=True))
    row_sum = jnp.zeros((rows, 1), jnp.float32)
    out = jnp.zeros((rows, head), jnp.float32)
    for s in range(STEPS):
        weight = jnp.where(fresh[s][1], jnp.exp(fresh[s][0] - row_max), 0.0)
        row_sum = row_sum + weight
        out = out + weight.astype(jnp.bfloat16).astype(jnp.float32) * value_new[s : s + 1]
    for c in range(blocks):
        weight = jnp.exp(score[:, c * width : (c + 1) * width] - row_max)
        weight = jnp.where(tokens[c : c + 1] < limit, weight, 0.0)
        row_sum = row_sum + jnp.sum(weight, 1, keepdims=True)
        values = held[c * block : (c + 1) * block, :, head:].reshape(width, head)
        out = out + jnp.dot(weight.astype(jnp.bfloat16), values, preferred_element_type=jnp.float32)

    diagonal = lax.broadcasted_iota(jnp.int32, (rows, head), 1) == row
    for p in range(packed.shape[0]):
        packed[p, 0:rows] = out
        packed[p, rows : rows + 1] = jnp.sum(jnp.where(diagonal, row_max, 0.0), 0, keepdims=True)
        packed[p, rows + 1 : rows + 2] = jnp.sum(jnp.where(diagonal, row_sum, 0.0), 0, keepdims=True)
        packed[p, rows + 2 :] = jnp.zeros((packed.shape[1] - rows - 2, head), jnp.float32)

    slots_copy.wait()

    @pl.when(is_source)
    def _():
        for piece, (low, size) in zip(pieces, LATER):

            def take(j, carry):
                piece[j] = held[slots_of[0, low + j]]
                return carry

            lax.fori_loop(0, size, take, 0)
        page_row = lax.broadcasted_iota(jnp.int32, (page_len, 2 * head), 0)
        entries = jnp.concatenate([key_new[:STEPS], value_new], 1)
        offsets = [limit + s for s in range(STEPS)]
        homes = [slots_of[0, offset // page_len] for offset in offsets]
        for i, slot in enumerate((homes[0], homes[-1])):
            page = held[slot].astype(jnp.float32)
            for s, offset in enumerate(offsets):
                here = jnp.logical_and(homes[s] == slot, page_row == offset % page_len)
                page = jnp.where(here, entries[s : s + 1], page)
            fixed[i] = page.astype(held.dtype)

    for store in stores:
        store.wait()


def attend(lengths, table, sums, b_query, b_key, b_value, cosine, sine, pool):
    group, head = b_query.shape
    rows = STEPS * group
    page = pool.shape[1:]
    return pl.pallas_call(
        attention_kernel,
        out_shape=(
            pltpu.VMEM((sums.shape[0], rows + 8, head), jnp.float32),
            pltpu.HBM(pool.shape, pool.dtype),
            jax.ShapeDtypeStruct((2,) + page, pool.dtype),
        )
        + tuple(pltpu.VMEM((size,) + page, pool.dtype) for _, size in LATER),
        in_specs=[SMEM, HBM] + [VMEM] * 6 + [HBM],
        out_specs=(VMEM, HBM, VMEM) + (VMEM,) * len(LATER),
        scratch_shapes=[
            pltpu.VMEM(pool.shape, pool.dtype),
            pltpu.VMEM((rows, pool.shape[0] * pool.shape[1]), jnp.float32),
            pltpu.VMEM(table.shape, table.dtype),
            pltpu.SMEM(table.shape, table.dtype),
            pltpu.SemaphoreType.DMA((CHUNKS + 2,)),
            pltpu.SemaphoreType.DMA((CHUNKS,)),
        ],
        compiler_params=params(24),
        name="attend",
    )(lengths, *in_hbm(table), sums, b_query, b_key, b_value, cosine, sine, *in_hbm(pool))


def project_kernel(parts, w_out, out):
    pairs, packed_rows, head = parts.shape
    rows = packed_rows - 8
    group = rows // STEPS
    requests = pairs // 2
    lane = lax.broadcasted_iota(jnp.int32, (rows, head), 1)
    diagonal = lane == lax.broadcasted_iota(jnp.int32, (rows, head), 0)

    def as_column(line):
        return jnp.sum(jnp.where(diagonal, line, 0.0), 1, keepdims=True)

    merged = []
    for r in range(requests):
        first_max, first_sum = (as_column(parts[r, rows + i : rows + i + 1]) for i in range(2))
        second_max, second_sum = (as_column(parts[r + requests, rows + i : rows + i + 1]) for i in range(2))
        top = jnp.maximum(first_max, second_max)
        first_weight = jnp.exp(first_max - top)
        second_weight = jnp.exp(second_max - top)
        joined = first_weight * parts[r, :rows] + second_weight * parts[r + requests, :rows]
        merged.append(joined / (first_weight * first_sum + second_weight * second_sum))
    lines = []
    for s in range(STEPS):
        for r in range(requests):
            lines.append(
                jnp.concatenate(
                    [merged[r][s * group + h : s * group + h + 1] for h in range(group)], 1
                )
            )
    attended = jnp.concatenate(lines, 0).astype(jnp.bfloat16)
    result = jnp.dot(attended, w_out[...], preferred_element_type=jnp.float32)
    for s in range(STEPS):
        out[s] = result[s * requests : (s + 1) * requests]


def project(parts, w_out):
    return pl.pallas_call(
        project_kernel,
        out_shape=jax.ShapeDtypeStruct((STEPS, parts.shape[0] // 2, w_out.shape[1]), jnp.float32),
        in_specs=[VMEM, VMEM],
        out_specs=VMEM,
        compiler_params=params(16),
        name="project",
    )(parts, w_out)


def place_kernel(table_in, plan_in, lengths, *refs, starts, patch):
    parts, (base, new_pool, table, plan, sems, sem) = refs[:-6], refs[-6:]
    del base
    pair_index = lax.axis_index("pair")
    requests = lengths.shape[0]
    table_copy = pltpu.make_async_copy(table_in, table, sems.at[0])
    plan_copy = pltpu.make_async_copy(plan_in, plan, sems.at[1])

    @pl.when(pair_index < requests)
    def _():
        table_copy.start()
        plan_copy.start()
        table_copy.wait()
        plan_copy.wait()
        count = moved_pages(plan, pair_index)
        placed = jnp.int32(0)
        for low, pages in zip(starts, parts):
            here = jnp.clip(count - low, 0, pages.shape[0])

            def start(j, carry):
                slot = table[0, PAGES_HALF + low + j]
                pltpu.make_async_copy(pages.at[j], new_pool.at[slot], sem).start()
                return carry

            lax.fori_loop(0, here, start, 0)
            placed = placed + here

        def wait(j, carry):
            pltpu.make_async_copy(parts[0].at[0], new_pool.at[0], sem).wait()
            return carry

        lax.fori_loop(0, placed, wait, 0)

    if patch:

        @pl.when(pair_index >= requests)
        def _():
            table_copy.start()
            table_copy.wait()
            page_len = new_pool.shape[1]
            first = lengths[pair_index - requests] - PAGES_HALF * page_len
            for i, offset in enumerate((first, first + STEPS - 1)):
                slot = table[0, offset // page_len]
                copy = pltpu.make_async_copy(parts[-1].at[i], new_pool.at[slot], sem)
                copy.start()
                copy.wait()


def place(table, plan, lengths, parts, starts, base, fixed=None):
    patch = fixed is not None
    parts = list(parts) + [fixed] * patch
    return pl.pallas_call(
        functools.partial(place_kernel, starts=starts, patch=patch),
        out_shape=pltpu.HBM(base.shape, base.dtype),
        in_specs=[HBM, HBM, SMEM] + [VMEM] * len(parts) + [HBM],
        out_specs=HBM,
        scratch_shapes=[
            pltpu.SMEM(table.shape, table.dtype),
            pltpu.SMEM(plan.shape, plan.dtype),
            pltpu.SemaphoreType.DMA((2,)),
            pltpu.SemaphoreType.DMA,
        ],
        input_output_aliases={3 + len(parts): 0},
        compiler_params=params(16),
        name="place",
    )(*in_hbm(table, plan), lengths, *parts, *in_hbm(base))


def local(
    normed, w_query, b_query, w_key, b_key, w_value, b_value, w_out, pool, page_table, lengths, plan
):
    pair_count = lax.axis_size("pair")
    tp_count = lax.axis_size("tp")
    requests = pair_count // 2
    head = w_key.shape[1]

    planned = plan.T
    partial, near, far, pieces = prepare(
        page_table, planned, normed, w_query, w_key, w_value, pool[0, 0], pair_count
    )
    bits = min(JOINT, requests)

    def tie(*values):
        return lax.optimization_barrier(values)

    def migrate(pages, members=range(requests)):
        return lax.ppermute(pages, "pair", [(r + requests, r) for r in members])

    either = lax.axis_index("rep") == 0

    def gather(values):
        return lax.all_to_all(values, "pair", split_axis=0, concat_axis=0, tiled=True)

    def exchange(code, values, pages):
        def send(members, values, pages):
            pages = migrate(pages, members) if members else jnp.zeros_like(pages)
            return lax.cond(either, gather, gather, values), pages

        members = [[r for r in range(requests) if code >> r % bits & 1] for code in range(1 << bits)]
        return lax.switch(code, [functools.partial(send, chosen) for chosen in members], values, pages)

    first = migrate(pieces[0])
    sums, far_pages = exchange(far, partial, pieces[2])
    sums, first = tie(sums, first)
    second = migrate(tie(pieces[1], sums)[0])

    frequency = rope_base ** (-(jnp.arange(head // 2, dtype=jnp.float32) * 2.0 / head))
    steps = jnp.minimum(jnp.arange(8, dtype=jnp.int32), STEPS - 1)
    position = (lengths[:, None] + steps[None, :]).astype(jnp.float32)[..., None]
    angles = position * frequency
    cosine = jnp.cos(angles)
    sine = jnp.sin(angles)
    cosine = jnp.concatenate([cosine, cosine], -1)
    sine = jnp.concatenate([-sine, sine], -1)

    packed, new_pool, fixed, *later = attend(
        lengths,
        page_table,
        sums,
        b_query.reshape(-1, head),
        b_key[None, :],
        b_value[None, :],
        cosine,
        sine,
        pool[0, 0],
    )
    parts, near_pages = exchange(near, packed, later[1])
    parts, second = tie(parts, second)
    third = migrate(tie(later[0], parts)[0])
    projected = project(parts, w_out)
    here = [first, second, near_pages, far_pages]
    starts = [0, FIRST, NEAR_AT, FAR_AT]
    new_pool = place(page_table, planned, lengths, here, starts, new_pool, fixed)
    if tp_count == 2:
        projected = projected + lax.ppermute(projected, "tp", [(0, 1), (1, 0)])
    else:
        projected = lax.psum(projected, "tp")
    new_pool = place(page_table, planned, lengths, [third], [FIRST + SECOND], new_pool)
    return projected, new_pool[None, None]


def solution(mesh):
    return jax.shard_map(
        local,
        mesh=mesh,
        in_specs=(
            P(None, "rep", "pair"),
            P("pair", "tp"),
            P("tp"),
            P("pair", "tp"),
            P("tp"),
            P("pair", "tp"),
            P("tp"),
            P("tp", "pair"),
            P(("rep", "pair"), "tp", None, None, None),
            P(("rep", "pair"), None),
            P("rep"),
            P("rep", None),
        ),
        out_specs=(P(None, "rep", "pair"), P(("rep", "pair"), "tp", None, None, None)),
        check_vma=False,
    )
```

```python
import functools
import math

import jax
import jax.numpy as jnp
from jax import lax
from jax.experimental import pallas as pl
from jax.experimental.pallas import tpu as pltpu
from jax.sharding import PartitionSpec as P

PAGES_HALF = 384
STEPS = 2
SECTION = 64
MOVED_MAX = STEPS * SECTION
FIRST, SECOND, BESIDE, THIRD = 18, 32, 12, 10
NEAR, FAR = 24, 32
BESIDE_AT = FIRST + SECOND
THIRD_AT = BESIDE_AT + BESIDE
NEAR_AT = THIRD_AT + THIRD
FAR_AT = NEAR_AT + NEAR
PIECES = ((0, FIRST), (FIRST, SECOND), (FAR_AT, FAR))
LATER = ((BESIDE_AT, BESIDE), (THIRD_AT, THIRD), (NEAR_AT, NEAR))
JOINT = 4
CHUNKS = 8
NEG = -1e30

rope_base = 1000000.0

VMEM = pl.BlockSpec(memory_space=pltpu.VMEM)
SMEM = pl.BlockSpec(memory_space=pltpu.SMEM)
HBM = pl.BlockSpec(memory_space=pltpu.HBM)


def in_hbm(*arrays):
    return tuple(pltpu.with_memory_space_constraint(a, pltpu.HBM) for a in arrays)


def params(mib):
    return pltpu.CompilerParams(vmem_limit_bytes=mib * 1024 * 1024)


def moved_pages(plan, request):
    count = plan[0, request]
    for s in range(1, STEPS):
        count = count + plan[s, request]
    return count


def prepare_kernel(table_in, plan_in, normed_in, w_query, w_key, w_value, pool, partial, near, far, *refs):
    pieces, (table, plan, normed, weights, index_sems, sems, page_sems) = refs[:-7], refs[-7:]
    pairs = partial.shape[0]
    requests = pairs // 2
    table_copy = pltpu.make_async_copy(table_in, table, index_sems.at[0])
    plan_copy = pltpu.make_async_copy(plan_in, plan, index_sems.at[1])
    table_copy.start()
    plan_copy.start()
    loads = [pltpu.make_async_copy(normed_in, normed, sems.at[3])]
    low = 0
    for i, weight in enumerate((w_query, w_key, w_value)):
        part = weights.at[:, low : low + weight.shape[1]]
        loads.append(pltpu.make_async_copy(weight, part, sems.at[i]))
        low += weight.shape[1]
    for copy in loads:
        copy.start()
    table_copy.wait()

    @pl.when(lax.axis_index("pair") >= requests)
    def _():
        for i, (low, size) in enumerate(PIECES):

            def start(j, carry):
                pltpu.make_async_copy(pool.at[table[0, low + j]], pieces[i].at[j], page_sems.at[i]).start()
                return carry

            lax.fori_loop(0, size, start, 0, unroll=2)

    plan_copy.wait()
    bits = min(JOINT, requests)
    for code, bound in ((near, NEAR_AT), (far, FAR_AT)):
        total = jnp.int32(0)
        for bit in range(bits):
            most = moved_pages(plan, bit)
            for r in range(bit + bits, requests, bits):
                most = jnp.maximum(most, moved_pages(plan, r))
            total = total + jnp.where(most > bound, 1 << bit, 0)
        code[0] = total
    for copy in loads:
        copy.wait()
    hidden = jnp.concatenate([normed[s].astype(jnp.float32) for s in range(STEPS)], 0).astype(jnp.bfloat16)
    result = jnp.dot(hidden, weights[...], preferred_element_type=jnp.float32)
    for p in range(pairs):
        for s in range(STEPS):
            row = s * requests + p % requests
            partial[p, s : s + 1] = result[row : row + 1]

    @pl.when(lax.axis_index("pair") >= requests)
    def _():
        for i, (_, size) in enumerate(PIECES):
            pltpu.make_async_copy(pool.at[pl.ds(0, size)], pieces[i], page_sems.at[i]).wait()


def prepare(table, plan, normed, w_query, w_key, w_value, pool, pairs):
    page = pool.shape[1:]
    wide = w_query.shape[1] + 2 * w_key.shape[1]
    partial, near, far, *pieces = pl.pallas_call(
        prepare_kernel,
        out_shape=(pltpu.VMEM((pairs, STEPS, wide), jnp.float32),)
        + (jax.ShapeDtypeStruct((1,), jnp.int32),) * 2
        + tuple(pltpu.VMEM((size,) + page, pool.dtype) for _, size in PIECES),
        in_specs=[HBM] * 7,
        out_specs=(VMEM, SMEM, SMEM) + (VMEM,) * len(PIECES),
        scratch_shapes=[
            pltpu.SMEM(table.shape, table.dtype),
            pltpu.SMEM(plan.shape, plan.dtype),
            pltpu.VMEM(normed.shape, normed.dtype),
            pltpu.VMEM((w_query.shape[0], wide), w_query.dtype),
            pltpu.SemaphoreType.DMA((2,)),
            pltpu.SemaphoreType.DMA((4,)),
            pltpu.SemaphoreType.DMA((len(PIECES),)),
        ],
        compiler_params=params(16),
        name="prepare",
    )(*in_hbm(table, plan, normed, w_query, w_key, w_value, pool))
    return partial, near.reshape(()), far.reshape(()), pieces


def page_order(table, slots):
    slot = lax.broadcasted_iota(jnp.int32, (slots, slots), 0)
    holds = jnp.where(slot == table, 1.0, 0.0).astype(jnp.bfloat16)
    index = lax.broadcasted_iota(jnp.int32, (8, slots), 1)
    digit = lax.broadcasted_iota(jnp.int32, (8, slots), 0)
    digits = jnp.where(digit == 0, index // 16, jnp.where(digit == 1, index % 16, 0))
    digits = digits.astype(jnp.float32).astype(jnp.bfloat16)
    return lax.dot_general(digits, holds, (((1,), (1,)), ((), ())), preferred_element_type=jnp.float32)


def attention_kernel(lengths, table_in, sums, b_query, b_key, b_value, cosine, sine, pool, packed, new_pool, fixed, *refs):
    pieces, (held, score, table, slots_of, sems, out_sems) = refs[: len(LATER)], refs[len(LATER) :]
    slots, page_len, _ = held.shape
    per = slots // CHUNKS
    table_copy = pltpu.make_async_copy(table_in, table, sems.at[CHUNKS])
    table_copy.start()
    slots_copy = pltpu.make_async_copy(table_in, slots_of, sems.at[CHUNKS + 1])
    slots_copy.start()
    copies = []
    for c in range(CHUNKS):
        part = pl.ds(c * per, per)
        copies.append(pltpu.make_async_copy(pool.at[part], held.at[part], sems.at[c]))
        copies[-1].start()
    requests = sums.shape[0] // 2
    group, head = b_query.shape
    rows = STEPS * group
    pair_index = lax.axis_index("pair")
    is_source = pair_index >= requests
    request = jnp.where(is_source, pair_index - requests, pair_index)
    half_tokens = PAGES_HALF * page_len
    limit = jnp.where(is_source, lengths[request] - half_tokens, half_tokens)

    blocks = CHUNKS // 2
    block = slots // blocks
    width = block * page_len
    table_copy.wait()
    digits = page_order(table[...], slots)
    digits = jnp.concatenate(
        [digits[d : d + 1, c * block : (c + 1) * block] for d in range(2) for c in range(blocks)], 0
    ).astype(jnp.bfloat16)
    spread = lax.broadcasted_iota(jnp.int32, (block, width), 1) // page_len
    spread = jnp.where(spread == lax.broadcasted_iota(jnp.int32, (block, width), 0), 1.0, 0.0)
    digits = jnp.dot(digits, spread.astype(jnp.bfloat16), preferred_element_type=jnp.float32)
    tokens = (digits[:blocks] * 16.0 + digits[blocks:]).astype(jnp.int32) * page_len
    tokens = tokens + lax.broadcasted_iota(jnp.int32, (blocks, width), 1) % page_len

    total = sums[0]
    for p in range(1, sums.shape[0]):
        total = total + sums[p]
    query = jnp.concatenate(
        [total[s : s + 1, h * head : (h + 1) * head] for s in range(STEPS) for h in range(group)], 0
    )
    query = query + jnp.concatenate([b_query[...]] * STEPS, 0)
    cos_new = cosine[request]
    sin_new = sine[request]
    row = lax.broadcasted_iota(jnp.int32, (rows, head), 0)
    cos_rows = jnp.where(row < group, cos_new[0:1], cos_new[1:2])
    sin_rows = jnp.where(row < group, sin_new[0:1], sin_new[1:2])
    query = (query * cos_rows + pltpu.roll(query, head // 2, 1) * sin_rows).astype(jnp.bfloat16)
    key_new = total[:, group * head : (group + 1) * head] + b_key[...]
    key_new = jnp.concatenate([key_new, jnp.zeros((8 - STEPS, head), jnp.float32)], 0)
    key_new = key_new * cos_new + pltpu.roll(key_new, head // 2, 1) * sin_new
    key_new = key_new.astype(jnp.bfloat16).astype(jnp.float32)
    value_new = total[:, (group + 1) * head :] + b_value[...]
    value_new = value_new.astype(jnp.bfloat16).astype(jnp.float32)
    scale = 1.0 / math.sqrt(head)

    column = lax.broadcasted_iota(jnp.int32, (rows, 1), 0)
    query_wide = query.astype(jnp.float32)
    fresh = []
    for s in range(STEPS):
        dots = jnp.sum(query_wide * key_new[s : s + 1], 1, keepdims=True) * scale
        seen = jnp.logical_and(is_source, column >= s * group)
        fresh.append((jnp.where(seen, dots, NEG), seen))
    row_max = jnp.maximum(fresh[0][0], fresh[1][0])

    stores = []
    for c in range(blocks):
        for i in range(c * CHUNKS // blocks, (c + 1) * CHUNKS // blocks):
            copies[i].wait()
            part = pl.ds(i * per, per)
            stores.append(pltpu.make_async_copy(held.at[part], new_pool.at[part], out_sems.at[i]))
            stores[-1].start()
        keys = held[c * block : (c + 1) * block, :, :head].reshape(width, head)
        part = lax.dot_general(query, keys, (((1,), (1,)), ((), ())), preferred_element_type=jnp.float32)
        part = jnp.where(tokens[c : c + 1] < limit, part * scale, NEG)
        score[:, c * width : (c + 1) * width] = part
        row_max = jnp.maximum(row_max, jnp.max(part, 1, keepdims=True))
    row_sum = jnp.zeros((rows, 1), jnp.float32)
    out = jnp.zeros((rows, head), jnp.float32)
    for s in range(STEPS):
        weight = jnp.where(fresh[s][1], jnp.exp(fresh[s][0] - row_max), 0.0)
        row_sum = row_sum + weight
        out = out + weight.astype(jnp.bfloat16).astype(jnp.float32) * value_new[s : s + 1]
    for c in range(blocks):
        weight = jnp.exp(score[:, c * width : (c + 1) * width] - row_max)
        weight = jnp.where(tokens[c : c + 1] < limit, weight, 0.0)
        row_sum = row_sum + jnp.sum(weight, 1, keepdims=True)
        values = held[c * block : (c + 1) * block, :, head:].reshape(width, head)
        out = out + jnp.dot(weight.astype(jnp.bfloat16), values, preferred_element_type=jnp.float32)

    diagonal = lax.broadcasted_iota(jnp.int32, (rows, head), 1) == row
    for p in range(packed.shape[0]):
        packed[p, 0:rows] = out
        packed[p, rows : rows + 1] = jnp.sum(jnp.where(diagonal, row_max, 0.0), 0, keepdims=True)
        packed[p, rows + 1 : rows + 2] = jnp.sum(jnp.where(diagonal, row_sum, 0.0), 0, keepdims=True)
        packed[p, rows + 2 :] = jnp.zeros((packed.shape[1] - rows - 2, head), jnp.float32)

    slots_copy.wait()

    @pl.when(is_source)
    def _():
        for piece, (low, size) in zip(pieces, LATER):

            def take(j, carry):
                piece[j] = held[slots_of[0, low + j]]
                return carry

            lax.fori_loop(0, size, take, 0)
        page_row = lax.broadcasted_iota(jnp.int32, (page_len, 2 * head), 0)
        entries = jnp.concatenate([key_new[:STEPS], value_new], 1)
        offsets = [limit + s for s in range(STEPS)]
        homes = [slots_of[0, offset // page_len] for offset in offsets]
        for i, slot in enumerate((homes[0], homes[-1])):
            page = held[slot].astype(jnp.float32)
            for s, offset in enumerate(offsets):
                here = jnp.logical_and(homes[s] == slot, page_row == offset % page_len)
                page = jnp.where(here, entries[s : s + 1], page)
            fixed[i] = page.astype(held.dtype)

    for store in stores:
        store.wait()


def attend(lengths, table, sums, b_query, b_key, b_value, cosine, sine, pool):
    group, head = b_query.shape
    rows = STEPS * group
    page = pool.shape[1:]
    return pl.pallas_call(
        attention_kernel,
        out_shape=(
            pltpu.VMEM((sums.shape[0], rows + 8, head), jnp.float32),
            pltpu.HBM(pool.shape, pool.dtype),
            jax.ShapeDtypeStruct((2,) + page, pool.dtype),
        )
        + tuple(pltpu.VMEM((size,) + page, pool.dtype) for _, size in LATER),
        in_specs=[SMEM, HBM] + [VMEM] * 6 + [HBM],
        out_specs=(VMEM, HBM, VMEM) + (VMEM,) * len(LATER),
        scratch_shapes=[
            pltpu.VMEM(pool.shape, pool.dtype),
            pltpu.VMEM((rows, pool.shape[0] * pool.shape[1]), jnp.float32),
            pltpu.VMEM(table.shape, table.dtype),
            pltpu.SMEM(table.shape, table.dtype),
            pltpu.SemaphoreType.DMA((CHUNKS + 2,)),
            pltpu.SemaphoreType.DMA((CHUNKS,)),
        ],
        compiler_params=params(24),
        name="attend",
    )(lengths, *in_hbm(table), sums, b_query, b_key, b_value, cosine, sine, *in_hbm(pool))


def project_kernel(parts, w_out, out):
    pairs, packed_rows, head = parts.shape
    rows = packed_rows - 8
    group = rows // STEPS
    requests = pairs // 2
    lane = lax.broadcasted_iota(jnp.int32, (rows, head), 1)
    diagonal = lane == lax.broadcasted_iota(jnp.int32, (rows, head), 0)

    def as_column(line):
        return jnp.sum(jnp.where(diagonal, line, 0.0), 1, keepdims=True)

    merged = []
    for r in range(requests):
        first_max, first_sum = (as_column(parts[r, rows + i : rows + i + 1]) for i in range(2))
        second_max, second_sum = (as_column(parts[r + requests, rows + i : rows + i + 1]) for i in range(2))
        top = jnp.maximum(first_max, second_max)
        first_weight = jnp.exp(first_max - top)
        second_weight = jnp.exp(second_max - top)
        joined = first_weight * parts[r, :rows] + second_weight * parts[r + requests, :rows]
        merged.append(joined / (first_weight * first_sum + second_weight * second_sum))
    lines = []
    for s in range(STEPS):
        for r in range(requests):
            lines.append(
                jnp.concatenate(
                    [merged[r][s * group + h : s * group + h + 1] for h in range(group)], 1
                )
            )
    attended = jnp.concatenate(lines, 0).astype(jnp.bfloat16)
    result = jnp.dot(attended, w_out[...], preferred_element_type=jnp.float32)
    for s in range(STEPS):
        out[s] = result[s * requests : (s + 1) * requests]


def project(parts, w_out):
    return pl.pallas_call(
        project_kernel,
        out_shape=jax.ShapeDtypeStruct((STEPS, parts.shape[0] // 2, w_out.shape[1]), jnp.float32),
        in_specs=[VMEM, VMEM],
        out_specs=VMEM,
        compiler_params=params(16),
        name="project",
    )(parts, w_out)


def place_kernel(table_in, plan_in, lengths, *refs, starts, patch):
    parts, (base, new_pool, table, plan, sems, sem) = refs[:-6], refs[-6:]
    del base
    pair_index = lax.axis_index("pair")
    requests = lengths.shape[0]
    table_copy = pltpu.make_async_copy(table_in, table, sems.at[0])
    plan_copy = pltpu.make_async_copy(plan_in, plan, sems.at[1])

    @pl.when(pair_index < requests)
    def _():
        table_copy.start()
        plan_copy.start()
        table_copy.wait()
        plan_copy.wait()
        count = moved_pages(plan, pair_index)
        placed = jnp.int32(0)
        for low, pages in zip(starts, parts):
            here = jnp.clip(count - low, 0, pages.shape[0])

            def start(j, carry):
                slot = table[0, PAGES_HALF + low + j]
                pltpu.make_async_copy(pages.at[j], new_pool.at[slot], sem).start()
                return carry

            lax.fori_loop(0, here, start, 0)
            placed = placed + here

        def wait(j, carry):
            pltpu.make_async_copy(parts[0].at[0], new_pool.at[0], sem).wait()
            return carry

        lax.fori_loop(0, placed, wait, 0)

    if patch:

        @pl.when(pair_index >= requests)
        def _():
            table_copy.start()
            table_copy.wait()
            page_len = new_pool.shape[1]
            first = lengths[pair_index - requests] - PAGES_HALF * page_len
            for i, offset in enumerate((first, first + STEPS - 1)):
                slot = table[0, offset // page_len]
                copy = pltpu.make_async_copy(parts[-1].at[i], new_pool.at[slot], sem)
                copy.start()
                copy.wait()


def place(table, plan, lengths, parts, starts, base, fixed=None):
    patch = fixed is not None
    parts = list(parts) + [fixed] * patch
    return pl.pallas_call(
        functools.partial(place_kernel, starts=starts, patch=patch),
        out_shape=pltpu.HBM(base.shape, base.dtype),
        in_specs=[HBM, HBM, SMEM] + [VMEM] * len(parts) + [HBM],
        out_specs=HBM,
        scratch_shapes=[
            pltpu.SMEM(table.shape, table.dtype),
            pltpu.SMEM(plan.shape, plan.dtype),
            pltpu.SemaphoreType.DMA((2,)),
            pltpu.SemaphoreType.DMA,
        ],
        input_output_aliases={3 + len(parts): 0},
        compiler_params=params(16),
        name="place",
    )(*in_hbm(table, plan), lengths, *parts, *in_hbm(base))


def blank_kernel(out):
    del out


def blank(like):
    return pl.pallas_call(
        blank_kernel,
        out_shape=jax.ShapeDtypeStruct(like.shape, like.dtype),
        out_specs=pl.BlockSpec(memory_space=pl.ANY),
        name="blank",
    )()


def local(
    normed, w_query, b_query, w_key, b_key, w_value, b_value, w_out, pool, page_table, lengths, plan
):
    pair_count = lax.axis_size("pair")
    tp_count = lax.axis_size("tp")
    requests = pair_count // 2
    head = w_key.shape[1]

    planned = plan.T
    partial, near, far, pieces = prepare(
        page_table, planned, normed, w_query, w_key, w_value, pool[0, 0], pair_count
    )
    bits = min(JOINT, requests)

    def tie(*values):
        return lax.optimization_barrier(values)

    def migrate(pages, members=range(requests)):
        return lax.ppermute(pages, "pair", [(r + requests, r) for r in members])

    either = lax.axis_index("rep") == 0

    def gather(values):
        return lax.all_to_all(values, "pair", split_axis=0, concat_axis=0, tiled=True)

    def choose(code, step, *values):
        members = [[r for r in range(requests) if code >> r % bits & 1] for code in range(1 << bits)]
        return lax.switch(code, [functools.partial(step, chosen) for chosen in members], *values)

    def some(members, pages):
        return migrate(pages, members) if members else blank(pages)

    def first_step(members, values, pages):
        return lax.cond(either, gather, gather, values), some(members, pages)

    def second_step(members, values, beside, pages):
        return gather(values), migrate(beside), some(members, pages)

    first = migrate(pieces[0])
    sums, far_pages = choose(far, first_step, partial, pieces[2])
    sums, first = tie(sums, first)
    second = migrate(tie(pieces[1], sums)[0])

    frequency = rope_base ** (-(jnp.arange(head // 2, dtype=jnp.float32) * 2.0 / head))
    steps = jnp.minimum(jnp.arange(8, dtype=jnp.int32), STEPS - 1)
    position = (lengths[:, None] + steps[None, :]).astype(jnp.float32)[..., None]
    angles = position * frequency
    cosine = jnp.cos(angles)
    sine = jnp.sin(angles)
    cosine = jnp.concatenate([cosine, cosine], -1)
    sine = jnp.concatenate([-sine, sine], -1)

    packed, new_pool, fixed, *later = attend(
        lengths,
        page_table,
        sums,
        b_query.reshape(-1, head),
        b_key[None, :],
        b_value[None, :],
        cosine,
        sine,
        pool[0, 0],
    )
    parts, beside, near_pages = choose(near, second_step, packed, later[0], later[2])
    parts, second = tie(parts, second)
    third = migrate(tie(later[1], parts)[0])
    projected = project(parts, w_out)
    here = [first, second, beside, near_pages, far_pages]
    starts = [0, FIRST, BESIDE_AT, NEAR_AT, FAR_AT]
    new_pool = place(page_table, planned, lengths, here, starts, new_pool, fixed)
    if tp_count == 2:
        projected = projected + lax.ppermute(projected, "tp", [(0, 1), (1, 0)])
    else:
        projected = lax.psum(projected, "tp")
    new_pool = place(page_table, planned, lengths, [third], [THIRD_AT], new_pool)
    return projected, new_pool[None, None]


def solution(mesh):
    return jax.shard_map(
        local,
        mesh=mesh,
        in_specs=(
            P(None, "rep", "pair"),
            P("pair", "tp"),
            P("tp"),
            P("pair", "tp"),
            P("tp"),
            P("pair", "tp"),
            P("tp"),
            P("tp", "pair"),
            P(("rep", "pair"), "tp", None, None, None),
            P(("rep", "pair"), None),
            P("rep"),
            P("rep", None),
        ),
        out_specs=(P(None, "rep", "pair"), P(("rep", "pair"), "tp", None, None, None)),
        check_vma=False,
    )
```

```python
import functools
import math

import jax
import jax.numpy as jnp
from jax import lax
from jax.experimental import pallas as pl
from jax.experimental.pallas import tpu as pltpu
from jax.sharding import PartitionSpec as P

PAGES_HALF = 384
STEPS = 2
SECTION = 64
MOVED_MAX = STEPS * SECTION
FIRST, SECOND, BESIDE, THIRD = 18, 32, 12, 10
NEAR, FAR = 24, 32
BESIDE_AT = FIRST + SECOND
THIRD_AT = BESIDE_AT + BESIDE
NEAR_AT = THIRD_AT + THIRD
FAR_AT = NEAR_AT + NEAR
PIECES = ((0, FIRST), (FIRST, SECOND), (FAR_AT, FAR))
LATER = ((BESIDE_AT, BESIDE), (THIRD_AT, THIRD), (NEAR_AT, NEAR))
JOINT = 4
CHUNKS = 8
NEG = -1e30

rope_base = 1000000.0

VMEM = pl.BlockSpec(memory_space=pltpu.VMEM)
SMEM = pl.BlockSpec(memory_space=pltpu.SMEM)
HBM = pl.BlockSpec(memory_space=pltpu.HBM)


def in_hbm(*arrays):
    return tuple(pltpu.with_memory_space_constraint(a, pltpu.HBM) for a in arrays)


def params(mib):
    return pltpu.CompilerParams(vmem_limit_bytes=mib * 1024 * 1024)


def moved_pages(plan, request):
    count = plan[0, request]
    for s in range(1, STEPS):
        count = count + plan[s, request]
    return count


def put_pages(table, count, parts, new_pool, sem):
    placed = jnp.int32(0)
    for low, pages in parts:
        here = jnp.clip(count - low, 0, pages.shape[0])

        def start(j, carry):
            slot = table[0, PAGES_HALF + low + j]
            pltpu.make_async_copy(pages.at[j], new_pool.at[slot], sem).start()
            return carry

        lax.fori_loop(0, here, start, 0)
        placed = placed + here

    def wait(j, carry):
        pltpu.make_async_copy(parts[0][1].at[0], new_pool.at[0], sem).wait()
        return carry

    lax.fori_loop(0, placed, wait, 0)


def prepare_kernel(table_in, plan_in, normed_in, w_query, w_key, w_value, pool, partial, near, far, *refs):
    pieces, (table, plan, normed, weights, index_sems, sems, page_sems) = refs[:-7], refs[-7:]
    pairs = partial.shape[0]
    requests = pairs // 2
    table_copy = pltpu.make_async_copy(table_in, table, index_sems.at[0])
    plan_copy = pltpu.make_async_copy(plan_in, plan, index_sems.at[1])
    table_copy.start()
    plan_copy.start()
    loads = [pltpu.make_async_copy(normed_in, normed, sems.at[3])]
    low = 0
    for i, weight in enumerate((w_query, w_key, w_value)):
        part = weights.at[:, low : low + weight.shape[1]]
        loads.append(pltpu.make_async_copy(weight, part, sems.at[i]))
        low += weight.shape[1]
    for copy in loads:
        copy.start()
    table_copy.wait()

    @pl.when(lax.axis_index("pair") >= requests)
    def _():
        for i, (low, size) in enumerate(PIECES):

            def start(j, carry):
                pltpu.make_async_copy(pool.at[table[0, low + j]], pieces[i].at[j], page_sems.at[i]).start()
                return carry

            lax.fori_loop(0, size, start, 0, unroll=2)

    plan_copy.wait()
    bits = min(JOINT, requests)
    for code, bound in ((near, NEAR_AT), (far, FAR_AT)):
        total = jnp.int32(0)
        for bit in range(bits):
            most = moved_pages(plan, bit)
            for r in range(bit + bits, requests, bits):
                most = jnp.maximum(most, moved_pages(plan, r))
            total = total + jnp.where(most > bound, 1 << bit, 0)
        code[0] = total
    for copy in loads:
        copy.wait()
    hidden = jnp.concatenate([normed[s].astype(jnp.float32) for s in range(STEPS)], 0).astype(jnp.bfloat16)
    result = jnp.dot(hidden, weights[...], preferred_element_type=jnp.float32)
    for p in range(pairs):
        for s in range(STEPS):
            row = s * requests + p % requests
            partial[p, s : s + 1] = result[row : row + 1]

    @pl.when(lax.axis_index("pair") >= requests)
    def _():
        for i, (_, size) in enumerate(PIECES):
            pltpu.make_async_copy(pool.at[pl.ds(0, size)], pieces[i], page_sems.at[i]).wait()


def prepare(table, plan, normed, w_query, w_key, w_value, pool, pairs):
    page = pool.shape[1:]
    wide = w_query.shape[1] + 2 * w_key.shape[1]
    partial, near, far, *pieces = pl.pallas_call(
        prepare_kernel,
        out_shape=(pltpu.VMEM((pairs, STEPS, wide), jnp.float32),)
        + (jax.ShapeDtypeStruct((1,), jnp.int32),) * 2
        + tuple(pltpu.VMEM((size,) + page, pool.dtype) for _, size in PIECES),
        in_specs=[HBM] * 7,
        out_specs=(VMEM, SMEM, SMEM) + (VMEM,) * len(PIECES),
        scratch_shapes=[
            pltpu.SMEM(table.shape, table.dtype),
            pltpu.SMEM(plan.shape, plan.dtype),
            pltpu.VMEM(normed.shape, normed.dtype),
            pltpu.VMEM((w_query.shape[0], wide), w_query.dtype),
            pltpu.SemaphoreType.DMA((2,)),
            pltpu.SemaphoreType.DMA((4,)),
            pltpu.SemaphoreType.DMA((len(PIECES),)),
        ],
        compiler_params=params(16),
        name="prepare",
    )(*in_hbm(table, plan, normed, w_query, w_key, w_value, pool))
    return partial, near.reshape(()), far.reshape(()), pieces


def page_order(table, slots):
    slot = lax.broadcasted_iota(jnp.int32, (slots, slots), 0)
    holds = jnp.where(slot == table, 1.0, 0.0).astype(jnp.bfloat16)
    index = lax.broadcasted_iota(jnp.int32, (8, slots), 1)
    digit = lax.broadcasted_iota(jnp.int32, (8, slots), 0)
    digits = jnp.where(digit == 0, index // 16, jnp.where(digit == 1, index % 16, 0))
    digits = digits.astype(jnp.float32).astype(jnp.bfloat16)
    return lax.dot_general(digits, holds, (((1,), (1,)), ((), ())), preferred_element_type=jnp.float32)


def attention_kernel(
    lengths, table_in, plan_in, sums, b_query, b_key, b_value, cosine, sine, early, far, pool,
    copies_out, new_pool, fixed, *refs
):
    pieces, refs = refs[: len(LATER)], refs[len(LATER) :]
    held, score, packed, table, slots_of, plan, sems, out_sems, send_sem, page_sem = refs
    slots, page_len, _ = held.shape
    per = slots // CHUNKS
    table_copy = pltpu.make_async_copy(table_in, table, sems.at[CHUNKS])
    table_copy.start()
    slots_copy = pltpu.make_async_copy(table_in, slots_of, sems.at[CHUNKS + 1])
    slots_copy.start()
    plan_copy = pltpu.make_async_copy(plan_in, plan, sems.at[CHUNKS + 2])
    plan_copy.start()
    copies = []
    for c in range(CHUNKS):
        part = pl.ds(c * per, per)
        copies.append(pltpu.make_async_copy(pool.at[part], held.at[part], sems.at[c]))
        copies[-1].start()
    requests = sums.shape[0] // 2
    group, head = b_query.shape
    rows = STEPS * group
    pair_index = lax.axis_index("pair")
    is_source = pair_index >= requests
    request = jnp.where(is_source, pair_index - requests, pair_index)
    half_tokens = PAGES_HALF * page_len
    limit = jnp.where(is_source, lengths[request] - half_tokens, half_tokens)

    blocks = CHUNKS // 2
    block = slots // blocks
    width = block * page_len
    table_copy.wait()
    digits = page_order(table[...], slots)
    digits = jnp.concatenate(
        [digits[d : d + 1, c * block : (c + 1) * block] for d in range(2) for c in range(blocks)], 0
    ).astype(jnp.bfloat16)
    spread = lax.broadcasted_iota(jnp.int32, (block, width), 1) // page_len
    spread = jnp.where(spread == lax.broadcasted_iota(jnp.int32, (block, width), 0), 1.0, 0.0)
    digits = jnp.dot(digits, spread.astype(jnp.bfloat16), preferred_element_type=jnp.float32)
    tokens = (digits[:blocks] * 16.0 + digits[blocks:]).astype(jnp.int32) * page_len
    tokens = tokens + lax.broadcasted_iota(jnp.int32, (blocks, width), 1) % page_len

    total = sums[0]
    for p in range(1, sums.shape[0]):
        total = total + sums[p]
    query = jnp.concatenate(
        [total[s : s + 1, h * head : (h + 1) * head] for s in range(STEPS) for h in range(group)], 0
    )
    query = query + jnp.concatenate([b_query[...]] * STEPS, 0)
    cos_new = cosine[request]
    sin_new = sine[request]
    row = lax.broadcasted_iota(jnp.int32, (rows, head), 0)
    cos_rows = jnp.where(row < group, cos_new[0:1], cos_new[1:2])
    sin_rows = jnp.where(row < group, sin_new[0:1], sin_new[1:2])
    query = (query * cos_rows + pltpu.roll(query, head // 2, 1) * sin_rows).astype(jnp.bfloat16)
    key_new = total[:, group * head : (group + 1) * head] + b_key[...]
    key_new = jnp.concatenate([key_new, jnp.zeros((8 - STEPS, head), jnp.float32)], 0)
    key_new = key_new * cos_new + pltpu.roll(key_new, head // 2, 1) * sin_new
    key_new = key_new.astype(jnp.bfloat16).astype(jnp.float32)
    value_new = total[:, (group + 1) * head :] + b_value[...]
    value_new = value_new.astype(jnp.bfloat16).astype(jnp.float32)
    scale = 1.0 / math.sqrt(head)

    column = lax.broadcasted_iota(jnp.int32, (rows, 1), 0)
    query_wide = query.astype(jnp.float32)
    fresh = []
    for s in range(STEPS):
        dots = jnp.sum(query_wide * key_new[s : s + 1], 1, keepdims=True) * scale
        seen = jnp.logical_and(is_source, column >= s * group)
        fresh.append((jnp.where(seen, dots, NEG), seen))
    row_max = jnp.maximum(fresh[0][0], fresh[1][0])

    stores = []
    for c in range(blocks):
        for i in range(c * CHUNKS // blocks, (c + 1) * CHUNKS // blocks):
            copies[i].wait()
            part = pl.ds(i * per, per)
            stores.append(pltpu.make_async_copy(held.at[part], new_pool.at[part], out_sems.at[i]))
            stores[-1].start()
        keys = held[c * block : (c + 1) * block, :, :head].reshape(width, head)
        part = lax.dot_general(query, keys, (((1,), (1,)), ((), ())), preferred_element_type=jnp.float32)
        part = jnp.where(tokens[c : c + 1] < limit, part * scale, NEG)
        score[:, c * width : (c + 1) * width] = part
        row_max = jnp.maximum(row_max, jnp.max(part, 1, keepdims=True))
    row_sum = jnp.zeros((rows, 1), jnp.float32)
    out = jnp.zeros((rows, head), jnp.float32)
    for s in range(STEPS):
        weight = jnp.where(fresh[s][1], jnp.exp(fresh[s][0] - row_max), 0.0)
        row_sum = row_sum + weight
        out = out + weight.astype(jnp.bfloat16).astype(jnp.float32) * value_new[s : s + 1]
    for c in range(blocks):
        weight = jnp.exp(score[:, c * width : (c + 1) * width] - row_max)
        weight = jnp.where(tokens[c : c + 1] < limit, weight, 0.0)
        row_sum = row_sum + jnp.sum(weight, 1, keepdims=True)
        values = held[c * block : (c + 1) * block, :, head:].reshape(width, head)
        out = out + jnp.dot(weight.astype(jnp.bfloat16), values, preferred_element_type=jnp.float32)

    diagonal = lax.broadcasted_iota(jnp.int32, (rows, head), 1) == row
    packed[0:rows] = out
    packed[rows : rows + 1] = jnp.sum(jnp.where(diagonal, row_max, 0.0), 0, keepdims=True)
    packed[rows + 1 : rows + 2] = jnp.sum(jnp.where(diagonal, row_sum, 0.0), 0, keepdims=True)
    packed[rows + 2 :] = jnp.zeros((packed.shape[0] - rows - 2, head), jnp.float32)
    sends = [
        pltpu.make_async_copy(packed, copies_out.at[p], send_sem.at[p]) for p in range(copies_out.shape[0])
    ]
    for send in sends:
        send.start()

    slots_copy.wait()

    @pl.when(is_source)
    def _():
        for piece, (low, size) in zip(pieces, LATER):

            def take(j, carry):
                piece[j] = held[slots_of[0, low + j]]
                return carry

            lax.fori_loop(0, size, take, 0)
        page_row = lax.broadcasted_iota(jnp.int32, (page_len, 2 * head), 0)
        entries = jnp.concatenate([key_new[:STEPS], value_new], 1)
        offsets = [limit + s for s in range(STEPS)]
        homes = [slots_of[0, offset // page_len] for offset in offsets]
        for i, slot in enumerate((homes[0], homes[-1])):
            page = held[slot].astype(jnp.float32)
            for s, offset in enumerate(offsets):
                here = jnp.logical_and(homes[s] == slot, page_row == offset % page_len)
                page = jnp.where(here, entries[s : s + 1], page)
            fixed[i] = page.astype(held.dtype)

    plan_copy.wait()
    for store in stores:
        store.wait()

    @pl.when(jnp.logical_not(is_source))
    def _():
        put_pages(slots_of, moved_pages(plan, request), [(0, early), (FAR_AT, far)], new_pool, page_sem)

    for send in sends:
        send.wait()


def attend(lengths, table, plan, sums, b_query, b_key, b_value, cosine, sine, early, far, pool):
    group, head = b_query.shape
    rows = STEPS * group
    page = pool.shape[1:]
    return pl.pallas_call(
        attention_kernel,
        out_shape=(
            pltpu.HBM((sums.shape[0], rows + 8, head), jnp.float32),
            pltpu.HBM(pool.shape, pool.dtype),
            jax.ShapeDtypeStruct((2,) + page, pool.dtype),
        )
        + tuple(pltpu.VMEM((size,) + page, pool.dtype) for _, size in LATER),
        in_specs=[SMEM, HBM, HBM] + [VMEM] * 8 + [HBM],
        out_specs=(HBM, HBM, VMEM) + (VMEM,) * len(LATER),
        scratch_shapes=[
            pltpu.VMEM(pool.shape, pool.dtype),
            pltpu.VMEM((rows, pool.shape[0] * pool.shape[1]), jnp.float32),
            pltpu.VMEM((rows + 8, head), jnp.float32),
            pltpu.VMEM(table.shape, table.dtype),
            pltpu.SMEM(table.shape, table.dtype),
            pltpu.SMEM(plan.shape, plan.dtype),
            pltpu.SemaphoreType.DMA((CHUNKS + 3,)),
            pltpu.SemaphoreType.DMA((CHUNKS,)),
            pltpu.SemaphoreType.DMA((sums.shape[0],)),
            pltpu.SemaphoreType.DMA,
        ],
        compiler_params=params(24),
        name="attend",
    )(
        lengths, *in_hbm(table, plan), sums, b_query, b_key, b_value, cosine, sine, early, far, *in_hbm(pool)
    )


def project_kernel(parts, w_out, out):
    pairs, packed_rows, head = parts.shape
    rows = packed_rows - 8
    group = rows // STEPS
    requests = pairs // 2
    lane = lax.broadcasted_iota(jnp.int32, (rows, head), 1)
    diagonal = lane == lax.broadcasted_iota(jnp.int32, (rows, head), 0)

    def as_column(line):
        return jnp.sum(jnp.where(diagonal, line, 0.0), 1, keepdims=True)

    merged = []
    for r in range(requests):
        first_max, first_sum = (as_column(parts[r, rows + i : rows + i + 1]) for i in range(2))
        second_max, second_sum = (as_column(parts[r + requests, rows + i : rows + i + 1]) for i in range(2))
        top = jnp.maximum(first_max, second_max)
        first_weight = jnp.exp(first_max - top)
        second_weight = jnp.exp(second_max - top)
        joined = first_weight * parts[r, :rows] + second_weight * parts[r + requests, :rows]
        merged.append(joined / (first_weight * first_sum + second_weight * second_sum))
    lines = []
    for s in range(STEPS):
        for r in range(requests):
            lines.append(
                jnp.concatenate(
                    [merged[r][s * group + h : s * group + h + 1] for h in range(group)], 1
                )
            )
    attended = jnp.concatenate(lines, 0).astype(jnp.bfloat16)
    result = jnp.dot(attended, w_out[...], preferred_element_type=jnp.float32)
    for s in range(STEPS):
        out[s] = result[s * requests : (s + 1) * requests]


def project(parts, w_out):
    return pl.pallas_call(
        project_kernel,
        out_shape=jax.ShapeDtypeStruct((STEPS, parts.shape[0] // 2, w_out.shape[1]), jnp.float32),
        in_specs=[VMEM, VMEM],
        out_specs=VMEM,
        compiler_params=params(16),
        name="project",
    )(parts, w_out)


def place_kernel(table_in, plan_in, lengths, *refs, starts, patch):
    parts, (base, new_pool, table, plan, sems, sem) = refs[:-6], refs[-6:]
    del base
    pair_index = lax.axis_index("pair")
    requests = lengths.shape[0]
    table_copy = pltpu.make_async_copy(table_in, table, sems.at[0])
    plan_copy = pltpu.make_async_copy(plan_in, plan, sems.at[1])
    table_copy.start()
    plan_copy.start()
    table_copy.wait()
    plan_copy.wait()

    @pl.when(pair_index < requests)
    def _():
        put_pages(table, moved_pages(plan, pair_index), list(zip(starts, parts)), new_pool, sem)

    if patch:

        @pl.when(pair_index >= requests)
        def _():
            page_len = new_pool.shape[1]
            first = lengths[pair_index - requests] - PAGES_HALF * page_len
            for i, offset in enumerate((first, first + STEPS - 1)):
                slot = table[0, offset // page_len]
                copy = pltpu.make_async_copy(parts[-1].at[i], new_pool.at[slot], sem)
                copy.start()
                copy.wait()


def finish_kernel(table_in, plan_in, lengths, own, other, *refs, starts, patch):
    refs, total = refs[:-6] + refs[-5:], refs[-6]
    place_kernel(table_in, plan_in, lengths, *refs, starts=starts, patch=patch)
    total[...] = own[...] + other[...]


def place(table, plan, lengths, parts, starts, base, fixed=None, halves=()):
    patch = fixed is not None
    parts = list(parts) + [fixed] * patch
    halves = list(halves)
    kernel = finish_kernel if halves else place_kernel
    totals = tuple(jax.ShapeDtypeStruct(half.shape, half.dtype) for half in halves[:1])
    result = pl.pallas_call(
        functools.partial(kernel, starts=starts, patch=patch),
        out_shape=totals + (pltpu.HBM(base.shape, base.dtype),),
        in_specs=[HBM, HBM, SMEM] + [VMEM] * (len(halves) + len(parts)) + [HBM],
        out_specs=(VMEM,) * len(totals) + (HBM,),
        scratch_shapes=[
            pltpu.SMEM(table.shape, table.dtype),
            pltpu.SMEM(plan.shape, plan.dtype),
            pltpu.SemaphoreType.DMA((2,)),
            pltpu.SemaphoreType.DMA,
        ],
        input_output_aliases={3 + len(halves) + len(parts): len(totals)},
        compiler_params=params(16),
        name="place",
    )(*in_hbm(table, plan), lengths, *halves, *parts, *in_hbm(base))
    return result if halves else result[0]


def blank_kernel(out):
    del out


def blank(like):
    return pl.pallas_call(
        blank_kernel,
        out_shape=jax.ShapeDtypeStruct(like.shape, like.dtype),
        out_specs=pl.BlockSpec(memory_space=pl.ANY),
        name="blank",
    )()


def local(
    normed, w_query, b_query, w_key, b_key, w_value, b_value, w_out, pool, page_table, lengths, plan
):
    pair_count = lax.axis_size("pair")
    tp_count = lax.axis_size("tp")
    requests = pair_count // 2
    head = w_key.shape[1]

    planned = plan.T
    partial, near, far, pieces = prepare(
        page_table, planned, normed, w_query, w_key, w_value, pool[0, 0], pair_count
    )
    bits = min(JOINT, requests)

    def tie(*values):
        return lax.optimization_barrier(values)

    def migrate(pages, members=range(requests)):
        return lax.ppermute(pages, "pair", [(r + requests, r) for r in members])

    either = lax.axis_index("rep") == 0

    def gather(values):
        return lax.all_to_all(values, "pair", split_axis=0, concat_axis=0, tiled=True)

    def choose(code, step, *values):
        members = [[r for r in range(requests) if code >> r % bits & 1] for code in range(1 << bits)]
        return lax.switch(code, [functools.partial(step, chosen) for chosen in members], *values)

    def some(members, pages):
        return migrate(pages, members) if members else blank(pages)

    def first_step(members, values, pages):
        return lax.cond(either, gather, gather, values), some(members, pages)

    def second_step(members, values, beside, pages):
        return gather(values), migrate(beside), some(members, pages)

    first = migrate(pieces[0])
    sums, far_pages = choose(far, first_step, partial, pieces[2])
    sums, first = tie(sums, first)
    second = migrate(tie(pieces[1], sums)[0])

    frequency = rope_base ** (-(jnp.arange(head // 2, dtype=jnp.float32) * 2.0 / head))
    steps = jnp.minimum(jnp.arange(8, dtype=jnp.int32), STEPS - 1)
    position = (lengths[:, None] + steps[None, :]).astype(jnp.float32)[..., None]
    angles = position * frequency
    cosine = jnp.cos(angles)
    sine = jnp.sin(angles)
    cosine = jnp.concatenate([cosine, cosine], -1)
    sine = jnp.concatenate([-sine, sine], -1)

    packed, new_pool, fixed, *later = attend(
        lengths,
        page_table,
        planned,
        sums,
        b_query.reshape(-1, head),
        b_key[None, :],
        b_value[None, :],
        cosine,
        sine,
        first,
        far_pages,
        pool[0, 0],
    )
    parts, beside, near_pages = choose(near, second_step, packed, later[0], later[2])
    parts, second = tie(parts, second)
    third = migrate(tie(later[1], parts)[0])
    projected = project(parts, w_out)
    here = [second, beside, near_pages]
    starts = [FIRST, BESIDE_AT, NEAR_AT]
    new_pool = place(page_table, planned, lengths, here, starts, new_pool, fixed)
    if tp_count == 2:
        halves = [projected, lax.ppermute(projected, "tp", [(0, 1), (1, 0)])]
        projected, new_pool = place(
            page_table, planned, lengths, [third], [THIRD_AT], new_pool, halves=halves
        )
    else:
        projected = lax.psum(projected, "tp")
        new_pool = place(page_table, planned, lengths, [third], [THIRD_AT], new_pool)
    return projected, new_pool[None, None]


def solution(mesh):
    return jax.shard_map(
        local,
        mesh=mesh,
        in_specs=(
            P(None, "rep", "pair"),
            P("pair", "tp"),
            P("tp"),
            P("pair", "tp"),
            P("tp"),
            P("pair", "tp"),
            P("tp"),
            P("tp", "pair"),
            P(("rep", "pair"), "tp", None, None, None),
            P(("rep", "pair"), None),
            P("rep"),
            P("rep", None),
        ),
        out_specs=(P(None, "rep", "pair"), P(("rep", "pair"), "tp", None, None, None)),
        check_vma=False,
    )
```

```python
import functools
import math

import jax
import jax.numpy as jnp
from jax import lax
from jax.experimental import pallas as pl
from jax.experimental.pallas import tpu as pltpu
from jax.sharding import PartitionSpec as P

PAGES_HALF = 384
STEPS = 2
SECTION = 64
MOVED_MAX = STEPS * SECTION
FIRST, SECOND, BESIDE, THIRD = 20, 32, 10, 10
NEAR, FAR = 26, 30
BESIDE_AT = FIRST + SECOND
THIRD_AT = BESIDE_AT + BESIDE
NEAR_AT = THIRD_AT + THIRD
FAR_AT = NEAR_AT + NEAR
PIECES = ((0, FIRST), (FIRST, SECOND), (FAR_AT, FAR))
LATER = ((BESIDE_AT, BESIDE), (THIRD_AT, THIRD), (NEAR_AT, NEAR))
JOINT = 4
CHUNKS = 8
NEG = -1e30

rope_base = 1000000.0

VMEM = pl.BlockSpec(memory_space=pltpu.VMEM)
SMEM = pl.BlockSpec(memory_space=pltpu.SMEM)
HBM = pl.BlockSpec(memory_space=pltpu.HBM)


def in_hbm(*arrays):
    return tuple(pltpu.with_memory_space_constraint(a, pltpu.HBM) for a in arrays)


def params(mib):
    return pltpu.CompilerParams(vmem_limit_bytes=mib * 1024 * 1024)


def moved_pages(plan, request):
    count = plan[0, request]
    for s in range(1, STEPS):
        count = count + plan[s, request]
    return count


def put_pages(table, count, parts, new_pool, sem):
    placed = jnp.int32(0)
    for low, pages in parts:
        here = jnp.clip(count - low, 0, pages.shape[0])

        def start(j, carry):
            slot = table[0, PAGES_HALF + low + j]
            pltpu.make_async_copy(pages.at[j], new_pool.at[slot], sem).start()
            return carry

        lax.fori_loop(0, here, start, 0)
        placed = placed + here

    def wait(j, carry):
        pltpu.make_async_copy(parts[0][1].at[0], new_pool.at[0], sem).wait()
        return carry

    lax.fori_loop(0, placed, wait, 0)


def prepare_kernel(table_in, plan_in, normed_in, w_query, w_key, w_value, pool, partial, near, far, *refs):
    pieces, (table, plan, normed, weights, index_sems, sems, page_sems) = refs[:-7], refs[-7:]
    pairs = partial.shape[0]
    requests = pairs // 2
    table_copy = pltpu.make_async_copy(table_in, table, index_sems.at[0])
    plan_copy = pltpu.make_async_copy(plan_in, plan, index_sems.at[1])
    table_copy.start()
    plan_copy.start()
    loads = [pltpu.make_async_copy(normed_in, normed, sems.at[3])]
    low = 0
    for i, weight in enumerate((w_query, w_key, w_value)):
        part = weights.at[:, low : low + weight.shape[1]]
        loads.append(pltpu.make_async_copy(weight, part, sems.at[i]))
        low += weight.shape[1]
    for copy in loads:
        copy.start()
    table_copy.wait()

    @pl.when(lax.axis_index("pair") >= requests)
    def _():
        for i, (low, size) in enumerate(PIECES):

            def start(j, carry):
                pltpu.make_async_copy(pool.at[table[0, low + j]], pieces[i].at[j], page_sems.at[i]).start()
                return carry

            lax.fori_loop(0, size, start, 0, unroll=2)

    plan_copy.wait()
    bits = min(JOINT, requests)
    for code, bound in ((near, NEAR_AT), (far, FAR_AT)):
        total = jnp.int32(0)
        for bit in range(bits):
            most = moved_pages(plan, bit)
            for r in range(bit + bits, requests, bits):
                most = jnp.maximum(most, moved_pages(plan, r))
            total = total + jnp.where(most > bound, 1 << bit, 0)
        code[0] = total
    for copy in loads:
        copy.wait()
    hidden = jnp.concatenate([normed[s].astype(jnp.float32) for s in range(STEPS)], 0).astype(jnp.bfloat16)
    result = jnp.dot(hidden, weights[...], preferred_element_type=jnp.float32)
    for r in range(requests):
        lines = jnp.concatenate([result[s * requests + r : s * requests + r + 1] for s in range(STEPS)], 0)
        for p in range(r, pairs, requests):
            partial[p] = lines

    @pl.when(lax.axis_index("pair") >= requests)
    def _():
        for i, (_, size) in enumerate(PIECES):
            pltpu.make_async_copy(pool.at[pl.ds(0, size)], pieces[i], page_sems.at[i]).wait()


def prepare(table, plan, normed, w_query, w_key, w_value, pool, pairs):
    page = pool.shape[1:]
    wide = w_query.shape[1] + 2 * w_key.shape[1]
    partial, near, far, *pieces = pl.pallas_call(
        prepare_kernel,
        out_shape=(jax.ShapeDtypeStruct((pairs, STEPS, wide), jnp.float32),)
        + (jax.ShapeDtypeStruct((1,), jnp.int32),) * 2
        + tuple(pltpu.VMEM((size,) + page, pool.dtype) for _, size in PIECES),
        in_specs=[HBM] * 7,
        out_specs=(VMEM, SMEM, SMEM) + (VMEM,) * len(PIECES),
        scratch_shapes=[
            pltpu.SMEM(table.shape, table.dtype),
            pltpu.SMEM(plan.shape, plan.dtype),
            pltpu.VMEM(normed.shape, normed.dtype),
            pltpu.VMEM((w_query.shape[0], wide), w_query.dtype),
            pltpu.SemaphoreType.DMA((2,)),
            pltpu.SemaphoreType.DMA((4,)),
            pltpu.SemaphoreType.DMA((len(PIECES),)),
        ],
        compiler_params=params(16),
        name="prepare",
    )(*in_hbm(table, plan, normed, w_query, w_key, w_value, pool))
    return partial, near.reshape(()), far.reshape(()), pieces


def page_order(table, slots):
    slot = lax.broadcasted_iota(jnp.int32, (slots, slots), 0)
    holds = jnp.where(slot == table, 1.0, 0.0).astype(jnp.bfloat16)
    index = lax.broadcasted_iota(jnp.int32, (8, slots), 1)
    digit = lax.broadcasted_iota(jnp.int32, (8, slots), 0)
    digits = jnp.where(digit == 0, index // 16, jnp.where(digit == 1, index % 16, 0))
    digits = digits.astype(jnp.float32).astype(jnp.bfloat16)
    return lax.dot_general(digits, holds, (((1,), (1,)), ((), ())), preferred_element_type=jnp.float32)


def attention_kernel(
    lengths, table_in, plan_in, sums, b_query, b_key, b_value, cosine, sine, early, far, pool,
    copies_out, new_pool, fixed, *refs
):
    pieces, refs = refs[: len(LATER)], refs[len(LATER) :]
    held, score, packed, table, slots_of, plan, sems, out_sems, send_sem, page_sem = refs
    slots, page_len, _ = held.shape
    per = slots // CHUNKS
    table_copy = pltpu.make_async_copy(table_in, table, sems.at[CHUNKS])
    table_copy.start()
    slots_copy = pltpu.make_async_copy(table_in, slots_of, sems.at[CHUNKS + 1])
    slots_copy.start()
    plan_copy = pltpu.make_async_copy(plan_in, plan, sems.at[CHUNKS + 2])
    plan_copy.start()
    copies = []
    for c in range(CHUNKS):
        part = pl.ds(c * per, per)
        copies.append(pltpu.make_async_copy(pool.at[part], held.at[part], sems.at[c]))
        copies[-1].start()
    requests = sums.shape[0] // 2
    group, head = b_query.shape
    rows = STEPS * group
    pair_index = lax.axis_index("pair")
    is_source = pair_index >= requests
    request = jnp.where(is_source, pair_index - requests, pair_index)
    half_tokens = PAGES_HALF * page_len
    limit = jnp.where(is_source, lengths[request] - half_tokens, half_tokens)

    blocks = CHUNKS // 2
    block = slots // blocks
    width = block * page_len
    table_copy.wait()
    digits = page_order(table[...], slots)
    digits = jnp.concatenate(
        [digits[d : d + 1, c * block : (c + 1) * block] for d in range(2) for c in range(blocks)], 0
    ).astype(jnp.bfloat16)
    spread = lax.broadcasted_iota(jnp.int32, (block, width), 1) // page_len
    spread = jnp.where(spread == lax.broadcasted_iota(jnp.int32, (block, width), 0), 1.0, 0.0)
    digits = jnp.dot(digits, spread.astype(jnp.bfloat16), preferred_element_type=jnp.float32)
    tokens = (digits[:blocks] * 16.0 + digits[blocks:]).astype(jnp.int32) * page_len
    tokens = tokens + lax.broadcasted_iota(jnp.int32, (blocks, width), 1) % page_len

    total = sums[0]
    for p in range(1, sums.shape[0]):
        total = total + sums[p]
    query = jnp.concatenate(
        [total[s : s + 1, h * head : (h + 1) * head] for s in range(STEPS) for h in range(group)], 0
    )
    query = query + jnp.concatenate([b_query[...]] * STEPS, 0)
    cos_new = cosine[request]
    sin_new = sine[request]
    row = lax.broadcasted_iota(jnp.int32, (rows, head), 0)
    cos_rows = jnp.where(row < group, cos_new[0:1], cos_new[1:2])
    sin_rows = jnp.where(row < group, sin_new[0:1], sin_new[1:2])
    query = (query * cos_rows + pltpu.roll(query, head // 2, 1) * sin_rows).astype(jnp.bfloat16)
    key_new = total[:, group * head : (group + 1) * head] + b_key[...]
    key_new = jnp.concatenate([key_new, jnp.zeros((8 - STEPS, head), jnp.float32)], 0)
    key_new = key_new * cos_new + pltpu.roll(key_new, head // 2, 1) * sin_new
    key_new = key_new.astype(jnp.bfloat16).astype(jnp.float32)
    value_new = total[:, (group + 1) * head :] + b_value[...]
    value_new = value_new.astype(jnp.bfloat16).astype(jnp.float32)
    scale = 1.0 / math.sqrt(head)

    column = lax.broadcasted_iota(jnp.int32, (rows, 1), 0)
    query_wide = query.astype(jnp.float32)
    fresh = []
    for s in range(STEPS):
        dots = jnp.sum(query_wide * key_new[s : s + 1], 1, keepdims=True) * scale
        seen = jnp.logical_and(is_source, column >= s * group)
        fresh.append((jnp.where(seen, dots, NEG), seen))
    row_max = jnp.maximum(fresh[0][0], fresh[1][0])

    stores = []
    for c in range(blocks):
        for i in range(c * CHUNKS // blocks, (c + 1) * CHUNKS // blocks):
            copies[i].wait()
            part = pl.ds(i * per, per)
            stores.append(pltpu.make_async_copy(held.at[part], new_pool.at[part], out_sems.at[i]))
            stores[-1].start()
        keys = held[c * block : (c + 1) * block, :, :head].reshape(width, head)
        part = lax.dot_general(query, keys, (((1,), (1,)), ((), ())), preferred_element_type=jnp.float32)
        part = jnp.where(tokens[c : c + 1] < limit, part * scale, NEG)
        score[:, c * width : (c + 1) * width] = part
        row_max = jnp.maximum(row_max, jnp.max(part, 1, keepdims=True))
    row_sum = jnp.zeros((rows, 1), jnp.float32)
    out = jnp.zeros((rows, head), jnp.float32)
    for s in range(STEPS):
        weight = jnp.where(fresh[s][1], jnp.exp(fresh[s][0] - row_max), 0.0)
        row_sum = row_sum + weight
        out = out + weight.astype(jnp.bfloat16).astype(jnp.float32) * value_new[s : s + 1]
    for c in range(blocks):
        weight = jnp.exp(score[:, c * width : (c + 1) * width] - row_max)
        weight = jnp.where(tokens[c : c + 1] < limit, weight, 0.0)
        row_sum = row_sum + jnp.sum(weight, 1, keepdims=True)
        values = held[c * block : (c + 1) * block, :, head:].reshape(width, head)
        out = out + jnp.dot(weight.astype(jnp.bfloat16), values, preferred_element_type=jnp.float32)

    diagonal = lax.broadcasted_iota(jnp.int32, (rows, head), 1) == row
    for i in range(rows):
        packed[:, i * head : (i + 1) * head] = out[i : i + 1]
    shifted = lax.broadcasted_iota(jnp.int32, (rows, head), 1) == row + rows
    packed[:, rows * head :] = jnp.sum(
        jnp.where(diagonal, row_max, 0.0) + jnp.where(shifted, row_sum, 0.0), 0, keepdims=True
    )
    sends = [
        pltpu.make_async_copy(packed, copies_out.at[p], send_sem.at[p]) for p in range(copies_out.shape[0])
    ]
    for send in sends:
        send.start()

    slots_copy.wait()

    @pl.when(is_source)
    def _():
        for piece, (low, size) in zip(pieces, LATER):

            def take(j, carry):
                piece[j] = held[slots_of[0, low + j]]
                return carry

            lax.fori_loop(0, size, take, 0)
        page_row = lax.broadcasted_iota(jnp.int32, (page_len, 2 * head), 0)
        entries = jnp.concatenate([key_new[:STEPS], value_new], 1)
        offsets = [limit + s for s in range(STEPS)]
        homes = [slots_of[0, offset // page_len] for offset in offsets]
        for i, slot in enumerate((homes[0], homes[-1])):
            page = held[slot].astype(jnp.float32)
            for s, offset in enumerate(offsets):
                here = jnp.logical_and(homes[s] == slot, page_row == offset % page_len)
                page = jnp.where(here, entries[s : s + 1], page)
            fixed[i] = page.astype(held.dtype)

    plan_copy.wait()
    for store in stores:
        store.wait()

    @pl.when(jnp.logical_not(is_source))
    def _():
        put_pages(slots_of, moved_pages(plan, request), [(0, early), (FAR_AT, far)], new_pool, page_sem)

    for send in sends:
        send.wait()


def attend(lengths, table, plan, sums, b_query, b_key, b_value, cosine, sine, early, far, pool):
    group, head = b_query.shape
    rows = STEPS * group
    page = pool.shape[1:]
    return pl.pallas_call(
        attention_kernel,
        out_shape=(
            pltpu.HBM((sums.shape[0], 1, (rows + 1) * head), jnp.float32),
            pltpu.HBM(pool.shape, pool.dtype),
            jax.ShapeDtypeStruct((2,) + page, pool.dtype),
        )
        + tuple(pltpu.VMEM((size,) + page, pool.dtype) for _, size in LATER),
        in_specs=[SMEM, HBM, HBM] + [VMEM] * 8 + [HBM],
        out_specs=(HBM, HBM, VMEM) + (VMEM,) * len(LATER),
        scratch_shapes=[
            pltpu.VMEM(pool.shape, pool.dtype),
            pltpu.VMEM((rows, pool.shape[0] * pool.shape[1]), jnp.float32),
            pltpu.VMEM((1, (rows + 1) * head), jnp.float32),
            pltpu.VMEM(table.shape, table.dtype),
            pltpu.SMEM(table.shape, table.dtype),
            pltpu.SMEM(plan.shape, plan.dtype),
            pltpu.SemaphoreType.DMA((CHUNKS + 3,)),
            pltpu.SemaphoreType.DMA((CHUNKS,)),
            pltpu.SemaphoreType.DMA((sums.shape[0],)),
            pltpu.SemaphoreType.DMA,
        ],
        compiler_params=params(24),
        name="attend",
    )(
        lengths, *in_hbm(table, plan), sums, b_query, b_key, b_value, cosine, sine, early, far, *in_hbm(pool)
    )


def project_kernel(head, parts, w_out, out):
    pairs, _, width = parts.shape
    rows = width // head - 1
    group = rows // STEPS
    requests = pairs // 2
    lane = lax.broadcasted_iota(jnp.int32, (rows, head), 1)
    row = lax.broadcasted_iota(jnp.int32, (rows, head), 0)

    def column(part, shift):
        line = parts[part, :, rows * head :]
        return jnp.sum(jnp.where(lane == row + shift, line, 0.0), 1, keepdims=True)

    lines = [[] for _ in range(STEPS)]
    for r in range(requests):
        tops = [column(part, 0) for part in (r, r + requests)]
        sums = [column(part, rows) for part in (r, r + requests)]
        top = jnp.maximum(*tops)
        weights = [jnp.exp(one - top) for one in tops]
        total = weights[0] * sums[0] + weights[1] * sums[1]
        shares = [weight / total for weight in weights]
        for s in range(STEPS):
            heads = []
            for i in range(s * group, (s + 1) * group):
                here = slice(i * head, (i + 1) * head)
                heads.append(
                    shares[0][i : i + 1] * parts[r, :, here] + shares[1][i : i + 1] * parts[r + requests, :, here]
                )
            lines[s].append(jnp.concatenate(heads, 1))
    attended = jnp.concatenate(sum(lines, []), 0).astype(jnp.bfloat16)
    result = jnp.dot(attended, w_out[...], preferred_element_type=jnp.float32)
    for s in range(STEPS):
        out[s] = result[s * requests : (s + 1) * requests]


def project(parts, w_out, head):
    return pl.pallas_call(
        functools.partial(project_kernel, head),
        out_shape=jax.ShapeDtypeStruct((STEPS, parts.shape[0] // 2, w_out.shape[1]), jnp.float32),
        in_specs=[VMEM, VMEM],
        out_specs=VMEM,
        compiler_params=params(16),
        name="project",
    )(parts, w_out)


def place_kernel(table_in, plan_in, lengths, *refs, starts, patch):
    parts, (base, new_pool, table, plan, sems, sem) = refs[:-6], refs[-6:]
    del base
    pair_index = lax.axis_index("pair")
    requests = lengths.shape[0]
    table_copy = pltpu.make_async_copy(table_in, table, sems.at[0])
    plan_copy = pltpu.make_async_copy(plan_in, plan, sems.at[1])
    table_copy.start()
    plan_copy.start()
    table_copy.wait()
    plan_copy.wait()

    @pl.when(pair_index < requests)
    def _():
        put_pages(table, moved_pages(plan, pair_index), list(zip(starts, parts)), new_pool, sem)

    if patch:

        @pl.when(pair_index >= requests)
        def _():
            page_len = new_pool.shape[1]
            first = lengths[pair_index - requests] - PAGES_HALF * page_len
            for i, offset in enumerate((first, first + STEPS - 1)):
                slot = table[0, offset // page_len]
                copy = pltpu.make_async_copy(parts[-1].at[i], new_pool.at[slot], sem)
                copy.start()
                copy.wait()


def place(table, plan, lengths, parts, starts, base, fixed=None):
    patch = fixed is not None
    parts = list(parts) + [fixed] * patch
    return pl.pallas_call(
        functools.partial(place_kernel, starts=starts, patch=patch),
        out_shape=pltpu.HBM(base.shape, base.dtype),
        in_specs=[HBM, HBM, SMEM] + [VMEM] * len(parts) + [HBM],
        out_specs=HBM,
        scratch_shapes=[
            pltpu.SMEM(table.shape, table.dtype),
            pltpu.SMEM(plan.shape, plan.dtype),
            pltpu.SemaphoreType.DMA((2,)),
            pltpu.SemaphoreType.DMA,
        ],
        input_output_aliases={3 + len(parts): 0},
        compiler_params=params(16),
        name="place",
    )(*in_hbm(table, plan), lengths, *parts, *in_hbm(base))


def blank_kernel(out):
    del out


def blank(like):
    return pl.pallas_call(
        blank_kernel,
        out_shape=jax.ShapeDtypeStruct(like.shape, like.dtype),
        out_specs=pl.BlockSpec(memory_space=pl.ANY),
        name="blank",
    )()


def local(
    normed, w_query, b_query, w_key, b_key, w_value, b_value, w_out, pool, page_table, lengths, plan
):
    pair_count = lax.axis_size("pair")
    tp_count = lax.axis_size("tp")
    requests = pair_count // 2
    head = w_key.shape[1]

    planned = plan.T
    partial, near, far, pieces = prepare(
        page_table, planned, normed, w_query, w_key, w_value, pool[0, 0], pair_count
    )
    bits = min(JOINT, requests)

    def tie(*values):
        return lax.optimization_barrier(values)

    def migrate(pages, members=range(requests)):
        return lax.ppermute(pages, "pair", [(r + requests, r) for r in members])

    either = lax.axis_index("rep") == 0

    def gather(values):
        return lax.all_to_all(values, "pair", split_axis=0, concat_axis=0, tiled=True)

    def choose(code, step, *values):
        members = [[r for r in range(requests) if code >> r % bits & 1] for code in range(1 << bits)]
        return lax.switch(code, [functools.partial(step, chosen) for chosen in members], *values)

    def some(members, pages):
        return migrate(pages, members) if members else blank(pages)

    def first_step(members, values, pages):
        return lax.cond(either, gather, gather, values), some(members, pages)

    def second_step(members, values, beside, pages):
        return gather(values), migrate(beside), some(members, pages)

    first = migrate(pieces[0])
    sums, far_pages = choose(far, first_step, partial, pieces[2])
    sums, first = tie(sums, first)
    second = migrate(tie(pieces[1], sums)[0])

    frequency = rope_base ** (-(jnp.arange(head // 2, dtype=jnp.float32) * 2.0 / head))
    steps = jnp.minimum(jnp.arange(8, dtype=jnp.int32), STEPS - 1)
    position = (lengths[:, None] + steps[None, :]).astype(jnp.float32)[..., None]
    angles = position * frequency
    cosine = jnp.cos(angles)
    sine = jnp.sin(angles)
    cosine = jnp.concatenate([cosine, cosine], -1)
    sine = jnp.concatenate([-sine, sine], -1)

    packed, new_pool, fixed, *later = attend(
        lengths,
        page_table,
        planned,
        sums,
        b_query.reshape(-1, head),
        b_key[None, :],
        b_value[None, :],
        cosine,
        sine,
        first,
        far_pages,
        pool[0, 0],
    )
    near, packed = tie(near, packed)
    parts, beside, near_pages = choose(near, second_step, packed, later[0], later[2])
    parts, second = tie(parts, second)
    third = migrate(tie(later[1], parts)[0])
    projected = project(parts, w_out, head)
    here = [second, beside, near_pages]
    starts = [FIRST, BESIDE_AT, NEAR_AT]
    new_pool = place(page_table, planned, lengths, here, starts, new_pool, fixed)
    if tp_count == 2:
        projected = projected + lax.ppermute(projected, "tp", [(0, 1), (1, 0)])
    else:
        projected = lax.psum(projected, "tp")
    third, projected = tie(third, projected)
    new_pool = place(page_table, planned, lengths, [third], [THIRD_AT], new_pool)
    return projected, new_pool[None, None]


def solution(mesh):
    return jax.shard_map(
        local,
        mesh=mesh,
        in_specs=(
            P(None, "rep", "pair"),
            P("pair", "tp"),
            P("tp"),
            P("pair", "tp"),
            P("tp"),
            P("pair", "tp"),
            P("tp"),
            P("tp", "pair"),
            P(("rep", "pair"), "tp", None, None, None),
            P(("rep", "pair"), None),
            P("rep"),
            P("rep", None),
        ),
        out_specs=(P(None, "rep", "pair"), P(("rep", "pair"), "tp", None, None, None)),
        check_vma=False,
    )
```

```python
import functools
import math

import jax
import jax.numpy as jnp
from jax import lax
from jax.experimental import pallas as pl
from jax.experimental.pallas import tpu as pltpu
from jax.sharding import PartitionSpec as P

PAGES_HALF = 384
STEPS = 2
SECTION = 64
MOVED_MAX = STEPS * SECTION
FIRST, SECOND, BESIDE, THIRD = 26, 30, 8, 10
NEAR, FAR = 26, 28
BESIDE_AT = FIRST + SECOND
THIRD_AT = BESIDE_AT + BESIDE
NEAR_AT = THIRD_AT + THIRD
FAR_AT = NEAR_AT + NEAR
PIECES = ((FIRST, SECOND), (FAR_AT, FAR))
LATER = ((BESIDE_AT, BESIDE), (THIRD_AT, THIRD), (NEAR_AT, NEAR))
JOINT = 4
CHUNKS = 8
NEG = -1e30

rope_base = 1000000.0

VMEM = pl.BlockSpec(memory_space=pltpu.VMEM)
SMEM = pl.BlockSpec(memory_space=pltpu.SMEM)
HBM = pl.BlockSpec(memory_space=pltpu.HBM)


def in_hbm(*arrays):
    return tuple(pltpu.with_memory_space_constraint(a, pltpu.HBM) for a in arrays)


def params(mib):
    return pltpu.CompilerParams(vmem_limit_bytes=mib * 1024 * 1024)


def moved_pages(plan, request):
    count = plan[0, request]
    for s in range(1, STEPS):
        count = count + plan[s, request]
    return count


def put_pages(table, count, parts, new_pool, sem):
    placed = jnp.int32(0)
    for low, pages in parts:
        here = jnp.clip(count - low, 0, pages.shape[0])

        def start(j, carry):
            slot = table[0, PAGES_HALF + low + j]
            pltpu.make_async_copy(pages.at[j], new_pool.at[slot], sem).start()
            return carry

        lax.fori_loop(0, here, start, 0)
        placed = placed + here

    def wait(j, carry):
        pltpu.make_async_copy(parts[0][1].at[0], new_pool.at[0], sem).wait()
        return carry

    lax.fori_loop(0, placed, wait, 0)


def collect_kernel(table_in, pool, piece, table, sem, page_sem):
    @pl.when(lax.axis_index("pair") >= lax.axis_size("pair") // 2)
    def _():
        table_copy = pltpu.make_async_copy(table_in, table, sem)
        table_copy.start()
        table_copy.wait()

        def start(j, carry):
            pltpu.make_async_copy(pool.at[table[0, j]], piece.at[j], page_sem).start()
            return carry

        lax.fori_loop(0, FIRST, start, 0, unroll=2)
        pltpu.make_async_copy(pool.at[pl.ds(0, FIRST)], piece, page_sem).wait()


def collect(table, pool):
    return pl.pallas_call(
        collect_kernel,
        out_shape=pltpu.VMEM((FIRST,) + pool.shape[1:], pool.dtype),
        in_specs=[HBM] * 2,
        out_specs=VMEM,
        scratch_shapes=[
            pltpu.SMEM(table.shape, table.dtype),
            pltpu.SemaphoreType.DMA,
            pltpu.SemaphoreType.DMA,
        ],
        compiler_params=params(16),
        name="collect",
    )(*in_hbm(table, pool))


def prepare_kernel(w_query, table_in, plan_in, normed_in, w_key, w_value, pool, partial, near, far, *refs):
    pieces, (table, plan, normed, weights, index_sems, sems, page_sems) = refs[:-7], refs[-7:]
    pairs = partial.shape[0]
    requests = pairs // 2
    head = w_key.shape[1]
    wide = w_query.shape[1]
    table_copy = pltpu.make_async_copy(table_in, table, index_sems.at[0])
    plan_copy = pltpu.make_async_copy(plan_in, plan, index_sems.at[1])
    table_copy.start()
    plan_copy.start()
    loads = [
        pltpu.make_async_copy(normed_in, normed, sems.at[0]),
        pltpu.make_async_copy(w_key, weights.at[:, :head], sems.at[1]),
        pltpu.make_async_copy(w_value, weights.at[:, head:], sems.at[2]),
    ]
    for copy in loads:
        copy.start()
    table_copy.wait()

    @pl.when(lax.axis_index("pair") >= requests)
    def _():
        for i, (low, size) in enumerate(PIECES):

            def start(j, carry):
                pltpu.make_async_copy(pool.at[table[0, low + j]], pieces[i].at[j], page_sems.at[i]).start()
                return carry

            lax.fori_loop(0, size, start, 0, unroll=2)

    plan_copy.wait()
    bits = min(JOINT, requests)
    for code, bound in ((near, NEAR_AT), (far, FAR_AT)):
        total = jnp.int32(0)
        for bit in range(bits):
            most = moved_pages(plan, bit)
            for r in range(bit + bits, requests, bits):
                most = jnp.maximum(most, moved_pages(plan, r))
            total = total + jnp.where(most > bound, 1 << bit, 0)
        code[0] = total
    for copy in loads:
        copy.wait()
    hidden = jnp.concatenate([normed[s].astype(jnp.float32) for s in range(STEPS)], 0).astype(jnp.bfloat16)
    query = jnp.dot(hidden, w_query[...], preferred_element_type=jnp.float32)
    rest = jnp.dot(hidden, weights[...], preferred_element_type=jnp.float32)
    for r in range(requests):
        lines = [slice(s * requests + r, s * requests + r + 1) for s in range(STEPS)]
        query_lines = jnp.concatenate([query[line] for line in lines], 0)
        rest_lines = jnp.concatenate([rest[line] for line in lines], 0)
        for p in range(r, pairs, requests):
            partial[p, :, :wide] = query_lines
            partial[p, :, wide:] = rest_lines

    @pl.when(lax.axis_index("pair") >= requests)
    def _():
        for i, (_, size) in enumerate(PIECES):
            pltpu.make_async_copy(pool.at[pl.ds(0, size)], pieces[i], page_sems.at[i]).wait()


def prepare(table, plan, normed, w_query, w_key, w_value, pool, pairs):
    page = pool.shape[1:]
    wide = w_query.shape[1] + 2 * w_key.shape[1]
    partial, near, far, *pieces = pl.pallas_call(
        prepare_kernel,
        out_shape=(jax.ShapeDtypeStruct((pairs, STEPS, wide), jnp.float32),)
        + (jax.ShapeDtypeStruct((1,), jnp.int32),) * 2
        + tuple(pltpu.VMEM((size,) + page, pool.dtype) for _, size in PIECES),
        in_specs=[VMEM] + [HBM] * 6,
        out_specs=(VMEM, SMEM, SMEM) + (VMEM,) * len(PIECES),
        scratch_shapes=[
            pltpu.SMEM(table.shape, table.dtype),
            pltpu.SMEM(plan.shape, plan.dtype),
            pltpu.VMEM(normed.shape, normed.dtype),
            pltpu.VMEM((w_key.shape[0], 2 * w_key.shape[1]), w_key.dtype),
            pltpu.SemaphoreType.DMA((2,)),
            pltpu.SemaphoreType.DMA((3,)),
            pltpu.SemaphoreType.DMA((len(PIECES),)),
        ],
        compiler_params=params(16),
        name="prepare",
    )(w_query, *in_hbm(table, plan, normed, w_key, w_value, pool))
    return partial, near.reshape(()), far.reshape(()), pieces


def page_order(table, slots):
    slot = lax.broadcasted_iota(jnp.int32, (slots, slots), 0)
    holds = jnp.where(slot == table, 1.0, 0.0).astype(jnp.bfloat16)
    index = lax.broadcasted_iota(jnp.int32, (8, slots), 1)
    digit = lax.broadcasted_iota(jnp.int32, (8, slots), 0)
    digits = jnp.where(digit == 0, index // 16, jnp.where(digit == 1, index % 16, 0))
    digits = digits.astype(jnp.float32).astype(jnp.bfloat16)
    return lax.dot_general(digits, holds, (((1,), (1,)), ((), ())), preferred_element_type=jnp.float32)


def attention_kernel(
    lengths, table_in, plan_in, sums, b_query, b_key, b_value, cosine, sine, early, far, pool,
    copies_out, new_pool, fixed, *refs
):
    pieces, refs = refs[: len(LATER)], refs[len(LATER) :]
    held, score, packed, table, slots_of, plan, sems, out_sems, send_sem, page_sem = refs
    slots, page_len, _ = held.shape
    per = slots // CHUNKS
    table_copy = pltpu.make_async_copy(table_in, table, sems.at[CHUNKS])
    table_copy.start()
    slots_copy = pltpu.make_async_copy(table_in, slots_of, sems.at[CHUNKS + 1])
    slots_copy.start()
    plan_copy = pltpu.make_async_copy(plan_in, plan, sems.at[CHUNKS + 2])
    plan_copy.start()
    copies = []
    for c in range(CHUNKS):
        part = pl.ds(c * per, per)
        copies.append(pltpu.make_async_copy(pool.at[part], held.at[part], sems.at[c]))
        copies[-1].start()
    requests = sums.shape[0] // 2
    group, head = b_query.shape
    rows = STEPS * group
    pair_index = lax.axis_index("pair")
    is_source = pair_index >= requests
    request = jnp.where(is_source, pair_index - requests, pair_index)
    half_tokens = PAGES_HALF * page_len
    limit = jnp.where(is_source, lengths[request] - half_tokens, half_tokens)

    blocks = CHUNKS // 2
    block = slots // blocks
    width = block * page_len
    table_copy.wait()
    digits = page_order(table[...], slots)
    digits = jnp.concatenate(
        [digits[d : d + 1, c * block : (c + 1) * block] for d in range(2) for c in range(blocks)], 0
    ).astype(jnp.bfloat16)
    spread = lax.broadcasted_iota(jnp.int32, (block, width), 1) // page_len
    spread = jnp.where(spread == lax.broadcasted_iota(jnp.int32, (block, width), 0), 1.0, 0.0)
    digits = jnp.dot(digits, spread.astype(jnp.bfloat16), preferred_element_type=jnp.float32)
    tokens = (digits[:blocks] * 16.0 + digits[blocks:]).astype(jnp.int32) * page_len
    tokens = tokens + lax.broadcasted_iota(jnp.int32, (blocks, width), 1) % page_len

    total = sums[0]
    for p in range(1, sums.shape[0]):
        total = total + sums[p]
    query = jnp.concatenate(
        [total[s : s + 1, h * head : (h + 1) * head] for s in range(STEPS) for h in range(group)], 0
    )
    query = query + jnp.concatenate([b_query[...]] * STEPS, 0)
    cos_new = cosine[request]
    sin_new = sine[request]
    row = lax.broadcasted_iota(jnp.int32, (rows, head), 0)
    cos_rows = jnp.where(row < group, cos_new[0:1], cos_new[1:2])
    sin_rows = jnp.where(row < group, sin_new[0:1], sin_new[1:2])
    query = (query * cos_rows + pltpu.roll(query, head // 2, 1) * sin_rows).astype(jnp.bfloat16)
    key_new = total[:, group * head : (group + 1) * head] + b_key[...]
    key_new = jnp.concatenate([key_new, jnp.zeros((8 - STEPS, head), jnp.float32)], 0)
    key_new = key_new * cos_new + pltpu.roll(key_new, head // 2, 1) * sin_new
    key_new = key_new.astype(jnp.bfloat16).astype(jnp.float32)
    value_new = total[:, (group + 1) * head :] + b_value[...]
    value_new = value_new.astype(jnp.bfloat16).astype(jnp.float32)
    scale = 1.0 / math.sqrt(head)

    column = lax.broadcasted_iota(jnp.int32, (rows, 1), 0)
    query_wide = query.astype(jnp.float32)
    fresh = []
    for s in range(STEPS):
        dots = jnp.sum(query_wide * key_new[s : s + 1], 1, keepdims=True) * scale
        seen = jnp.logical_and(is_source, column >= s * group)
        fresh.append((jnp.where(seen, dots, NEG), seen))
    row_max = jnp.maximum(fresh[0][0], fresh[1][0])

    stores = []
    for c in range(blocks):
        for i in range(c * CHUNKS // blocks, (c + 1) * CHUNKS // blocks):
            copies[i].wait()
            part = pl.ds(i * per, per)
            stores.append(pltpu.make_async_copy(held.at[part], new_pool.at[part], out_sems.at[i]))
            stores[-1].start()
        keys = held[c * block : (c + 1) * block, :, :head].reshape(width, head)
        part = lax.dot_general(query, keys, (((1,), (1,)), ((), ())), preferred_element_type=jnp.float32)
        part = jnp.where(tokens[c : c + 1] < limit, part * scale, NEG)
        score[:, c * width : (c + 1) * width] = part
        row_max = jnp.maximum(row_max, jnp.max(part, 1, keepdims=True))
    row_sum = jnp.zeros((rows, 1), jnp.float32)
    out = jnp.zeros((rows, head), jnp.float32)
    for s in range(STEPS):
        weight = jnp.where(fresh[s][1], jnp.exp(fresh[s][0] - row_max), 0.0)
        row_sum = row_sum + weight
        out = out + weight.astype(jnp.bfloat16).astype(jnp.float32) * value_new[s : s + 1]
    for c in range(blocks):
        weight = jnp.exp(score[:, c * width : (c + 1) * width] - row_max)
        weight = jnp.where(tokens[c : c + 1] < limit, weight, 0.0)
        row_sum = row_sum + jnp.sum(weight, 1, keepdims=True)
        values = held[c * block : (c + 1) * block, :, head:].reshape(width, head)
        out = out + jnp.dot(weight.astype(jnp.bfloat16), values, preferred_element_type=jnp.float32)

    diagonal = lax.broadcasted_iota(jnp.int32, (rows, head), 1) == row
    for i in range(rows):
        packed[:, i * head : (i + 1) * head] = out[i : i + 1]
    shifted = lax.broadcasted_iota(jnp.int32, (rows, head), 1) == row + rows
    packed[:, rows * head :] = jnp.sum(
        jnp.where(diagonal, row_max, 0.0) + jnp.where(shifted, row_sum, 0.0), 0, keepdims=True
    )
    sends = [
        pltpu.make_async_copy(packed, copies_out.at[p], send_sem.at[p]) for p in range(copies_out.shape[0])
    ]
    for send in sends:
        send.start()

    slots_copy.wait()

    @pl.when(is_source)
    def _():
        for piece, (low, size) in zip(pieces, LATER):

            def take(j, carry):
                piece[j] = held[slots_of[0, low + j]]
                return carry

            lax.fori_loop(0, size, take, 0)
        page_row = lax.broadcasted_iota(jnp.int32, (page_len, 2 * head), 0)
        entries = jnp.concatenate([key_new[:STEPS], value_new], 1)
        offsets = [limit + s for s in range(STEPS)]
        homes = [slots_of[0, offset // page_len] for offset in offsets]
        for i, slot in enumerate((homes[0], homes[-1])):
            page = held[slot].astype(jnp.float32)
            for s, offset in enumerate(offsets):
                here = jnp.logical_and(homes[s] == slot, page_row == offset % page_len)
                page = jnp.where(here, entries[s : s + 1], page)
            fixed[i] = page.astype(held.dtype)

    plan_copy.wait()
    for store in stores:
        store.wait()

    @pl.when(jnp.logical_not(is_source))
    def _():
        put_pages(slots_of, moved_pages(plan, request), [(0, early), (FAR_AT, far)], new_pool, page_sem)

    for send in sends:
        send.wait()


def attend(lengths, table, plan, sums, b_query, b_key, b_value, cosine, sine, early, far, pool):
    group, head = b_query.shape
    rows = STEPS * group
    page = pool.shape[1:]
    return pl.pallas_call(
        attention_kernel,
        out_shape=(
            pltpu.HBM((sums.shape[0], 1, (rows + 1) * head), jnp.float32),
            pltpu.HBM(pool.shape, pool.dtype),
            jax.ShapeDtypeStruct((2,) + page, pool.dtype),
        )
        + tuple(pltpu.VMEM((size,) + page, pool.dtype) for _, size in LATER),
        in_specs=[SMEM, HBM, HBM] + [VMEM] * 8 + [HBM],
        out_specs=(HBM, HBM, VMEM) + (VMEM,) * len(LATER),
        scratch_shapes=[
            pltpu.VMEM(pool.shape, pool.dtype),
            pltpu.VMEM((rows, pool.shape[0] * pool.shape[1]), jnp.float32),
            pltpu.VMEM((1, (rows + 1) * head), jnp.float32),
            pltpu.VMEM(table.shape, table.dtype),
            pltpu.SMEM(table.shape, table.dtype),
            pltpu.SMEM(plan.shape, plan.dtype),
            pltpu.SemaphoreType.DMA((CHUNKS + 3,)),
            pltpu.SemaphoreType.DMA((CHUNKS,)),
            pltpu.SemaphoreType.DMA((sums.shape[0],)),
            pltpu.SemaphoreType.DMA,
        ],
        compiler_params=params(24),
        name="attend",
    )(
        lengths, *in_hbm(table, plan), sums, b_query, b_key, b_value, cosine, sine, early, far, *in_hbm(pool)
    )


def project_kernel(head, parts, w_out, out):
    pairs, _, width = parts.shape
    rows = width // head - 1
    group = rows // STEPS
    requests = pairs // 2
    lane = lax.broadcasted_iota(jnp.int32, (rows, head), 1)
    row = lax.broadcasted_iota(jnp.int32, (rows, head), 0)

    def column(part, shift):
        line = parts[part, :, rows * head :]
        return jnp.sum(jnp.where(lane == row + shift, line, 0.0), 1, keepdims=True)

    lines = [[] for _ in range(STEPS)]
    for r in range(requests):
        tops = [column(part, 0) for part in (r, r + requests)]
        sums = [column(part, rows) for part in (r, r + requests)]
        top = jnp.maximum(*tops)
        weights = [jnp.exp(one - top) for one in tops]
        total = weights[0] * sums[0] + weights[1] * sums[1]
        shares = [weight / total for weight in weights]
        for s in range(STEPS):
            heads = []
            for i in range(s * group, (s + 1) * group):
                here = slice(i * head, (i + 1) * head)
                heads.append(
                    shares[0][i : i + 1] * parts[r, :, here] + shares[1][i : i + 1] * parts[r + requests, :, here]
                )
            lines[s].append(jnp.concatenate(heads, 1))
    attended = jnp.concatenate(sum(lines, []), 0).astype(jnp.bfloat16)
    result = jnp.dot(attended, w_out[...], preferred_element_type=jnp.float32)
    for s in range(STEPS):
        out[s] = result[s * requests : (s + 1) * requests]


def project(parts, w_out, head):
    return pl.pallas_call(
        functools.partial(project_kernel, head),
        out_shape=jax.ShapeDtypeStruct((STEPS, parts.shape[0] // 2, w_out.shape[1]), jnp.float32),
        in_specs=[VMEM, VMEM],
        out_specs=VMEM,
        compiler_params=params(16),
        name="project",
    )(parts, w_out)


def place_kernel(table_in, plan_in, lengths, *refs, starts, patch):
    parts, (base, new_pool, table, plan, sems, sem) = refs[:-6], refs[-6:]
    del base
    pair_index = lax.axis_index("pair")
    requests = lengths.shape[0]
    table_copy = pltpu.make_async_copy(table_in, table, sems.at[0])
    plan_copy = pltpu.make_async_copy(plan_in, plan, sems.at[1])
    table_copy.start()
    plan_copy.start()
    table_copy.wait()
    plan_copy.wait()

    @pl.when(pair_index < requests)
    def _():
        put_pages(table, moved_pages(plan, pair_index), list(zip(starts, parts)), new_pool, sem)

    if patch:

        @pl.when(pair_index >= requests)
        def _():
            page_len = new_pool.shape[1]
            first = lengths[pair_index - requests] - PAGES_HALF * page_len
            for i, offset in enumerate((first, first + STEPS - 1)):
                slot = table[0, offset // page_len]
                copy = pltpu.make_async_copy(parts[-1].at[i], new_pool.at[slot], sem)
                copy.start()
                copy.wait()


def place(table, plan, lengths, parts, starts, base, fixed=None):
    patch = fixed is not None
    parts = list(parts) + [fixed] * patch
    return pl.pallas_call(
        functools.partial(place_kernel, starts=starts, patch=patch),
        out_shape=pltpu.HBM(base.shape, base.dtype),
        in_specs=[HBM, HBM, SMEM] + [VMEM] * len(parts) + [HBM],
        out_specs=HBM,
        scratch_shapes=[
            pltpu.SMEM(table.shape, table.dtype),
            pltpu.SMEM(plan.shape, plan.dtype),
            pltpu.SemaphoreType.DMA((2,)),
            pltpu.SemaphoreType.DMA,
        ],
        input_output_aliases={3 + len(parts): 0},
        compiler_params=params(16),
        name="place",
    )(*in_hbm(table, plan), lengths, *parts, *in_hbm(base))


def blank_kernel(out):
    del out


def blank(like):
    return pl.pallas_call(
        blank_kernel,
        out_shape=jax.ShapeDtypeStruct(like.shape, like.dtype),
        out_specs=pl.BlockSpec(memory_space=pl.ANY),
        name="blank",
    )()


def local(
    normed, w_query, b_query, w_key, b_key, w_value, b_value, w_out, pool, page_table, lengths, plan
):
    pair_count = lax.axis_size("pair")
    tp_count = lax.axis_size("tp")
    requests = pair_count // 2
    head = w_key.shape[1]

    planned = plan.T
    opening = collect(page_table, pool[0, 0])
    partial, near, far, pieces = prepare(
        page_table, planned, normed, w_query, w_key, w_value, pool[0, 0], pair_count
    )
    bits = min(JOINT, requests)

    def tie(*values):
        return lax.optimization_barrier(values)

    def migrate(pages, members=range(requests)):
        return lax.ppermute(pages, "pair", [(r + requests, r) for r in members])

    either = lax.axis_index("rep") == 0

    def gather(values):
        return lax.all_to_all(values, "pair", split_axis=0, concat_axis=0, tiled=True)

    def choose(code, step, *values):
        members = [[r for r in range(requests) if code >> r % bits & 1] for code in range(1 << bits)]
        return lax.switch(code, [functools.partial(step, chosen) for chosen in members], *values)

    def some(members, pages):
        return migrate(pages, members) if members else blank(pages)

    def first_step(members, values, pages):
        return lax.cond(either, gather, gather, values), some(members, pages)

    def second_step(members, values, beside, pages):
        return gather(values), migrate(beside), some(members, pages)

    first = migrate(opening)
    sums, far_pages = choose(far, first_step, partial, pieces[1])
    sums, first = tie(sums, first)
    second = migrate(tie(pieces[0], sums)[0])

    frequency = rope_base ** (-(jnp.arange(head // 2, dtype=jnp.float32) * 2.0 / head))
    steps = jnp.minimum(jnp.arange(8, dtype=jnp.int32), STEPS - 1)
    position = (lengths[:, None] + steps[None, :]).astype(jnp.float32)[..., None]
    angles = position * frequency
    cosine = jnp.cos(angles)
    sine = jnp.sin(angles)
    cosine = jnp.concatenate([cosine, cosine], -1)
    sine = jnp.concatenate([-sine, sine], -1)

    packed, new_pool, fixed, *later = attend(
        lengths,
        page_table,
        planned,
        sums,
        b_query.reshape(-1, head),
        b_key[None, :],
        b_value[None, :],
        cosine,
        sine,
        first,
        far_pages,
        pool[0, 0],
    )
    near, packed = tie(near, packed)
    parts, beside, near_pages = choose(near, second_step, packed, later[0], later[2])
    parts, second = tie(parts, second)
    third = migrate(tie(later[1], parts)[0])
    projected = project(parts, w_out, head)
    here = [second, beside, near_pages]
    starts = [FIRST, BESIDE_AT, NEAR_AT]
    new_pool = place(page_table, planned, lengths, here, starts, new_pool, fixed)
    if tp_count == 2:
        projected = projected + lax.ppermute(projected, "tp", [(0, 1), (1, 0)])
    else:
        projected = lax.psum(projected, "tp")
    third, projected = tie(third, projected)
    new_pool = place(page_table, planned, lengths, [third], [THIRD_AT], new_pool)
    return projected, new_pool[None, None]


def solution(mesh):
    return jax.shard_map(
        local,
        mesh=mesh,
        in_specs=(
            P(None, "rep", "pair"),
            P("pair", "tp"),
            P("tp"),
            P("pair", "tp"),
            P("tp"),
            P("pair", "tp"),
            P("tp"),
            P("tp", "pair"),
            P(("rep", "pair"), "tp", None, None, None),
            P(("rep", "pair"), None),
            P("rep"),
            P("rep", None),
        ),
        out_specs=(P(None, "rep", "pair"), P(("rep", "pair"), "tp", None, None, None)),
        check_vma=False,
    )
```

```python
import functools
import math

import jax
import jax.numpy as jnp
from jax import lax
from jax.experimental import pallas as pl
from jax.experimental.pallas import tpu as pltpu
from jax.sharding import PartitionSpec as P

PAGES_HALF = 384
STEPS = 2
SECTION = 64
MOVED_MAX = STEPS * SECTION
FIRST, SECOND, BESIDE, THIRD = 26, 30, 8, 10
NEAR, FAR = 26, 28
BESIDE_AT = FIRST + SECOND
THIRD_AT = BESIDE_AT + BESIDE
NEAR_AT = THIRD_AT + THIRD
FAR_AT = NEAR_AT + NEAR
PIECES = ((FIRST, SECOND), (FAR_AT, FAR))
LATER = ((BESIDE_AT, BESIDE), (THIRD_AT, THIRD), (NEAR_AT, NEAR))
JOINT = 4
CHUNKS = 8
NEG = -1e30

rope_base = 1000000.0

VMEM = pl.BlockSpec(memory_space=pltpu.VMEM)
SMEM = pl.BlockSpec(memory_space=pltpu.SMEM)
HBM = pl.BlockSpec(memory_space=pltpu.HBM)


def in_hbm(*arrays):
    return tuple(pltpu.with_memory_space_constraint(a, pltpu.HBM) for a in arrays)


def params(mib):
    return pltpu.CompilerParams(vmem_limit_bytes=mib * 1024 * 1024)


def moved_pages(plan, request):
    count = plan[0, request]
    for s in range(1, STEPS):
        count = count + plan[s, request]
    return count


def put_pages(table, count, parts, new_pool, sem):
    placed = jnp.int32(0)
    for low, pages in parts:
        here = jnp.clip(count - low, 0, pages.shape[0])

        def start(j, carry):
            slot = table[0, PAGES_HALF + low + j]
            pltpu.make_async_copy(pages.at[j], new_pool.at[slot], sem).start()
            return carry

        lax.fori_loop(0, here, start, 0)
        placed = placed + here

    def wait(j, carry):
        pltpu.make_async_copy(parts[0][1].at[0], new_pool.at[0], sem).wait()
        return carry

    lax.fori_loop(0, placed, wait, 0)


def collect_kernel(table_in, pool, piece, table, sem, page_sem):
    @pl.when(lax.axis_index("pair") >= lax.axis_size("pair") // 2)
    def _():
        table_copy = pltpu.make_async_copy(table_in, table, sem)
        table_copy.start()
        table_copy.wait()

        def start(j, carry):
            pltpu.make_async_copy(pool.at[table[0, j]], piece.at[j], page_sem).start()
            return carry

        lax.fori_loop(0, FIRST, start, 0, unroll=2)
        pltpu.make_async_copy(pool.at[pl.ds(0, FIRST)], piece, page_sem).wait()


def collect(table, pool):
    return pl.pallas_call(
        collect_kernel,
        out_shape=pltpu.VMEM((FIRST,) + pool.shape[1:], pool.dtype),
        in_specs=[HBM] * 2,
        out_specs=VMEM,
        scratch_shapes=[
            pltpu.SMEM(table.shape, table.dtype),
            pltpu.SemaphoreType.DMA,
            pltpu.SemaphoreType.DMA,
        ],
        compiler_params=params(16),
        name="collect",
    )(*in_hbm(table, pool))


def prepare_kernel(normed, w_query, w_key, w_value, table_in, plan_in, pool, partial, near, far, *refs):
    pieces, (table, plan, index_sems, page_sems) = refs[:-4], refs[-4:]
    pairs = partial.shape[0]
    requests = pairs // 2
    table_copy = pltpu.make_async_copy(table_in, table, index_sems.at[0])
    plan_copy = pltpu.make_async_copy(plan_in, plan, index_sems.at[1])
    table_copy.start()
    plan_copy.start()
    table_copy.wait()

    @pl.when(lax.axis_index("pair") >= requests)
    def _():
        for i, (low, size) in enumerate(PIECES):

            def start(j, carry):
                pltpu.make_async_copy(pool.at[table[0, low + j]], pieces[i].at[j], page_sems.at[i]).start()
                return carry

            lax.fori_loop(0, size, start, 0, unroll=2)

    plan_copy.wait()
    bits = min(JOINT, requests)
    for code, bound in ((near, NEAR_AT), (far, FAR_AT)):
        total = jnp.int32(0)
        for bit in range(bits):
            most = moved_pages(plan, bit)
            for r in range(bit + bits, requests, bits):
                most = jnp.maximum(most, moved_pages(plan, r))
            total = total + jnp.where(most > bound, 1 << bit, 0)
        code[0] = total
    hidden = jnp.concatenate([normed[s].astype(jnp.float32) for s in range(STEPS)], 0).astype(jnp.bfloat16)
    results = []
    low = 0
    for weight in (w_query, w_key, w_value):
        results.append((low, jnp.dot(hidden, weight[...], preferred_element_type=jnp.float32)))
        low += weight.shape[1]
    for r in range(requests):
        lines = [slice(s * requests + r, s * requests + r + 1) for s in range(STEPS)]
        for low, result in results:
            both = jnp.concatenate([result[line] for line in lines], 0)
            for p in range(r, pairs, requests):
                partial[p, :, low : low + result.shape[1]] = both

    @pl.when(lax.axis_index("pair") >= requests)
    def _():
        for i, (_, size) in enumerate(PIECES):
            pltpu.make_async_copy(pool.at[pl.ds(0, size)], pieces[i], page_sems.at[i]).wait()


def prepare(table, plan, normed, w_query, w_key, w_value, pool, pairs):
    page = pool.shape[1:]
    wide = w_query.shape[1] + 2 * w_key.shape[1]
    partial, near, far, *pieces = pl.pallas_call(
        prepare_kernel,
        out_shape=(jax.ShapeDtypeStruct((pairs, STEPS, wide), jnp.float32),)
        + (jax.ShapeDtypeStruct((1,), jnp.int32),) * 2
        + tuple(pltpu.VMEM((size,) + page, pool.dtype) for _, size in PIECES),
        in_specs=[VMEM] * 4 + [HBM] * 3,
        out_specs=(VMEM, SMEM, SMEM) + (VMEM,) * len(PIECES),
        scratch_shapes=[
            pltpu.SMEM(table.shape, table.dtype),
            pltpu.SMEM(plan.shape, plan.dtype),
            pltpu.SemaphoreType.DMA((2,)),
            pltpu.SemaphoreType.DMA((len(PIECES),)),
        ],
        compiler_params=params(16),
        name="prepare",
    )(normed, w_query, w_key, w_value, *in_hbm(table, plan, pool))
    return partial, near.reshape(()), far.reshape(()), pieces


def page_order(table, slots):
    slot = lax.broadcasted_iota(jnp.int32, (slots, slots), 0)
    holds = jnp.where(slot == table, 1.0, 0.0).astype(jnp.bfloat16)
    index = lax.broadcasted_iota(jnp.int32, (8, slots), 1)
    digit = lax.broadcasted_iota(jnp.int32, (8, slots), 0)
    digits = jnp.where(digit == 0, index // 16, jnp.where(digit == 1, index % 16, 0))
    digits = digits.astype(jnp.float32).astype(jnp.bfloat16)
    return lax.dot_general(digits, holds, (((1,), (1,)), ((), ())), preferred_element_type=jnp.float32)


def attention_kernel(
    lengths, table_in, plan_in, sums, b_query, b_key, b_value, cosine, sine, early, far, pool,
    copies_out, new_pool, fixed, *refs
):
    pieces, refs = refs[: len(LATER)], refs[len(LATER) :]
    held, score, packed, table, slots_of, plan, sems, out_sems, send_sem, page_sem = refs
    slots, page_len, _ = held.shape
    per = slots // CHUNKS
    table_copy = pltpu.make_async_copy(table_in, table, sems.at[CHUNKS])
    table_copy.start()
    slots_copy = pltpu.make_async_copy(table_in, slots_of, sems.at[CHUNKS + 1])
    slots_copy.start()
    plan_copy = pltpu.make_async_copy(plan_in, plan, sems.at[CHUNKS + 2])
    plan_copy.start()
    copies = []
    for c in range(CHUNKS):
        part = pl.ds(c * per, per)
        copies.append(pltpu.make_async_copy(pool.at[part], held.at[part], sems.at[c]))
        copies[-1].start()
    requests = sums.shape[0] // 2
    group, head = b_query.shape
    rows = STEPS * group
    pair_index = lax.axis_index("pair")
    is_source = pair_index >= requests
    request = jnp.where(is_source, pair_index - requests, pair_index)
    half_tokens = PAGES_HALF * page_len
    limit = jnp.where(is_source, lengths[request] - half_tokens, half_tokens)

    blocks = CHUNKS // 2
    block = slots // blocks
    width = block * page_len
    table_copy.wait()
    digits = page_order(table[...], slots)
    digits = jnp.concatenate(
        [digits[d : d + 1, c * block : (c + 1) * block] for d in range(2) for c in range(blocks)], 0
    ).astype(jnp.bfloat16)
    spread = lax.broadcasted_iota(jnp.int32, (block, width), 1) // page_len
    spread = jnp.where(spread == lax.broadcasted_iota(jnp.int32, (block, width), 0), 1.0, 0.0)
    digits = jnp.dot(digits, spread.astype(jnp.bfloat16), preferred_element_type=jnp.float32)
    tokens = (digits[:blocks] * 16.0 + digits[blocks:]).astype(jnp.int32) * page_len
    tokens = tokens + lax.broadcasted_iota(jnp.int32, (blocks, width), 1) % page_len

    total = sums[0]
    for p in range(1, sums.shape[0]):
        total = total + sums[p]
    query = jnp.concatenate(
        [total[s : s + 1, h * head : (h + 1) * head] for s in range(STEPS) for h in range(group)], 0
    )
    query = query + jnp.concatenate([b_query[...]] * STEPS, 0)
    cos_new = cosine[request]
    sin_new = sine[request]
    row = lax.broadcasted_iota(jnp.int32, (rows, head), 0)
    cos_rows = jnp.where(row < group, cos_new[0:1], cos_new[1:2])
    sin_rows = jnp.where(row < group, sin_new[0:1], sin_new[1:2])
    query = (query * cos_rows + pltpu.roll(query, head // 2, 1) * sin_rows).astype(jnp.bfloat16)
    key_new = total[:, group * head : (group + 1) * head] + b_key[...]
    key_new = jnp.concatenate([key_new, jnp.zeros((8 - STEPS, head), jnp.float32)], 0)
    key_new = key_new * cos_new + pltpu.roll(key_new, head // 2, 1) * sin_new
    key_new = key_new.astype(jnp.bfloat16).astype(jnp.float32)
    value_new = total[:, (group + 1) * head :] + b_value[...]
    value_new = value_new.astype(jnp.bfloat16).astype(jnp.float32)
    scale = 1.0 / math.sqrt(head)

    column = lax.broadcasted_iota(jnp.int32, (rows, 1), 0)
    query_wide = query.astype(jnp.float32)
    fresh = []
    for s in range(STEPS):
        dots = jnp.sum(query_wide * key_new[s : s + 1], 1, keepdims=True) * scale
        seen = jnp.logical_and(is_source, column >= s * group)
        fresh.append((jnp.where(seen, dots, NEG), seen))
    row_max = jnp.maximum(fresh[0][0], fresh[1][0])

    stores = []
    for c in range(blocks):
        for i in range(c * CHUNKS // blocks, (c + 1) * CHUNKS // blocks):
            copies[i].wait()
            part = pl.ds(i * per, per)
            stores.append(pltpu.make_async_copy(held.at[part], new_pool.at[part], out_sems.at[i]))
            stores[-1].start()
        keys = held[c * block : (c + 1) * block, :, :head].reshape(width, head)
        part = lax.dot_general(query, keys, (((1,), (1,)), ((), ())), preferred_element_type=jnp.float32)
        part = jnp.where(tokens[c : c + 1] < limit, part * scale, NEG)
        score[:, c * width : (c + 1) * width] = part
        row_max = jnp.maximum(row_max, jnp.max(part, 1, keepdims=True))
    row_sum = jnp.zeros((rows, 1), jnp.float32)
    out = jnp.zeros((rows, head), jnp.float32)
    for s in range(STEPS):
        weight = jnp.where(fresh[s][1], jnp.exp(fresh[s][0] - row_max), 0.0)
        row_sum = row_sum + weight
        out = out + weight.astype(jnp.bfloat16).astype(jnp.float32) * value_new[s : s + 1]
    for c in range(blocks):
        weight = jnp.exp(score[:, c * width : (c + 1) * width] - row_max)
        weight = jnp.where(tokens[c : c + 1] < limit, weight, 0.0)
        row_sum = row_sum + jnp.sum(weight, 1, keepdims=True)
        values = held[c * block : (c + 1) * block, :, head:].reshape(width, head)
        out = out + jnp.dot(weight.astype(jnp.bfloat16), values, preferred_element_type=jnp.float32)

    diagonal = lax.broadcasted_iota(jnp.int32, (rows, head), 1) == row
    for i in range(rows):
        packed[:, i * head : (i + 1) * head] = out[i : i + 1]
    shifted = lax.broadcasted_iota(jnp.int32, (rows, head), 1) == row + rows
    packed[:, rows * head :] = jnp.sum(
        jnp.where(diagonal, row_max, 0.0) + jnp.where(shifted, row_sum, 0.0), 0, keepdims=True
    )
    sends = [
        pltpu.make_async_copy(packed, copies_out.at[p], send_sem.at[p]) for p in range(copies_out.shape[0])
    ]
    for send in sends:
        send.start()

    slots_copy.wait()

    @pl.when(is_source)
    def _():
        for piece, (low, size) in zip(pieces, LATER):

            def take(j, carry):
                piece[j] = held[slots_of[0, low + j]]
                return carry

            lax.fori_loop(0, size, take, 0)
        page_row = lax.broadcasted_iota(jnp.int32, (page_len, 2 * head), 0)
        entries = jnp.concatenate([key_new[:STEPS], value_new], 1)
        offsets = [limit + s for s in range(STEPS)]
        homes = [slots_of[0, offset // page_len] for offset in offsets]
        for i, slot in enumerate((homes[0], homes[-1])):
            page = held[slot].astype(jnp.float32)
            for s, offset in enumerate(offsets):
                here = jnp.logical_and(homes[s] == slot, page_row == offset % page_len)
                page = jnp.where(here, entries[s : s + 1], page)
            fixed[i] = page.astype(held.dtype)

    plan_copy.wait()
    for store in stores:
        store.wait()

    @pl.when(jnp.logical_not(is_source))
    def _():
        put_pages(slots_of, moved_pages(plan, request), [(0, early), (FAR_AT, far)], new_pool, page_sem)

    for send in sends:
        send.wait()


def attend(lengths, table, plan, sums, b_query, b_key, b_value, cosine, sine, early, far, pool):
    group, head = b_query.shape
    rows = STEPS * group
    page = pool.shape[1:]
    return pl.pallas_call(
        attention_kernel,
        out_shape=(
            pltpu.HBM((sums.shape[0], 1, (rows + 1) * head), jnp.float32),
            pltpu.HBM(pool.shape, pool.dtype),
            jax.ShapeDtypeStruct((2,) + page, pool.dtype),
        )
        + tuple(pltpu.VMEM((size,) + page, pool.dtype) for _, size in LATER),
        in_specs=[SMEM, HBM, HBM] + [VMEM] * 8 + [HBM],
        out_specs=(HBM, HBM, VMEM) + (VMEM,) * len(LATER),
        scratch_shapes=[
            pltpu.VMEM(pool.shape, pool.dtype),
            pltpu.VMEM((rows, pool.shape[0] * pool.shape[1]), jnp.float32),
            pltpu.VMEM((1, (rows + 1) * head), jnp.float32),
            pltpu.VMEM(table.shape, table.dtype),
            pltpu.SMEM(table.shape, table.dtype),
            pltpu.SMEM(plan.shape, plan.dtype),
            pltpu.SemaphoreType.DMA((CHUNKS + 3,)),
            pltpu.SemaphoreType.DMA((CHUNKS,)),
            pltpu.SemaphoreType.DMA((sums.shape[0],)),
            pltpu.SemaphoreType.DMA,
        ],
        compiler_params=params(24),
        name="attend",
    )(
        lengths, *in_hbm(table, plan), sums, b_query, b_key, b_value, cosine, sine, early, far, *in_hbm(pool)
    )


def project_kernel(head, parts, w_out, out):
    pairs, _, width = parts.shape
    rows = width // head - 1
    group = rows // STEPS
    requests = pairs // 2
    lane = lax.broadcasted_iota(jnp.int32, (rows, head), 1)
    row = lax.broadcasted_iota(jnp.int32, (rows, head), 0)

    def column(part, shift):
        line = parts[part, :, rows * head :]
        return jnp.sum(jnp.where(lane == row + shift, line, 0.0), 1, keepdims=True)

    lines = [[] for _ in range(STEPS)]
    for r in range(requests):
        tops = [column(part, 0) for part in (r, r + requests)]
        sums = [column(part, rows) for part in (r, r + requests)]
        top = jnp.maximum(*tops)
        weights = [jnp.exp(one - top) for one in tops]
        total = weights[0] * sums[0] + weights[1] * sums[1]
        shares = [weight / total for weight in weights]
        for s in range(STEPS):
            heads = []
            for i in range(s * group, (s + 1) * group):
                here = slice(i * head, (i + 1) * head)
                heads.append(
                    shares[0][i : i + 1] * parts[r, :, here] + shares[1][i : i + 1] * parts[r + requests, :, here]
                )
            lines[s].append(jnp.concatenate(heads, 1))
    attended = jnp.concatenate(sum(lines, []), 0).astype(jnp.bfloat16)
    result = jnp.dot(attended, w_out[...], preferred_element_type=jnp.float32)
    for s in range(STEPS):
        out[s] = result[s * requests : (s + 1) * requests]


def project(parts, w_out, head):
    return pl.pallas_call(
        functools.partial(project_kernel, head),
        out_shape=jax.ShapeDtypeStruct((STEPS, parts.shape[0] // 2, w_out.shape[1]), jnp.float32),
        in_specs=[VMEM, VMEM],
        out_specs=VMEM,
        compiler_params=params(16),
        name="project",
    )(parts, w_out)


def place_kernel(table, plan, lengths, *refs, starts, patch):
    parts, (base, new_pool, sem) = refs[:-3], refs[-3:]
    del base
    pair_index = lax.axis_index("pair")
    requests = lengths.shape[0]

    @pl.when(pair_index < requests)
    def _():
        put_pages(table, moved_pages(plan, pair_index), list(zip(starts, parts)), new_pool, sem)

    if patch:

        @pl.when(pair_index >= requests)
        def _():
            page_len = new_pool.shape[1]
            first = lengths[pair_index - requests] - PAGES_HALF * page_len
            for i, offset in enumerate((first, first + STEPS - 1)):
                slot = table[0, offset // page_len]
                copy = pltpu.make_async_copy(parts[-1].at[i], new_pool.at[slot], sem)
                copy.start()
                copy.wait()


def place(table, plan, lengths, parts, starts, base, fixed=None):
    patch = fixed is not None
    parts = list(parts) + [fixed] * patch
    return pl.pallas_call(
        functools.partial(place_kernel, starts=starts, patch=patch),
        out_shape=pltpu.HBM(base.shape, base.dtype),
        in_specs=[SMEM] * 3 + [VMEM] * len(parts) + [HBM],
        out_specs=HBM,
        scratch_shapes=[
            pltpu.SemaphoreType.DMA,
        ],
        input_output_aliases={3 + len(parts): 0},
        compiler_params=params(16),
        name="place",
    )(table, plan, lengths, *parts, *in_hbm(base))


def blank_kernel(out):
    del out


def blank(like):
    return pl.pallas_call(
        blank_kernel,
        out_shape=jax.ShapeDtypeStruct(like.shape, like.dtype),
        out_specs=pl.BlockSpec(memory_space=pl.ANY),
        name="blank",
    )()


def local(
    normed, w_query, b_query, w_key, b_key, w_value, b_value, w_out, pool, page_table, lengths, plan
):
    pair_count = lax.axis_size("pair")
    tp_count = lax.axis_size("tp")
    requests = pair_count // 2
    head = w_key.shape[1]

    planned = plan.T
    opening = collect(page_table, pool[0, 0])
    partial, near, far, pieces = prepare(
        page_table, planned, normed, w_query, w_key, w_value, pool[0, 0], pair_count
    )
    bits = min(JOINT, requests)

    def tie(*values):
        return lax.optimization_barrier(values)

    def migrate(pages, members=range(requests)):
        return lax.ppermute(pages, "pair", [(r + requests, r) for r in members])

    either = lax.axis_index("rep") == 0

    def gather(values):
        return lax.all_to_all(values, "pair", split_axis=0, concat_axis=0, tiled=True)

    def choose(code, step, *values):
        members = [[r for r in range(requests) if code >> r % bits & 1] for code in range(1 << bits)]
        return lax.switch(code, [functools.partial(step, chosen) for chosen in members], *values)

    def some(members, pages):
        return migrate(pages, members) if members else blank(pages)

    def first_step(members, values, pages):
        return lax.cond(either, gather, gather, values), some(members, pages)

    def second_step(members, values, beside, pages):
        return gather(values), migrate(beside), some(members, pages)

    first = migrate(opening)
    sums, far_pages = choose(far, first_step, partial, pieces[1])
    sums, first = tie(sums, first)
    second = migrate(tie(pieces[0], sums)[0])

    frequency = rope_base ** (-(jnp.arange(head // 2, dtype=jnp.float32) * 2.0 / head))
    steps = jnp.minimum(jnp.arange(8, dtype=jnp.int32), STEPS - 1)
    position = (lengths[:, None] + steps[None, :]).astype(jnp.float32)[..., None]
    angles = position * frequency
    cosine = jnp.cos(angles)
    sine = jnp.sin(angles)
    cosine = jnp.concatenate([cosine, cosine], -1)
    sine = jnp.concatenate([-sine, sine], -1)

    packed, new_pool, fixed, *later = attend(
        lengths,
        page_table,
        planned,
        sums,
        b_query.reshape(-1, head),
        b_key[None, :],
        b_value[None, :],
        cosine,
        sine,
        first,
        far_pages,
        pool[0, 0],
    )
    near, packed = tie(near, packed)
    parts, beside, near_pages = choose(near, second_step, packed, later[0], later[2])
    parts, second = tie(parts, second)
    third = migrate(tie(later[1], parts)[0])
    projected = project(parts, w_out, head)
    here = [second, beside, near_pages]
    starts = [FIRST, BESIDE_AT, NEAR_AT]
    new_pool = place(page_table, planned, lengths, here, starts, new_pool, fixed)
    if tp_count == 2:
        projected = projected + lax.ppermute(projected, "tp", [(0, 1), (1, 0)])
    else:
        projected = lax.psum(projected, "tp")
    third, projected = tie(third, projected)
    new_pool = place(page_table, planned, lengths, [third], [THIRD_AT], new_pool)
    return projected, new_pool[None, None]


def solution(mesh):
    return jax.shard_map(
        local,
        mesh=mesh,
        in_specs=(
            P(None, "rep", "pair"),
            P("pair", "tp"),
            P("tp"),
            P("pair", "tp"),
            P("tp"),
            P("pair", "tp"),
            P("tp"),
            P("tp", "pair"),
            P(("rep", "pair"), "tp", None, None, None),
            P(("rep", "pair"), None),
            P("rep"),
            P("rep", None),
        ),
        out_specs=(P(None, "rep", "pair"), P(("rep", "pair"), "tp", None, None, None)),
        check_vma=False,
    )
```

```python
import functools
import math

import jax
import jax.numpy as jnp
from jax import lax
from jax.experimental import pallas as pl
from jax.experimental.pallas import tpu as pltpu
from jax.sharding import PartitionSpec as P

PAGES_HALF = 384
STEPS = 2
SECTION = 64
MOVED_MAX = STEPS * SECTION
FIRST, SECOND, BESIDE, THIRD = 26, 30, 8, 10
NEAR, FAR = 26, 28
BESIDE_AT = FIRST + SECOND
THIRD_AT = BESIDE_AT + BESIDE
NEAR_AT = THIRD_AT + THIRD
FAR_AT = NEAR_AT + NEAR
PIECES = ((FIRST, SECOND), (FAR_AT, FAR))
LATER = ((BESIDE_AT, BESIDE), (THIRD_AT, THIRD), (NEAR_AT, NEAR))
JOINT = 4
CHUNKS = 8
NEG = -1e30

rope_base = 1000000.0

VMEM = pl.BlockSpec(memory_space=pltpu.VMEM)
SMEM = pl.BlockSpec(memory_space=pltpu.SMEM)
HBM = pl.BlockSpec(memory_space=pltpu.HBM)


def in_hbm(*arrays):
    return tuple(pltpu.with_memory_space_constraint(a, pltpu.HBM) for a in arrays)


def params(mib):
    return pltpu.CompilerParams(vmem_limit_bytes=mib * 1024 * 1024)


def moved_pages(plan, request):
    count = plan[0, request]
    for s in range(1, STEPS):
        count = count + plan[s, request]
    return count


def put_pages(table, count, parts, new_pool, sem):
    placed = jnp.int32(0)
    for low, pages in parts:
        here = jnp.clip(count - low, 0, pages.shape[0])

        def start(j, carry):
            slot = table[0, PAGES_HALF + low + j]
            pltpu.make_async_copy(pages.at[j], new_pool.at[slot], sem).start()
            return carry

        lax.fori_loop(0, here, start, 0)
        placed = placed + here

    def wait(j, carry):
        pltpu.make_async_copy(parts[0][1].at[0], new_pool.at[0], sem).wait()
        return carry

    lax.fori_loop(0, placed, wait, 0)


def collect_kernel(table_in, pool, piece, table, sem, page_sem):
    @pl.when(lax.axis_index("pair") >= lax.axis_size("pair") // 2)
    def _():
        table_copy = pltpu.make_async_copy(table_in, table, sem)
        table_copy.start()
        table_copy.wait()

        def start(j, carry):
            pltpu.make_async_copy(pool.at[table[0, j]], piece.at[j], page_sem).start()
            return carry

        lax.fori_loop(0, FIRST, start, 0, unroll=2)
        pltpu.make_async_copy(pool.at[pl.ds(0, FIRST)], piece, page_sem).wait()


def collect(table, pool):
    return pl.pallas_call(
        collect_kernel,
        out_shape=pltpu.VMEM((FIRST,) + pool.shape[1:], pool.dtype),
        in_specs=[HBM] * 2,
        out_specs=VMEM,
        scratch_shapes=[
            pltpu.SMEM(table.shape, table.dtype),
            pltpu.SemaphoreType.DMA,
            pltpu.SemaphoreType.DMA,
        ],
        compiler_params=params(16),
        name="collect",
    )(*in_hbm(table, pool))


def prepare_kernel(w_query, table, plan, normed_in, w_key, w_value, pool, partial, near, far, *refs):
    pieces, (normed, weights, sems, page_sems) = refs[:-4], refs[-4:]
    pairs = partial.shape[0]
    requests = pairs // 2
    head = w_key.shape[1]
    wide = w_query.shape[1]
    loads = [
        pltpu.make_async_copy(normed_in, normed, sems.at[0]),
        pltpu.make_async_copy(w_key, weights.at[:, :head], sems.at[1]),
        pltpu.make_async_copy(w_value, weights.at[:, head:], sems.at[2]),
    ]
    for copy in loads:
        copy.start()

    @pl.when(lax.axis_index("pair") >= requests)
    def _():
        for i, (low, size) in enumerate(PIECES):

            def start(j, carry):
                pltpu.make_async_copy(pool.at[table[0, low + j]], pieces[i].at[j], page_sems.at[i]).start()
                return carry

            lax.fori_loop(0, size, start, 0, unroll=2)

    bits = min(JOINT, requests)
    for code, bound in ((near, NEAR_AT), (far, FAR_AT)):
        total = jnp.int32(0)
        for bit in range(bits):
            most = moved_pages(plan, bit)
            for r in range(bit + bits, requests, bits):
                most = jnp.maximum(most, moved_pages(plan, r))
            total = total + jnp.where(most > bound, 1 << bit, 0)
        code[0] = total
    for copy in loads:
        copy.wait()
    hidden = jnp.concatenate([normed[s].astype(jnp.float32) for s in range(STEPS)], 0).astype(jnp.bfloat16)
    query = jnp.dot(hidden, w_query[...], preferred_element_type=jnp.float32)
    rest = jnp.dot(hidden, weights[...], preferred_element_type=jnp.float32)
    for r in range(requests):
        lines = [slice(s * requests + r, s * requests + r + 1) for s in range(STEPS)]
        query_lines = jnp.concatenate([query[line] for line in lines], 0)
        rest_lines = jnp.concatenate([rest[line] for line in lines], 0)
        for p in range(r, pairs, requests):
            partial[p, :, :wide] = query_lines
            partial[p, :, wide:] = rest_lines

    @pl.when(lax.axis_index("pair") >= requests)
    def _():
        for i, (_, size) in enumerate(PIECES):
            pltpu.make_async_copy(pool.at[pl.ds(0, size)], pieces[i], page_sems.at[i]).wait()


def prepare(table, plan, normed, w_query, w_key, w_value, pool, pairs):
    page = pool.shape[1:]
    wide = w_query.shape[1] + 2 * w_key.shape[1]
    partial, near, far, *pieces = pl.pallas_call(
        prepare_kernel,
        out_shape=(jax.ShapeDtypeStruct((pairs, STEPS, wide), jnp.float32),)
        + (jax.ShapeDtypeStruct((1,), jnp.int32),) * 2
        + tuple(pltpu.VMEM((size,) + page, pool.dtype) for _, size in PIECES),
        in_specs=[VMEM, SMEM, SMEM] + [HBM] * 4,
        out_specs=(VMEM, SMEM, SMEM) + (VMEM,) * len(PIECES),
        scratch_shapes=[
            pltpu.VMEM(normed.shape, normed.dtype),
            pltpu.VMEM((w_key.shape[0], 2 * w_key.shape[1]), w_key.dtype),
            pltpu.SemaphoreType.DMA((3,)),
            pltpu.SemaphoreType.DMA((len(PIECES),)),
        ],
        compiler_params=params(16),
        name="prepare",
    )(w_query, table, plan, *in_hbm(normed, w_key, w_value, pool))
    return partial, near.reshape(()), far.reshape(()), pieces


def page_order(table, slots):
    slot = lax.broadcasted_iota(jnp.int32, (slots, slots), 0)
    holds = jnp.where(slot == table, 1.0, 0.0).astype(jnp.bfloat16)
    index = lax.broadcasted_iota(jnp.int32, (8, slots), 1)
    digit = lax.broadcasted_iota(jnp.int32, (8, slots), 0)
    digits = jnp.where(digit == 0, index // 16, jnp.where(digit == 1, index % 16, 0))
    digits = digits.astype(jnp.float32).astype(jnp.bfloat16)
    return lax.dot_general(digits, holds, (((1,), (1,)), ((), ())), preferred_element_type=jnp.float32)


def attention_kernel(
    lengths, table_in, plan_in, sums, b_query, b_key, b_value, cosine, sine, early, far, pool,
    copies_out, new_pool, fixed, *refs
):
    pieces, refs = refs[: len(LATER)], refs[len(LATER) :]
    held, score, packed, table, slots_of, plan, sems, out_sems, send_sem, page_sem = refs
    slots, page_len, _ = held.shape
    per = slots // CHUNKS
    table_copy = pltpu.make_async_copy(table_in, table, sems.at[CHUNKS])
    table_copy.start()
    slots_copy = pltpu.make_async_copy(table_in, slots_of, sems.at[CHUNKS + 1])
    slots_copy.start()
    plan_copy = pltpu.make_async_copy(plan_in, plan, sems.at[CHUNKS + 2])
    plan_copy.start()
    copies = []
    for c in range(CHUNKS):
        part = pl.ds(c * per, per)
        copies.append(pltpu.make_async_copy(pool.at[part], held.at[part], sems.at[c]))
        copies[-1].start()
    requests = sums.shape[0] // 2
    group, head = b_query.shape
    rows = STEPS * group
    pair_index = lax.axis_index("pair")
    is_source = pair_index >= requests
    request = jnp.where(is_source, pair_index - requests, pair_index)
    half_tokens = PAGES_HALF * page_len
    limit = jnp.where(is_source, lengths[request] - half_tokens, half_tokens)

    blocks = CHUNKS // 2
    block = slots // blocks
    width = block * page_len
    table_copy.wait()
    digits = page_order(table[...], slots)
    digits = jnp.concatenate(
        [digits[d : d + 1, c * block : (c + 1) * block] for d in range(2) for c in range(blocks)], 0
    ).astype(jnp.bfloat16)
    spread = lax.broadcasted_iota(jnp.int32, (block, width), 1) // page_len
    spread = jnp.where(spread == lax.broadcasted_iota(jnp.int32, (block, width), 0), 1.0, 0.0)
    digits = jnp.dot(digits, spread.astype(jnp.bfloat16), preferred_element_type=jnp.float32)
    tokens = (digits[:blocks] * 16.0 + digits[blocks:]).astype(jnp.int32) * page_len
    tokens = tokens + lax.broadcasted_iota(jnp.int32, (blocks, width), 1) % page_len

    total = sums[0]
    for p in range(1, sums.shape[0]):
        total = total + sums[p]
    query = jnp.concatenate(
        [total[s : s + 1, h * head : (h + 1) * head] for s in range(STEPS) for h in range(group)], 0
    )
    query = query + jnp.concatenate([b_query[...]] * STEPS, 0)
    cos_new = cosine[request]
    sin_new = sine[request]
    row = lax.broadcasted_iota(jnp.int32, (rows, head), 0)
    cos_rows = jnp.where(row < group, cos_new[0:1], cos_new[1:2])
    sin_rows = jnp.where(row < group, sin_new[0:1], sin_new[1:2])
    query = (query * cos_rows + pltpu.roll(query, head // 2, 1) * sin_rows).astype(jnp.bfloat16)
    key_new = total[:, group * head : (group + 1) * head] + b_key[...]
    key_new = jnp.concatenate([key_new, jnp.zeros((8 - STEPS, head), jnp.float32)], 0)
    key_new = key_new * cos_new + pltpu.roll(key_new, head // 2, 1) * sin_new
    key_new = key_new.astype(jnp.bfloat16).astype(jnp.float32)
    value_new = total[:, (group + 1) * head :] + b_value[...]
    value_new = value_new.astype(jnp.bfloat16).astype(jnp.float32)
    scale = 1.0 / math.sqrt(head)

    column = lax.broadcasted_iota(jnp.int32, (rows, 1), 0)
    query_wide = query.astype(jnp.float32)
    fresh = []
    for s in range(STEPS):
        dots = jnp.sum(query_wide * key_new[s : s + 1], 1, keepdims=True) * scale
        seen = jnp.logical_and(is_source, column >= s * group)
        fresh.append((jnp.where(seen, dots, NEG), seen))
    row_max = jnp.maximum(fresh[0][0], fresh[1][0])

    stores = []
    for c in range(blocks):
        for i in range(c * CHUNKS // blocks, (c + 1) * CHUNKS // blocks):
            copies[i].wait()
            part = pl.ds(i * per, per)
            stores.append(pltpu.make_async_copy(held.at[part], new_pool.at[part], out_sems.at[i]))
            stores[-1].start()
        keys = held[c * block : (c + 1) * block, :, :head].reshape(width, head)
        part = lax.dot_general(query, keys, (((1,), (1,)), ((), ())), preferred_element_type=jnp.float32)
        part = jnp.where(tokens[c : c + 1] < limit, part * scale, NEG)
        score[:, c * width : (c + 1) * width] = part
        row_max = jnp.maximum(row_max, jnp.max(part, 1, keepdims=True))
    row_sum = jnp.zeros((rows, 1), jnp.float32)
    out = jnp.zeros((rows, head), jnp.float32)
    for s in range(STEPS):
        weight = jnp.where(fresh[s][1], jnp.exp(fresh[s][0] - row_max), 0.0)
        row_sum = row_sum + weight
        out = out + weight.astype(jnp.bfloat16).astype(jnp.float32) * value_new[s : s + 1]
    for c in range(blocks):
        weight = jnp.exp(score[:, c * width : (c + 1) * width] - row_max)
        weight = jnp.where(tokens[c : c + 1] < limit, weight, 0.0)
        row_sum = row_sum + jnp.sum(weight, 1, keepdims=True)
        values = held[c * block : (c + 1) * block, :, head:].reshape(width, head)
        out = out + jnp.dot(weight.astype(jnp.bfloat16), values, preferred_element_type=jnp.float32)

    diagonal = lax.broadcasted_iota(jnp.int32, (rows, head), 1) == row
    for i in range(rows):
        packed[:, i * head : (i + 1) * head] = out[i : i + 1]
    shifted = lax.broadcasted_iota(jnp.int32, (rows, head), 1) == row + rows
    packed[:, rows * head :] = jnp.sum(
        jnp.where(diagonal, row_max, 0.0) + jnp.where(shifted, row_sum, 0.0), 0, keepdims=True
    )
    sends = [
        pltpu.make_async_copy(packed, copies_out.at[p], send_sem.at[p]) for p in range(copies_out.shape[0])
    ]
    for send in sends:
        send.start()

    slots_copy.wait()

    @pl.when(is_source)
    def _():
        for piece, (low, size) in zip(pieces, LATER):

            def take(j, carry):
                piece[j] = held[slots_of[0, low + j]]
                return carry

            lax.fori_loop(0, size, take, 0)
        page_row = lax.broadcasted_iota(jnp.int32, (page_len, 2 * head), 0)
        entries = jnp.concatenate([key_new[:STEPS], value_new], 1)
        offsets = [limit + s for s in range(STEPS)]
        homes = [slots_of[0, offset // page_len] for offset in offsets]
        for i, slot in enumerate((homes[0], homes[-1])):
            page = held[slot].astype(jnp.float32)
            for s, offset in enumerate(offsets):
                here = jnp.logical_and(homes[s] == slot, page_row == offset % page_len)
                page = jnp.where(here, entries[s : s + 1], page)
            fixed[i] = page.astype(held.dtype)

    plan_copy.wait()
    for store in stores:
        store.wait()

    @pl.when(jnp.logical_not(is_source))
    def _():
        put_pages(slots_of, moved_pages(plan, request), [(0, early), (FAR_AT, far)], new_pool, page_sem)

    for send in sends:
        send.wait()


def attend(lengths, table, plan, sums, b_query, b_key, b_value, cosine, sine, early, far, pool):
    group, head = b_query.shape
    rows = STEPS * group
    page = pool.shape[1:]
    return pl.pallas_call(
        attention_kernel,
        out_shape=(
            pltpu.HBM((sums.shape[0], 1, (rows + 1) * head), jnp.float32),
            pltpu.HBM(pool.shape, pool.dtype),
            jax.ShapeDtypeStruct((2,) + page, pool.dtype),
        )
        + tuple(pltpu.VMEM((size,) + page, pool.dtype) for _, size in LATER),
        in_specs=[SMEM, HBM, HBM] + [VMEM] * 8 + [HBM],
        out_specs=(HBM, HBM, VMEM) + (VMEM,) * len(LATER),
        scratch_shapes=[
            pltpu.VMEM(pool.shape, pool.dtype),
            pltpu.VMEM((rows, pool.shape[0] * pool.shape[1]), jnp.float32),
            pltpu.VMEM((1, (rows + 1) * head), jnp.float32),
            pltpu.VMEM(table.shape, table.dtype),
            pltpu.SMEM(table.shape, table.dtype),
            pltpu.SMEM(plan.shape, plan.dtype),
            pltpu.SemaphoreType.DMA((CHUNKS + 3,)),
            pltpu.SemaphoreType.DMA((CHUNKS,)),
            pltpu.SemaphoreType.DMA((sums.shape[0],)),
            pltpu.SemaphoreType.DMA,
        ],
        compiler_params=params(24),
        name="attend",
    )(
        lengths, *in_hbm(table, plan), sums, b_query, b_key, b_value, cosine, sine, early, far, *in_hbm(pool)
    )


def project_kernel(head, parts, w_out, out):
    pairs, _, width = parts.shape
    rows = width // head - 1
    group = rows // STEPS
    requests = pairs // 2
    lane = lax.broadcasted_iota(jnp.int32, (rows, head), 1)
    row = lax.broadcasted_iota(jnp.int32, (rows, head), 0)

    def column(part, shift):
        line = parts[part, :, rows * head :]
        return jnp.sum(jnp.where(lane == row + shift, line, 0.0), 1, keepdims=True)

    lines = [[] for _ in range(STEPS)]
    for r in range(requests):
        tops = [column(part, 0) for part in (r, r + requests)]
        sums = [column(part, rows) for part in (r, r + requests)]
        top = jnp.maximum(*tops)
        weights = [jnp.exp(one - top) for one in tops]
        total = weights[0] * sums[0] + weights[1] * sums[1]
        shares = [weight / total for weight in weights]
        for s in range(STEPS):
            heads = []
            for i in range(s * group, (s + 1) * group):
                here = slice(i * head, (i + 1) * head)
                heads.append(
                    shares[0][i : i + 1] * parts[r, :, here] + shares[1][i : i + 1] * parts[r + requests, :, here]
                )
            lines[s].append(jnp.concatenate(heads, 1))
    attended = jnp.concatenate(sum(lines, []), 0).astype(jnp.bfloat16)
    result = jnp.dot(attended, w_out[...], preferred_element_type=jnp.float32)
    for s in range(STEPS):
        out[s] = result[s * requests : (s + 1) * requests]


def project(parts, w_out, head):
    return pl.pallas_call(
        functools.partial(project_kernel, head),
        out_shape=jax.ShapeDtypeStruct((STEPS, parts.shape[0] // 2, w_out.shape[1]), jnp.float32),
        in_specs=[VMEM, VMEM],
        out_specs=VMEM,
        compiler_params=params(16),
        name="project",
    )(parts, w_out)


def place_kernel(table, plan, lengths, *refs, starts, patch):
    parts, (base, new_pool, sem) = refs[:-3], refs[-3:]
    del base
    pair_index = lax.axis_index("pair")
    requests = lengths.shape[0]

    @pl.when(pair_index < requests)
    def _():
        put_pages(table, moved_pages(plan, pair_index), list(zip(starts, parts)), new_pool, sem)

    if patch:

        @pl.when(pair_index >= requests)
        def _():
            page_len = new_pool.shape[1]
            first = lengths[pair_index - requests] - PAGES_HALF * page_len
            for i, offset in enumerate((first, first + STEPS - 1)):
                slot = table[0, offset // page_len]
                copy = pltpu.make_async_copy(parts[-1].at[i], new_pool.at[slot], sem)
                copy.start()
                copy.wait()


def place(table, plan, lengths, parts, starts, base, fixed=None):
    patch = fixed is not None
    parts = list(parts) + [fixed] * patch
    return pl.pallas_call(
        functools.partial(place_kernel, starts=starts, patch=patch),
        out_shape=pltpu.HBM(base.shape, base.dtype),
        in_specs=[SMEM] * 3 + [VMEM] * len(parts) + [HBM],
        out_specs=HBM,
        scratch_shapes=[
            pltpu.SemaphoreType.DMA,
        ],
        input_output_aliases={3 + len(parts): 0},
        compiler_params=params(16),
        name="place",
    )(table, plan, lengths, *parts, *in_hbm(base))


def blank_kernel(out):
    del out


def blank(like):
    return pl.pallas_call(
        blank_kernel,
        out_shape=jax.ShapeDtypeStruct(like.shape, like.dtype),
        out_specs=pl.BlockSpec(memory_space=pl.ANY),
        name="blank",
    )()


def local(
    normed, w_query, b_query, w_key, b_key, w_value, b_value, w_out, pool, page_table, lengths, plan
):
    pair_count = lax.axis_size("pair")
    tp_count = lax.axis_size("tp")
    requests = pair_count // 2
    head = w_key.shape[1]

    planned = plan.T
    opening = collect(page_table, pool[0, 0])
    partial, near, far, pieces = prepare(
        page_table, planned, normed, w_query, w_key, w_value, pool[0, 0], pair_count
    )
    bits = min(JOINT, requests)

    def tie(*values):
        return lax.optimization_barrier(values)

    def migrate(pages, members=range(requests)):
        return lax.ppermute(pages, "pair", [(r + requests, r) for r in members])

    either = lax.axis_index("rep") == 0

    def gather(values):
        return lax.all_to_all(values, "pair", split_axis=0, concat_axis=0, tiled=True)

    def choose(code, step, *values):
        members = [[r for r in range(requests) if code >> r % bits & 1] for code in range(1 << bits)]
        return lax.switch(code, [functools.partial(step, chosen) for chosen in members], *values)

    def some(members, pages):
        return migrate(pages, members) if members else blank(pages)

    def first_step(members, values, pages):
        return lax.cond(either, gather, gather, values), some(members, pages)

    def second_step(members, values, beside, pages):
        return gather(values), migrate(beside), some(members, pages)

    first = migrate(opening)
    sums, far_pages = choose(far, first_step, partial, pieces[1])
    sums, first = tie(sums, first)
    second = migrate(tie(pieces[0], sums)[0])

    frequency = rope_base ** (-(jnp.arange(head // 2, dtype=jnp.float32) * 2.0 / head))
    steps = jnp.minimum(jnp.arange(8, dtype=jnp.int32), STEPS - 1)
    position = (lengths[:, None] + steps[None, :]).astype(jnp.float32)[..., None]
    angles = position * frequency
    cosine = jnp.cos(angles)
    sine = jnp.sin(angles)
    cosine = jnp.concatenate([cosine, cosine], -1)
    sine = jnp.concatenate([-sine, sine], -1)

    packed, new_pool, fixed, *later = attend(
        lengths,
        page_table,
        planned,
        sums,
        b_query.reshape(-1, head),
        b_key[None, :],
        b_value[None, :],
        cosine,
        sine,
        first,
        far_pages,
        pool[0, 0],
    )
    near, packed = tie(near, packed)
    parts, beside, near_pages = choose(near, second_step, packed, later[0], later[2])
    parts, second = tie(parts, second)
    third = migrate(tie(later[1], parts)[0])
    projected = project(parts, w_out, head)
    here = [second, beside, near_pages]
    starts = [FIRST, BESIDE_AT, NEAR_AT]
    new_pool = place(page_table, planned, lengths, here, starts, new_pool, fixed)
    if tp_count == 2:
        projected = projected + lax.ppermute(projected, "tp", [(0, 1), (1, 0)])
    else:
        projected = lax.psum(projected, "tp")
    third, projected = tie(third, projected)
    new_pool = place(page_table, planned, lengths, [third], [THIRD_AT], new_pool)
    return projected, new_pool[None, None]


def solution(mesh):
    return jax.shard_map(
        local,
        mesh=mesh,
        in_specs=(
            P(None, "rep", "pair"),
            P("pair", "tp"),
            P("tp"),
            P("pair", "tp"),
            P("tp"),
            P("pair", "tp"),
            P("tp"),
            P("tp", "pair"),
            P(("rep", "pair"), "tp", None, None, None),
            P(("rep", "pair"), None),
            P("rep"),
            P("rep", None),
        ),
        out_specs=(P(None, "rep", "pair"), P(("rep", "pair"), "tp", None, None, None)),
        check_vma=False,
    )
```

```python
import functools
import math

import jax
import jax.numpy as jnp
from jax import lax
from jax.experimental import pallas as pl
from jax.experimental.pallas import tpu as pltpu
from jax.sharding import PartitionSpec as P

PAGES_HALF = 384
STEPS = 2
SECTION = 64
MOVED_MAX = STEPS * SECTION
FIRST, SECOND, BESIDE, THIRD = 26, 32, 9, 7
NEAR, FAR = 26, 28
BESIDE_AT = FIRST + SECOND
THIRD_AT = BESIDE_AT + BESIDE
NEAR_AT = THIRD_AT + THIRD
FAR_AT = NEAR_AT + NEAR
PIECES = ((FIRST, SECOND), (FAR_AT, FAR))
LATER = ((BESIDE_AT, BESIDE), (THIRD_AT, THIRD), (NEAR_AT, NEAR))
JOINT = 4
CHUNKS = 8
NEG = -1e30

rope_base = 1000000.0

VMEM = pl.BlockSpec(memory_space=pltpu.VMEM)
SMEM = pl.BlockSpec(memory_space=pltpu.SMEM)
HBM = pl.BlockSpec(memory_space=pltpu.HBM)


def in_hbm(*arrays):
    return tuple(pltpu.with_memory_space_constraint(a, pltpu.HBM) for a in arrays)


def params(mib):
    return pltpu.CompilerParams(vmem_limit_bytes=mib * 1024 * 1024)


def moved_pages(plan, request):
    count = plan[0, request]
    for s in range(1, STEPS):
        count = count + plan[s, request]
    return count


def put_pages(table, count, parts, new_pool, sem):
    placed = jnp.int32(0)
    for low, pages in parts:
        here = jnp.clip(count - low, 0, pages.shape[0])

        def start(j, carry):
            slot = table[0, PAGES_HALF + low + j]
            pltpu.make_async_copy(pages.at[j], new_pool.at[slot], sem).start()
            return carry

        lax.fori_loop(0, here, start, 0)
        placed = placed + here

    def wait(j, carry):
        pltpu.make_async_copy(parts[0][1].at[0], new_pool.at[0], sem).wait()
        return carry

    lax.fori_loop(0, placed, wait, 0)


def collect_kernel(table_in, pool, piece, table, sem, page_sem):
    @pl.when(lax.axis_index("pair") >= lax.axis_size("pair") // 2)
    def _():
        table_copy = pltpu.make_async_copy(table_in, table, sem)
        table_copy.start()
        table_copy.wait()

        def start(j, carry):
            pltpu.make_async_copy(pool.at[table[0, j]], piece.at[j], page_sem).start()
            return carry

        lax.fori_loop(0, FIRST, start, 0, unroll=2)
        pltpu.make_async_copy(pool.at[pl.ds(0, FIRST)], piece, page_sem).wait()


def collect(table, pool):
    return pl.pallas_call(
        collect_kernel,
        out_shape=pltpu.VMEM((FIRST,) + pool.shape[1:], pool.dtype),
        in_specs=[HBM] * 2,
        out_specs=VMEM,
        scratch_shapes=[
            pltpu.SMEM(table.shape, table.dtype),
            pltpu.SemaphoreType.DMA,
            pltpu.SemaphoreType.DMA,
        ],
        compiler_params=params(16),
        name="collect",
    )(*in_hbm(table, pool))


def prepare_kernel(w_query, table_in, plan_in, normed_in, w_key, w_value, pool, partial, near, far, *refs):
    pieces, (table, plan, normed, weights, index_sems, sems, page_sems) = refs[:-7], refs[-7:]
    pairs = partial.shape[0]
    requests = pairs // 2
    head = w_key.shape[1]
    wide = w_query.shape[1]
    table_copy = pltpu.make_async_copy(table_in, table, index_sems.at[0])
    plan_copy = pltpu.make_async_copy(plan_in, plan, index_sems.at[1])
    table_copy.start()
    plan_copy.start()
    loads = [
        pltpu.make_async_copy(normed_in, normed, sems.at[0]),
        pltpu.make_async_copy(w_key, weights.at[:, :head], sems.at[1]),
        pltpu.make_async_copy(w_value, weights.at[:, head:], sems.at[2]),
    ]
    for copy in loads:
        copy.start()
    table_copy.wait()

    @pl.when(lax.axis_index("pair") >= requests)
    def _():
        for i, (low, size) in enumerate(PIECES):

            def start(j, carry):
                pltpu.make_async_copy(pool.at[table[0, low + j]], pieces[i].at[j], page_sems.at[i]).start()
                return carry

            lax.fori_loop(0, size, start, 0, unroll=2)

    plan_copy.wait()
    bits = min(JOINT, requests)
    for code, bound in ((near, NEAR_AT), (far, FAR_AT)):
        total = jnp.int32(0)
        for bit in range(bits):
            most = moved_pages(plan, bit)
            for r in range(bit + bits, requests, bits):
                most = jnp.maximum(most, moved_pages(plan, r))
            total = total + jnp.where(most > bound, 1 << bit, 0)
        code[0] = total
    for copy in loads:
        copy.wait()
    hidden = jnp.concatenate([normed[s].astype(jnp.float32) for s in range(STEPS)], 0).astype(jnp.bfloat16)
    query = jnp.dot(hidden, w_query[...], preferred_element_type=jnp.float32)
    rest = jnp.dot(hidden, weights[...], preferred_element_type=jnp.float32)
    for r in range(requests):
        lines = [slice(s * requests + r, s * requests + r + 1) for s in range(STEPS)]
        query_lines = jnp.concatenate([query[line] for line in lines], 0)
        rest_lines = jnp.concatenate([rest[line] for line in lines], 0)
        for p in range(r, pairs, requests):
            partial[p, :, :wide] = query_lines
            partial[p, :, wide:] = rest_lines

    @pl.when(lax.axis_index("pair") >= requests)
    def _():
        for i, (_, size) in enumerate(PIECES):
            pltpu.make_async_copy(pool.at[pl.ds(0, size)], pieces[i], page_sems.at[i]).wait()


def prepare(table, plan, normed, w_query, w_key, w_value, pool, pairs):
    page = pool.shape[1:]
    wide = w_query.shape[1] + 2 * w_key.shape[1]
    partial, near, far, *pieces = pl.pallas_call(
        prepare_kernel,
        out_shape=(jax.ShapeDtypeStruct((pairs, STEPS, wide), jnp.float32),)
        + (jax.ShapeDtypeStruct((1,), jnp.int32),) * 2
        + tuple(pltpu.VMEM((size,) + page, pool.dtype) for _, size in PIECES),
        in_specs=[VMEM] + [HBM] * 6,
        out_specs=(VMEM, SMEM, SMEM) + (VMEM,) * len(PIECES),
        scratch_shapes=[
            pltpu.SMEM(table.shape, table.dtype),
            pltpu.SMEM(plan.shape, plan.dtype),
            pltpu.VMEM(normed.shape, normed.dtype),
            pltpu.VMEM((w_key.shape[0], 2 * w_key.shape[1]), w_key.dtype),
            pltpu.SemaphoreType.DMA((2,)),
            pltpu.SemaphoreType.DMA((3,)),
            pltpu.SemaphoreType.DMA((len(PIECES),)),
        ],
        compiler_params=params(16),
        name="prepare",
    )(w_query, *in_hbm(table, plan, normed, w_key, w_value, pool))
    return partial, near.reshape(()), far.reshape(()), pieces


def page_order(table, slots):
    slot = lax.broadcasted_iota(jnp.int32, (slots, slots), 0)
    holds = jnp.where(slot == table, 1.0, 0.0).astype(jnp.bfloat16)
    index = lax.broadcasted_iota(jnp.int32, (8, slots), 1)
    digit = lax.broadcasted_iota(jnp.int32, (8, slots), 0)
    digits = jnp.where(digit == 0, index // 16, jnp.where(digit == 1, index % 16, 0))
    digits = digits.astype(jnp.float32).astype(jnp.bfloat16)
    return lax.dot_general(digits, holds, (((1,), (1,)), ((), ())), preferred_element_type=jnp.float32)


def attention_kernel(
    lengths, table_in, plan_in, sums, b_query, b_key, b_value, cosine, sine, early, far, pool,
    copies_out, new_pool, fixed, *refs
):
    pieces, refs = refs[: len(LATER)], refs[len(LATER) :]
    held, score, packed, table, slots_of, plan, sems, out_sems, send_sem, page_sem = refs
    slots, page_len, _ = held.shape
    per = slots // CHUNKS
    table_copy = pltpu.make_async_copy(table_in, table, sems.at[CHUNKS])
    table_copy.start()
    slots_copy = pltpu.make_async_copy(table_in, slots_of, sems.at[CHUNKS + 1])
    slots_copy.start()
    plan_copy = pltpu.make_async_copy(plan_in, plan, sems.at[CHUNKS + 2])
    plan_copy.start()
    copies = []
    for c in range(CHUNKS):
        part = pl.ds(c * per, per)
        copies.append(pltpu.make_async_copy(pool.at[part], held.at[part], sems.at[c]))
        copies[-1].start()
    requests = sums.shape[0] // 2
    group, head = b_query.shape
    rows = STEPS * group
    pair_index = lax.axis_index("pair")
    is_source = pair_index >= requests
    request = jnp.where(is_source, pair_index - requests, pair_index)
    half_tokens = PAGES_HALF * page_len
    limit = jnp.where(is_source, lengths[request] - half_tokens, half_tokens)

    blocks = CHUNKS // 2
    block = slots // blocks
    width = block * page_len
    table_copy.wait()
    digits = page_order(table[...], slots)
    digits = jnp.concatenate(
        [digits[d : d + 1, c * block : (c + 1) * block] for d in range(2) for c in range(blocks)], 0
    ).astype(jnp.bfloat16)
    spread = lax.broadcasted_iota(jnp.int32, (block, width), 1) // page_len
    spread = jnp.where(spread == lax.broadcasted_iota(jnp.int32, (block, width), 0), 1.0, 0.0)
    digits = jnp.dot(digits, spread.astype(jnp.bfloat16), preferred_element_type=jnp.float32)
    tokens = (digits[:blocks] * 16.0 + digits[blocks:]).astype(jnp.int32) * page_len
    tokens = tokens + lax.broadcasted_iota(jnp.int32, (blocks, width), 1) % page_len

    total = sums[0]
    for p in range(1, sums.shape[0]):
        total = total + sums[p]
    query = jnp.concatenate(
        [total[s : s + 1, h * head : (h + 1) * head] for s in range(STEPS) for h in range(group)], 0
    )
    query = query + jnp.concatenate([b_query[...]] * STEPS, 0)
    cos_new = cosine[request]
    sin_new = sine[request]
    row = lax.broadcasted_iota(jnp.int32, (rows, head), 0)
    cos_rows = jnp.where(row < group, cos_new[0:1], cos_new[1:2])
    sin_rows = jnp.where(row < group, sin_new[0:1], sin_new[1:2])
    query = (query * cos_rows + pltpu.roll(query, head // 2, 1) * sin_rows).astype(jnp.bfloat16)
    key_new = total[:, group * head : (group + 1) * head] + b_key[...]
    key_new = jnp.concatenate([key_new, jnp.zeros((8 - STEPS, head), jnp.float32)], 0)
    key_new = key_new * cos_new + pltpu.roll(key_new, head // 2, 1) * sin_new
    key_new = key_new.astype(jnp.bfloat16).astype(jnp.float32)
    value_new = total[:, (group + 1) * head :] + b_value[...]
    value_new = value_new.astype(jnp.bfloat16).astype(jnp.float32)
    scale = 1.0 / math.sqrt(head)

    column = lax.broadcasted_iota(jnp.int32, (rows, 1), 0)
    query_wide = query.astype(jnp.float32)
    fresh = []
    for s in range(STEPS):
        dots = jnp.sum(query_wide * key_new[s : s + 1], 1, keepdims=True) * scale
        seen = jnp.logical_and(is_source, column >= s * group)
        fresh.append((jnp.where(seen, dots, NEG), seen))
    row_max = jnp.maximum(fresh[0][0], fresh[1][0])

    stores = []
    for c in range(blocks):
        for i in range(c * CHUNKS // blocks, (c + 1) * CHUNKS // blocks):
            copies[i].wait()
            part = pl.ds(i * per, per)
            stores.append(pltpu.make_async_copy(held.at[part], new_pool.at[part], out_sems.at[i]))
            stores[-1].start()
        keys = held[c * block : (c + 1) * block, :, :head].reshape(width, head)
        part = lax.dot_general(query, keys, (((1,), (1,)), ((), ())), preferred_element_type=jnp.float32)
        part = jnp.where(tokens[c : c + 1] < limit, part * scale, NEG)
        score[:, c * width : (c + 1) * width] = part
        row_max = jnp.maximum(row_max, jnp.max(part, 1, keepdims=True))
    row_sum = jnp.zeros((rows, 1), jnp.float32)
    out = jnp.zeros((rows, head), jnp.float32)
    for s in range(STEPS):
        weight = jnp.where(fresh[s][1], jnp.exp(fresh[s][0] - row_max), 0.0)
        row_sum = row_sum + weight
        out = out + weight.astype(jnp.bfloat16).astype(jnp.float32) * value_new[s : s + 1]
    for c in range(blocks):
        weight = jnp.exp(score[:, c * width : (c + 1) * width] - row_max)
        weight = jnp.where(tokens[c : c + 1] < limit, weight, 0.0)
        row_sum = row_sum + jnp.sum(weight, 1, keepdims=True)
        values = held[c * block : (c + 1) * block, :, head:].reshape(width, head)
        out = out + jnp.dot(weight.astype(jnp.bfloat16), values, preferred_element_type=jnp.float32)

    diagonal = lax.broadcasted_iota(jnp.int32, (rows, head), 1) == row
    for i in range(rows):
        packed[:, i * head : (i + 1) * head] = out[i : i + 1]
    shifted = lax.broadcasted_iota(jnp.int32, (rows, head), 1) == row + rows
    packed[:, rows * head :] = jnp.sum(
        jnp.where(diagonal, row_max, 0.0) + jnp.where(shifted, row_sum, 0.0), 0, keepdims=True
    )
    sends = [
        pltpu.make_async_copy(packed, copies_out.at[p], send_sem.at[p]) for p in range(copies_out.shape[0])
    ]
    for send in sends:
        send.start()

    slots_copy.wait()

    @pl.when(is_source)
    def _():
        for piece, (low, size) in zip(pieces, LATER):

            def take(j, carry):
                piece[j] = held[slots_of[0, low + j]]
                return carry

            lax.fori_loop(0, size, take, 0)
        page_row = lax.broadcasted_iota(jnp.int32, (page_len, 2 * head), 0)
        entries = jnp.concatenate([key_new[:STEPS], value_new], 1)
        offsets = [limit + s for s in range(STEPS)]
        homes = [slots_of[0, offset // page_len] for offset in offsets]
        for i, slot in enumerate((homes[0], homes[-1])):
            page = held[slot].astype(jnp.float32)
            for s, offset in enumerate(offsets):
                here = jnp.logical_and(homes[s] == slot, page_row == offset % page_len)
                page = jnp.where(here, entries[s : s + 1], page)
            fixed[i] = page.astype(held.dtype)

    plan_copy.wait()
    for store in stores:
        store.wait()

    @pl.when(jnp.logical_not(is_source))
    def _():
        put_pages(slots_of, moved_pages(plan, request), [(0, early), (FAR_AT, far)], new_pool, page_sem)

    for send in sends:
        send.wait()


def attend(lengths, table, plan, sums, b_query, b_key, b_value, cosine, sine, early, far, pool):
    group, head = b_query.shape
    rows = STEPS * group
    page = pool.shape[1:]
    return pl.pallas_call(
        attention_kernel,
        out_shape=(
            pltpu.HBM((sums.shape[0], 1, (rows + 1) * head), jnp.float32),
            pltpu.HBM(pool.shape, pool.dtype),
            jax.ShapeDtypeStruct((2,) + page, pool.dtype),
        )
        + tuple(pltpu.VMEM((size,) + page, pool.dtype) for _, size in LATER),
        in_specs=[SMEM, HBM, HBM] + [VMEM] * 8 + [HBM],
        out_specs=(HBM, HBM, VMEM) + (VMEM,) * len(LATER),
        scratch_shapes=[
            pltpu.VMEM(pool.shape, pool.dtype),
            pltpu.VMEM((rows, pool.shape[0] * pool.shape[1]), jnp.float32),
            pltpu.VMEM((1, (rows + 1) * head), jnp.float32),
            pltpu.VMEM(table.shape, table.dtype),
            pltpu.SMEM(table.shape, table.dtype),
            pltpu.SMEM(plan.shape, plan.dtype),
            pltpu.SemaphoreType.DMA((CHUNKS + 3,)),
            pltpu.SemaphoreType.DMA((CHUNKS,)),
            pltpu.SemaphoreType.DMA((sums.shape[0],)),
            pltpu.SemaphoreType.DMA,
        ],
        compiler_params=params(24),
        name="attend",
    )(
        lengths, *in_hbm(table, plan), sums, b_query, b_key, b_value, cosine, sine, early, far, *in_hbm(pool)
    )


def project_kernel(head, parts, w_out, out):
    pairs, _, width = parts.shape
    rows = width // head - 1
    group = rows // STEPS
    requests = pairs // 2
    lane = lax.broadcasted_iota(jnp.int32, (rows, head), 1)
    row = lax.broadcasted_iota(jnp.int32, (rows, head), 0)

    def column(part, shift):
        line = parts[part, :, rows * head :]
        return jnp.sum(jnp.where(lane == row + shift, line, 0.0), 1, keepdims=True)

    lines = [[] for _ in range(STEPS)]
    for r in range(requests):
        tops = [column(part, 0) for part in (r, r + requests)]
        sums = [column(part, rows) for part in (r, r + requests)]
        top = jnp.maximum(*tops)
        weights = [jnp.exp(one - top) for one in tops]
        total = weights[0] * sums[0] + weights[1] * sums[1]
        shares = [weight / total for weight in weights]
        for s in range(STEPS):
            heads = []
            for i in range(s * group, (s + 1) * group):
                here = slice(i * head, (i + 1) * head)
                heads.append(
                    shares[0][i : i + 1] * parts[r, :, here] + shares[1][i : i + 1] * parts[r + requests, :, here]
                )
            lines[s].append(jnp.concatenate(heads, 1))
    attended = jnp.concatenate(sum(lines, []), 0).astype(jnp.bfloat16)
    result = jnp.dot(attended, w_out[...], preferred_element_type=jnp.float32)
    for s in range(STEPS):
        out[s] = result[s * requests : (s + 1) * requests]


def project(parts, w_out, head):
    return pl.pallas_call(
        functools.partial(project_kernel, head),
        out_shape=jax.ShapeDtypeStruct((STEPS, parts.shape[0] // 2, w_out.shape[1]), jnp.float32),
        in_specs=[VMEM, VMEM],
        out_specs=VMEM,
        compiler_params=params(16),
        name="project",
    )(parts, w_out)


def place_kernel(table, plan, lengths, *refs, starts, patch):
    parts, (base, new_pool, sem) = refs[:-3], refs[-3:]
    del base
    pair_index = lax.axis_index("pair")
    requests = lengths.shape[0]

    @pl.when(pair_index < requests)
    def _():
        put_pages(table, moved_pages(plan, pair_index), list(zip(starts, parts)), new_pool, sem)

    if patch:

        @pl.when(pair_index >= requests)
        def _():
            page_len = new_pool.shape[1]
            first = lengths[pair_index - requests] - PAGES_HALF * page_len
            for i, offset in enumerate((first, first + STEPS - 1)):
                slot = table[0, offset // page_len]
                copy = pltpu.make_async_copy(parts[-1].at[i], new_pool.at[slot], sem)
                copy.start()
                copy.wait()


def place(table, plan, lengths, parts, starts, base, fixed=None):
    patch = fixed is not None
    parts = list(parts) + [fixed] * patch
    return pl.pallas_call(
        functools.partial(place_kernel, starts=starts, patch=patch),
        out_shape=pltpu.HBM(base.shape, base.dtype),
        in_specs=[SMEM] * 3 + [VMEM] * len(parts) + [HBM],
        out_specs=HBM,
        scratch_shapes=[
            pltpu.SemaphoreType.DMA,
        ],
        input_output_aliases={3 + len(parts): 0},
        compiler_params=params(16),
        name="place",
    )(table, plan, lengths, *parts, *in_hbm(base))


def blank_kernel(out):
    del out


def blank(like):
    return pl.pallas_call(
        blank_kernel,
        out_shape=jax.ShapeDtypeStruct(like.shape, like.dtype),
        out_specs=pl.BlockSpec(memory_space=pl.ANY),
        name="blank",
    )()


def local(
    normed, w_query, b_query, w_key, b_key, w_value, b_value, w_out, pool, page_table, lengths, plan
):
    pair_count = lax.axis_size("pair")
    tp_count = lax.axis_size("tp")
    requests = pair_count // 2
    head = w_key.shape[1]

    planned = plan.T
    opening = collect(page_table, pool[0, 0])
    partial, near, far, pieces = prepare(
        page_table, planned, normed, w_query, w_key, w_value, pool[0, 0], pair_count
    )
    bits = min(JOINT, requests)

    def tie(*values):
        return lax.optimization_barrier(values)

    def migrate(pages, members=range(requests)):
        return lax.ppermute(pages, "pair", [(r + requests, r) for r in members])

    either = lax.axis_index("rep") == 0

    def gather(values):
        return lax.all_to_all(values, "pair", split_axis=0, concat_axis=0, tiled=True)

    def choose(code, step, *values):
        members = [[r for r in range(requests) if code >> r % bits & 1] for code in range(1 << bits)]
        return lax.switch(code, [functools.partial(step, chosen) for chosen in members], *values)

    def some(members, pages):
        return migrate(pages, members) if members else blank(pages)

    def first_step(members, values, pages):
        return lax.cond(either, gather, gather, values), some(members, pages)

    def second_step(members, values, beside, pages):
        return gather(values), migrate(beside), some(members, pages)

    first = migrate(opening)
    sums, far_pages = choose(far, first_step, partial, pieces[1])
    sums, first = tie(sums, first)
    second = migrate(tie(pieces[0], sums)[0])

    frequency = rope_base ** (-(jnp.arange(head // 2, dtype=jnp.float32) * 2.0 / head))
    steps = jnp.minimum(jnp.arange(8, dtype=jnp.int32), STEPS - 1)
    position = (lengths[:, None] + steps[None, :]).astype(jnp.float32)[..., None]
    angles = position * frequency
    cosine = jnp.cos(angles)
    sine = jnp.sin(angles)
    cosine = jnp.concatenate([cosine, cosine], -1)
    sine = jnp.concatenate([-sine, sine], -1)

    packed, new_pool, fixed, *later = attend(
        lengths,
        page_table,
        planned,
        sums,
        b_query.reshape(-1, head),
        b_key[None, :],
        b_value[None, :],
        cosine,
        sine,
        first,
        far_pages,
        pool[0, 0],
    )
    near, packed = tie(near, packed)
    parts, beside, near_pages = choose(near, second_step, packed, later[0], later[2])
    parts, second = tie(parts, second)
    third = migrate(tie(later[1], parts)[0])
    projected = project(parts, w_out, head)
    here = [second, beside, near_pages]
    starts = [FIRST, BESIDE_AT, NEAR_AT]
    new_pool = place(page_table, planned, lengths, here, starts, new_pool, fixed)
    if tp_count == 2:
        projected = projected + lax.ppermute(projected, "tp", [(0, 1), (1, 0)])
    else:
        projected = lax.psum(projected, "tp")
    third, projected = tie(third, projected)
    new_pool = place(page_table, planned, lengths, [third], [THIRD_AT], new_pool)
    return projected, new_pool[None, None]


def solution(mesh):
    return jax.shard_map(
        local,
        mesh=mesh,
        in_specs=(
            P(None, "rep", "pair"),
            P("pair", "tp"),
            P("tp"),
            P("pair", "tp"),
            P("tp"),
            P("pair", "tp"),
            P("tp"),
            P("tp", "pair"),
            P(("rep", "pair"), "tp", None, None, None),
            P(("rep", "pair"), None),
            P("rep"),
            P("rep", None),
        ),
        out_specs=(P(None, "rep", "pair"), P(("rep", "pair"), "tp", None, None, None)),
        check_vma=False,
    )
```

```python
import functools
import math

import jax
import jax.numpy as jnp
from jax import lax
from jax.experimental import pallas as pl
from jax.experimental.pallas import tpu as pltpu
from jax.sharding import PartitionSpec as P

PAGES_HALF = 384
STEPS = 2
SECTION = 64
MOVED_MAX = STEPS * SECTION
FIRST, SECOND, BESIDE, THIRD = 26, 32, 9, 7
NEAR, FAR = 25, 29
BESIDE_AT = FIRST + SECOND
THIRD_AT = BESIDE_AT + BESIDE
NEAR_AT = THIRD_AT + THIRD
FAR_AT = NEAR_AT + NEAR
PIECES = ((FIRST, SECOND), (FAR_AT, FAR))
LATER = ((BESIDE_AT, BESIDE), (THIRD_AT, THIRD), (NEAR_AT, NEAR))
JOINT = 4
CHUNKS = 8
NEG = -1e30

rope_base = 1000000.0

VMEM = pl.BlockSpec(memory_space=pltpu.VMEM)
SMEM = pl.BlockSpec(memory_space=pltpu.SMEM)
HBM = pl.BlockSpec(memory_space=pltpu.HBM)


def in_hbm(*arrays):
    return tuple(pltpu.with_memory_space_constraint(a, pltpu.HBM) for a in arrays)


def params(mib):
    return pltpu.CompilerParams(vmem_limit_bytes=mib * 1024 * 1024)


def moved_pages(plan, request):
    count = plan[0, request]
    for s in range(1, STEPS):
        count = count + plan[s, request]
    return count


def put_pages(table, count, parts, new_pool, sem):
    placed = jnp.int32(0)
    for low, pages in parts:
        here = jnp.clip(count - low, 0, pages.shape[0])

        def start(j, carry):
            slot = table[0, PAGES_HALF + low + j]
            pltpu.make_async_copy(pages.at[j], new_pool.at[slot], sem).start()
            return carry

        lax.fori_loop(0, here, start, 0)
        placed = placed + here

    def wait(j, carry):
        pltpu.make_async_copy(parts[0][1].at[0], new_pool.at[0], sem).wait()
        return carry

    lax.fori_loop(0, placed, wait, 0)


def collect_kernel(table_in, pool, piece, table, sem, page_sem):
    @pl.when(lax.axis_index("pair") >= lax.axis_size("pair") // 2)
    def _():
        table_copy = pltpu.make_async_copy(table_in, table, sem)
        table_copy.start()
        table_copy.wait()

        def start(j, carry):
            pltpu.make_async_copy(pool.at[table[0, j]], piece.at[j], page_sem).start()
            return carry

        lax.fori_loop(0, FIRST, start, 0, unroll=2)
        pltpu.make_async_copy(pool.at[pl.ds(0, FIRST)], piece, page_sem).wait()


def collect(table, pool):
    return pl.pallas_call(
        collect_kernel,
        out_shape=pltpu.VMEM((FIRST,) + pool.shape[1:], pool.dtype),
        in_specs=[HBM] * 2,
        out_specs=VMEM,
        scratch_shapes=[
            pltpu.SMEM(table.shape, table.dtype),
            pltpu.SemaphoreType.DMA,
            pltpu.SemaphoreType.DMA,
        ],
        compiler_params=params(16),
        name="collect",
    )(*in_hbm(table, pool))


def prepare_kernel(w_query, table_in, plan_in, normed_in, w_key, w_value, pool, partial, near, far, *refs):
    pieces, (table, plan, normed, weights, index_sems, sems, page_sems) = refs[:-7], refs[-7:]
    pairs = partial.shape[0]
    requests = pairs // 2
    head = w_key.shape[1]
    wide = w_query.shape[1]
    table_copy = pltpu.make_async_copy(table_in, table, index_sems.at[0])
    plan_copy = pltpu.make_async_copy(plan_in, plan, index_sems.at[1])
    table_copy.start()
    plan_copy.start()
    loads = [
        pltpu.make_async_copy(normed_in, normed, sems.at[0]),
        pltpu.make_async_copy(w_key, weights.at[:, :head], sems.at[1]),
        pltpu.make_async_copy(w_value, weights.at[:, head:], sems.at[2]),
    ]
    for copy in loads:
        copy.start()
    table_copy.wait()

    @pl.when(lax.axis_index("pair") >= requests)
    def _():
        for i, (low, size) in enumerate(PIECES):

            def start(j, carry):
                pltpu.make_async_copy(pool.at[table[0, low + j]], pieces[i].at[j], page_sems.at[i]).start()
                return carry

            lax.fori_loop(0, size, start, 0, unroll=2)

    plan_copy.wait()
    bits = min(JOINT, requests)
    for code, bound in ((near, NEAR_AT), (far, FAR_AT)):
        total = jnp.int32(0)
        for bit in range(bits):
            most = moved_pages(plan, bit)
            for r in range(bit + bits, requests, bits):
                most = jnp.maximum(most, moved_pages(plan, r))
            total = total + jnp.where(most > bound, 1 << bit, 0)
        code[0] = total
    for copy in loads:
        copy.wait()
    hidden = jnp.concatenate([normed[s].astype(jnp.float32) for s in range(STEPS)], 0).astype(jnp.bfloat16)
    query = jnp.dot(hidden, w_query[...], preferred_element_type=jnp.float32)
    rest = jnp.dot(hidden, weights[...], preferred_element_type=jnp.float32)
    for r in range(requests):
        lines = [slice(s * requests + r, s * requests + r + 1) for s in range(STEPS)]
        query_lines = jnp.concatenate([query[line] for line in lines], 0)
        rest_lines = jnp.concatenate([rest[line] for line in lines], 0)
        for p in range(r, pairs, requests):
            partial[p, :, :wide] = query_lines
            partial[p, :, wide:] = rest_lines

    @pl.when(lax.axis_index("pair") >= requests)
    def _():
        for i, (_, size) in enumerate(PIECES):
            pltpu.make_async_copy(pool.at[pl.ds(0, size)], pieces[i], page_sems.at[i]).wait()


def prepare(table, plan, normed, w_query, w_key, w_value, pool, pairs):
    page = pool.shape[1:]
    wide = w_query.shape[1] + 2 * w_key.shape[1]
    partial, near, far, *pieces = pl.pallas_call(
        prepare_kernel,
        out_shape=(jax.ShapeDtypeStruct((pairs, STEPS, wide), jnp.float32),)
        + (jax.ShapeDtypeStruct((1,), jnp.int32),) * 2
        + tuple(pltpu.VMEM((size,) + page, pool.dtype) for _, size in PIECES),
        in_specs=[VMEM] + [HBM] * 6,
        out_specs=(VMEM, SMEM, SMEM) + (VMEM,) * len(PIECES),
        scratch_shapes=[
            pltpu.SMEM(table.shape, table.dtype),
            pltpu.SMEM(plan.shape, plan.dtype),
            pltpu.VMEM(normed.shape, normed.dtype),
            pltpu.VMEM((w_key.shape[0], 2 * w_key.shape[1]), w_key.dtype),
            pltpu.SemaphoreType.DMA((2,)),
            pltpu.SemaphoreType.DMA((3,)),
            pltpu.SemaphoreType.DMA((len(PIECES),)),
        ],
        compiler_params=params(16),
        name="prepare",
    )(w_query, *in_hbm(table, plan, normed, w_key, w_value, pool))
    return partial, near.reshape(()), far.reshape(()), pieces


def page_order(table, slots):
    slot = lax.broadcasted_iota(jnp.int32, (slots, slots), 0)
    holds = jnp.where(slot == table, 1.0, 0.0).astype(jnp.bfloat16)
    index = lax.broadcasted_iota(jnp.int32, (8, slots), 1)
    digit = lax.broadcasted_iota(jnp.int32, (8, slots), 0)
    digits = jnp.where(digit == 0, index // 16, jnp.where(digit == 1, index % 16, 0))
    digits = digits.astype(jnp.float32).astype(jnp.bfloat16)
    return lax.dot_general(digits, holds, (((1,), (1,)), ((), ())), preferred_element_type=jnp.float32)


def attention_kernel(
    lengths, table_in, plan_in, sums, b_query, b_key, b_value, cosine, sine, early, far, pool,
    copies_out, new_pool, fixed, *refs
):
    pieces, refs = refs[: len(LATER)], refs[len(LATER) :]
    held, score, packed, table, slots_of, plan, sems, out_sems, send_sem, page_sem = refs
    slots, page_len, _ = held.shape
    per = slots // CHUNKS
    table_copy = pltpu.make_async_copy(table_in, table, sems.at[CHUNKS])
    table_copy.start()
    slots_copy = pltpu.make_async_copy(table_in, slots_of, sems.at[CHUNKS + 1])
    slots_copy.start()
    plan_copy = pltpu.make_async_copy(plan_in, plan, sems.at[CHUNKS + 2])
    plan_copy.start()
    copies = []
    for c in range(CHUNKS):
        part = pl.ds(c * per, per)
        copies.append(pltpu.make_async_copy(pool.at[part], held.at[part], sems.at[c]))
        copies[-1].start()
    requests = sums.shape[0] // 2
    group, head = b_query.shape
    rows = STEPS * group
    pair_index = lax.axis_index("pair")
    is_source = pair_index >= requests
    request = jnp.where(is_source, pair_index - requests, pair_index)
    half_tokens = PAGES_HALF * page_len
    limit = jnp.where(is_source, lengths[request] - half_tokens, half_tokens)

    blocks = CHUNKS // 2
    block = slots // blocks
    width = block * page_len
    table_copy.wait()
    digits = page_order(table[...], slots)
    digits = jnp.concatenate(
        [digits[d : d + 1, c * block : (c + 1) * block] for d in range(2) for c in range(blocks)], 0
    ).astype(jnp.bfloat16)
    spread = lax.broadcasted_iota(jnp.int32, (block, width), 1) // page_len
    spread = jnp.where(spread == lax.broadcasted_iota(jnp.int32, (block, width), 0), 1.0, 0.0)
    digits = jnp.dot(digits, spread.astype(jnp.bfloat16), preferred_element_type=jnp.float32)
    tokens = (digits[:blocks] * 16.0 + digits[blocks:]).astype(jnp.int32) * page_len
    tokens = tokens + lax.broadcasted_iota(jnp.int32, (blocks, width), 1) % page_len

    total = sums[0]
    for p in range(1, sums.shape[0]):
        total = total + sums[p]
    query = jnp.concatenate(
        [total[s : s + 1, h * head : (h + 1) * head] for s in range(STEPS) for h in range(group)], 0
    )
    query = query + jnp.concatenate([b_query[...]] * STEPS, 0)
    cos_new = cosine[request]
    sin_new = sine[request]
    row = lax.broadcasted_iota(jnp.int32, (rows, head), 0)
    cos_rows = jnp.where(row < group, cos_new[0:1], cos_new[1:2])
    sin_rows = jnp.where(row < group, sin_new[0:1], sin_new[1:2])
    query = (query * cos_rows + pltpu.roll(query, head // 2, 1) * sin_rows).astype(jnp.bfloat16)
    key_new = total[:, group * head : (group + 1) * head] + b_key[...]
    key_new = jnp.concatenate([key_new, jnp.zeros((8 - STEPS, head), jnp.float32)], 0)
    key_new = key_new * cos_new + pltpu.roll(key_new, head // 2, 1) * sin_new
    key_new = key_new.astype(jnp.bfloat16).astype(jnp.float32)
    value_new = total[:, (group + 1) * head :] + b_value[...]
    value_new = value_new.astype(jnp.bfloat16).astype(jnp.float32)
    scale = 1.0 / math.sqrt(head)

    column = lax.broadcasted_iota(jnp.int32, (rows, 1), 0)
    query_wide = query.astype(jnp.float32)
    fresh = []
    for s in range(STEPS):
        dots = jnp.sum(query_wide * key_new[s : s + 1], 1, keepdims=True) * scale
        seen = jnp.logical_and(is_source, column >= s * group)
        fresh.append((jnp.where(seen, dots, NEG), seen))
    row_max = jnp.maximum(fresh[0][0], fresh[1][0])

    stores = []
    for c in range(blocks):
        for i in range(c * CHUNKS // blocks, (c + 1) * CHUNKS // blocks):
            copies[i].wait()
            part = pl.ds(i * per, per)
            stores.append(pltpu.make_async_copy(held.at[part], new_pool.at[part], out_sems.at[i]))
            stores[-1].start()
        keys = held[c * block : (c + 1) * block, :, :head].reshape(width, head)
        part = lax.dot_general(query, keys, (((1,), (1,)), ((), ())), preferred_element_type=jnp.float32)
        part = jnp.where(tokens[c : c + 1] < limit, part * scale, NEG)
        score[:, c * width : (c + 1) * width] = part
        row_max = jnp.maximum(row_max, jnp.max(part, 1, keepdims=True))
    row_sum = jnp.zeros((rows, 1), jnp.float32)
    out = jnp.zeros((rows, head), jnp.float32)
    for s in range(STEPS):
        weight = jnp.where(fresh[s][1], jnp.exp(fresh[s][0] - row_max), 0.0)
        row_sum = row_sum + weight
        out = out + weight.astype(jnp.bfloat16).astype(jnp.float32) * value_new[s : s + 1]
    for c in range(blocks):
        weight = jnp.exp(score[:, c * width : (c + 1) * width] - row_max)
        weight = jnp.where(tokens[c : c + 1] < limit, weight, 0.0)
        row_sum = row_sum + jnp.sum(weight, 1, keepdims=True)
        values = held[c * block : (c + 1) * block, :, head:].reshape(width, head)
        out = out + jnp.dot(weight.astype(jnp.bfloat16), values, preferred_element_type=jnp.float32)

    diagonal = lax.broadcasted_iota(jnp.int32, (rows, head), 1) == row
    for i in range(rows):
        packed[:, i * head : (i + 1) * head] = out[i : i + 1]
    shifted = lax.broadcasted_iota(jnp.int32, (rows, head), 1) == row + rows
    packed[:, rows * head :] = jnp.sum(
        jnp.where(diagonal, row_max, 0.0) + jnp.where(shifted, row_sum, 0.0), 0, keepdims=True
    )
    sends = [
        pltpu.make_async_copy(packed, copies_out.at[p], send_sem.at[p]) for p in range(copies_out.shape[0])
    ]
    for send in sends:
        send.start()

    slots_copy.wait()

    @pl.when(is_source)
    def _():
        for piece, (low, size) in zip(pieces, LATER):

            def take(j, carry):
                piece[j] = held[slots_of[0, low + j]]
                return carry

            lax.fori_loop(0, size, take, 0)
        page_row = lax.broadcasted_iota(jnp.int32, (page_len, 2 * head), 0)
        entries = jnp.concatenate([key_new[:STEPS], value_new], 1)
        offsets = [limit + s for s in range(STEPS)]
        homes = [slots_of[0, offset // page_len] for offset in offsets]
        for i, slot in enumerate((homes[0], homes[-1])):
            page = held[slot].astype(jnp.float32)
            for s, offset in enumerate(offsets):
                here = jnp.logical_and(homes[s] == slot, page_row == offset % page_len)
                page = jnp.where(here, entries[s : s + 1], page)
            fixed[i] = page.astype(held.dtype)

    plan_copy.wait()
    for store in stores:
        store.wait()

    @pl.when(jnp.logical_not(is_source))
    def _():
        put_pages(slots_of, moved_pages(plan, request), [(0, early), (FAR_AT, far)], new_pool, page_sem)

    for send in sends:
        send.wait()


def attend(lengths, table, plan, sums, b_query, b_key, b_value, cosine, sine, early, far, pool):
    group, head = b_query.shape
    rows = STEPS * group
    page = pool.shape[1:]
    return pl.pallas_call(
        attention_kernel,
        out_shape=(
            pltpu.HBM((sums.shape[0], 1, (rows + 1) * head), jnp.float32),
            pltpu.HBM(pool.shape, pool.dtype),
            jax.ShapeDtypeStruct((2,) + page, pool.dtype),
        )
        + tuple(pltpu.VMEM((size,) + page, pool.dtype) for _, size in LATER),
        in_specs=[SMEM, HBM, HBM] + [VMEM] * 8 + [HBM],
        out_specs=(HBM, HBM, VMEM) + (VMEM,) * len(LATER),
        scratch_shapes=[
            pltpu.VMEM(pool.shape, pool.dtype),
            pltpu.VMEM((rows, pool.shape[0] * pool.shape[1]), jnp.float32),
            pltpu.VMEM((1, (rows + 1) * head), jnp.float32),
            pltpu.VMEM(table.shape, table.dtype),
            pltpu.SMEM(table.shape, table.dtype),
            pltpu.SMEM(plan.shape, plan.dtype),
            pltpu.SemaphoreType.DMA((CHUNKS + 3,)),
            pltpu.SemaphoreType.DMA((CHUNKS,)),
            pltpu.SemaphoreType.DMA((sums.shape[0],)),
            pltpu.SemaphoreType.DMA,
        ],
        compiler_params=params(24),
        name="attend",
    )(
        lengths, *in_hbm(table, plan), sums, b_query, b_key, b_value, cosine, sine, early, far, *in_hbm(pool)
    )


def project_kernel(head, parts, w_out, out):
    pairs, _, width = parts.shape
    rows = width // head - 1
    group = rows // STEPS
    requests = pairs // 2
    lane = lax.broadcasted_iota(jnp.int32, (rows, head), 1)
    row = lax.broadcasted_iota(jnp.int32, (rows, head), 0)

    def column(part, shift):
        line = parts[part, :, rows * head :]
        return jnp.sum(jnp.where(lane == row + shift, line, 0.0), 1, keepdims=True)

    lines = [[] for _ in range(STEPS)]
    for r in range(requests):
        tops = [column(part, 0) for part in (r, r + requests)]
        sums = [column(part, rows) for part in (r, r + requests)]
        top = jnp.maximum(*tops)
        weights = [jnp.exp(one - top) for one in tops]
        total = weights[0] * sums[0] + weights[1] * sums[1]
        shares = [weight / total for weight in weights]
        for s in range(STEPS):
            heads = []
            for i in range(s * group, (s + 1) * group):
                here = slice(i * head, (i + 1) * head)
                heads.append(
                    shares[0][i : i + 1] * parts[r, :, here] + shares[1][i : i + 1] * parts[r + requests, :, here]
                )
            lines[s].append(jnp.concatenate(heads, 1))
    attended = jnp.concatenate(sum(lines, []), 0).astype(jnp.bfloat16)
    result = jnp.dot(attended, w_out[...], preferred_element_type=jnp.float32)
    for s in range(STEPS):
        out[s] = result[s * requests : (s + 1) * requests]


def project(parts, w_out, head):
    return pl.pallas_call(
        functools.partial(project_kernel, head),
        out_shape=jax.ShapeDtypeStruct((STEPS, parts.shape[0] // 2, w_out.shape[1]), jnp.float32),
        in_specs=[VMEM, VMEM],
        out_specs=VMEM,
        compiler_params=params(16),
        name="project",
    )(parts, w_out)


def place_kernel(table, plan, lengths, *refs, starts, patch):
    parts, (base, new_pool, sem) = refs[:-3], refs[-3:]
    del base
    pair_index = lax.axis_index("pair")
    requests = lengths.shape[0]

    @pl.when(pair_index < requests)
    def _():
        put_pages(table, moved_pages(plan, pair_index), list(zip(starts, parts)), new_pool, sem)

    if patch:

        @pl.when(pair_index >= requests)
        def _():
            page_len = new_pool.shape[1]
            first = lengths[pair_index - requests] - PAGES_HALF * page_len
            for i, offset in enumerate((first, first + STEPS - 1)):
                slot = table[0, offset // page_len]
                copy = pltpu.make_async_copy(parts[-1].at[i], new_pool.at[slot], sem)
                copy.start()
                copy.wait()


def place(table, plan, lengths, parts, starts, base, fixed=None):
    patch = fixed is not None
    parts = list(parts) + [fixed] * patch
    return pl.pallas_call(
        functools.partial(place_kernel, starts=starts, patch=patch),
        out_shape=pltpu.HBM(base.shape, base.dtype),
        in_specs=[SMEM] * 3 + [VMEM] * len(parts) + [HBM],
        out_specs=HBM,
        scratch_shapes=[
            pltpu.SemaphoreType.DMA,
        ],
        input_output_aliases={3 + len(parts): 0},
        compiler_params=params(16),
        name="place",
    )(table, plan, lengths, *parts, *in_hbm(base))


def blank_kernel(out):
    del out


def blank(like):
    return pl.pallas_call(
        blank_kernel,
        out_shape=jax.ShapeDtypeStruct(like.shape, like.dtype),
        out_specs=pl.BlockSpec(memory_space=pl.ANY),
        name="blank",
    )()


def local(
    normed, w_query, b_query, w_key, b_key, w_value, b_value, w_out, pool, page_table, lengths, plan
):
    pair_count = lax.axis_size("pair")
    tp_count = lax.axis_size("tp")
    requests = pair_count // 2
    head = w_key.shape[1]

    planned = plan.T
    opening = collect(page_table, pool[0, 0])
    partial, near, far, pieces = prepare(
        page_table, planned, normed, w_query, w_key, w_value, pool[0, 0], pair_count
    )
    bits = min(JOINT, requests)

    def tie(*values):
        return lax.optimization_barrier(values)

    def migrate(pages, members=range(requests)):
        return lax.ppermute(pages, "pair", [(r + requests, r) for r in members])

    def gather(values):
        return lax.all_to_all(values, "pair", split_axis=0, concat_axis=0, tiled=True)

    def choose(code, step, *values):
        members = [[r for r in range(requests) if number >> r % bits & 1] for number in range(1 << bits)]
        branches = [jax.make_jaxpr(functools.partial(step, chosen))(*values) for chosen in members]
        return lax.cond_p.bind(code, *values, branches=tuple(branches))

    def some(members, pages):
        return migrate(pages, members) if members else blank(pages)

    def first_step(members, values, pages):
        either = lax.axis_index("rep") == 0
        return lax.cond(either, gather, gather, values), some(members, pages)

    def second_step(members, values, beside, pages):
        return gather(values), migrate(beside), some(members, pages)

    first = migrate(opening)
    sums, far_pages = choose(far, first_step, partial, pieces[1])
    sums, first = tie(sums, first)
    second = migrate(tie(pieces[0], sums)[0])

    frequency = rope_base ** (-(jnp.arange(head // 2, dtype=jnp.float32) * 2.0 / head))
    steps = jnp.minimum(jnp.arange(8, dtype=jnp.int32), STEPS - 1)
    position = (lengths[:, None] + steps[None, :]).astype(jnp.float32)[..., None]
    angles = position * frequency
    cosine = jnp.cos(angles)
    sine = jnp.sin(angles)
    cosine = jnp.concatenate([cosine, cosine], -1)
    sine = jnp.concatenate([-sine, sine], -1)

    packed, new_pool, fixed, *later = attend(
        lengths,
        page_table,
        planned,
        sums,
        b_query.reshape(-1, head),
        b_key[None, :],
        b_value[None, :],
        cosine,
        sine,
        first,
        far_pages,
        pool[0, 0],
    )
    near, packed = tie(near, packed)
    parts, beside, near_pages = choose(near, second_step, packed, later[0], later[2])
    parts, second = tie(parts, second)
    third = migrate(tie(later[1], parts)[0])
    projected = project(parts, w_out, head)
    here = [second, beside, near_pages]
    starts = [FIRST, BESIDE_AT, NEAR_AT]
    new_pool = place(page_table, planned, lengths, here, starts, new_pool, fixed)
    if tp_count == 2:
        projected = projected + lax.ppermute(projected, "tp", [(0, 1), (1, 0)])
    else:
        projected = lax.psum(projected, "tp")
    third, projected = tie(third, projected)
    new_pool = place(page_table, planned, lengths, [third], [THIRD_AT], new_pool)
    return projected, new_pool[None, None]


def solution(mesh):
    return jax.shard_map(
        local,
        mesh=mesh,
        in_specs=(
            P(None, "rep", "pair"),
            P("pair", "tp"),
            P("tp"),
            P("pair", "tp"),
            P("tp"),
            P("pair", "tp"),
            P("tp"),
            P("tp", "pair"),
            P(("rep", "pair"), "tp", None, None, None),
            P(("rep", "pair"), None),
            P("rep"),
            P("rep", None),
        ),
        out_specs=(P(None, "rep", "pair"), P(("rep", "pair"), "tp", None, None, None)),
        check_vma=False,
    )
```

```python
import functools
import math

import jax
import jax.numpy as jnp
from jax import lax
from jax.experimental import pallas as pl
from jax.experimental.pallas import tpu as pltpu
from jax.sharding import PartitionSpec as P

PAGES_HALF = 384
STEPS = 2
SECTION = 64
MOVED_MAX = STEPS * SECTION
FIRST, SECOND, BESIDE = 26, 34, 14
NEAR, FAR = 25, 29
BESIDE_AT = FIRST + SECOND
NEAR_AT = BESIDE_AT + BESIDE
FAR_AT = NEAR_AT + NEAR
PIECES = ((FIRST, SECOND), (FAR_AT, FAR))
LATER = ((BESIDE_AT, BESIDE), (NEAR_AT, NEAR))
JOINT = 4
CHUNKS = 8
NEG = -1e30

rope_base = 1000000.0

VMEM = pl.BlockSpec(memory_space=pltpu.VMEM)
SMEM = pl.BlockSpec(memory_space=pltpu.SMEM)
HBM = pl.BlockSpec(memory_space=pltpu.HBM)


def in_hbm(*arrays):
    return tuple(pltpu.with_memory_space_constraint(a, pltpu.HBM) for a in arrays)


def params(mib):
    return pltpu.CompilerParams(vmem_limit_bytes=mib * 1024 * 1024)


def moved_pages(plan, request):
    count = plan[0, request]
    for s in range(1, STEPS):
        count = count + plan[s, request]
    return count


def put_pages(table, count, parts, new_pool, sem):
    placed = jnp.int32(0)
    for low, pages in parts:
        here = jnp.clip(count - low, 0, pages.shape[0])

        def start(j, carry):
            slot = table[0, PAGES_HALF + low + j]
            pltpu.make_async_copy(pages.at[j], new_pool.at[slot], sem).start()
            return carry

        lax.fori_loop(0, here, start, 0)
        placed = placed + here

    def wait(j, carry):
        pltpu.make_async_copy(parts[0][1].at[0], new_pool.at[0], sem).wait()
        return carry

    lax.fori_loop(0, placed, wait, 0)


def collect_kernel(table_in, pool, piece, table, sem, page_sem):
    @pl.when(lax.axis_index("pair") >= lax.axis_size("pair") // 2)
    def _():
        table_copy = pltpu.make_async_copy(table_in, table, sem)
        table_copy.start()
        table_copy.wait()

        def start(j, carry):
            pltpu.make_async_copy(pool.at[table[0, j]], piece.at[j], page_sem).start()
            return carry

        lax.fori_loop(0, FIRST, start, 0, unroll=2)
        pltpu.make_async_copy(pool.at[pl.ds(0, FIRST)], piece, page_sem).wait()


def collect(table, pool):
    return pl.pallas_call(
        collect_kernel,
        out_shape=pltpu.VMEM((FIRST,) + pool.shape[1:], pool.dtype),
        in_specs=[HBM] * 2,
        out_specs=VMEM,
        scratch_shapes=[
            pltpu.SMEM(table.shape, table.dtype),
            pltpu.SemaphoreType.DMA,
            pltpu.SemaphoreType.DMA,
        ],
        compiler_params=params(16),
        name="collect",
    )(*in_hbm(table, pool))


def prepare_kernel(w_query, table_in, plan_in, normed_in, w_key, w_value, pool, partial, near, far, *refs):
    pieces, (table, plan, normed, weights, index_sems, sems, page_sems) = refs[:-7], refs[-7:]
    pairs = partial.shape[0]
    requests = pairs // 2
    head = w_key.shape[1]
    wide = w_query.shape[1]
    table_copy = pltpu.make_async_copy(table_in, table, index_sems.at[0])
    plan_copy = pltpu.make_async_copy(plan_in, plan, index_sems.at[1])
    table_copy.start()
    plan_copy.start()
    loads = [
        pltpu.make_async_copy(normed_in, normed, sems.at[0]),
        pltpu.make_async_copy(w_key, weights.at[:, :head], sems.at[1]),
        pltpu.make_async_copy(w_value, weights.at[:, head:], sems.at[2]),
    ]
    for copy in loads:
        copy.start()
    table_copy.wait()

    @pl.when(lax.axis_index("pair") >= requests)
    def _():
        for i, (low, size) in enumerate(PIECES):

            def start(j, carry):
                pltpu.make_async_copy(pool.at[table[0, low + j]], pieces[i].at[j], page_sems.at[i]).start()
                return carry

            lax.fori_loop(0, size, start, 0, unroll=2)

    plan_copy.wait()
    bits = min(JOINT, requests)
    for code, bound in ((near, NEAR_AT), (far, FAR_AT)):
        total = jnp.int32(0)
        for bit in range(bits):
            most = moved_pages(plan, bit)
            for r in range(bit + bits, requests, bits):
                most = jnp.maximum(most, moved_pages(plan, r))
            total = total + jnp.where(most > bound, 1 << bit, 0)
        code[0] = total
    for copy in loads:
        copy.wait()
    hidden = jnp.concatenate([normed[s].astype(jnp.float32) for s in range(STEPS)], 0).astype(jnp.bfloat16)
    query = jnp.dot(hidden, w_query[...], preferred_element_type=jnp.float32)
    rest = jnp.dot(hidden, weights[...], preferred_element_type=jnp.float32)
    for r in range(requests):
        lines = [slice(s * requests + r, s * requests + r + 1) for s in range(STEPS)]
        query_lines = jnp.concatenate([query[line] for line in lines], 0)
        rest_lines = jnp.concatenate([rest[line] for line in lines], 0)
        for p in range(r, pairs, requests):
            partial[p, :, :wide] = query_lines
            partial[p, :, wide:] = rest_lines

    @pl.when(lax.axis_index("pair") >= requests)
    def _():
        for i, (_, size) in enumerate(PIECES):
            pltpu.make_async_copy(pool.at[pl.ds(0, size)], pieces[i], page_sems.at[i]).wait()


def prepare(table, plan, normed, w_query, w_key, w_value, pool, pairs):
    page = pool.shape[1:]
    wide = w_query.shape[1] + 2 * w_key.shape[1]
    partial, near, far, *pieces = pl.pallas_call(
        prepare_kernel,
        out_shape=(jax.ShapeDtypeStruct((pairs, STEPS, wide), jnp.float32),)
        + (jax.ShapeDtypeStruct((1,), jnp.int32),) * 2
        + tuple(pltpu.VMEM((size,) + page, pool.dtype) for _, size in PIECES),
        in_specs=[VMEM] + [HBM] * 6,
        out_specs=(VMEM, SMEM, SMEM) + (VMEM,) * len(PIECES),
        scratch_shapes=[
            pltpu.SMEM(table.shape, table.dtype),
            pltpu.SMEM(plan.shape, plan.dtype),
            pltpu.VMEM(normed.shape, normed.dtype),
            pltpu.VMEM((w_key.shape[0], 2 * w_key.shape[1]), w_key.dtype),
            pltpu.SemaphoreType.DMA((2,)),
            pltpu.SemaphoreType.DMA((3,)),
            pltpu.SemaphoreType.DMA((len(PIECES),)),
        ],
        compiler_params=params(16),
        name="prepare",
    )(w_query, *in_hbm(table, plan, normed, w_key, w_value, pool))
    return partial, near.reshape(()), far.reshape(()), pieces


def page_order(table, slots):
    slot = lax.broadcasted_iota(jnp.int32, (slots, slots), 0)
    holds = jnp.where(slot == table, 1.0, 0.0).astype(jnp.bfloat16)
    index = lax.broadcasted_iota(jnp.int32, (8, slots), 1)
    digit = lax.broadcasted_iota(jnp.int32, (8, slots), 0)
    digits = jnp.where(digit == 0, index // 16, jnp.where(digit == 1, index % 16, 0))
    digits = digits.astype(jnp.float32).astype(jnp.bfloat16)
    return lax.dot_general(digits, holds, (((1,), (1,)), ((), ())), preferred_element_type=jnp.float32)


def attention_kernel(
    lengths, table_in, plan_in, sums, b_query, b_key, b_value, cosine, sine, early, far, pool,
    copies_out, new_pool, fixed, *refs
):
    pieces, refs = refs[: len(LATER)], refs[len(LATER) :]
    held, score, packed, table, slots_of, plan, sems, out_sems, send_sem, page_sem = refs
    slots, page_len, _ = held.shape
    per = slots // CHUNKS
    table_copy = pltpu.make_async_copy(table_in, table, sems.at[CHUNKS])
    table_copy.start()
    slots_copy = pltpu.make_async_copy(table_in, slots_of, sems.at[CHUNKS + 1])
    slots_copy.start()
    plan_copy = pltpu.make_async_copy(plan_in, plan, sems.at[CHUNKS + 2])
    plan_copy.start()
    copies = []
    for c in range(CHUNKS):
        part = pl.ds(c * per, per)
        copies.append(pltpu.make_async_copy(pool.at[part], held.at[part], sems.at[c]))
        copies[-1].start()
    requests = sums.shape[0] // 2
    group, head = b_query.shape
    rows = STEPS * group
    pair_index = lax.axis_index("pair")
    is_source = pair_index >= requests
    request = jnp.where(is_source, pair_index - requests, pair_index)
    half_tokens = PAGES_HALF * page_len
    limit = jnp.where(is_source, lengths[request] - half_tokens, half_tokens)

    blocks = CHUNKS // 2
    block = slots // blocks
    width = block * page_len
    table_copy.wait()
    digits = page_order(table[...], slots)
    digits = jnp.concatenate(
        [digits[d : d + 1, c * block : (c + 1) * block] for d in range(2) for c in range(blocks)], 0
    ).astype(jnp.bfloat16)
    spread = lax.broadcasted_iota(jnp.int32, (block, width), 1) // page_len
    spread = jnp.where(spread == lax.broadcasted_iota(jnp.int32, (block, width), 0), 1.0, 0.0)
    digits = jnp.dot(digits, spread.astype(jnp.bfloat16), preferred_element_type=jnp.float32)
    tokens = (digits[:blocks] * 16.0 + digits[blocks:]).astype(jnp.int32) * page_len
    tokens = tokens + lax.broadcasted_iota(jnp.int32, (blocks, width), 1) % page_len

    total = sums[0]
    for p in range(1, sums.shape[0]):
        total = total + sums[p]
    query = jnp.concatenate(
        [total[s : s + 1, h * head : (h + 1) * head] for s in range(STEPS) for h in range(group)], 0
    )
    query = query + jnp.concatenate([b_query[...]] * STEPS, 0)
    cos_new = cosine[request]
    sin_new = sine[request]
    row = lax.broadcasted_iota(jnp.int32, (rows, head), 0)
    cos_rows = jnp.where(row < group, cos_new[0:1], cos_new[1:2])
    sin_rows = jnp.where(row < group, sin_new[0:1], sin_new[1:2])
    query = (query * cos_rows + pltpu.roll(query, head // 2, 1) * sin_rows).astype(jnp.bfloat16)
    key_new = total[:, group * head : (group + 1) * head] + b_key[...]
    key_new = jnp.concatenate([key_new, jnp.zeros((8 - STEPS, head), jnp.float32)], 0)
    key_new = key_new * cos_new + pltpu.roll(key_new, head // 2, 1) * sin_new
    key_new = key_new.astype(jnp.bfloat16).astype(jnp.float32)
    value_new = total[:, (group + 1) * head :] + b_value[...]
    value_new = value_new.astype(jnp.bfloat16).astype(jnp.float32)
    scale = 1.0 / math.sqrt(head)

    column = lax.broadcasted_iota(jnp.int32, (rows, 1), 0)
    query_wide = query.astype(jnp.float32)
    fresh = []
    for s in range(STEPS):
        dots = jnp.sum(query_wide * key_new[s : s + 1], 1, keepdims=True) * scale
        seen = jnp.logical_and(is_source, column >= s * group)
        fresh.append((jnp.where(seen, dots, NEG), seen))
    row_max = jnp.maximum(fresh[0][0], fresh[1][0])

    stores = []
    for c in range(blocks):
        for i in range(c * CHUNKS // blocks, (c + 1) * CHUNKS // blocks):
            copies[i].wait()
            part = pl.ds(i * per, per)
            stores.append(pltpu.make_async_copy(held.at[part], new_pool.at[part], out_sems.at[i]))
            stores[-1].start()
        keys = held[c * block : (c + 1) * block, :, :head].reshape(width, head)
        part = lax.dot_general(query, keys, (((1,), (1,)), ((), ())), preferred_element_type=jnp.float32)
        part = jnp.where(tokens[c : c + 1] < limit, part * scale, NEG)
        score[:, c * width : (c + 1) * width] = part
        row_max = jnp.maximum(row_max, jnp.max(part, 1, keepdims=True))
    row_sum = jnp.zeros((rows, 1), jnp.float32)
    out = jnp.zeros((rows, head), jnp.float32)
    for s in range(STEPS):
        weight = jnp.where(fresh[s][1], jnp.exp(fresh[s][0] - row_max), 0.0)
        row_sum = row_sum + weight
        out = out + weight.astype(jnp.bfloat16).astype(jnp.float32) * value_new[s : s + 1]
    for c in range(blocks):
        weight = jnp.exp(score[:, c * width : (c + 1) * width] - row_max)
        weight = jnp.where(tokens[c : c + 1] < limit, weight, 0.0)
        row_sum = row_sum + jnp.sum(weight, 1, keepdims=True)
        values = held[c * block : (c + 1) * block, :, head:].reshape(width, head)
        out = out + jnp.dot(weight.astype(jnp.bfloat16), values, preferred_element_type=jnp.float32)

    diagonal = lax.broadcasted_iota(jnp.int32, (rows, head), 1) == row
    for i in range(rows):
        packed[:, i * head : (i + 1) * head] = out[i : i + 1]
    shifted = lax.broadcasted_iota(jnp.int32, (rows, head), 1) == row + rows
    packed[:, rows * head :] = jnp.sum(
        jnp.where(diagonal, row_max, 0.0) + jnp.where(shifted, row_sum, 0.0), 0, keepdims=True
    )
    sends = [
        pltpu.make_async_copy(packed, copies_out.at[p], send_sem.at[p]) for p in range(copies_out.shape[0])
    ]
    for send in sends:
        send.start()

    slots_copy.wait()

    @pl.when(is_source)
    def _():
        for piece, (low, size) in zip(pieces, LATER):

            def take(j, carry):
                piece[j] = held[slots_of[0, low + j]]
                return carry

            lax.fori_loop(0, size, take, 0)
        page_row = lax.broadcasted_iota(jnp.int32, (page_len, 2 * head), 0)
        entries = jnp.concatenate([key_new[:STEPS], value_new], 1)
        offsets = [limit + s for s in range(STEPS)]
        homes = [slots_of[0, offset // page_len] for offset in offsets]
        for i, slot in enumerate((homes[0], homes[-1])):
            page = held[slot].astype(jnp.float32)
            for s, offset in enumerate(offsets):
                here = jnp.logical_and(homes[s] == slot, page_row == offset % page_len)
                page = jnp.where(here, entries[s : s + 1], page)
            fixed[i] = page.astype(held.dtype)

    plan_copy.wait()
    for store in stores:
        store.wait()

    @pl.when(jnp.logical_not(is_source))
    def _():
        put_pages(slots_of, moved_pages(plan, request), [(0, early), (FAR_AT, far)], new_pool, page_sem)

    for send in sends:
        send.wait()


def attend(lengths, table, plan, sums, b_query, b_key, b_value, cosine, sine, early, far, pool):
    group, head = b_query.shape
    rows = STEPS * group
    page = pool.shape[1:]
    return pl.pallas_call(
        attention_kernel,
        out_shape=(
            pltpu.HBM((sums.shape[0], 1, (rows + 1) * head), jnp.float32),
            pltpu.HBM(pool.shape, pool.dtype),
            jax.ShapeDtypeStruct((2,) + page, pool.dtype),
        )
        + tuple(pltpu.VMEM((size,) + page, pool.dtype) for _, size in LATER),
        in_specs=[SMEM, HBM, HBM] + [VMEM] * 8 + [HBM],
        out_specs=(HBM, HBM, VMEM) + (VMEM,) * len(LATER),
        scratch_shapes=[
            pltpu.VMEM(pool.shape, pool.dtype),
            pltpu.VMEM((rows, pool.shape[0] * pool.shape[1]), jnp.float32),
            pltpu.VMEM((1, (rows + 1) * head), jnp.float32),
            pltpu.VMEM(table.shape, table.dtype),
            pltpu.SMEM(table.shape, table.dtype),
            pltpu.SMEM(plan.shape, plan.dtype),
            pltpu.SemaphoreType.DMA((CHUNKS + 3,)),
            pltpu.SemaphoreType.DMA((CHUNKS,)),
            pltpu.SemaphoreType.DMA((sums.shape[0],)),
            pltpu.SemaphoreType.DMA,
        ],
        compiler_params=params(24),
        name="attend",
    )(
        lengths, *in_hbm(table, plan), sums, b_query, b_key, b_value, cosine, sine, early, far, *in_hbm(pool)
    )


def project_kernel(head, parts, w_out, out):
    pairs, _, width = parts.shape
    rows = width // head - 1
    group = rows // STEPS
    requests = pairs // 2
    lane = lax.broadcasted_iota(jnp.int32, (rows, head), 1)
    row = lax.broadcasted_iota(jnp.int32, (rows, head), 0)

    def column(part, shift):
        line = parts[part, :, rows * head :]
        return jnp.sum(jnp.where(lane == row + shift, line, 0.0), 1, keepdims=True)

    lines = [[] for _ in range(STEPS)]
    for r in range(requests):
        tops = [column(part, 0) for part in (r, r + requests)]
        sums = [column(part, rows) for part in (r, r + requests)]
        top = jnp.maximum(*tops)
        weights = [jnp.exp(one - top) for one in tops]
        total = weights[0] * sums[0] + weights[1] * sums[1]
        shares = [weight / total for weight in weights]
        for s in range(STEPS):
            heads = []
            for i in range(s * group, (s + 1) * group):
                here = slice(i * head, (i + 1) * head)
                heads.append(
                    shares[0][i : i + 1] * parts[r, :, here] + shares[1][i : i + 1] * parts[r + requests, :, here]
                )
            lines[s].append(jnp.concatenate(heads, 1))
    attended = jnp.concatenate(sum(lines, []), 0).astype(jnp.bfloat16)
    result = jnp.dot(attended, w_out[...], preferred_element_type=jnp.float32)
    for s in range(STEPS):
        out[s] = result[s * requests : (s + 1) * requests]


def project(parts, w_out, head):
    return pl.pallas_call(
        functools.partial(project_kernel, head),
        out_shape=jax.ShapeDtypeStruct((STEPS, parts.shape[0] // 2, w_out.shape[1]), jnp.float32),
        in_specs=[VMEM, VMEM],
        out_specs=VMEM,
        compiler_params=params(16),
        name="project",
    )(parts, w_out)


def place_kernel(table, plan, lengths, *refs, starts, patch):
    parts, (base, new_pool, sem) = refs[:-3], refs[-3:]
    del base
    pair_index = lax.axis_index("pair")
    requests = lengths.shape[0]

    @pl.when(pair_index < requests)
    def _():
        put_pages(table, moved_pages(plan, pair_index), list(zip(starts, parts)), new_pool, sem)

    if patch:

        @pl.when(pair_index >= requests)
        def _():
            page_len = new_pool.shape[1]
            first = lengths[pair_index - requests] - PAGES_HALF * page_len
            for i, offset in enumerate((first, first + STEPS - 1)):
                slot = table[0, offset // page_len]
                copy = pltpu.make_async_copy(parts[-1].at[i], new_pool.at[slot], sem)
                copy.start()
                copy.wait()


def place(table, plan, lengths, parts, starts, base, fixed=None):
    patch = fixed is not None
    parts = list(parts) + [fixed] * patch
    return pl.pallas_call(
        functools.partial(place_kernel, starts=starts, patch=patch),
        out_shape=pltpu.HBM(base.shape, base.dtype),
        in_specs=[SMEM] * 3 + [VMEM] * len(parts) + [HBM],
        out_specs=HBM,
        scratch_shapes=[
            pltpu.SemaphoreType.DMA,
        ],
        input_output_aliases={3 + len(parts): 0},
        compiler_params=params(16),
        name="place",
    )(table, plan, lengths, *parts, *in_hbm(base))


def blank_kernel(out):
    del out


def blank(like):
    return pl.pallas_call(
        blank_kernel,
        out_shape=jax.ShapeDtypeStruct(like.shape, like.dtype),
        out_specs=pl.BlockSpec(memory_space=pl.ANY),
        name="blank",
    )()


def local(
    normed, w_query, b_query, w_key, b_key, w_value, b_value, w_out, pool, page_table, lengths, plan
):
    pair_count = lax.axis_size("pair")
    tp_count = lax.axis_size("tp")
    requests = pair_count // 2
    head = w_key.shape[1]

    planned = plan.T
    opening = collect(page_table, pool[0, 0])
    partial, near, far, pieces = prepare(
        page_table, planned, normed, w_query, w_key, w_value, pool[0, 0], pair_count
    )
    bits = min(JOINT, requests)

    def tie(*values):
        return lax.optimization_barrier(values)

    def migrate(pages, members=range(requests)):
        return lax.ppermute(pages, "pair", [(r + requests, r) for r in members])

    either = lax.axis_index("rep") == 0

    def gather(values):
        return lax.all_to_all(values, "pair", split_axis=0, concat_axis=0, tiled=True)

    def choose(code, step, *values):
        members = [[r for r in range(requests) if code >> r % bits & 1] for code in range(1 << bits)]
        return lax.switch(code, [functools.partial(step, chosen) for chosen in members], *values)

    def some(members, pages):
        return migrate(pages, members) if members else blank(pages)

    def first_step(members, values, pages):
        return lax.cond(either, gather, gather, values), some(members, pages)

    def second_step(members, values, beside, pages):
        return gather(values), migrate(beside), some(members, pages)

    first = migrate(opening)
    sums, far_pages = choose(far, first_step, partial, pieces[1])
    sums, first = tie(sums, first)
    second = migrate(tie(pieces[0], sums)[0])

    frequency = rope_base ** (-(jnp.arange(head // 2, dtype=jnp.float32) * 2.0 / head))
    steps = jnp.minimum(jnp.arange(8, dtype=jnp.int32), STEPS - 1)
    position = (lengths[:, None] + steps[None, :]).astype(jnp.float32)[..., None]
    angles = position * frequency
    cosine = jnp.cos(angles)
    sine = jnp.sin(angles)
    cosine = jnp.concatenate([cosine, cosine], -1)
    sine = jnp.concatenate([-sine, sine], -1)

    packed, new_pool, fixed, *later = attend(
        lengths,
        page_table,
        planned,
        sums,
        b_query.reshape(-1, head),
        b_key[None, :],
        b_value[None, :],
        cosine,
        sine,
        first,
        far_pages,
        pool[0, 0],
    )
    near, packed = tie(near, packed)
    parts, beside, near_pages = choose(near, second_step, packed, later[0], later[1])
    parts, second = tie(parts, second)
    projected = project(parts, w_out, head)
    here = [second, beside, near_pages]
    starts = [FIRST, BESIDE_AT, NEAR_AT]
    new_pool = place(page_table, planned, lengths, here, starts, new_pool, fixed)
    if tp_count == 2:
        projected = projected + lax.ppermute(projected, "tp", [(0, 1), (1, 0)])
    else:
        projected = lax.psum(projected, "tp")
    return projected, new_pool[None, None]


def solution(mesh):
    return jax.shard_map(
        local,
        mesh=mesh,
        in_specs=(
            P(None, "rep", "pair"),
            P("pair", "tp"),
            P("tp"),
            P("pair", "tp"),
            P("tp"),
            P("pair", "tp"),
            P("tp"),
            P("tp", "pair"),
            P(("rep", "pair"), "tp", None, None, None),
            P(("rep", "pair"), None),
            P("rep"),
            P("rep", None),
        ),
        out_specs=(P(None, "rep", "pair"), P(("rep", "pair"), "tp", None, None, None)),
        check_vma=False,
    )
```

```python
import functools
import math

import jax
import jax.numpy as jnp
from jax import lax
from jax.experimental import pallas as pl
from jax.experimental.pallas import tpu as pltpu
from jax.sharding import PartitionSpec as P

PAGES_HALF = 384
STEPS = 2
SECTION = 64
MOVED_MAX = STEPS * SECTION
FIRST, SECOND, BESIDE, THIRD = 26, 32, 9, 7
NEAR, FAR = 26, 28
BESIDE_AT = FIRST + SECOND
THIRD_AT = BESIDE_AT + BESIDE
NEAR_AT = THIRD_AT + THIRD
FAR_AT = NEAR_AT + NEAR
PIECES = ((FIRST, SECOND), (FAR_AT, FAR))
LATER = ((BESIDE_AT, BESIDE), (THIRD_AT, THIRD), (NEAR_AT, NEAR))
JOINT = 4
CHUNKS = 16
NEG = -1e30

rope_base = 1000000.0

VMEM = pl.BlockSpec(memory_space=pltpu.VMEM)
SMEM = pl.BlockSpec(memory_space=pltpu.SMEM)
HBM = pl.BlockSpec(memory_space=pltpu.HBM)


def in_hbm(*arrays):
    return tuple(pltpu.with_memory_space_constraint(a, pltpu.HBM) for a in arrays)


def params(mib):
    return pltpu.CompilerParams(vmem_limit_bytes=mib * 1024 * 1024)


def moved_pages(plan, request):
    count = plan[0, request]
    for s in range(1, STEPS):
        count = count + plan[s, request]
    return count


def put_pages(table, count, parts, new_pool, sem):
    placed = jnp.int32(0)
    for low, pages in parts:
        here = jnp.clip(count - low, 0, pages.shape[0])

        def start(j, carry):
            slot = table[0, PAGES_HALF + low + j]
            pltpu.make_async_copy(pages.at[j], new_pool.at[slot], sem).start()
            return carry

        lax.fori_loop(0, here, start, 0)
        placed = placed + here

    def wait(j, carry):
        pltpu.make_async_copy(parts[0][1].at[0], new_pool.at[0], sem).wait()
        return carry

    lax.fori_loop(0, placed, wait, 0)


def collect_kernel(table_in, pool, piece, table, sem, page_sem):
    @pl.when(lax.axis_index("pair") >= lax.axis_size("pair") // 2)
    def _():
        table_copy = pltpu.make_async_copy(table_in, table, sem)
        table_copy.start()
        table_copy.wait()

        def start(j, carry):
            pltpu.make_async_copy(pool.at[table[0, j]], piece.at[j], page_sem).start()
            return carry

        lax.fori_loop(0, FIRST, start, 0, unroll=2)
        pltpu.make_async_copy(pool.at[pl.ds(0, FIRST)], piece, page_sem).wait()


def collect(table, pool):
    return pl.pallas_call(
        collect_kernel,
        out_shape=pltpu.VMEM((FIRST,) + pool.shape[1:], pool.dtype),
        in_specs=[HBM] * 2,
        out_specs=VMEM,
        scratch_shapes=[
            pltpu.SMEM(table.shape, table.dtype),
            pltpu.SemaphoreType.DMA,
            pltpu.SemaphoreType.DMA,
        ],
        compiler_params=params(16),
        name="collect",
    )(*in_hbm(table, pool))


def prepare_kernel(w_query, table_in, plan_in, normed_in, w_key, w_value, pool, partial, near, far, *refs):
    pieces, (table, plan, normed, weights, index_sems, sems, page_sems) = refs[:-7], refs[-7:]
    pairs = partial.shape[0]
    requests = pairs // 2
    head = w_key.shape[1]
    wide = w_query.shape[1]
    table_copy = pltpu.make_async_copy(table_in, table, index_sems.at[0])
    plan_copy = pltpu.make_async_copy(plan_in, plan, index_sems.at[1])
    table_copy.start()
    plan_copy.start()
    loads = [
        pltpu.make_async_copy(normed_in, normed, sems.at[0]),
        pltpu.make_async_copy(w_key, weights.at[:, :head], sems.at[1]),
        pltpu.make_async_copy(w_value, weights.at[:, head:], sems.at[2]),
    ]
    for copy in loads:
        copy.start()
    table_copy.wait()

    @pl.when(lax.axis_index("pair") >= requests)
    def _():
        for i, (low, size) in enumerate(PIECES):

            def start(j, carry):
                pltpu.make_async_copy(pool.at[table[0, low + j]], pieces[i].at[j], page_sems.at[i]).start()
                return carry

            lax.fori_loop(0, size, start, 0, unroll=2)

    plan_copy.wait()
    bits = min(JOINT, requests)
    for code, bound in ((near, NEAR_AT), (far, FAR_AT)):
        total = jnp.int32(0)
        for bit in range(bits):
            most = moved_pages(plan, bit)
            for r in range(bit + bits, requests, bits):
                most = jnp.maximum(most, moved_pages(plan, r))
            total = total + jnp.where(most > bound, 1 << bit, 0)
        code[0] = total
    for copy in loads:
        copy.wait()
    hidden = jnp.concatenate([normed[s].astype(jnp.float32) for s in range(STEPS)], 0).astype(jnp.bfloat16)
    query = jnp.dot(hidden, w_query[...], preferred_element_type=jnp.float32)
    rest = jnp.dot(hidden, weights[...], preferred_element_type=jnp.float32)
    for r in range(requests):
        lines = [slice(s * requests + r, s * requests + r + 1) for s in range(STEPS)]
        query_lines = jnp.concatenate([query[line] for line in lines], 0)
        rest_lines = jnp.concatenate([rest[line] for line in lines], 0)
        for p in range(r, pairs, requests):
            partial[p, :, :wide] = query_lines
            partial[p, :, wide:] = rest_lines

    @pl.when(lax.axis_index("pair") >= requests)
    def _():
        for i, (_, size) in enumerate(PIECES):
            pltpu.make_async_copy(pool.at[pl.ds(0, size)], pieces[i], page_sems.at[i]).wait()


def prepare(table, plan, normed, w_query, w_key, w_value, pool, pairs):
    page = pool.shape[1:]
    wide = w_query.shape[1] + 2 * w_key.shape[1]
    partial, near, far, *pieces = pl.pallas_call(
        prepare_kernel,
        out_shape=(jax.ShapeDtypeStruct((pairs, STEPS, wide), jnp.float32),)
        + (jax.ShapeDtypeStruct((1,), jnp.int32),) * 2
        + tuple(pltpu.VMEM((size,) + page, pool.dtype) for _, size in PIECES),
        in_specs=[VMEM] + [HBM] * 6,
        out_specs=(VMEM, SMEM, SMEM) + (VMEM,) * len(PIECES),
        scratch_shapes=[
            pltpu.SMEM(table.shape, table.dtype),
            pltpu.SMEM(plan.shape, plan.dtype),
            pltpu.VMEM(normed.shape, normed.dtype),
            pltpu.VMEM((w_key.shape[0], 2 * w_key.shape[1]), w_key.dtype),
            pltpu.SemaphoreType.DMA((2,)),
            pltpu.SemaphoreType.DMA((3,)),
            pltpu.SemaphoreType.DMA((len(PIECES),)),
        ],
        compiler_params=params(16),
        name="prepare",
    )(w_query, *in_hbm(table, plan, normed, w_key, w_value, pool))
    return partial, near.reshape(()), far.reshape(()), pieces


def page_order(table, slots):
    slot = lax.broadcasted_iota(jnp.int32, (slots, slots), 0)
    holds = jnp.where(slot == table, 1.0, 0.0).astype(jnp.bfloat16)
    index = lax.broadcasted_iota(jnp.int32, (8, slots), 1)
    digit = lax.broadcasted_iota(jnp.int32, (8, slots), 0)
    digits = jnp.where(digit == 0, index // 16, jnp.where(digit == 1, index % 16, 0))
    digits = digits.astype(jnp.float32).astype(jnp.bfloat16)
    return lax.dot_general(digits, holds, (((1,), (1,)), ((), ())), preferred_element_type=jnp.float32)


def attention_kernel(
    lengths, table_in, plan_in, sums, b_query, b_key, b_value, cosine, sine, early, far, pool,
    copies_out, new_pool, fixed, *refs
):
    pieces, refs = refs[: len(LATER)], refs[len(LATER) :]
    held, score, packed, table, slots_of, plan, sems, out_sems, send_sem, page_sem = refs
    slots, page_len, _ = held.shape
    per = slots // CHUNKS
    table_copy = pltpu.make_async_copy(table_in, table, sems.at[CHUNKS])
    table_copy.start()
    slots_copy = pltpu.make_async_copy(table_in, slots_of, sems.at[CHUNKS + 1])
    slots_copy.start()
    plan_copy = pltpu.make_async_copy(plan_in, plan, sems.at[CHUNKS + 2])
    plan_copy.start()
    copies = []
    for c in range(CHUNKS):
        part = pl.ds(c * per, per)
        copies.append(pltpu.make_async_copy(pool.at[part], held.at[part], sems.at[c]))
        copies[-1].start()
    requests = sums.shape[0] // 2
    group, head = b_query.shape
    rows = STEPS * group
    pair_index = lax.axis_index("pair")
    is_source = pair_index >= requests
    request = jnp.where(is_source, pair_index - requests, pair_index)
    half_tokens = PAGES_HALF * page_len
    limit = jnp.where(is_source, lengths[request] - half_tokens, half_tokens)

    blocks = CHUNKS // 2
    block = slots // blocks
    width = block * page_len
    table_copy.wait()
    digits = page_order(table[...], slots)
    digits = jnp.concatenate(
        [digits[d : d + 1, c * block : (c + 1) * block] for d in range(2) for c in range(blocks)], 0
    ).astype(jnp.bfloat16)
    spread = lax.broadcasted_iota(jnp.int32, (block, width), 1) // page_len
    spread = jnp.where(spread == lax.broadcasted_iota(jnp.int32, (block, width), 0), 1.0, 0.0)
    digits = jnp.dot(digits, spread.astype(jnp.bfloat16), preferred_element_type=jnp.float32)
    tokens = (digits[:blocks] * 16.0 + digits[blocks:]).astype(jnp.int32) * page_len
    tokens = tokens + lax.broadcasted_iota(jnp.int32, (blocks, width), 1) % page_len

    total = sums[0]
    for p in range(1, sums.shape[0]):
        total = total + sums[p]
    query = jnp.concatenate(
        [total[s : s + 1, h * head : (h + 1) * head] for s in range(STEPS) for h in range(group)], 0
    )
    query = query + jnp.concatenate([b_query[...]] * STEPS, 0)
    cos_new = cosine[request]
    sin_new = sine[request]
    row = lax.broadcasted_iota(jnp.int32, (rows, head), 0)
    cos_rows = jnp.where(row < group, cos_new[0:1], cos_new[1:2])
    sin_rows = jnp.where(row < group, sin_new[0:1], sin_new[1:2])
    query = (query * cos_rows + pltpu.roll(query, head // 2, 1) * sin_rows).astype(jnp.bfloat16)
    key_new = total[:, group * head : (group + 1) * head] + b_key[...]
    key_new = jnp.concatenate([key_new, jnp.zeros((8 - STEPS, head), jnp.float32)], 0)
    key_new = key_new * cos_new + pltpu.roll(key_new, head // 2, 1) * sin_new
    key_new = key_new.astype(jnp.bfloat16).astype(jnp.float32)
    value_new = total[:, (group + 1) * head :] + b_value[...]
    value_new = value_new.astype(jnp.bfloat16).astype(jnp.float32)
    scale = 1.0 / math.sqrt(head)

    column = lax.broadcasted_iota(jnp.int32, (rows, 1), 0)
    query_wide = query.astype(jnp.float32)
    fresh = []
    for s in range(STEPS):
        dots = jnp.sum(query_wide * key_new[s : s + 1], 1, keepdims=True) * scale
        seen = jnp.logical_and(is_source, column >= s * group)
        fresh.append((jnp.where(seen, dots, NEG), seen))
    row_max = jnp.maximum(fresh[0][0], fresh[1][0])

    stores = []
    for c in range(blocks):
        for i in range(c * CHUNKS // blocks, (c + 1) * CHUNKS // blocks):
            copies[i].wait()
            part = pl.ds(i * per, per)
            stores.append(pltpu.make_async_copy(held.at[part], new_pool.at[part], out_sems.at[i]))
            stores[-1].start()
        keys = held[c * block : (c + 1) * block, :, :head].reshape(width, head)
        part = lax.dot_general(query, keys, (((1,), (1,)), ((), ())), preferred_element_type=jnp.float32)
        part = jnp.where(tokens[c : c + 1] < limit, part * scale, NEG)
        score[:, c * width : (c + 1) * width] = part
        row_max = jnp.maximum(row_max, jnp.max(part, 1, keepdims=True))
    row_sum = jnp.zeros((rows, 1), jnp.float32)
    out = jnp.zeros((rows, head), jnp.float32)
    for s in range(STEPS):
        weight = jnp.where(fresh[s][1], jnp.exp(fresh[s][0] - row_max), 0.0)
        row_sum = row_sum + weight
        out = out + weight.astype(jnp.bfloat16).astype(jnp.float32) * value_new[s : s + 1]
    for c in range(blocks):
        weight = jnp.exp(score[:, c * width : (c + 1) * width] - row_max)
        weight = jnp.where(tokens[c : c + 1] < limit, weight, 0.0)
        row_sum = row_sum + jnp.sum(weight, 1, keepdims=True)
        values = held[c * block : (c + 1) * block, :, head:].reshape(width, head)
        out = out + jnp.dot(weight.astype(jnp.bfloat16), values, preferred_element_type=jnp.float32)

    diagonal = lax.broadcasted_iota(jnp.int32, (rows, head), 1) == row
    for i in range(rows):
        packed[:, i * head : (i + 1) * head] = out[i : i + 1]
    shifted = lax.broadcasted_iota(jnp.int32, (rows, head), 1) == row + rows
    packed[:, rows * head :] = jnp.sum(
        jnp.where(diagonal, row_max, 0.0) + jnp.where(shifted, row_sum, 0.0), 0, keepdims=True
    )
    sends = [
        pltpu.make_async_copy(packed, copies_out.at[p], send_sem.at[p]) for p in range(copies_out.shape[0])
    ]
    for send in sends:
        send.start()

    slots_copy.wait()

    @pl.when(is_source)
    def _():
        for piece, (low, size) in zip(pieces, LATER):

            def take(j, carry):
                piece[j] = held[slots_of[0, low + j]]
                return carry

            lax.fori_loop(0, size, take, 0)
        page_row = lax.broadcasted_iota(jnp.int32, (page_len, 2 * head), 0)
        entries = jnp.concatenate([key_new[:STEPS], value_new], 1)
        offsets = [limit + s for s in range(STEPS)]
        homes = [slots_of[0, offset // page_len] for offset in offsets]
        for i, slot in enumerate((homes[0], homes[-1])):
            page = held[slot].astype(jnp.float32)
            for s, offset in enumerate(offsets):
                here = jnp.logical_and(homes[s] == slot, page_row == offset % page_len)
                page = jnp.where(here, entries[s : s + 1], page)
            fixed[i] = page.astype(held.dtype)

    plan_copy.wait()
    for store in stores:
        store.wait()

    @pl.when(jnp.logical_not(is_source))
    def _():
        put_pages(slots_of, moved_pages(plan, request), [(0, early), (FAR_AT, far)], new_pool, page_sem)

    for send in sends:
        send.wait()


def attend(lengths, table, plan, sums, b_query, b_key, b_value, cosine, sine, early, far, pool):
    group, head = b_query.shape
    rows = STEPS * group
    page = pool.shape[1:]
    return pl.pallas_call(
        attention_kernel,
        out_shape=(
            pltpu.HBM((sums.shape[0], 1, (rows + 1) * head), jnp.float32),
            pltpu.HBM(pool.shape, pool.dtype),
            jax.ShapeDtypeStruct((2,) + page, pool.dtype),
        )
        + tuple(pltpu.VMEM((size,) + page, pool.dtype) for _, size in LATER),
        in_specs=[SMEM, HBM, HBM] + [VMEM] * 8 + [HBM],
        out_specs=(HBM, HBM, VMEM) + (VMEM,) * len(LATER),
        scratch_shapes=[
            pltpu.VMEM(pool.shape, pool.dtype),
            pltpu.VMEM((rows, pool.shape[0] * pool.shape[1]), jnp.float32),
            pltpu.VMEM((1, (rows + 1) * head), jnp.float32),
            pltpu.VMEM(table.shape, table.dtype),
            pltpu.SMEM(table.shape, table.dtype),
            pltpu.SMEM(plan.shape, plan.dtype),
            pltpu.SemaphoreType.DMA((CHUNKS + 3,)),
            pltpu.SemaphoreType.DMA((CHUNKS,)),
            pltpu.SemaphoreType.DMA((sums.shape[0],)),
            pltpu.SemaphoreType.DMA,
        ],
        compiler_params=params(24),
        name="attend",
    )(
        lengths, *in_hbm(table, plan), sums, b_query, b_key, b_value, cosine, sine, early, far, *in_hbm(pool)
    )


def project_kernel(head, parts, w_out, out):
    pairs, _, width = parts.shape
    rows = width // head - 1
    group = rows // STEPS
    requests = pairs // 2
    lane = lax.broadcasted_iota(jnp.int32, (rows, head), 1)
    row = lax.broadcasted_iota(jnp.int32, (rows, head), 0)

    def column(part, shift):
        line = parts[part, :, rows * head :]
        return jnp.sum(jnp.where(lane == row + shift, line, 0.0), 1, keepdims=True)

    lines = [[] for _ in range(STEPS)]
    for r in range(requests):
        tops = [column(part, 0) for part in (r, r + requests)]
        sums = [column(part, rows) for part in (r, r + requests)]
        top = jnp.maximum(*tops)
        weights = [jnp.exp(one - top) for one in tops]
        total = weights[0] * sums[0] + weights[1] * sums[1]
        shares = [weight / total for weight in weights]
        for s in range(STEPS):
            heads = []
            for i in range(s * group, (s + 1) * group):
                here = slice(i * head, (i + 1) * head)
                heads.append(
                    shares[0][i : i + 1] * parts[r, :, here] + shares[1][i : i + 1] * parts[r + requests, :, here]
                )
            lines[s].append(jnp.concatenate(heads, 1))
    attended = jnp.concatenate(sum(lines, []), 0).astype(jnp.bfloat16)
    result = jnp.dot(attended, w_out[...], preferred_element_type=jnp.float32)
    for s in range(STEPS):
        out[s] = result[s * requests : (s + 1) * requests]


def project(parts, w_out, head):
    return pl.pallas_call(
        functools.partial(project_kernel, head),
        out_shape=jax.ShapeDtypeStruct((STEPS, parts.shape[0] // 2, w_out.shape[1]), jnp.float32),
        in_specs=[VMEM, VMEM],
        out_specs=VMEM,
        compiler_params=params(16),
        name="project",
    )(parts, w_out)


def place_kernel(table, plan, lengths, *refs, starts, patch):
    parts, (base, new_pool, sem) = refs[:-3], refs[-3:]
    del base
    pair_index = lax.axis_index("pair")
    requests = lengths.shape[0]

    @pl.when(pair_index < requests)
    def _():
        put_pages(table, moved_pages(plan, pair_index), list(zip(starts, parts)), new_pool, sem)

    if patch:

        @pl.when(pair_index >= requests)
        def _():
            page_len = new_pool.shape[1]
            first = lengths[pair_index - requests] - PAGES_HALF * page_len
            for i, offset in enumerate((first, first + STEPS - 1)):
                slot = table[0, offset // page_len]
                copy = pltpu.make_async_copy(parts[-1].at[i], new_pool.at[slot], sem)
                copy.start()
                copy.wait()


def place(table, plan, lengths, parts, starts, base, fixed=None):
    patch = fixed is not None
    parts = list(parts) + [fixed] * patch
    return pl.pallas_call(
        functools.partial(place_kernel, starts=starts, patch=patch),
        out_shape=pltpu.HBM(base.shape, base.dtype),
        in_specs=[SMEM] * 3 + [VMEM] * len(parts) + [HBM],
        out_specs=HBM,
        scratch_shapes=[
            pltpu.SemaphoreType.DMA,
        ],
        input_output_aliases={3 + len(parts): 0},
        compiler_params=params(16),
        name="place",
    )(table, plan, lengths, *parts, *in_hbm(base))


def blank_kernel(out):
    del out


def blank(like):
    return pl.pallas_call(
        blank_kernel,
        out_shape=jax.ShapeDtypeStruct(like.shape, like.dtype),
        out_specs=pl.BlockSpec(memory_space=pl.ANY),
        name="blank",
    )()


def local(
    normed, w_query, b_query, w_key, b_key, w_value, b_value, w_out, pool, page_table, lengths, plan
):
    pair_count = lax.axis_size("pair")
    tp_count = lax.axis_size("tp")
    requests = pair_count // 2
    head = w_key.shape[1]

    planned = plan.T
    opening = collect(page_table, pool[0, 0])
    partial, near, far, pieces = prepare(
        page_table, planned, normed, w_query, w_key, w_value, pool[0, 0], pair_count
    )
    bits = min(JOINT, requests)

    def tie(*values):
        return lax.optimization_barrier(values)

    def migrate(pages, members=range(requests)):
        return lax.ppermute(pages, "pair", [(r + requests, r) for r in members])

    either = lax.axis_index("rep") == 0

    def gather(values):
        return lax.all_to_all(values, "pair", split_axis=0, concat_axis=0, tiled=True)

    def choose(code, step, *values):
        members = [[r for r in range(requests) if code >> r % bits & 1] for code in range(1 << bits)]
        return lax.switch(code, [functools.partial(step, chosen) for chosen in members], *values)

    def some(members, pages):
        return migrate(pages, members) if members else blank(pages)

    def first_step(members, values, pages):
        return lax.cond(either, gather, gather, values), some(members, pages)

    def second_step(members, values, beside, pages):
        return gather(values), migrate(beside), some(members, pages)

    first = migrate(opening)
    sums, far_pages = choose(far, first_step, partial, pieces[1])
    sums, first = tie(sums, first)
    second = migrate(tie(pieces[0], sums)[0])

    frequency = rope_base ** (-(jnp.arange(head // 2, dtype=jnp.float32) * 2.0 / head))
    steps = jnp.minimum(jnp.arange(8, dtype=jnp.int32), STEPS - 1)
    position = (lengths[:, None] + steps[None, :]).astype(jnp.float32)[..., None]
    angles = position * frequency
    cosine = jnp.cos(angles)
    sine = jnp.sin(angles)
    cosine = jnp.concatenate([cosine, cosine], -1)
    sine = jnp.concatenate([-sine, sine], -1)

    packed, new_pool, fixed, *later = attend(
        lengths,
        page_table,
        planned,
        sums,
        b_query.reshape(-1, head),
        b_key[None, :],
        b_value[None, :],
        cosine,
        sine,
        first,
        far_pages,
        pool[0, 0],
    )
    near, packed = tie(near, packed)
    parts, beside, near_pages = choose(near, second_step, packed, later[0], later[2])
    parts, second = tie(parts, second)
    third = migrate(tie(later[1], parts)[0])
    projected = project(parts, w_out, head)
    here = [second, beside, near_pages]
    starts = [FIRST, BESIDE_AT, NEAR_AT]
    new_pool = place(page_table, planned, lengths, here, starts, new_pool, fixed)
    if tp_count == 2:
        projected = projected + lax.ppermute(projected, "tp", [(0, 1), (1, 0)])
    else:
        projected = lax.psum(projected, "tp")
    third, projected = tie(third, projected)
    new_pool = place(page_table, planned, lengths, [third], [THIRD_AT], new_pool)
    return projected, new_pool[None, None]


def solution(mesh):
    return jax.shard_map(
        local,
        mesh=mesh,
        in_specs=(
            P(None, "rep", "pair"),
            P("pair", "tp"),
            P("tp"),
            P("pair", "tp"),
            P("tp"),
            P("pair", "tp"),
            P("tp"),
            P("tp", "pair"),
            P(("rep", "pair"), "tp", None, None, None),
            P(("rep", "pair"), None),
            P("rep"),
            P("rep", None),
        ),
        out_specs=(P(None, "rep", "pair"), P(("rep", "pair"), "tp", None, None, None)),
        check_vma=False,
    )
```

```python
import functools
import math

import jax
import jax.numpy as jnp
from jax import lax
from jax.experimental import pallas as pl
from jax.experimental.pallas import tpu as pltpu
from jax.sharding import PartitionSpec as P

PAGES_HALF = 384
STEPS = 2
SECTION = 64
MOVED_MAX = STEPS * SECTION
FIRST, SECOND, BESIDE, THIRD = 26, 32, 9, 7
NEAR, FAR = 26, 28
BESIDE_AT = FIRST + SECOND
THIRD_AT = BESIDE_AT + BESIDE
NEAR_AT = THIRD_AT + THIRD
FAR_AT = NEAR_AT + NEAR
PIECES = ((FIRST, SECOND), (FAR_AT, FAR))
LATER = ((BESIDE_AT, BESIDE), (THIRD_AT, THIRD), (NEAR_AT, NEAR))
JOINT = 4
CHUNKS = 4
NEG = -1e30

rope_base = 1000000.0

VMEM = pl.BlockSpec(memory_space=pltpu.VMEM)
SMEM = pl.BlockSpec(memory_space=pltpu.SMEM)
HBM = pl.BlockSpec(memory_space=pltpu.HBM)


def in_hbm(*arrays):
    return tuple(pltpu.with_memory_space_constraint(a, pltpu.HBM) for a in arrays)


def params(mib):
    return pltpu.CompilerParams(vmem_limit_bytes=mib * 1024 * 1024)


def moved_pages(plan, request):
    count = plan[0, request]
    for s in range(1, STEPS):
        count = count + plan[s, request]
    return count


def put_pages(table, count, parts, new_pool, sem):
    placed = jnp.int32(0)
    for low, pages in parts:
        here = jnp.clip(count - low, 0, pages.shape[0])

        def start(j, carry):
            slot = table[0, PAGES_HALF + low + j]
            pltpu.make_async_copy(pages.at[j], new_pool.at[slot], sem).start()
            return carry

        lax.fori_loop(0, here, start, 0)
        placed = placed + here

    def wait(j, carry):
        pltpu.make_async_copy(parts[0][1].at[0], new_pool.at[0], sem).wait()
        return carry

    lax.fori_loop(0, placed, wait, 0)


def collect_kernel(table_in, pool, piece, table, sem, page_sem):
    @pl.when(lax.axis_index("pair") >= lax.axis_size("pair") // 2)
    def _():
        table_copy = pltpu.make_async_copy(table_in, table, sem)
        table_copy.start()
        table_copy.wait()

        def start(j, carry):
            pltpu.make_async_copy(pool.at[table[0, j]], piece.at[j], page_sem).start()
            return carry

        lax.fori_loop(0, FIRST, start, 0, unroll=2)
        pltpu.make_async_copy(pool.at[pl.ds(0, FIRST)], piece, page_sem).wait()


def collect(table, pool):
    return pl.pallas_call(
        collect_kernel,
        out_shape=pltpu.VMEM((FIRST,) + pool.shape[1:], pool.dtype),
        in_specs=[HBM] * 2,
        out_specs=VMEM,
        scratch_shapes=[
            pltpu.SMEM(table.shape, table.dtype),
            pltpu.SemaphoreType.DMA,
            pltpu.SemaphoreType.DMA,
        ],
        compiler_params=params(16),
        name="collect",
    )(*in_hbm(table, pool))


def prepare_kernel(w_query, table_in, plan_in, normed_in, w_key, w_value, pool, partial, near, far, *refs):
    pieces, (table, plan, normed, weights, index_sems, sems, page_sems) = refs[:-7], refs[-7:]
    pairs = partial.shape[0]
    requests = pairs // 2
    head = w_key.shape[1]
    wide = w_query.shape[1]
    table_copy = pltpu.make_async_copy(table_in, table, index_sems.at[0])
    plan_copy = pltpu.make_async_copy(plan_in, plan, index_sems.at[1])
    table_copy.start()
    plan_copy.start()
    loads = [
        pltpu.make_async_copy(normed_in, normed, sems.at[0]),
        pltpu.make_async_copy(w_key, weights.at[:, :head], sems.at[1]),
        pltpu.make_async_copy(w_value, weights.at[:, head:], sems.at[2]),
    ]
    for copy in loads:
        copy.start()
    table_copy.wait()

    @pl.when(lax.axis_index("pair") >= requests)
    def _():
        for i, (low, size) in enumerate(PIECES):

            def start(j, carry):
                pltpu.make_async_copy(pool.at[table[0, low + j]], pieces[i].at[j], page_sems.at[i]).start()
                return carry

            lax.fori_loop(0, size, start, 0, unroll=2)

    plan_copy.wait()
    bits = min(JOINT, requests)
    for code, bound in ((near, NEAR_AT), (far, FAR_AT)):
        total = jnp.int32(0)
        for bit in range(bits):
            most = moved_pages(plan, bit)
            for r in range(bit + bits, requests, bits):
                most = jnp.maximum(most, moved_pages(plan, r))
            total = total + jnp.where(most > bound, 1 << bit, 0)
        code[0] = total
    for copy in loads:
        copy.wait()
    hidden = jnp.concatenate([normed[s].astype(jnp.float32) for s in range(STEPS)], 0).astype(jnp.bfloat16)
    query = jnp.dot(hidden, w_query[...], preferred_element_type=jnp.float32)
    rest = jnp.dot(hidden, weights[...], preferred_element_type=jnp.float32)
    for r in range(requests):
        lines = [slice(s * requests + r, s * requests + r + 1) for s in range(STEPS)]
        query_lines = jnp.concatenate([query[line] for line in lines], 0)
        rest_lines = jnp.concatenate([rest[line] for line in lines], 0)
        for p in range(r, pairs, requests):
            partial[p, :, :wide] = query_lines
            partial[p, :, wide:] = rest_lines

    @pl.when(lax.axis_index("pair") >= requests)
    def _():
        for i, (_, size) in enumerate(PIECES):
            pltpu.make_async_copy(pool.at[pl.ds(0, size)], pieces[i], page_sems.at[i]).wait()


def prepare(table, plan, normed, w_query, w_key, w_value, pool, pairs):
    page = pool.shape[1:]
    wide = w_query.shape[1] + 2 * w_key.shape[1]
    partial, near, far, *pieces = pl.pallas_call(
        prepare_kernel,
        out_shape=(jax.ShapeDtypeStruct((pairs, STEPS, wide), jnp.float32),)
        + (jax.ShapeDtypeStruct((1,), jnp.int32),) * 2
        + tuple(pltpu.VMEM((size,) + page, pool.dtype) for _, size in PIECES),
        in_specs=[VMEM] + [HBM] * 6,
        out_specs=(VMEM, SMEM, SMEM) + (VMEM,) * len(PIECES),
        scratch_shapes=[
            pltpu.SMEM(table.shape, table.dtype),
            pltpu.SMEM(plan.shape, plan.dtype),
            pltpu.VMEM(normed.shape, normed.dtype),
            pltpu.VMEM((w_key.shape[0], 2 * w_key.shape[1]), w_key.dtype),
            pltpu.SemaphoreType.DMA((2,)),
            pltpu.SemaphoreType.DMA((3,)),
            pltpu.SemaphoreType.DMA((len(PIECES),)),
        ],
        compiler_params=params(16),
        name="prepare",
    )(w_query, *in_hbm(table, plan, normed, w_key, w_value, pool))
    return partial, near.reshape(()), far.reshape(()), pieces


def page_order(table, slots):
    slot = lax.broadcasted_iota(jnp.int32, (slots, slots), 0)
    holds = jnp.where(slot == table, 1.0, 0.0).astype(jnp.bfloat16)
    index = lax.broadcasted_iota(jnp.int32, (8, slots), 1)
    digit = lax.broadcasted_iota(jnp.int32, (8, slots), 0)
    digits = jnp.where(digit == 0, index // 16, jnp.where(digit == 1, index % 16, 0))
    digits = digits.astype(jnp.float32).astype(jnp.bfloat16)
    return lax.dot_general(digits, holds, (((1,), (1,)), ((), ())), preferred_element_type=jnp.float32)


def attention_kernel(
    lengths, table_in, plan_in, sums, b_query, b_key, b_value, cosine, sine, early, far, pool,
    copies_out, new_pool, fixed, *refs
):
    pieces, refs = refs[: len(LATER)], refs[len(LATER) :]
    held, score, packed, table, slots_of, plan, sems, out_sems, send_sem, page_sem = refs
    slots, page_len, _ = held.shape
    per = slots // CHUNKS
    table_copy = pltpu.make_async_copy(table_in, table, sems.at[CHUNKS])
    table_copy.start()
    slots_copy = pltpu.make_async_copy(table_in, slots_of, sems.at[CHUNKS + 1])
    slots_copy.start()
    plan_copy = pltpu.make_async_copy(plan_in, plan, sems.at[CHUNKS + 2])
    plan_copy.start()
    copies = []
    for c in range(CHUNKS):
        part = pl.ds(c * per, per)
        copies.append(pltpu.make_async_copy(pool.at[part], held.at[part], sems.at[c]))
        copies[-1].start()
    requests = sums.shape[0] // 2
    group, head = b_query.shape
    rows = STEPS * group
    pair_index = lax.axis_index("pair")
    is_source = pair_index >= requests
    request = jnp.where(is_source, pair_index - requests, pair_index)
    half_tokens = PAGES_HALF * page_len
    limit = jnp.where(is_source, lengths[request] - half_tokens, half_tokens)

    blocks = CHUNKS // 2
    block = slots // blocks
    width = block * page_len
    table_copy.wait()
    digits = page_order(table[...], slots)
    digits = jnp.concatenate(
        [digits[d : d + 1, c * block : (c + 1) * block] for d in range(2) for c in range(blocks)], 0
    ).astype(jnp.bfloat16)
    spread = lax.broadcasted_iota(jnp.int32, (block, width), 1) // page_len
    spread = jnp.where(spread == lax.broadcasted_iota(jnp.int32, (block, width), 0), 1.0, 0.0)
    digits = jnp.dot(digits, spread.astype(jnp.bfloat16), preferred_element_type=jnp.float32)
    tokens = (digits[:blocks] * 16.0 + digits[blocks:]).astype(jnp.int32) * page_len
    tokens = tokens + lax.broadcasted_iota(jnp.int32, (blocks, width), 1) % page_len

    total = sums[0]
    for p in range(1, sums.shape[0]):
        total = total + sums[p]
    query = jnp.concatenate(
        [total[s : s + 1, h * head : (h + 1) * head] for s in range(STEPS) for h in range(group)], 0
    )
    query = query + jnp.concatenate([b_query[...]] * STEPS, 0)
    cos_new = cosine[request]
    sin_new = sine[request]
    row = lax.broadcasted_iota(jnp.int32, (rows, head), 0)
    cos_rows = jnp.where(row < group, cos_new[0:1], cos_new[1:2])
    sin_rows = jnp.where(row < group, sin_new[0:1], sin_new[1:2])
    query = (query * cos_rows + pltpu.roll(query, head // 2, 1) * sin_rows).astype(jnp.bfloat16)
    key_new = total[:, group * head : (group + 1) * head] + b_key[...]
    key_new = jnp.concatenate([key_new, jnp.zeros((8 - STEPS, head), jnp.float32)], 0)
    key_new = key_new * cos_new + pltpu.roll(key_new, head // 2, 1) * sin_new
    key_new = key_new.astype(jnp.bfloat16).astype(jnp.float32)
    value_new = total[:, (group + 1) * head :] + b_value[...]
    value_new = value_new.astype(jnp.bfloat16).astype(jnp.float32)
    scale = 1.0 / math.sqrt(head)

    column = lax.broadcasted_iota(jnp.int32, (rows, 1), 0)
    query_wide = query.astype(jnp.float32)
    fresh = []
    for s in range(STEPS):
        dots = jnp.sum(query_wide * key_new[s : s + 1], 1, keepdims=True) * scale
        seen = jnp.logical_and(is_source, column >= s * group)
        fresh.append((jnp.where(seen, dots, NEG), seen))
    row_max = jnp.maximum(fresh[0][0], fresh[1][0])

    stores = []
    for c in range(blocks):
        for i in range(c * CHUNKS // blocks, (c + 1) * CHUNKS // blocks):
            copies[i].wait()
            part = pl.ds(i * per, per)
            stores.append(pltpu.make_async_copy(held.at[part], new_pool.at[part], out_sems.at[i]))
            stores[-1].start()
        keys = held[c * block : (c + 1) * block, :, :head].reshape(width, head)
        part = lax.dot_general(query, keys, (((1,), (1,)), ((), ())), preferred_element_type=jnp.float32)
        part = jnp.where(tokens[c : c + 1] < limit, part * scale, NEG)
        score[:, c * width : (c + 1) * width] = part
        row_max = jnp.maximum(row_max, jnp.max(part, 1, keepdims=True))
    row_sum = jnp.zeros((rows, 1), jnp.float32)
    out = jnp.zeros((rows, head), jnp.float32)
    for s in range(STEPS):
        weight = jnp.where(fresh[s][1], jnp.exp(fresh[s][0] - row_max), 0.0)
        row_sum = row_sum + weight
        out = out + weight.astype(jnp.bfloat16).astype(jnp.float32) * value_new[s : s + 1]
    for c in range(blocks):
        weight = jnp.exp(score[:, c * width : (c + 1) * width] - row_max)
        weight = jnp.where(tokens[c : c + 1] < limit, weight, 0.0)
        row_sum = row_sum + jnp.sum(weight, 1, keepdims=True)
        values = held[c * block : (c + 1) * block, :, head:].reshape(width, head)
        out = out + jnp.dot(weight.astype(jnp.bfloat16), values, preferred_element_type=jnp.float32)

    diagonal = lax.broadcasted_iota(jnp.int32, (rows, head), 1) == row
    for i in range(rows):
        packed[:, i * head : (i + 1) * head] = out[i : i + 1]
    shifted = lax.broadcasted_iota(jnp.int32, (rows, head), 1) == row + rows
    packed[:, rows * head :] = jnp.sum(
        jnp.where(diagonal, row_max, 0.0) + jnp.where(shifted, row_sum, 0.0), 0, keepdims=True
    )
    sends = [
        pltpu.make_async_copy(packed, copies_out.at[p], send_sem.at[p]) for p in range(copies_out.shape[0])
    ]
    for send in sends:
        send.start()

    slots_copy.wait()

    @pl.when(is_source)
    def _():
        for piece, (low, size) in zip(pieces, LATER):

            def take(j, carry):
                piece[j] = held[slots_of[0, low + j]]
                return carry

            lax.fori_loop(0, size, take, 0)
        page_row = lax.broadcasted_iota(jnp.int32, (page_len, 2 * head), 0)
        entries = jnp.concatenate([key_new[:STEPS], value_new], 1)
        offsets = [limit + s for s in range(STEPS)]
        homes = [slots_of[0, offset // page_len] for offset in offsets]
        for i, slot in enumerate((homes[0], homes[-1])):
            page = held[slot].astype(jnp.float32)
            for s, offset in enumerate(offsets):
                here = jnp.logical_and(homes[s] == slot, page_row == offset % page_len)
                page = jnp.where(here, entries[s : s + 1], page)
            fixed[i] = page.astype(held.dtype)

    plan_copy.wait()
    for store in stores:
        store.wait()

    @pl.when(jnp.logical_not(is_source))
    def _():
        put_pages(slots_of, moved_pages(plan, request), [(0, early), (FAR_AT, far)], new_pool, page_sem)

    for send in sends:
        send.wait()


def attend(lengths, table, plan, sums, b_query, b_key, b_value, cosine, sine, early, far, pool):
    group, head = b_query.shape
    rows = STEPS * group
    page = pool.shape[1:]
    return pl.pallas_call(
        attention_kernel,
        out_shape=(
            pltpu.HBM((sums.shape[0], 1, (rows + 1) * head), jnp.float32),
            pltpu.HBM(pool.shape, pool.dtype),
            jax.ShapeDtypeStruct((2,) + page, pool.dtype),
        )
        + tuple(pltpu.VMEM((size,) + page, pool.dtype) for _, size in LATER),
        in_specs=[SMEM, HBM, HBM] + [VMEM] * 8 + [HBM],
        out_specs=(HBM, HBM, VMEM) + (VMEM,) * len(LATER),
        scratch_shapes=[
            pltpu.VMEM(pool.shape, pool.dtype),
            pltpu.VMEM((rows, pool.shape[0] * pool.shape[1]), jnp.float32),
            pltpu.VMEM((1, (rows + 1) * head), jnp.float32),
            pltpu.VMEM(table.shape, table.dtype),
            pltpu.SMEM(table.shape, table.dtype),
            pltpu.SMEM(plan.shape, plan.dtype),
            pltpu.SemaphoreType.DMA((CHUNKS + 3,)),
            pltpu.SemaphoreType.DMA((CHUNKS,)),
            pltpu.SemaphoreType.DMA((sums.shape[0],)),
            pltpu.SemaphoreType.DMA,
        ],
        compiler_params=params(24),
        name="attend",
    )(
        lengths, *in_hbm(table, plan), sums, b_query, b_key, b_value, cosine, sine, early, far, *in_hbm(pool)
    )


def project_kernel(head, parts, w_out, out):
    pairs, _, width = parts.shape
    rows = width // head - 1
    group = rows // STEPS
    requests = pairs // 2
    lane = lax.broadcasted_iota(jnp.int32, (rows, head), 1)
    row = lax.broadcasted_iota(jnp.int32, (rows, head), 0)

    def column(part, shift):
        line = parts[part, :, rows * head :]
        return jnp.sum(jnp.where(lane == row + shift, line, 0.0), 1, keepdims=True)

    lines = [[] for _ in range(STEPS)]
    for r in range(requests):
        tops = [column(part, 0) for part in (r, r + requests)]
        sums = [column(part, rows) for part in (r, r + requests)]
        top = jnp.maximum(*tops)
        weights = [jnp.exp(one - top) for one in tops]
        total = weights[0] * sums[0] + weights[1] * sums[1]
        shares = [weight / total for weight in weights]
        for s in range(STEPS):
            heads = []
            for i in range(s * group, (s + 1) * group):
                here = slice(i * head, (i + 1) * head)
                heads.append(
                    shares[0][i : i + 1] * parts[r, :, here] + shares[1][i : i + 1] * parts[r + requests, :, here]
                )
            lines[s].append(jnp.concatenate(heads, 1))
    attended = jnp.concatenate(sum(lines, []), 0).astype(jnp.bfloat16)
    result = jnp.dot(attended, w_out[...], preferred_element_type=jnp.float32)
    for s in range(STEPS):
        out[s] = result[s * requests : (s + 1) * requests]


def project(parts, w_out, head):
    return pl.pallas_call(
        functools.partial(project_kernel, head),
        out_shape=jax.ShapeDtypeStruct((STEPS, parts.shape[0] // 2, w_out.shape[1]), jnp.float32),
        in_specs=[VMEM, VMEM],
        out_specs=VMEM,
        compiler_params=params(16),
        name="project",
    )(parts, w_out)


def place_kernel(table, plan, lengths, *refs, starts, patch):
    parts, (base, new_pool, sem) = refs[:-3], refs[-3:]
    del base
    pair_index = lax.axis_index("pair")
    requests = lengths.shape[0]

    @pl.when(pair_index < requests)
    def _():
        put_pages(table, moved_pages(plan, pair_index), list(zip(starts, parts)), new_pool, sem)

    if patch:

        @pl.when(pair_index >= requests)
        def _():
            page_len = new_pool.shape[1]
            first = lengths[pair_index - requests] - PAGES_HALF * page_len
            for i, offset in enumerate((first, first + STEPS - 1)):
                slot = table[0, offset // page_len]
                copy = pltpu.make_async_copy(parts[-1].at[i], new_pool.at[slot], sem)
                copy.start()
                copy.wait()


def place(table, plan, lengths, parts, starts, base, fixed=None):
    patch = fixed is not None
    parts = list(parts) + [fixed] * patch
    return pl.pallas_call(
        functools.partial(place_kernel, starts=starts, patch=patch),
        out_shape=pltpu.HBM(base.shape, base.dtype),
        in_specs=[SMEM] * 3 + [VMEM] * len(parts) + [HBM],
        out_specs=HBM,
        scratch_shapes=[
            pltpu.SemaphoreType.DMA,
        ],
        input_output_aliases={3 + len(parts): 0},
        compiler_params=params(16),
        name="place",
    )(table, plan, lengths, *parts, *in_hbm(base))


def blank_kernel(out):
    del out


def blank(like):
    return pl.pallas_call(
        blank_kernel,
        out_shape=jax.ShapeDtypeStruct(like.shape, like.dtype),
        out_specs=pl.BlockSpec(memory_space=pl.ANY),
        name="blank",
    )()


def local(
    normed, w_query, b_query, w_key, b_key, w_value, b_value, w_out, pool, page_table, lengths, plan
):
    pair_count = lax.axis_size("pair")
    tp_count = lax.axis_size("tp")
    requests = pair_count // 2
    head = w_key.shape[1]

    planned = plan.T
    opening = collect(page_table, pool[0, 0])
    partial, near, far, pieces = prepare(
        page_table, planned, normed, w_query, w_key, w_value, pool[0, 0], pair_count
    )
    bits = min(JOINT, requests)

    def tie(*values):
        return lax.optimization_barrier(values)

    def migrate(pages, members=range(requests)):
        return lax.ppermute(pages, "pair", [(r + requests, r) for r in members])

    either = lax.axis_index("rep") == 0

    def gather(values):
        return lax.all_to_all(values, "pair", split_axis=0, concat_axis=0, tiled=True)

    def choose(code, step, *values):
        members = [[r for r in range(requests) if code >> r % bits & 1] for code in range(1 << bits)]
        return lax.switch(code, [functools.partial(step, chosen) for chosen in members], *values)

    def some(members, pages):
        return migrate(pages, members) if members else blank(pages)

    def first_step(members, values, pages):
        return lax.cond(either, gather, gather, values), some(members, pages)

    def second_step(members, values, beside, pages):
        return gather(values), migrate(beside), some(members, pages)

    first = migrate(opening)
    sums, far_pages = choose(far, first_step, partial, pieces[1])
    sums, first = tie(sums, first)
    second = migrate(tie(pieces[0], sums)[0])

    frequency = rope_base ** (-(jnp.arange(head // 2, dtype=jnp.float32) * 2.0 / head))
    steps = jnp.minimum(jnp.arange(8, dtype=jnp.int32), STEPS - 1)
    position = (lengths[:, None] + steps[None, :]).astype(jnp.float32)[..., None]
    angles = position * frequency
    cosine = jnp.cos(angles)
    sine = jnp.sin(angles)
    cosine = jnp.concatenate([cosine, cosine], -1)
    sine = jnp.concatenate([-sine, sine], -1)

    packed, new_pool, fixed, *later = attend(
        lengths,
        page_table,
        planned,
        sums,
        b_query.reshape(-1, head),
        b_key[None, :],
        b_value[None, :],
        cosine,
        sine,
        first,
        far_pages,
        pool[0, 0],
    )
    near, packed = tie(near, packed)
    parts, beside, near_pages = choose(near, second_step, packed, later[0], later[2])
    parts, second = tie(parts, second)
    third = migrate(tie(later[1], parts)[0])
    projected = project(parts, w_out, head)
    here = [second, beside, near_pages]
    starts = [FIRST, BESIDE_AT, NEAR_AT]
    new_pool = place(page_table, planned, lengths, here, starts, new_pool, fixed)
    if tp_count == 2:
        projected = projected + lax.ppermute(projected, "tp", [(0, 1), (1, 0)])
    else:
        projected = lax.psum(projected, "tp")
    third, projected = tie(third, projected)
    new_pool = place(page_table, planned, lengths, [third], [THIRD_AT], new_pool)
    return projected, new_pool[None, None]


def solution(mesh):
    return jax.shard_map(
        local,
        mesh=mesh,
        in_specs=(
            P(None, "rep", "pair"),
            P("pair", "tp"),
            P("tp"),
            P("pair", "tp"),
            P("tp"),
            P("pair", "tp"),
            P("tp"),
            P("tp", "pair"),
            P(("rep", "pair"), "tp", None, None, None),
            P(("rep", "pair"), None),
            P("rep"),
            P("rep", None),
        ),
        out_specs=(P(None, "rep", "pair"), P(("rep", "pair"), "tp", None, None, None)),
        check_vma=False,
    )
```

```python
import functools
import math

import jax
import jax.numpy as jnp
from jax import lax
from jax.experimental import pallas as pl
from jax.experimental.pallas import tpu as pltpu
from jax.sharding import PartitionSpec as P

PAGES_HALF = 384
STEPS = 2
SECTION = 64
MOVED_MAX = STEPS * SECTION
FIRST, SECOND, BESIDE, THIRD = 26, 32, 9, 7
NEAR, FAR = 26, 28
BESIDE_AT = FIRST + SECOND
THIRD_AT = BESIDE_AT + BESIDE
NEAR_AT = THIRD_AT + THIRD
FAR_AT = NEAR_AT + NEAR
PIECES = ((FIRST, SECOND), (FAR_AT, FAR))
LATER = ((BESIDE_AT, BESIDE), (THIRD_AT, THIRD), (NEAR_AT, NEAR))
JOINT = 4
CHUNKS = 4
NEG = -1e30

rope_base = 1000000.0

VMEM = pl.BlockSpec(memory_space=pltpu.VMEM)
SMEM = pl.BlockSpec(memory_space=pltpu.SMEM)
HBM = pl.BlockSpec(memory_space=pltpu.HBM)


def in_hbm(*arrays):
    return tuple(pltpu.with_memory_space_constraint(a, pltpu.HBM) for a in arrays)


def params(mib):
    return pltpu.CompilerParams(vmem_limit_bytes=mib * 1024 * 1024)


def moved_pages(plan, request):
    count = plan[0, request]
    for s in range(1, STEPS):
        count = count + plan[s, request]
    return count


def put_pages(table, count, parts, new_pool, sem):
    placed = jnp.int32(0)
    for low, pages in parts:
        here = jnp.clip(count - low, 0, pages.shape[0])

        def start(j, carry):
            slot = table[0, PAGES_HALF + low + j]
            pltpu.make_async_copy(pages.at[j], new_pool.at[slot], sem).start()
            return carry

        lax.fori_loop(0, here, start, 0)
        placed = placed + here

    def wait(j, carry):
        pltpu.make_async_copy(parts[0][1].at[0], new_pool.at[0], sem).wait()
        return carry

    lax.fori_loop(0, placed, wait, 0)


def collect_kernel(table_in, pool, piece, table, sem, page_sem):
    @pl.when(lax.axis_index("pair") >= lax.axis_size("pair") // 2)
    def _():
        table_copy = pltpu.make_async_copy(table_in, table, sem)
        table_copy.start()
        table_copy.wait()

        def start(j, carry):
            pltpu.make_async_copy(pool.at[table[0, j]], piece.at[j], page_sem).start()
            return carry

        lax.fori_loop(0, FIRST, start, 0, unroll=2)
        pltpu.make_async_copy(pool.at[pl.ds(0, FIRST)], piece, page_sem).wait()


def collect(table, pool):
    return pl.pallas_call(
        collect_kernel,
        out_shape=pltpu.VMEM((FIRST,) + pool.shape[1:], pool.dtype),
        in_specs=[HBM] * 2,
        out_specs=VMEM,
        scratch_shapes=[
            pltpu.SMEM(table.shape, table.dtype),
            pltpu.SemaphoreType.DMA,
            pltpu.SemaphoreType.DMA,
        ],
        compiler_params=params(16),
        name="collect",
    )(*in_hbm(table, pool))


def prepare_kernel(w_query, table_in, plan_in, normed_in, w_key, w_value, pool, partial, near, far, *refs):
    pieces, (table, plan, normed, weights, index_sems, sems, page_sems) = refs[:-7], refs[-7:]
    pairs = partial.shape[0]
    requests = pairs // 2
    head = w_key.shape[1]
    wide = w_query.shape[1]
    table_copy = pltpu.make_async_copy(table_in, table, index_sems.at[0])
    plan_copy = pltpu.make_async_copy(plan_in, plan, index_sems.at[1])
    table_copy.start()
    plan_copy.start()
    loads = [
        pltpu.make_async_copy(normed_in, normed, sems.at[0]),
        pltpu.make_async_copy(w_key, weights.at[:, :head], sems.at[1]),
        pltpu.make_async_copy(w_value, weights.at[:, head:], sems.at[2]),
    ]
    for copy in loads:
        copy.start()
    table_copy.wait()

    @pl.when(lax.axis_index("pair") >= requests)
    def _():
        for i, (low, size) in enumerate(PIECES):

            def start(j, carry):
                pltpu.make_async_copy(pool.at[table[0, low + j]], pieces[i].at[j], page_sems.at[i]).start()
                return carry

            lax.fori_loop(0, size, start, 0, unroll=2)

    plan_copy.wait()
    bits = min(JOINT, requests)
    for code, bound in ((near, NEAR_AT), (far, FAR_AT)):
        total = jnp.int32(0)
        for bit in range(bits):
            most = moved_pages(plan, bit)
            for r in range(bit + bits, requests, bits):
                most = jnp.maximum(most, moved_pages(plan, r))
            total = total + jnp.where(most > bound, 1 << bit, 0)
        code[0] = total
    for copy in loads:
        copy.wait()
    hidden = jnp.concatenate([normed[s].astype(jnp.float32) for s in range(STEPS)], 0).astype(jnp.bfloat16)
    query = jnp.dot(hidden, w_query[...], preferred_element_type=jnp.float32)
    rest = jnp.dot(hidden, weights[...], preferred_element_type=jnp.float32)
    for r in range(requests):
        lines = [slice(s * requests + r, s * requests + r + 1) for s in range(STEPS)]
        query_lines = jnp.concatenate([query[line] for line in lines], 0)
        rest_lines = jnp.concatenate([rest[line] for line in lines], 0)
        for p in range(r, pairs, requests):
            partial[p, :, :wide] = query_lines
            partial[p, :, wide:] = rest_lines

    @pl.when(lax.axis_index("pair") >= requests)
    def _():
        for i, (_, size) in enumerate(PIECES):
            pltpu.make_async_copy(pool.at[pl.ds(0, size)], pieces[i], page_sems.at[i]).wait()


def prepare(table, plan, normed, w_query, w_key, w_value, pool, pairs):
    page = pool.shape[1:]
    wide = w_query.shape[1] + 2 * w_key.shape[1]
    partial, near, far, *pieces = pl.pallas_call(
        prepare_kernel,
        out_shape=(jax.ShapeDtypeStruct((pairs, STEPS, wide), jnp.float32),)
        + (jax.ShapeDtypeStruct((1,), jnp.int32),) * 2
        + tuple(pltpu.VMEM((size,) + page, pool.dtype) for _, size in PIECES),
        in_specs=[VMEM] + [HBM] * 6,
        out_specs=(VMEM, SMEM, SMEM) + (VMEM,) * len(PIECES),
        scratch_shapes=[
            pltpu.SMEM(table.shape, table.dtype),
            pltpu.SMEM(plan.shape, plan.dtype),
            pltpu.VMEM(normed.shape, normed.dtype),
            pltpu.VMEM((w_key.shape[0], 2 * w_key.shape[1]), w_key.dtype),
            pltpu.SemaphoreType.DMA((2,)),
            pltpu.SemaphoreType.DMA((3,)),
            pltpu.SemaphoreType.DMA((len(PIECES),)),
        ],
        compiler_params=params(16),
        name="prepare",
    )(w_query, *in_hbm(table, plan, normed, w_key, w_value, pool))
    return partial, near.reshape(()), far.reshape(()), pieces


def page_order(table, slots):
    slot = lax.broadcasted_iota(jnp.int32, (slots, slots), 0)
    holds = jnp.where(slot == table, 1.0, 0.0).astype(jnp.bfloat16)
    index = lax.broadcasted_iota(jnp.int32, (8, slots), 1)
    digit = lax.broadcasted_iota(jnp.int32, (8, slots), 0)
    digits = jnp.where(digit == 0, index // 16, jnp.where(digit == 1, index % 16, 0))
    digits = digits.astype(jnp.float32).astype(jnp.bfloat16)
    return lax.dot_general(digits, holds, (((1,), (1,)), ((), ())), preferred_element_type=jnp.float32)


def attention_kernel(
    lengths, table_in, plan_in, sums, b_query, b_key, b_value, cosine, sine, early, far, pool,
    copies_out, new_pool, fixed, *refs
):
    pieces, refs = refs[: len(LATER)], refs[len(LATER) :]
    held, score, packed, table, slots_of, plan, sems, out_sems, send_sem, page_sem = refs
    slots, page_len, _ = held.shape
    per = slots // CHUNKS
    table_copy = pltpu.make_async_copy(table_in, table, sems.at[CHUNKS])
    table_copy.start()
    slots_copy = pltpu.make_async_copy(table_in, slots_of, sems.at[CHUNKS + 1])
    slots_copy.start()
    plan_copy = pltpu.make_async_copy(plan_in, plan, sems.at[CHUNKS + 2])
    plan_copy.start()
    copies = []
    for c in range(CHUNKS):
        part = pl.ds(c * per, per)
        copies.append(pltpu.make_async_copy(pool.at[part], held.at[part], sems.at[c]))
        copies[-1].start()
    requests = sums.shape[0] // 2
    group, head = b_query.shape
    rows = STEPS * group
    pair_index = lax.axis_index("pair")
    is_source = pair_index >= requests
    request = jnp.where(is_source, pair_index - requests, pair_index)
    half_tokens = PAGES_HALF * page_len
    limit = jnp.where(is_source, lengths[request] - half_tokens, half_tokens)

    blocks = CHUNKS // 2
    block = slots // blocks
    width = block * page_len
    table_copy.wait()
    digits = page_order(table[...], slots)
    digits = jnp.concatenate(
        [digits[d : d + 1, c * block : (c + 1) * block] for d in range(2) for c in range(blocks)], 0
    ).astype(jnp.bfloat16)
    spread = lax.broadcasted_iota(jnp.int32, (block, width), 1) // page_len
    spread = jnp.where(spread == lax.broadcasted_iota(jnp.int32, (block, width), 0), 1.0, 0.0)
    digits = jnp.dot(digits, spread.astype(jnp.bfloat16), preferred_element_type=jnp.float32)
    tokens = (digits[:blocks] * 16.0 + digits[blocks:]).astype(jnp.int32) * page_len
    tokens = tokens + lax.broadcasted_iota(jnp.int32, (blocks, width), 1) % page_len

    stores = []

    def pass_on():
        i = len(stores)
        copies[i].wait()
        part = pl.ds(i * per, per)
        stores.append(pltpu.make_async_copy(held.at[part], new_pool.at[part], out_sems.at[i]))
        stores[-1].start()

    pass_on()
    total = sums[0]
    for p in range(1, sums.shape[0]):
        total = total + sums[p]
    query = jnp.concatenate(
        [total[s : s + 1, h * head : (h + 1) * head] for s in range(STEPS) for h in range(group)], 0
    )
    query = query + jnp.concatenate([b_query[...]] * STEPS, 0)
    cos_new = cosine[request]
    sin_new = sine[request]
    row = lax.broadcasted_iota(jnp.int32, (rows, head), 0)
    cos_rows = jnp.where(row < group, cos_new[0:1], cos_new[1:2])
    sin_rows = jnp.where(row < group, sin_new[0:1], sin_new[1:2])
    query = (query * cos_rows + pltpu.roll(query, head // 2, 1) * sin_rows).astype(jnp.bfloat16)
    key_new = total[:, group * head : (group + 1) * head] + b_key[...]
    key_new = jnp.concatenate([key_new, jnp.zeros((8 - STEPS, head), jnp.float32)], 0)
    key_new = key_new * cos_new + pltpu.roll(key_new, head // 2, 1) * sin_new
    key_new = key_new.astype(jnp.bfloat16).astype(jnp.float32)
    value_new = total[:, (group + 1) * head :] + b_value[...]
    value_new = value_new.astype(jnp.bfloat16).astype(jnp.float32)
    scale = 1.0 / math.sqrt(head)

    column = lax.broadcasted_iota(jnp.int32, (rows, 1), 0)
    query_wide = query.astype(jnp.float32)
    fresh = []
    for s in range(STEPS):
        dots = jnp.sum(query_wide * key_new[s : s + 1], 1, keepdims=True) * scale
        seen = jnp.logical_and(is_source, column >= s * group)
        fresh.append((jnp.where(seen, dots, NEG), seen))
    row_max = jnp.maximum(fresh[0][0], fresh[1][0])

    pass_on()
    for c in range(blocks):
        while len(stores) < (c + 1) * CHUNKS // blocks:
            pass_on()
        keys = held[c * block : (c + 1) * block, :, :head].reshape(width, head)
        part = lax.dot_general(query, keys, (((1,), (1,)), ((), ())), preferred_element_type=jnp.float32)
        part = jnp.where(tokens[c : c + 1] < limit, part * scale, NEG)
        score[:, c * width : (c + 1) * width] = part
        row_max = jnp.maximum(row_max, jnp.max(part, 1, keepdims=True))
    row_sum = jnp.zeros((rows, 1), jnp.float32)
    out = jnp.zeros((rows, head), jnp.float32)
    for s in range(STEPS):
        weight = jnp.where(fresh[s][1], jnp.exp(fresh[s][0] - row_max), 0.0)
        row_sum = row_sum + weight
        out = out + weight.astype(jnp.bfloat16).astype(jnp.float32) * value_new[s : s + 1]
    for c in range(blocks):
        weight = jnp.exp(score[:, c * width : (c + 1) * width] - row_max)
        weight = jnp.where(tokens[c : c + 1] < limit, weight, 0.0)
        row_sum = row_sum + jnp.sum(weight, 1, keepdims=True)
        values = held[c * block : (c + 1) * block, :, head:].reshape(width, head)
        out = out + jnp.dot(weight.astype(jnp.bfloat16), values, preferred_element_type=jnp.float32)

    diagonal = lax.broadcasted_iota(jnp.int32, (rows, head), 1) == row
    for i in range(rows):
        packed[:, i * head : (i + 1) * head] = out[i : i + 1]
    shifted = lax.broadcasted_iota(jnp.int32, (rows, head), 1) == row + rows
    packed[:, rows * head :] = jnp.sum(
        jnp.where(diagonal, row_max, 0.0) + jnp.where(shifted, row_sum, 0.0), 0, keepdims=True
    )
    sends = [
        pltpu.make_async_copy(packed, copies_out.at[p], send_sem.at[p]) for p in range(copies_out.shape[0])
    ]
    for send in sends:
        send.start()

    slots_copy.wait()

    @pl.when(is_source)
    def _():
        for piece, (low, size) in zip(pieces, LATER):

            def take(j, carry):
                piece[j] = held[slots_of[0, low + j]]
                return carry

            lax.fori_loop(0, size, take, 0)
        page_row = lax.broadcasted_iota(jnp.int32, (page_len, 2 * head), 0)
        entries = jnp.concatenate([key_new[:STEPS], value_new], 1)
        offsets = [limit + s for s in range(STEPS)]
        homes = [slots_of[0, offset // page_len] for offset in offsets]
        for i, slot in enumerate((homes[0], homes[-1])):
            page = held[slot].astype(jnp.float32)
            for s, offset in enumerate(offsets):
                here = jnp.logical_and(homes[s] == slot, page_row == offset % page_len)
                page = jnp.where(here, entries[s : s + 1], page)
            fixed[i] = page.astype(held.dtype)

    plan_copy.wait()
    for store in stores:
        store.wait()

    @pl.when(jnp.logical_not(is_source))
    def _():
        put_pages(slots_of, moved_pages(plan, request), [(0, early), (FAR_AT, far)], new_pool, page_sem)

    for send in sends:
        send.wait()


def attend(lengths, table, plan, sums, b_query, b_key, b_value, cosine, sine, early, far, pool):
    group, head = b_query.shape
    rows = STEPS * group
    page = pool.shape[1:]
    return pl.pallas_call(
        attention_kernel,
        out_shape=(
            pltpu.HBM((sums.shape[0], 1, (rows + 1) * head), jnp.float32),
            pltpu.HBM(pool.shape, pool.dtype),
            jax.ShapeDtypeStruct((2,) + page, pool.dtype),
        )
        + tuple(pltpu.VMEM((size,) + page, pool.dtype) for _, size in LATER),
        in_specs=[SMEM, HBM, HBM] + [VMEM] * 8 + [HBM],
        out_specs=(HBM, HBM, VMEM) + (VMEM,) * len(LATER),
        scratch_shapes=[
            pltpu.VMEM(pool.shape, pool.dtype),
            pltpu.VMEM((rows, pool.shape[0] * pool.shape[1]), jnp.float32),
            pltpu.VMEM((1, (rows + 1) * head), jnp.float32),
            pltpu.VMEM(table.shape, table.dtype),
            pltpu.SMEM(table.shape, table.dtype),
            pltpu.SMEM(plan.shape, plan.dtype),
            pltpu.SemaphoreType.DMA((CHUNKS + 3,)),
            pltpu.SemaphoreType.DMA((CHUNKS,)),
            pltpu.SemaphoreType.DMA((sums.shape[0],)),
            pltpu.SemaphoreType.DMA,
        ],
        compiler_params=params(24),
        name="attend",
    )(
        lengths, *in_hbm(table, plan), sums, b_query, b_key, b_value, cosine, sine, early, far, *in_hbm(pool)
    )


def project_kernel(head, parts, w_out, out):
    pairs, _, width = parts.shape
    rows = width // head - 1
    group = rows // STEPS
    requests = pairs // 2
    lane = lax.broadcasted_iota(jnp.int32, (rows, head), 1)
    row = lax.broadcasted_iota(jnp.int32, (rows, head), 0)

    def column(part, shift):
        line = parts[part, :, rows * head :]
        return jnp.sum(jnp.where(lane == row + shift, line, 0.0), 1, keepdims=True)

    lines = [[] for _ in range(STEPS)]
    for r in range(requests):
        tops = [column(part, 0) for part in (r, r + requests)]
        sums = [column(part, rows) for part in (r, r + requests)]
        top = jnp.maximum(*tops)
        weights = [jnp.exp(one - top) for one in tops]
        total = weights[0] * sums[0] + weights[1] * sums[1]
        shares = [weight / total for weight in weights]
        for s in range(STEPS):
            heads = []
            for i in range(s * group, (s + 1) * group):
                here = slice(i * head, (i + 1) * head)
                heads.append(
                    shares[0][i : i + 1] * parts[r, :, here] + shares[1][i : i + 1] * parts[r + requests, :, here]
                )
            lines[s].append(jnp.concatenate(heads, 1))
    attended = jnp.concatenate(sum(lines, []), 0).astype(jnp.bfloat16)
    result = jnp.dot(attended, w_out[...], preferred_element_type=jnp.float32)
    for s in range(STEPS):
        out[s] = result[s * requests : (s + 1) * requests]


def project(parts, w_out, head):
    return pl.pallas_call(
        functools.partial(project_kernel, head),
        out_shape=jax.ShapeDtypeStruct((STEPS, parts.shape[0] // 2, w_out.shape[1]), jnp.float32),
        in_specs=[VMEM, VMEM],
        out_specs=VMEM,
        compiler_params=params(16),
        name="project",
    )(parts, w_out)


def place_kernel(table, plan, lengths, *refs, starts, patch):
    parts, (base, new_pool, sem) = refs[:-3], refs[-3:]
    del base
    pair_index = lax.axis_index("pair")
    requests = lengths.shape[0]

    @pl.when(pair_index < requests)
    def _():
        put_pages(table, moved_pages(plan, pair_index), list(zip(starts, parts)), new_pool, sem)

    if patch:

        @pl.when(pair_index >= requests)
        def _():
            page_len = new_pool.shape[1]
            first = lengths[pair_index - requests] - PAGES_HALF * page_len
            for i, offset in enumerate((first, first + STEPS - 1)):
                slot = table[0, offset // page_len]
                copy = pltpu.make_async_copy(parts[-1].at[i], new_pool.at[slot], sem)
                copy.start()
                copy.wait()


def place(table, plan, lengths, parts, starts, base, fixed=None):
    patch = fixed is not None
    parts = list(parts) + [fixed] * patch
    return pl.pallas_call(
        functools.partial(place_kernel, starts=starts, patch=patch),
        out_shape=pltpu.HBM(base.shape, base.dtype),
        in_specs=[SMEM] * 3 + [VMEM] * len(parts) + [HBM],
        out_specs=HBM,
        scratch_shapes=[
            pltpu.SemaphoreType.DMA,
        ],
        input_output_aliases={3 + len(parts): 0},
        compiler_params=params(16),
        name="place",
    )(table, plan, lengths, *parts, *in_hbm(base))


def blank_kernel(out):
    del out


def blank(like):
    return pl.pallas_call(
        blank_kernel,
        out_shape=jax.ShapeDtypeStruct(like.shape, like.dtype),
        out_specs=pl.BlockSpec(memory_space=pl.ANY),
        name="blank",
    )()


def local(
    normed, w_query, b_query, w_key, b_key, w_value, b_value, w_out, pool, page_table, lengths, plan
):
    pair_count = lax.axis_size("pair")
    tp_count = lax.axis_size("tp")
    requests = pair_count // 2
    head = w_key.shape[1]

    planned = plan.T
    opening = collect(page_table, pool[0, 0])
    partial, near, far, pieces = prepare(
        page_table, planned, normed, w_query, w_key, w_value, pool[0, 0], pair_count
    )
    bits = min(JOINT, requests)

    def tie(*values):
        return lax.optimization_barrier(values)

    def migrate(pages, members=range(requests)):
        return lax.ppermute(pages, "pair", [(r + requests, r) for r in members])

    either = lax.axis_index("rep") == 0

    def gather(values):
        return lax.all_to_all(values, "pair", split_axis=0, concat_axis=0, tiled=True)

    def choose(code, step, *values):
        members = [[r for r in range(requests) if code >> r % bits & 1] for code in range(1 << bits)]
        return lax.switch(code, [functools.partial(step, chosen) for chosen in members], *values)

    def some(members, pages):
        return migrate(pages, members) if members else blank(pages)

    def first_step(members, values, pages):
        return lax.cond(either, gather, gather, values), some(members, pages)

    def second_step(members, values, beside, pages):
        return gather(values), migrate(beside), some(members, pages)

    first = migrate(opening)
    sums, far_pages = choose(far, first_step, partial, pieces[1])
    sums, first = tie(sums, first)
    second = migrate(tie(pieces[0], sums)[0])

    frequency = rope_base ** (-(jnp.arange(head // 2, dtype=jnp.float32) * 2.0 / head))
    steps = jnp.minimum(jnp.arange(8, dtype=jnp.int32), STEPS - 1)
    position = (lengths[:, None] + steps[None, :]).astype(jnp.float32)[..., None]
    angles = position * frequency
    cosine = jnp.cos(angles)
    sine = jnp.sin(angles)
    cosine = jnp.concatenate([cosine, cosine], -1)
    sine = jnp.concatenate([-sine, sine], -1)

    packed, new_pool, fixed, *later = attend(
        lengths,
        page_table,
        planned,
        sums,
        b_query.reshape(-1, head),
        b_key[None, :],
        b_value[None, :],
        cosine,
        sine,
        first,
        far_pages,
        pool[0, 0],
    )
    near, packed = tie(near, packed)
    parts, beside, near_pages = choose(near, second_step, packed, later[0], later[2])
    parts, second = tie(parts, second)
    third = migrate(tie(later[1], parts)[0])
    projected = project(parts, w_out, head)
    here = [second, beside, near_pages]
    starts = [FIRST, BESIDE_AT, NEAR_AT]
    new_pool = place(page_table, planned, lengths, here, starts, new_pool, fixed)
    if tp_count == 2:
        projected = projected + lax.ppermute(projected, "tp", [(0, 1), (1, 0)])
    else:
        projected = lax.psum(projected, "tp")
    third, projected = tie(third, projected)
    new_pool = place(page_table, planned, lengths, [third], [THIRD_AT], new_pool)
    return projected, new_pool[None, None]


def solution(mesh):
    return jax.shard_map(
        local,
        mesh=mesh,
        in_specs=(
            P(None, "rep", "pair"),
            P("pair", "tp"),
            P("tp"),
            P("pair", "tp"),
            P("tp"),
            P("pair", "tp"),
            P("tp"),
            P("tp", "pair"),
            P(("rep", "pair"), "tp", None, None, None),
            P(("rep", "pair"), None),
            P("rep"),
            P("rep", None),
        ),
        out_specs=(P(None, "rep", "pair"), P(("rep", "pair"), "tp", None, None, None)),
        check_vma=False,
    )
```

```python
import functools
import math

import jax
import jax.numpy as jnp
from jax import lax
from jax.experimental import pallas as pl
from jax.experimental.pallas import tpu as pltpu
from jax.sharding import PartitionSpec as P

PAGES_HALF = 384
STEPS = 2
SECTION = 64
MOVED_MAX = STEPS * SECTION
FIRST, SECOND, BESIDE, THIRD = 26, 32, 9, 7
NEAR, FAR = 26, 28
BESIDE_AT = FIRST + SECOND
THIRD_AT = BESIDE_AT + BESIDE
NEAR_AT = THIRD_AT + THIRD
FAR_AT = NEAR_AT + NEAR
PIECES = ((FIRST, SECOND), (FAR_AT, FAR))
LATER = ((BESIDE_AT, BESIDE), (THIRD_AT, THIRD), (NEAR_AT, NEAR))
JOINT = 4
CHUNKS = 4
NEG = -1e30

rope_base = 1000000.0

VMEM = pl.BlockSpec(memory_space=pltpu.VMEM)
SMEM = pl.BlockSpec(memory_space=pltpu.SMEM)
HBM = pl.BlockSpec(memory_space=pltpu.HBM)


def in_hbm(*arrays):
    return tuple(pltpu.with_memory_space_constraint(a, pltpu.HBM) for a in arrays)


def params(mib):
    return pltpu.CompilerParams(vmem_limit_bytes=mib * 1024 * 1024)


def moved_pages(plan, request):
    count = plan[0, request]
    for s in range(1, STEPS):
        count = count + plan[s, request]
    return count


def put_pages(table, count, parts, new_pool, sem):
    placed = jnp.int32(0)
    for low, pages in parts:
        here = jnp.clip(count - low, 0, pages.shape[0])

        def start(j, carry):
            slot = table[0, PAGES_HALF + low + j]
            pltpu.make_async_copy(pages.at[j], new_pool.at[slot], sem).start()
            return carry

        lax.fori_loop(0, here, start, 0)
        placed = placed + here

    def wait(j, carry):
        pltpu.make_async_copy(parts[0][1].at[0], new_pool.at[0], sem).wait()
        return carry

    lax.fori_loop(0, placed, wait, 0)


def collect_kernel(table_in, pool, piece, table, sem, page_sem):
    @pl.when(lax.axis_index("pair") >= lax.axis_size("pair") // 2)
    def _():
        table_copy = pltpu.make_async_copy(table_in, table, sem)
        table_copy.start()
        table_copy.wait()

        def start(j, carry):
            pltpu.make_async_copy(pool.at[table[0, j]], piece.at[j], page_sem).start()
            return carry

        lax.fori_loop(0, FIRST, start, 0, unroll=2)
        pltpu.make_async_copy(pool.at[pl.ds(0, FIRST)], piece, page_sem).wait()


def collect(table, pool):
    return pl.pallas_call(
        collect_kernel,
        out_shape=pltpu.VMEM((FIRST,) + pool.shape[1:], pool.dtype),
        in_specs=[HBM] * 2,
        out_specs=VMEM,
        scratch_shapes=[
            pltpu.SMEM(table.shape, table.dtype),
            pltpu.SemaphoreType.DMA,
            pltpu.SemaphoreType.DMA,
        ],
        compiler_params=params(16),
        name="collect",
    )(*in_hbm(table, pool))


def prepare_kernel(w_query, table_in, plan_in, normed_in, w_key, w_value, pool, partial, near, far, *refs):
    pieces, (table, plan, normed, weights, index_sems, sems, page_sems) = refs[:-7], refs[-7:]
    pairs = partial.shape[0]
    requests = pairs // 2
    head = w_key.shape[1]
    wide = w_query.shape[1]
    table_copy = pltpu.make_async_copy(table_in, table, index_sems.at[0])
    plan_copy = pltpu.make_async_copy(plan_in, plan, index_sems.at[1])
    table_copy.start()
    plan_copy.start()
    loads = [
        pltpu.make_async_copy(normed_in, normed, sems.at[0]),
        pltpu.make_async_copy(w_key, weights.at[:, :head], sems.at[1]),
        pltpu.make_async_copy(w_value, weights.at[:, head:], sems.at[2]),
    ]
    for copy in loads:
        copy.start()
    table_copy.wait()

    @pl.when(lax.axis_index("pair") >= requests)
    def _():
        for i, (low, size) in enumerate(PIECES):

            def start(j, carry):
                pltpu.make_async_copy(pool.at[table[0, low + j]], pieces[i].at[j], page_sems.at[i]).start()
                return carry

            lax.fori_loop(0, size, start, 0, unroll=2)

    plan_copy.wait()
    bits = min(JOINT, requests)
    for code, bound in ((near, NEAR_AT), (far, FAR_AT)):
        total = jnp.int32(0)
        for bit in range(bits):
            most = moved_pages(plan, bit)
            for r in range(bit + bits, requests, bits):
                most = jnp.maximum(most, moved_pages(plan, r))
            total = total + jnp.where(most > bound, 1 << bit, 0)
        code[0] = total
    for copy in loads:
        copy.wait()
    hidden = jnp.concatenate([normed[s].astype(jnp.float32) for s in range(STEPS)], 0).astype(jnp.bfloat16)
    query = jnp.dot(hidden, w_query[...], preferred_element_type=jnp.float32)
    rest = jnp.dot(hidden, weights[...], preferred_element_type=jnp.float32)
    for r in range(requests):
        lines = [slice(s * requests + r, s * requests + r + 1) for s in range(STEPS)]
        query_lines = jnp.concatenate([query[line] for line in lines], 0)
        rest_lines = jnp.concatenate([rest[line] for line in lines], 0)
        for p in range(r, pairs, requests):
            partial[p, :, :wide] = query_lines
            partial[p, :, wide:] = rest_lines

    @pl.when(lax.axis_index("pair") >= requests)
    def _():
        for i, (_, size) in enumerate(PIECES):
            pltpu.make_async_copy(pool.at[pl.ds(0, size)], pieces[i], page_sems.at[i]).wait()


def prepare(table, plan, normed, w_query, w_key, w_value, pool, pairs):
    page = pool.shape[1:]
    wide = w_query.shape[1] + 2 * w_key.shape[1]
    partial, near, far, *pieces = pl.pallas_call(
        prepare_kernel,
        out_shape=(jax.ShapeDtypeStruct((pairs, STEPS, wide), jnp.float32),)
        + (jax.ShapeDtypeStruct((1,), jnp.int32),) * 2
        + tuple(pltpu.VMEM((size,) + page, pool.dtype) for _, size in PIECES),
        in_specs=[VMEM] + [HBM] * 6,
        out_specs=(VMEM, SMEM, SMEM) + (VMEM,) * len(PIECES),
        scratch_shapes=[
            pltpu.SMEM(table.shape, table.dtype),
            pltpu.SMEM(plan.shape, plan.dtype),
            pltpu.VMEM(normed.shape, normed.dtype),
            pltpu.VMEM((w_key.shape[0], 2 * w_key.shape[1]), w_key.dtype),
            pltpu.SemaphoreType.DMA((2,)),
            pltpu.SemaphoreType.DMA((3,)),
            pltpu.SemaphoreType.DMA((len(PIECES),)),
        ],
        compiler_params=params(16),
        name="prepare",
    )(w_query, *in_hbm(table, plan, normed, w_key, w_value, pool))
    return partial, near.reshape(()), far.reshape(()), pieces


def page_order(table, slots):
    slot = lax.broadcasted_iota(jnp.int32, (slots, slots), 0)
    holds = jnp.where(slot == table, 1.0, 0.0).astype(jnp.bfloat16)
    index = lax.broadcasted_iota(jnp.int32, (8, slots), 1)
    digit = lax.broadcasted_iota(jnp.int32, (8, slots), 0)
    digits = jnp.where(digit == 0, index // 16, jnp.where(digit == 1, index % 16, 0))
    digits = digits.astype(jnp.float32).astype(jnp.bfloat16)
    return lax.dot_general(digits, holds, (((1,), (1,)), ((), ())), preferred_element_type=jnp.float32)


def attention_kernel(
    lengths, table_in, plan_in, sums, b_query, b_key, b_value, cosine, sine, early, far, pool,
    copies_out, new_pool, fixed, *refs
):
    pieces, refs = refs[: len(LATER)], refs[len(LATER) :]
    held, score, packed, table, slots_of, plan, sems, out_sems, send_sem, page_sem = refs
    slots, page_len, _ = held.shape
    per = slots // CHUNKS
    table_copy = pltpu.make_async_copy(table_in, table, sems.at[CHUNKS])
    table_copy.start()
    slots_copy = pltpu.make_async_copy(table_in, slots_of, sems.at[CHUNKS + 1])
    slots_copy.start()
    plan_copy = pltpu.make_async_copy(plan_in, plan, sems.at[CHUNKS + 2])
    plan_copy.start()
    copies = []
    for c in range(CHUNKS):
        part = pl.ds(c * per, per)
        copies.append(pltpu.make_async_copy(pool.at[part], held.at[part], sems.at[c]))
        copies[-1].start()
    requests = sums.shape[0] // 2
    group, head = b_query.shape
    rows = STEPS * group
    pair_index = lax.axis_index("pair")
    is_source = pair_index >= requests
    request = jnp.where(is_source, pair_index - requests, pair_index)
    half_tokens = PAGES_HALF * page_len
    limit = jnp.where(is_source, lengths[request] - half_tokens, half_tokens)

    blocks = CHUNKS // 2
    block = slots // blocks
    width = block * page_len
    table_copy.wait()
    digits = page_order(table[...], slots)
    digits = jnp.concatenate(
        [digits[d : d + 1, c * block : (c + 1) * block] for d in range(2) for c in range(blocks)], 0
    ).astype(jnp.bfloat16)
    spread = lax.broadcasted_iota(jnp.int32, (block, width), 1) // page_len
    spread = jnp.where(spread == lax.broadcasted_iota(jnp.int32, (block, width), 0), 1.0, 0.0)
    digits = jnp.dot(digits, spread.astype(jnp.bfloat16), preferred_element_type=jnp.float32)
    tokens = (digits[:blocks] * 16.0 + digits[blocks:]).astype(jnp.int32) * page_len
    tokens = tokens + lax.broadcasted_iota(jnp.int32, (blocks, width), 1) % page_len

    total = sums[0]
    for p in range(1, sums.shape[0]):
        total = total + sums[p]
    query = jnp.concatenate(
        [total[s : s + 1, h * head : (h + 1) * head] for s in range(STEPS) for h in range(group)], 0
    )
    query = query + jnp.concatenate([b_query[...]] * STEPS, 0)
    cos_new = cosine[request]
    sin_new = sine[request]
    row = lax.broadcasted_iota(jnp.int32, (rows, head), 0)
    cos_rows = jnp.where(row < group, cos_new[0:1], cos_new[1:2])
    sin_rows = jnp.where(row < group, sin_new[0:1], sin_new[1:2])
    query = (query * cos_rows + pltpu.roll(query, head // 2, 1) * sin_rows).astype(jnp.bfloat16)
    key_new = total[:, group * head : (group + 1) * head] + b_key[...]
    key_new = jnp.concatenate([key_new, jnp.zeros((8 - STEPS, head), jnp.float32)], 0)
    key_new = key_new * cos_new + pltpu.roll(key_new, head // 2, 1) * sin_new
    key_new = key_new.astype(jnp.bfloat16).astype(jnp.float32)
    value_new = total[:, (group + 1) * head :] + b_value[...]
    value_new = value_new.astype(jnp.bfloat16).astype(jnp.float32)
    scale = 1.0 / math.sqrt(head)

    column = lax.broadcasted_iota(jnp.int32, (rows, 1), 0)
    query_wide = query.astype(jnp.float32)
    fresh = []
    for s in range(STEPS):
        dots = jnp.sum(query_wide * key_new[s : s + 1], 1, keepdims=True) * scale
        seen = jnp.logical_and(is_source, column >= s * group)
        fresh.append((jnp.where(seen, dots, NEG), seen))
    row_max = jnp.maximum(fresh[0][0], fresh[1][0])

    stores = []
    for c in range(blocks):
        for i in range(c * CHUNKS // blocks, (c + 1) * CHUNKS // blocks):
            copies[i].wait()
            part = pl.ds(i * per, per)
            stores.append(pltpu.make_async_copy(held.at[part], new_pool.at[part], out_sems.at[i]))
            stores[-1].start()
        keys = held[c * block : (c + 1) * block, :, :head].reshape(width, head)
        part = lax.dot_general(query, keys, (((1,), (1,)), ((), ())), preferred_element_type=jnp.float32)
        part = jnp.where(tokens[c : c + 1] < limit, part * scale, NEG)
        score[:, c * width : (c + 1) * width] = part
        row_max = jnp.maximum(row_max, jnp.max(part, 1, keepdims=True))
    row_sum = jnp.zeros((rows, 1), jnp.float32)
    out = jnp.zeros((rows, head), jnp.float32)
    for s in range(STEPS):
        weight = jnp.where(fresh[s][1], jnp.exp(fresh[s][0] - row_max), 0.0)
        row_sum = row_sum + weight
        out = out + weight.astype(jnp.bfloat16).astype(jnp.float32) * value_new[s : s + 1]
    for c in range(blocks):
        weight = jnp.exp(score[:, c * width : (c + 1) * width] - row_max)
        row_sum = row_sum + jnp.sum(weight, 1, keepdims=True)
        values = held[c * block : (c + 1) * block, :, head:].reshape(width, head)
        out = out + jnp.dot(weight.astype(jnp.bfloat16), values, preferred_element_type=jnp.float32)

    diagonal = lax.broadcasted_iota(jnp.int32, (rows, head), 1) == row
    for i in range(rows):
        packed[:, i * head : (i + 1) * head] = out[i : i + 1]
    shifted = lax.broadcasted_iota(jnp.int32, (rows, head), 1) == row + rows
    packed[:, rows * head :] = jnp.sum(
        jnp.where(diagonal, row_max, 0.0) + jnp.where(shifted, row_sum, 0.0), 0, keepdims=True
    )
    sends = [
        pltpu.make_async_copy(packed, copies_out.at[p], send_sem.at[p]) for p in range(copies_out.shape[0])
    ]
    for send in sends:
        send.start()

    slots_copy.wait()

    @pl.when(is_source)
    def _():
        for piece, (low, size) in zip(pieces, LATER):

            def take(j, carry):
                piece[j] = held[slots_of[0, low + j]]
                return carry

            lax.fori_loop(0, size, take, 0)
        page_row = lax.broadcasted_iota(jnp.int32, (page_len, 2 * head), 0)
        entries = jnp.concatenate([key_new[:STEPS], value_new], 1)
        offsets = [limit + s for s in range(STEPS)]
        homes = [slots_of[0, offset // page_len] for offset in offsets]
        for i, slot in enumerate((homes[0], homes[-1])):
            page = held[slot].astype(jnp.float32)
            for s, offset in enumerate(offsets):
                here = jnp.logical_and(homes[s] == slot, page_row == offset % page_len)
                page = jnp.where(here, entries[s : s + 1], page)
            fixed[i] = page.astype(held.dtype)

    plan_copy.wait()
    for store in stores:
        store.wait()

    @pl.when(jnp.logical_not(is_source))
    def _():
        put_pages(slots_of, moved_pages(plan, request), [(0, early), (FAR_AT, far)], new_pool, page_sem)

    for send in sends:
        send.wait()


def attend(lengths, table, plan, sums, b_query, b_key, b_value, cosine, sine, early, far, pool):
    group, head = b_query.shape
    rows = STEPS * group
    page = pool.shape[1:]
    return pl.pallas_call(
        attention_kernel,
        out_shape=(
            pltpu.HBM((sums.shape[0], 1, (rows + 1) * head), jnp.float32),
            pltpu.HBM(pool.shape, pool.dtype),
            jax.ShapeDtypeStruct((2,) + page, pool.dtype),
        )
        + tuple(pltpu.VMEM((size,) + page, pool.dtype) for _, size in LATER),
        in_specs=[SMEM, HBM, HBM] + [VMEM] * 8 + [HBM],
        out_specs=(HBM, HBM, VMEM) + (VMEM,) * len(LATER),
        scratch_shapes=[
            pltpu.VMEM(pool.shape, pool.dtype),
            pltpu.VMEM((rows, pool.shape[0] * pool.shape[1]), jnp.float32),
            pltpu.VMEM((1, (rows + 1) * head), jnp.float32),
            pltpu.VMEM(table.shape, table.dtype),
            pltpu.SMEM(table.shape, table.dtype),
            pltpu.SMEM(plan.shape, plan.dtype),
            pltpu.SemaphoreType.DMA((CHUNKS + 3,)),
            pltpu.SemaphoreType.DMA((CHUNKS,)),
            pltpu.SemaphoreType.DMA((sums.shape[0],)),
            pltpu.SemaphoreType.DMA,
        ],
        compiler_params=params(24),
        name="attend",
    )(
        lengths, *in_hbm(table, plan), sums, b_query, b_key, b_value, cosine, sine, early, far, *in_hbm(pool)
    )


def project_kernel(head, parts, w_out, out):
    pairs, _, width = parts.shape
    rows = width // head - 1
    group = rows // STEPS
    requests = pairs // 2
    lane = lax.broadcasted_iota(jnp.int32, (rows, head), 1)
    row = lax.broadcasted_iota(jnp.int32, (rows, head), 0)

    def column(part, shift):
        line = parts[part, :, rows * head :]
        return jnp.sum(jnp.where(lane == row + shift, line, 0.0), 1, keepdims=True)

    lines = [[] for _ in range(STEPS)]
    for r in range(requests):
        tops = [column(part, 0) for part in (r, r + requests)]
        sums = [column(part, rows) for part in (r, r + requests)]
        top = jnp.maximum(*tops)
        weights = [jnp.exp(one - top) for one in tops]
        total = weights[0] * sums[0] + weights[1] * sums[1]
        shares = [weight / total for weight in weights]
        for s in range(STEPS):
            heads = []
            for i in range(s * group, (s + 1) * group):
                here = slice(i * head, (i + 1) * head)
                heads.append(
                    shares[0][i : i + 1] * parts[r, :, here] + shares[1][i : i + 1] * parts[r + requests, :, here]
                )
            lines[s].append(jnp.concatenate(heads, 1))
    attended = jnp.concatenate(sum(lines, []), 0).astype(jnp.bfloat16)
    result = jnp.dot(attended, w_out[...], preferred_element_type=jnp.float32)
    for s in range(STEPS):
        out[s] = result[s * requests : (s + 1) * requests]


def project(parts, w_out, head):
    return pl.pallas_call(
        functools.partial(project_kernel, head),
        out_shape=jax.ShapeDtypeStruct((STEPS, parts.shape[0] // 2, w_out.shape[1]), jnp.float32),
        in_specs=[VMEM, VMEM],
        out_specs=VMEM,
        compiler_params=params(16),
        name="project",
    )(parts, w_out)


def place_kernel(table, plan, lengths, *refs, starts, patch):
    parts, (base, new_pool, sem) = refs[:-3], refs[-3:]
    del base
    pair_index = lax.axis_index("pair")
    requests = lengths.shape[0]

    @pl.when(pair_index < requests)
    def _():
        put_pages(table, moved_pages(plan, pair_index), list(zip(starts, parts)), new_pool, sem)

    if patch:

        @pl.when(pair_index >= requests)
        def _():
            page_len = new_pool.shape[1]
            first = lengths[pair_index - requests] - PAGES_HALF * page_len
            for i, offset in enumerate((first, first + STEPS - 1)):
                slot = table[0, offset // page_len]
                copy = pltpu.make_async_copy(parts[-1].at[i], new_pool.at[slot], sem)
                copy.start()
                copy.wait()


def place(table, plan, lengths, parts, starts, base, fixed=None):
    patch = fixed is not None
    parts = list(parts) + [fixed] * patch
    return pl.pallas_call(
        functools.partial(place_kernel, starts=starts, patch=patch),
        out_shape=pltpu.HBM(base.shape, base.dtype),
        in_specs=[SMEM] * 3 + [VMEM] * len(parts) + [HBM],
        out_specs=HBM,
        scratch_shapes=[
            pltpu.SemaphoreType.DMA,
        ],
        input_output_aliases={3 + len(parts): 0},
        compiler_params=params(16),
        name="place",
    )(table, plan, lengths, *parts, *in_hbm(base))


def blank_kernel(out):
    del out


def blank(like):
    return pl.pallas_call(
        blank_kernel,
        out_shape=jax.ShapeDtypeStruct(like.shape, like.dtype),
        out_specs=pl.BlockSpec(memory_space=pl.ANY),
        name="blank",
    )()


def local(
    normed, w_query, b_query, w_key, b_key, w_value, b_value, w_out, pool, page_table, lengths, plan
):
    pair_count = lax.axis_size("pair")
    tp_count = lax.axis_size("tp")
    requests = pair_count // 2
    head = w_key.shape[1]

    planned = plan.T
    opening = collect(page_table, pool[0, 0])
    partial, near, far, pieces = prepare(
        page_table, planned, normed, w_query, w_key, w_value, pool[0, 0], pair_count
    )
    bits = min(JOINT, requests)

    def tie(*values):
        return lax.optimization_barrier(values)

    def migrate(pages, members=range(requests)):
        return lax.ppermute(pages, "pair", [(r + requests, r) for r in members])

    either = lax.axis_index("rep") == 0

    def gather(values):
        return lax.all_to_all(values, "pair", split_axis=0, concat_axis=0, tiled=True)

    def choose(code, step, *values):
        members = [[r for r in range(requests) if code >> r % bits & 1] for code in range(1 << bits)]
        return lax.switch(code, [functools.partial(step, chosen) for chosen in members], *values)

    def some(members, pages):
        return migrate(pages, members) if members else blank(pages)

    def first_step(members, values, pages):
        return lax.cond(either, gather, gather, values), some(members, pages)

    def second_step(members, values, beside, pages):
        return gather(values), migrate(beside), some(members, pages)

    first = migrate(opening)
    sums, far_pages = choose(far, first_step, partial, pieces[1])
    sums, first = tie(sums, first)
    second = migrate(tie(pieces[0], sums)[0])

    frequency = rope_base ** (-(jnp.arange(head // 2, dtype=jnp.float32) * 2.0 / head))
    steps = jnp.minimum(jnp.arange(8, dtype=jnp.int32), STEPS - 1)
    position = (lengths[:, None] + steps[None, :]).astype(jnp.float32)[..., None]
    angles = position * frequency
    cosine = jnp.cos(angles)
    sine = jnp.sin(angles)
    cosine = jnp.concatenate([cosine, cosine], -1)
    sine = jnp.concatenate([-sine, sine], -1)

    packed, new_pool, fixed, *later = attend(
        lengths,
        page_table,
        planned,
        sums,
        b_query.reshape(-1, head),
        b_key[None, :],
        b_value[None, :],
        cosine,
        sine,
        first,
        far_pages,
        pool[0, 0],
    )
    near, packed = tie(near, packed)
    parts, beside, near_pages = choose(near, second_step, packed, later[0], later[2])
    parts, second = tie(parts, second)
    third = migrate(tie(later[1], parts)[0])
    projected = project(parts, w_out, head)
    here = [second, beside, near_pages]
    starts = [FIRST, BESIDE_AT, NEAR_AT]
    new_pool = place(page_table, planned, lengths, here, starts, new_pool, fixed)
    if tp_count == 2:
        projected = projected + lax.ppermute(projected, "tp", [(0, 1), (1, 0)])
    else:
        projected = lax.psum(projected, "tp")
    third, projected = tie(third, projected)
    new_pool = place(page_table, planned, lengths, [third], [THIRD_AT], new_pool)
    return projected, new_pool[None, None]


def solution(mesh):
    return jax.shard_map(
        local,
        mesh=mesh,
        in_specs=(
            P(None, "rep", "pair"),
            P("pair", "tp"),
            P("tp"),
            P("pair", "tp"),
            P("tp"),
            P("pair", "tp"),
            P("tp"),
            P("tp", "pair"),
            P(("rep", "pair"), "tp", None, None, None),
            P(("rep", "pair"), None),
            P("rep"),
            P("rep", None),
        ),
        out_specs=(P(None, "rep", "pair"), P(("rep", "pair"), "tp", None, None, None)),
        check_vma=False,
    )
```
